32 devices in a mesh: lat: 16 (over z, y, core), rad: 2 (over x).
Axes of the slice: x: 2, y: 2, z: 4, core: 2. Of those that a mesh axis runs over, the one named last changes fastest.
Arguments:
- tracer_values: float32 [16, 2, 3, 49152], P('lat', 'rad'), may hold values from 0 to 1
- tracer_cell: int32 [16, 2, 49152], P('lat', 'rad'), may hold values from 0 to 18431, as said below
- tracer_count: int32 [16, 2, 3], P('lat', 'rad'), may hold values from 2048 to 16384, as said below
- base_viscosity: float32 [192, 24, 128], P('lat', 'rad'), may hold values from 0.3 to 3
- velocity: float32 [3, 192, 24, 128], P(None, 'lat', 'rad'), may hold values from -6 to 6
- forcing: float32 [3, 192, 24, 128], P(None, 'lat', 'rad'), may hold values from -4 to 4
Outputs:
- smoothed: float32 [3, 192, 24, 128], P(None, 'lat', 'rad')
- composition: float32 [2, 192, 24, 128], P(None, 'lat', 'rad')
The draws below stay inside these ranges and needn't reach their ends.
Inputs may be any that keep to these rules, and one draw needn't show every extreme that they name: `tracer_count`: in group g of a device (0: going to the device one lower along lat, 1: staying, 2: going to the device one higher) slots 0 to count - 1 hold tracers and the rest are empty; for every group some device has all 16384 slots in use (used slots, live or not). `tracer_cell`: index ((x * 12) + r) * 128 + y of a cell in the block of the device the tracer goes to, at the same rad index; tracers of slots below 16384 land in the last 2 x-planes of their device, tracers of slots from 32768 on in the first 2 x-planes.
All inputs are finite; a program needn't handle non-finite values.
Results may differ from the reference program's by a relative error of at most 0.0003.
The reference program's roundings to bfloat16 on the way (of `tracer_loads`) count: a program that leaves them out, or rounds other values in their place, can miss the bound.
Values sent between devices are 32-bit elements; how exact they have to be, the bound alone decides.
No kernel may reach another device: no remote copies, remote signals or barrier semaphores. Data moves between devices by JAX's collectives and lax.ppermute only.
A program may use at most 64 MiB of HBM per device.

```python
import math
import jax
import jax.numpy as jnp
from jax import lax

CX = 12
CR = 12
NY = 128
CAP = 16384
MIG = 2
SWEEPS = 2
LAT_DEVICES = 16
RAD_DEVICES = 2
NX = 192
NR = 24
SLOTS = 49152


def draw_tracer_cell(key, part):
    key_any, key_lower, key_upper, key_radial, key_side = jax.random.split(key, 5)
    array_shape = (LAT_DEVICES, RAD_DEVICES, 3 * CAP)
    slot_index = lax.broadcasted_iota(jnp.int32, array_shape, 2)
    group_index = slot_index // CAP
    plane_any = jax.random.randint(key_any, array_shape, 0, CX)
    plane_lower = jax.random.randint(key_lower, array_shape, CX - MIG, CX)
    plane_upper = jax.random.randint(key_upper, array_shape, 0, MIG)
    plane_index = jnp.where(group_index == 0, plane_lower, jnp.where(group_index == 2, plane_upper, plane_any))
    radial_index = jax.random.randint(key_radial, array_shape, 0, CR)
    side_index = jax.random.randint(key_side, array_shape, 0, NY)
    return ((plane_index * CR + radial_index) * NY + side_index).astype(jnp.int32)


def draw_tracer_count(key, part):
    key_base, key_heavy, key_band, key_full = jax.random.split(key, 4)
    count_shape = (LAT_DEVICES, RAD_DEVICES, 3)
    regular = jax.random.randint(key_base, count_shape, CAP // 8, CAP // 2 + 1)
    heavy_count = jax.random.randint(key_heavy, count_shape, 3 * CAP // 4, CAP + 1)
    band_start = jax.random.randint(key_band, (), 0, LAT_DEVICES)
    lateral = lax.broadcasted_iota(jnp.int32, count_shape, 0)
    in_band = (lateral - band_start) % LAT_DEVICES < max(1, LAT_DEVICES // 8)
    counts = jnp.where(in_band, heavy_count, regular)
    radial_full = jax.random.randint(key_full, (), 0, RAD_DEVICES)
    counts = counts.at[band_start, radial_full, :].set(CAP)
    light_device = (band_start + LAT_DEVICES // 2) % LAT_DEVICES
    counts = counts.at[light_device, 0, 0].set(CAP // 8)
    return counts.astype(jnp.int32)


def draw_forcing(key, part):
    key_noise = jax.random.fold_in(key, 0)
    field_shape = (3, NX, NR, NY)
    noise = jax.random.normal(key_noise, field_shape, jnp.float32)
    return jnp.clip(0.5 * noise, -4.0, 4.0).astype(jnp.float32)


def level_of(rng, extent, pieces, least, top_value):
    level, own = 1.0, jax.random.fold_in(rng, 6)
    for dim, blocks in pieces:
        steps = jnp.exp(jax.random.uniform(jax.random.fold_in(own, dim), (blocks,), jnp.float32, least / len(pieces), top_value / len(pieces)))
        level = level * jnp.repeat(steps, extent[dim] // blocks).reshape([-1 if axis == dim else 1 for axis in range(len(extent))])
    return level


def bell_draw(rng, dims, scale, limit, pieces=(), dtype=jnp.bfloat16):
    array = jax.random.normal(rng, dims, jnp.float32) * scale
    if len(pieces) > 0:
        array = level_of(rng, dims, pieces, -0.22, 0.18) * array
    return jnp.clip(array, min=-limit, max=limit).astype(dtype)


def setup_inputs(seed: int = 0) -> dict:
    key_of = jax.random.split(jax.random.key(seed), 7)
    tracer_values = jnp.clip(1.0 * jax.random.uniform(key_of[0], (LAT_DEVICES, RAD_DEVICES, 3, SLOTS), jnp.float32) ** level_of(key_of[0], (LAT_DEVICES, RAD_DEVICES, 3, SLOTS), ((0, 16), (1, 2)), -0.2, 0.2), 0.0, 1.0)
    tracer_cell = draw_tracer_cell(jax.random.fold_in(key_of[6], 71), 0)
    tracer_count = draw_tracer_count(jax.random.fold_in(key_of[6], 71), 0)
    base_viscosity = jnp.clip(jnp.exp(math.log(3.0) - 2.3025851 * jax.random.uniform(key_of[3], (NX, NR, NY), jnp.float32) ** level_of(key_of[3], (NX, NR, NY), ((0, 16), (1, 2)), -0.2, 0.2)), 0.3, 3.0)
    velocity = bell_draw(key_of[4], (3, NX, NR, NY), 1.0, 6.0, ((1, 16), (2, 2)), jnp.float32)
    forcing = draw_forcing(jax.random.fold_in(key_of[6], 71), 0)
    return {"tracer_values": tracer_values, "tracer_cell": tracer_cell, "tracer_count": tracer_count, "base_viscosity": base_viscosity, "velocity": velocity, "forcing": forcing}


LATERAL = 0.015625
RADIAL = 32.0
BUOYANCY = 0.1
PRIOR_WEIGHT = 0.5
CONTRAST_BASALT = 2.3
CONTRAST_MELT = 1.5


def face_terms(viscosity):
    padded = jnp.pad(viscosity, 1)
    face_west = LATERAL * 0.5 * (viscosity + padded[:-2, 1:-1, 1:-1])
    face_east = LATERAL * 0.5 * (viscosity + padded[2:, 1:-1, 1:-1])
    face_south = LATERAL * 0.5 * (viscosity + padded[1:-1, 1:-1, :-2])
    face_north = LATERAL * 0.5 * (viscosity + padded[1:-1, 1:-1, 2:])
    face_below = RADIAL * 0.5 * (viscosity + padded[1:-1, :-2, 1:-1])
    face_above = RADIAL * 0.5 * (viscosity + padded[1:-1, 2:, 1:-1])
    return face_west, face_east, face_south, face_north, face_below, face_above


def line_solve(diagonal, lower_band, upper_band, right_side):
    diag_rows = jnp.moveaxis(diagonal, 1, 0)
    lower_rows = jnp.moveaxis(lower_band, 1, 0)
    upper_rows = jnp.moveaxis(upper_band, 1, 0)
    right_rows = jnp.moveaxis(right_side, 2, 0)

    def forward(carried, inputs):
        upper_prev, right_prev = carried
        diag_row, lower_row, upper_row, right_row = inputs
        pivot_row = diag_row - lower_row * upper_prev
        upper_next = upper_row / pivot_row
        right_next = (right_row - lower_row * right_prev) / pivot_row
        return (upper_next, right_next), (upper_next, right_next)

    start_state = (jnp.zeros((NX, NY), jnp.float32), jnp.zeros((3, NX, NY), jnp.float32))
    final_state, eliminated = lax.scan(forward, start_state, (diag_rows, lower_rows, upper_rows, right_rows))

    def backward(solved_next, inputs):
        upper_row, right_row = inputs
        solved = right_row - upper_row * solved_next
        return solved, solved

    final_value, solved_rows = lax.scan(backward, jnp.zeros((3, NX, NY), jnp.float32), eliminated, reverse=True)
    return jnp.moveaxis(solved_rows, 0, 2)


def reference(tracer_values, tracer_cell, tracer_count, base_viscosity, velocity, forcing):
    grid_shape = (LAT_DEVICES, RAD_DEVICES, SLOTS)
    slot_index = lax.broadcasted_iota(jnp.int32, grid_shape, 2)
    lateral = lax.broadcasted_iota(jnp.int32, grid_shape, 0)
    radial = lax.broadcasted_iota(jnp.int32, grid_shape, 1)
    group_index = slot_index // CAP
    within = slot_index - group_index * CAP
    count_slot = jnp.take_along_axis(tracer_count, group_index, axis=2)
    target = lateral + group_index - 1
    is_valid = (within < count_slot) & (target >= 0) & (target < LAT_DEVICES)
    weight = jnp.where(is_valid, 0.5 + tracer_values[:, :, 0, :], jnp.float32(0.0))
    rounded = jnp.stack([weight, weight * tracer_values[:, :, 1, :], weight * tracer_values[:, :, 2, :]]).astype(jnp.bfloat16)
    rounded = lax.optimization_barrier(rounded)
    tracer_loads = rounded.astype(jnp.float32)
    column_x = jnp.clip(target, 0, LAT_DEVICES - 1) * CX + tracer_cell // (CR * NY)
    column_r = radial * CR + (tracer_cell // NY) % CR
    column_y = tracer_cell % NY
    flat_cell = ((column_x * NR + column_r) * NY + column_y).astype(jnp.int32).reshape(-1)
    cell_sums = jax.ops.segment_sum(tracer_loads.reshape(3, -1).T, flat_cell, num_segments=NX * NR * NY)
    cell_sums = cell_sums.T.reshape(3, NX, NR, NY)
    total_weight = cell_sums[0] + PRIOR_WEIGHT
    basalt_share = cell_sums[1] / total_weight
    melt_share = cell_sums[2] / total_weight
    viscosity = base_viscosity * jnp.exp(CONTRAST_BASALT * basalt_share - CONTRAST_MELT * melt_share)
    face_west, face_east, face_south, face_north, face_below, face_above = face_terms(viscosity)
    diagonal = face_west + face_east + face_south + face_north + face_below + face_above
    source = jnp.concatenate([forcing[:2], (forcing[2] - BUOYANCY * basalt_share)[None]], 0)
    radial_index = lax.broadcasted_iota(jnp.int32, (NX, NR, NY), 1)
    lower_band = -face_below
    upper_band = jnp.where(radial_index < NR - 1, -face_above, jnp.float32(0.0))
    current = velocity
    for sweep_index in range(SWEEPS):
        padded = jnp.pad(current, ((0, 0), (1, 1), (0, 0), (1, 1)))
        right_side = source + face_west * padded[:, :-2, :, 1:-1] + face_east * padded[:, 2:, :, 1:-1] + face_south * padded[:, 1:-1, :, :-2] + face_north * padded[:, 1:-1, :, 2:]
        current = line_solve(diagonal, lower_band, upper_band, right_side)
    composition = jnp.stack([basalt_share, melt_share])
    return current, composition
```

```python
import functools

import jax
import jax.numpy as jnp
from jax import lax
from jax.experimental import pallas as pl
from jax.experimental.pallas import tpu as pltpu
from jax.sharding import PartitionSpec as P

SWEEPS = 2
MIGRATION_PLANES = 2

LATERAL = 0.015625
RADIAL = 32.0
BUOYANCY = 0.1
PRIOR_WEIGHT = 0.5
CONTRAST_BASALT = 2.3
CONTRAST_MELT = 1.5

BF16_ROWS = 16


def round_up(value, multiple):
    return -(-value // multiple) * multiple


def split_index(index, count):
    if count & (count - 1) == 0:
        return lax.shift_right_logical(index, count.bit_length() - 1), index & (count - 1)
    quotient = lax.div(index, count)
    return quotient, index - quotient * count


def payload_sections(cells_radial):
    pair = MIGRATION_PLANES * cells_radial
    starts = [0, 3 * pair, 6 * pair, 9 * pair, 10 * pair]
    return starts, round_up(10 * pair + 3 * cells_radial, 8)


def spread_row(row):
    return jnp.broadcast_to(row, (BF16_ROWS, row.shape[1])).astype(jnp.bfloat16)


def hot_tiles(index, row_total):
    lane_total = index.shape[1]
    iota = lax.broadcasted_iota(jnp.int32, (BF16_ROWS, lane_total), 0)
    return [
        index == (iota + first).astype(jnp.float32).astype(jnp.bfloat16)
        for first in range(0, row_total, BF16_ROWS)
    ]


def hot_product(loads, high, low, high_rows, low_rows):
    left, right = [], []
    zero = jnp.zeros((BF16_ROWS, high.shape[1]), jnp.bfloat16)
    one = jnp.ones((BF16_ROWS, high.shape[1]), jnp.bfloat16)
    for row in range(high.shape[0]):
        pick = slice(row, row + 1)
        high_masks = hot_tiles(spread_row(high[pick]), high_rows)
        low_masks = hot_tiles(spread_row(low[pick]), low_rows)
        spread = [spread_row(load[pick]) for load in loads]
        left.append(
            jnp.concatenate(
                [jnp.where(mask, load, zero) for load in spread for mask in high_masks], 0
            )
        )
        right.append(jnp.concatenate([jnp.where(mask, one, zero) for mask in low_masks], 0))
    return lax.dot_general(
        jnp.concatenate(left, 1),
        jnp.concatenate(right, 1),
        (((1,), (1,)), ((), ())),
        preferred_element_type=jnp.float32,
    )


def tracer_kernel(
    block_rows,
    counts_ref,
    values_ref,
    cells_ref,
    base_ref,
    velocity_ref,
    forcing_ref,
    stay_ref,
    first_ref,
    second_ref,
    stay_sums,
    moved_sums,
    payload,
):
    cells_lateral, cells_radial, cells_side = base_ref.shape
    plane_total = cells_lateral * cells_radial
    half_planes = plane_total // 2
    half_rows = round_up(half_planes, BF16_ROWS)
    moved_planes = MIGRATION_PLANES * cells_radial
    moved_rows = round_up(moved_planes, BF16_ROWS)
    lane_total = values_ref.shape[2]
    group_rows = values_ref.shape[1] // 3
    stay_sums[...] = jnp.zeros_like(stay_sums)
    moved_sums[...] = jnp.zeros_like(moved_sums)

    def loads_of(group, first_row):
        rows = pl.ds(pl.multiple_of(group * group_rows + first_row, block_rows), block_rows)
        shape = (block_rows, lane_total)
        slot = (first_row + lax.broadcasted_iota(jnp.int32, shape, 0)) * lane_total
        slot = slot + lax.broadcasted_iota(jnp.int32, shape, 1)
        weight = jnp.where(
            slot < counts_ref[0, 0, group], 0.5 + values_ref[0, rows, :], jnp.float32(0.0)
        )
        loads = [weight, weight * values_ref[1, rows, :], weight * values_ref[2, rows, :]]
        plane, side = split_index(cells_ref[rows, :], cells_side)
        return loads, plane, side

    def step(index, carried):
        first_row = index * block_rows
        loads, plane, side = loads_of(1, first_row)
        upper = plane >= half_planes
        high = jnp.where(upper, plane - half_planes, plane).astype(jnp.float32)
        low = jnp.where(upper, side + cells_side, side).astype(jnp.float32)
        stay_sums[...] += hot_product(loads, high, low, half_rows, 2 * cells_side)
        for slot, group in enumerate((0, 2)):
            loads, plane, side = loads_of(group, first_row)
            if group == 0:
                plane = plane - (plane_total - moved_planes)
            moved_sums[slot] += hot_product(
                loads, plane.astype(jnp.float32), side.astype(jnp.float32), moved_rows, cells_side
            )
        return carried

    lax.fori_loop(0, group_rows // block_rows, step, 0)

    for q in range(3):
        rows = pl.ds(q * half_rows, half_planes)
        stay_ref[q, 0:half_planes, :] = stay_sums[rows, 0:cells_side]
        stay_ref[q, half_planes:plane_total, :] = stay_sums[rows, cells_side : 2 * cells_side]

    starts, _ = payload_sections(cells_radial)
    odd = lax.rem(lax.axis_index("lat"), 2)
    for upward in (0, 1):
        place = odd if upward else 1 - odd
        first_plane = cells_lateral - MIGRATION_PLANES if upward else 0
        outer_plane = cells_lateral - 1 if upward else 0
        for q in range(3):
            payload[place, pl.ds(starts[0] + q * moved_planes, moved_planes), :] = moved_sums[
                upward, pl.ds(q * moved_rows, moved_planes), :
            ]
            payload[place, pl.ds(starts[1] + q * moved_planes, moved_planes), :] = stay_ref[
                q, pl.ds(first_plane * cells_radial, moved_planes), :
            ]
            for offset in range(MIGRATION_PLANES):
                payload[
                    place,
                    pl.ds(starts[2] + q * moved_planes + offset * cells_radial, cells_radial),
                    :,
                ] = velocity_ref[q, first_plane + offset]
            payload[place, pl.ds(starts[4] + q * cells_radial, cells_radial), :] = forcing_ref[
                q, outer_plane
            ]
        for offset in range(MIGRATION_PLANES):
            payload[place, pl.ds(starts[3] + offset * cells_radial, cells_radial), :] = base_ref[
                first_plane + offset
            ]
    first_ref[...] = payload[0]
    second_ref[...] = payload[1]


def tracer_sums(tracer_values, tracer_cell, tracer_count, base_viscosity, velocity, forcing):
    cells_lateral, cells_radial, cells_side = base_viscosity.shape
    plane_total = cells_lateral * cells_radial
    lane_total = 128
    values = tracer_values.reshape(3, -1, lane_total)
    cells = tracer_cell.reshape(-1, lane_total)
    group_rows = cells.shape[0] // 3
    _, payload_rows = payload_sections(cells_radial)
    half_rows = round_up(plane_total // 2, BF16_ROWS)
    moved_rows = round_up(MIGRATION_PLANES * cells_radial, BF16_ROWS)
    vmem = pl.BlockSpec(memory_space=pltpu.VMEM)
    payload = jax.ShapeDtypeStruct((payload_rows, cells_side), jnp.float32)
    return pl.pallas_call(
        functools.partial(tracer_kernel, 8),
        out_shape=(
            jax.ShapeDtypeStruct((3, plane_total, cells_side), jnp.float32),
            payload,
            payload,
        ),
        in_specs=[pl.BlockSpec(memory_space=pltpu.SMEM)] + [vmem] * 5,
        out_specs=(vmem, vmem, vmem),
        scratch_shapes=[
            pltpu.VMEM((3 * half_rows, 2 * cells_side), jnp.float32),
            pltpu.VMEM((2, 3 * moved_rows, cells_side), jnp.float32),
            pltpu.VMEM((2, payload_rows, cells_side), jnp.float32),
        ],
        compiler_params=pltpu.CompilerParams(vmem_limit_bytes=32 * 2**20),
        cost_estimate=pl.CostEstimate(
            flops=6 * group_rows * lane_total * plane_total * cells_side // 8,
            bytes_accessed=4 * (values.size + cells.size),
            transcendentals=0,
        ),
        name="tracer_sums",
    )(tracer_count, values, cells, base_viscosity, velocity, forcing)


def pair_swaps(first, second):
    count = lax.axis_size("lat")
    received = []
    for payload, start in ((first, 0), (second, 1)):
        pairs = [(low, low + 1) for low in range(start, count - 1, 2)]
        received.append(lax.ppermute(payload, "lat", pairs + [(b, a) for a, b in pairs]))
    return received


def shift_planes(block, step):
    return pltpu.roll(block, step % block.shape[0], 0)


def shift_side(block, step):
    lane_total = block.shape[1]
    lane = lax.broadcasted_iota(jnp.int32, block.shape, 1)
    inside = lane >= step if step > 0 else lane < lane_total + step
    return jnp.where(inside, pltpu.roll(block, step % lane_total, 1), jnp.float32(0.0))


def neighbours(block):
    return (
        shift_planes(block, 1),
        shift_planes(block, -1),
        shift_side(block, 1),
        shift_side(block, -1),
    )


def total_of(terms):
    result = terms[0]
    for term in terms[1:]:
        result = result + term
    return result


def inside_grid(shape, margin, cells_lateral):
    plane = lax.broadcasted_iota(jnp.int32, shape, 0)
    lateral = lax.axis_index("lat")
    first = jnp.where(lateral == 0, margin, 1)
    last = jnp.where(lateral == lax.axis_size("lat") - 1, margin + cells_lateral, shape[0] - 1)
    return (plane >= first) & (plane < last)


def eliminate_kernel(
    stay_ref,
    first_ref,
    second_ref,
    from_first_ref,
    from_second_ref,
    base_ref,
    velocity_ref,
    forcing_ref,
    composition_ref,
    message_ref,
    parts_ref,
    fields,
):
    cells_lateral, cells_radial, cells_side = base_ref.shape
    margin = MIGRATION_PLANES
    planes = cells_lateral + 2 * margin
    pitch = fields.shape[1] // planes
    moved_planes = margin * cells_radial
    starts, _ = payload_sections(cells_radial)
    odd = lax.rem(lax.axis_index("lat"), 2) == 1
    BASE, VELOCITY, SOURCE = 3, 4, 7

    def sent(upward, start, rows):
        part = pl.ds(start, rows)
        mine_first = odd if not upward else jnp.logical_not(odd)
        return jnp.where(mine_first, first_ref[part, :], second_ref[part, :])

    def arrived(from_above, start, rows):
        part = pl.ds(start, rows)
        is_first = odd if not from_above else jnp.logical_not(odd)
        return jnp.where(is_first, from_first_ref[part, :], from_second_ref[part, :])

    def put(field, plane, value):
        fields[field, pl.ds(plane * pitch, cells_radial), :] = value

    for q in range(3):
        for x in range(cells_lateral):
            mine = stay_ref[q, pl.ds(x * cells_radial, cells_radial), :]
            if x < margin:
                row = q * moved_planes + x * cells_radial
                mine = mine + arrived(False, starts[0] + row, cells_radial)
            if x >= cells_lateral - margin:
                row = q * moved_planes + (x - cells_lateral + margin) * cells_radial
                mine = mine + arrived(True, starts[0] + row, cells_radial)
            put(q, margin + x, mine)
            put(VELOCITY + q, margin + x, velocity_ref[q, x])
            put(SOURCE + q, margin + x, forcing_ref[q, x])
        for offset in range(margin):
            row = q * moved_planes + offset * cells_radial
            for above in (False, True):
                plane = offset + (margin + cells_lateral if above else 0)
                put(
                    q,
                    plane,
                    sent(above, starts[0] + row, cells_radial)
                    + arrived(above, starts[1] + row, cells_radial),
                )
                put(VELOCITY + q, plane, arrived(above, starts[2] + row, cells_radial))
        put(
            SOURCE + q,
            margin - 1,
            arrived(False, starts[4] + q * cells_radial, cells_radial),
        )
        put(
            SOURCE + q,
            margin + cells_lateral,
            arrived(True, starts[4] + q * cells_radial, cells_radial),
        )
        for plane in (0, planes - 1):
            put(SOURCE + q, plane, jnp.zeros((cells_radial, cells_side), jnp.float32))
    for x in range(cells_lateral):
        put(BASE, margin + x, base_ref[x])
    for offset in range(margin):
        for above in (False, True):
            plane = offset + (margin + cells_lateral if above else 0)
            put(BASE, plane, arrived(above, starts[3] + offset * cells_radial, cells_radial))

    for plane in range(planes):
        rows = pl.ds(plane * pitch, cells_radial)
        total_weight = fields[0, rows, :] + PRIOR_WEIGHT
        basalt_share = fields[1, rows, :] / total_weight
        melt_share = fields[2, rows, :] / total_weight
        fields[BASE, rows, :] = fields[BASE, rows, :] * jnp.exp(
            CONTRAST_BASALT * basalt_share - CONTRAST_MELT * melt_share
        )
        fields[SOURCE + 2, rows, :] = fields[SOURCE + 2, rows, :] - BUOYANCY * basalt_share
        if margin <= plane < margin + cells_lateral:
            composition_ref[0, plane - margin] = basalt_share
            composition_ref[1, plane - margin] = melt_share

    lower_block = lax.axis_index("rad") == 0

    def radial(field, t):
        row = jnp.where(lower_block, t, cells_radial - 1 - t)
        return fields[field, pl.ds(row, planes, stride=pitch), :]

    shape = (planes, cells_side)
    valid = inside_grid(shape, margin, cells_lateral)
    nothing = jnp.zeros(shape, jnp.float32)
    last = cells_radial - 1
    viscosity = [radial(BASE, t) for t in range(cells_radial)]
    lateral_faces = [
        [LATERAL * 0.5 * (here + there) for there in neighbours(here)] for here in viscosity
    ]
    radial_faces = [RADIAL * 0.5 * viscosity[0]] + [
        RADIAL * 0.5 * (viscosity[t - 1] + viscosity[t]) for t in range(1, cells_radial)
    ]

    excess = total_of(lateral_faces[0]) + radial_faces[0]
    inverse, coupling = [], []
    for t in range(last):
        inverse.append(1.0 / (excess + radial_faces[t + 1]))
        coupling.append(radial_faces[t + 1] * inverse[t])
        excess = total_of(lateral_faces[t + 1]) + coupling[t] * excess

    def lateral_terms(t, around):
        return [face * there for face, there in zip(lateral_faces[t], around)]

    def forward(right_side):
        eliminated = [right_side[0]]
        for t in range(1, cells_radial):
            eliminated.append(right_side[t] + coupling[t - 1] * eliminated[t - 1])
        return eliminated

    def backward(eliminated):
        solved = [nothing]
        for t in range(last - 1, -1, -1):
            solved.append(eliminated[t] * inverse[t] + coupling[t] * solved[-1])
        return solved[::-1]

    response = [jnp.ones(shape, jnp.float32)]
    for t in range(last - 1, -1, -1):
        response.append(coupling[t] * response[-1])
    response = response[::-1]

    message_ref[pl.ds(0, planes), :] = viscosity[last]
    message_ref[pl.ds(planes, planes), :] = excess
    short_start = 5 * planes

    def put_short(index, value):
        message_ref[pl.ds(short_start + index * cells_lateral, cells_lateral), :] = value[
            margin : margin + cells_lateral
        ]

    parts = []
    for q in range(3):
        source = [radial(SOURCE + q, t) for t in range(cells_radial)]
        eliminated = forward(
            [
                total_of([source[t]] + lateral_terms(t, neighbours(radial(VELOCITY + q, t))))
                for t in range(cells_radial)
            ]
        )
        message_ref[pl.ds((2 + q) * planes, planes), :] = eliminated[last]
        particular = [jnp.where(valid, value, 0.0) for value in backward(eliminated)]
        eliminated = forward(
            [
                total_of([source[t]] + lateral_terms(t, neighbours(particular[t])))
                for t in range(cells_radial)
            ]
        )
        put_short(q, eliminated[last])
        parts.append(backward(eliminated))
    around = [neighbours(jnp.where(valid, value, 0.0)) for value in response]
    for side in range(4):
        eliminated = forward([lateral_faces[t][side] * around[t][side] for t in range(cells_radial)])
        put_short(3 + side, eliminated[last])
        parts.append(backward(eliminated))
    parts.append(response)
    for index, part in enumerate(parts):
        for t in range(cells_radial):
            parts_ref[index, t] = part[t]
    unused = short_start + 7 * cells_lateral
    message_ref[pl.ds(unused, message_ref.shape[0] - unused), :] = jnp.zeros(
        (message_ref.shape[0] - unused, cells_side), jnp.float32
    )


def message_rows(cells_lateral):
    planes = cells_lateral + 2 * MIGRATION_PLANES
    return round_up(5 * planes + 7 * cells_lateral + MIGRATION_PLANES, 8)


def eliminate(stay, sent, received, base_viscosity, velocity, forcing):
    cells_lateral, cells_radial, cells_side = base_viscosity.shape
    planes = cells_lateral + 2 * MIGRATION_PLANES
    pitch = round_up(cells_radial, 8)
    vmem = pl.BlockSpec(memory_space=pltpu.VMEM)
    return pl.pallas_call(
        eliminate_kernel,
        out_shape=(
            jax.ShapeDtypeStruct((2,) + base_viscosity.shape, jnp.float32),
            jax.ShapeDtypeStruct((message_rows(cells_lateral), cells_side), jnp.float32),
            jax.ShapeDtypeStruct((8, cells_radial, planes, cells_side), jnp.float32),
        ),
        in_specs=[vmem] * 8,
        out_specs=(vmem, vmem, vmem),
        scratch_shapes=[pltpu.VMEM((10, planes * pitch, cells_side), jnp.float32)],
        compiler_params=pltpu.CompilerParams(vmem_limit_bytes=32 * 2**20),
        name="eliminate",
    )(stay, *sent, *received, base_viscosity, velocity, forcing)


def join_kernel(mine_ref, other_ref, parts_ref, smoothed_ref, lines):
    _, cells_lateral, cells_radial, cells_side = smoothed_ref.shape
    margin = MIGRATION_PLANES
    planes = cells_lateral + 2 * margin
    pitch = lines.shape[0] // cells_lateral
    shape = (planes, cells_side)
    valid = inside_grid(shape, margin, cells_lateral)
    lower_block = lax.axis_index("rad") == 0

    def long(ref, index):
        return ref[pl.ds(index * planes, planes), :]

    def short(ref, index):
        return ref[pl.ds(5 * planes + index * cells_lateral - margin, planes), :]

    face = RADIAL * 0.5 * (long(mine_ref, 0) + long(other_ref, 0))
    excess, other_excess = long(mine_ref, 1), long(other_ref, 1)
    scale = 1.0 / (excess * other_excess + face * (excess + other_excess))
    own_weight = (other_excess + face) * scale
    other_weight = (excess + face) * scale
    cross = face * scale
    factors = [short(mine_ref, 3 + side) for side in range(4)]
    other_factors = [short(other_ref, 3 + side) for side in range(4)]
    for q in range(3):
        right, other_right = long(mine_ref, 2 + q), long(other_ref, 2 + q)
        own = jnp.where(valid, own_weight * right + cross * other_right, 0.0)
        other = jnp.where(valid, other_weight * other_right + cross * right, 0.0)
        around, other_around = neighbours(own), neighbours(other)
        right = total_of(
            [short(mine_ref, q)] + [factor * there for factor, there in zip(factors, around)]
        )
        other_right = total_of(
            [short(other_ref, q)]
            + [factor * there for factor, there in zip(other_factors, other_around)]
        )
        final = own_weight * right + cross * other_right
        for t in range(cells_radial):
            value = parts_ref[q, t] + parts_ref[7, t] * final
            for side in range(4):
                value = value + parts_ref[3 + side, t] * around[side]
            row = jnp.where(lower_block, t, cells_radial - 1 - t)
            lines[pl.ds(row, cells_lateral, stride=pitch), :] = value[
                margin : margin + cells_lateral
            ]
        for x in range(cells_lateral):
            smoothed_ref[q, x] = lines[pl.ds(x * pitch, cells_radial), :]


def join(message, other, parts, like):
    cells_lateral, cells_radial, cells_side = like.shape[1:]
    pitch = round_up(cells_radial, 8)
    vmem = pl.BlockSpec(memory_space=pltpu.VMEM)
    return pl.pallas_call(
        join_kernel,
        out_shape=jax.ShapeDtypeStruct(like.shape, jnp.float32),
        in_specs=[vmem] * 3,
        out_specs=vmem,
        scratch_shapes=[pltpu.VMEM((cells_lateral * pitch, cells_side), jnp.float32)],
        compiler_params=pltpu.CompilerParams(vmem_limit_bytes=32 * 2**20),
        name="join",
    )(message, other, parts)


def extended(block, sides, width):
    for axis, dim in sides:
        count = lax.axis_size(axis)
        forward = [(i, i + 1) for i in range(count - 1)]
        backward = [(target, source) for source, target in forward]
        low = lax.ppermute(
            lax.slice_in_dim(block, block.shape[dim] - width, None, axis=dim), axis, forward
        )
        high = lax.ppermute(lax.slice_in_dim(block, 0, width, axis=dim), axis, backward)
        block = jnp.concatenate([low, block, high], axis=dim)
    return block


def block_factor(diagonal, lower_band, upper_band):
    pivots = []
    upper_scaled = []
    for row_index in range(diagonal.shape[1]):
        if row_index == 0:
            pivot_row = diagonal[:, 0]
        else:
            pivot_row = diagonal[:, row_index] - lower_band[:, row_index] * upper_scaled[-1]
        pivots.append(pivot_row)
        upper_scaled.append(upper_band[:, row_index] / pivot_row)
    return (pivots, upper_scaled)


def block_solve(pivots, upper_scaled, lower_band, right_side):
    row_total = len(pivots)
    modified = []
    for row_index in range(row_total):
        if row_index == 0:
            value_row = right_side[:, :, 0] / pivots[0]
        else:
            value_row = (
                right_side[:, :, row_index] - lower_band[:, row_index] * modified[-1]
            ) / pivots[row_index]
        modified.append(value_row)
    solved = [modified[-1]]
    for row_index in range(row_total - 2, -1, -1):
        solved.append(modified[row_index] - upper_scaled[row_index] * solved[-1])
    ordered = solved[::-1]
    return jnp.stack(ordered, 2)


def interface_solve(coefficients):
    column_total = coefficients.shape[2]

    def forward(carried, inputs):
        offset, carried_slope = carried
        left_first, right_first, left_last, right_last, free_first, free_last = inputs
        divisor = 1.0 - left_first * carried_slope
        first_fixed = (free_first + left_first * offset) / divisor
        first_slope = right_first / divisor
        next_offset = free_last + left_last * (offset + carried_slope * first_fixed)
        next_slope = left_last * carried_slope * first_slope + right_last
        return ((next_offset, next_slope), (first_fixed, first_slope, next_offset, next_slope))

    start_state = (
        jnp.zeros((3, column_total), jnp.float32),
        jnp.zeros((column_total,), jnp.float32),
    )
    scan_inputs = (
        coefficients[:, 0],
        coefficients[:, 1],
        coefficients[:, 2],
        coefficients[:, 3],
        coefficients[:, 4:7],
        coefficients[:, 7:10],
    )
    final_state, eliminated = lax.scan(forward, start_state, scan_inputs)

    def backward(first_next, inputs):
        fixed_first, slope_first, fixed_last, slope_last = inputs
        first_value = fixed_first + slope_first * first_next
        last_value = fixed_last + slope_last * first_next
        return (first_value, (first_value, last_value))

    final_first, values_pair = lax.scan(
        backward, jnp.zeros((3, column_total), jnp.float32), eliminated, reverse=True
    )
    first_values, last_values = values_pair
    nothing_row = jnp.zeros((1, 3, column_total), jnp.float32)
    from_below = jnp.concatenate([nothing_row, last_values[:-1]], 0)
    from_above = jnp.concatenate([first_values[1:], nothing_row], 0)
    return jnp.concatenate([from_below, from_above], 1)


def reduced_boundary(interface):
    gathered = lax.all_gather(interface, "rad", axis=0, tiled=True)
    solved = interface_solve(gathered)
    return lax.dynamic_index_in_dim(solved, lax.axis_index("rad"), 0, keepdims=False)


def many_blocks(stay, received, base_viscosity, velocity, forcing):
    cells_lateral, cells_radial, cells_side = base_viscosity.shape
    moved_rows = MIGRATION_PLANES * cells_radial
    odd = lax.rem(lax.axis_index("lat"), 2) == 1
    from_below = jnp.where(odd, received[0], received[1])[: 3 * moved_rows]
    from_above = jnp.where(odd, received[1], received[0])[: 3 * moved_rows]
    totals = stay.at[:, :moved_rows].add(from_below.reshape(3, moved_rows, cells_side))
    totals = totals.at[:, -moved_rows:].add(from_above.reshape(3, moved_rows, cells_side))
    grouped = totals.reshape(3, cells_lateral, cells_radial, cells_side)
    total_weight = grouped[0] + PRIOR_WEIGHT
    basalt_share = grouped[1] / total_weight
    melt_share = grouped[2] / total_weight
    viscosity = base_viscosity * jnp.exp(
        CONTRAST_BASALT * basalt_share - CONTRAST_MELT * melt_share
    )
    viscosity_pad = extended(viscosity, (("lat", 0), ("rad", 1)), 1)
    side_pad = jnp.pad(viscosity, ((0, 0), (0, 0), (1, 1)))
    face_west = LATERAL * 0.5 * (viscosity + viscosity_pad[:-2, 1:-1])
    face_east = LATERAL * 0.5 * (viscosity + viscosity_pad[2:, 1:-1])
    face_south = LATERAL * 0.5 * (viscosity + side_pad[:, :, :-2])
    face_north = LATERAL * 0.5 * (viscosity + side_pad[:, :, 2:])
    face_below = RADIAL * 0.5 * (viscosity + viscosity_pad[1:-1, :-2])
    face_above = RADIAL * 0.5 * (viscosity + viscosity_pad[1:-1, 2:])
    diagonal = face_west + face_east + face_south + face_north + face_below + face_above
    source = jnp.concatenate([forcing[:2], (forcing[2] - BUOYANCY * basalt_share)[None]], 0)
    lower_band = -face_below
    upper_band = -face_above
    pivots, upper_scaled = block_factor(diagonal, lower_band, upper_band)
    radial_iota = lax.broadcasted_iota(jnp.int32, viscosity.shape, 1)
    response_side = jnp.stack(
        [
            jnp.where(radial_iota == 0, face_below, jnp.float32(0.0)),
            jnp.where(radial_iota == cells_radial - 1, face_above, jnp.float32(0.0)),
        ]
    )
    response = block_solve(pivots, upper_scaled, lower_band, response_side)
    current = velocity
    for sweep_index in range(SWEEPS):
        velocity_pad = extended(current, (("lat", 1),), 1)
        side_velocity = jnp.pad(current, ((0, 0), (0, 0), (0, 0), (1, 1)))
        right_side = (
            source
            + face_west * velocity_pad[:, :-2]
            + face_east * velocity_pad[:, 2:]
            + face_south * side_velocity[..., :-2]
            + face_north * side_velocity[..., 2:]
        )
        particular = block_solve(pivots, upper_scaled, lower_band, right_side)
        interface = jnp.concatenate(
            [response[:, :, 0], response[:, :, -1], particular[:, :, 0], particular[:, :, -1]], 0
        )
        interface = interface.reshape(1, 10, cells_lateral * cells_side)
        boundary = reduced_boundary(interface).reshape(6, cells_lateral, 1, cells_side)
        current = particular + response[0][None] * boundary[:3] + response[1][None] * boundary[3:]
    composition = jnp.stack([basalt_share, melt_share])
    return (current, composition)

def local(tracer_values, tracer_cell, tracer_count, base_viscosity, velocity, forcing):
    stay, *sent = tracer_sums(
        tracer_values, tracer_cell, tracer_count, base_viscosity, velocity, forcing
    )
    received = pair_swaps(*sent)
    if lax.axis_size("rad") != 2:
        return many_blocks(stay, received, base_viscosity, velocity, forcing)
    composition, message, parts = eliminate(
        stay, sent, received, base_viscosity, velocity, forcing
    )
    other = lax.ppermute(message, "rad", [(0, 1), (1, 0)])
    return join(message, other, parts, velocity), composition


def solution(mesh):
    return jax.shard_map(
        local,
        mesh=mesh,
        in_specs=(
            P("lat", "rad", None, None),
            P("lat", "rad", None),
            P("lat", "rad", None),
            P("lat", "rad", None),
            P(None, "lat", "rad", None),
            P(None, "lat", "rad", None),
        ),
        out_specs=(P(None, "lat", "rad", None), P(None, "lat", "rad", None)),
        check_vma=False,
    )
```

```python
import functools

import jax
import jax.numpy as jnp
from jax import lax
from jax.experimental import pallas as pl
from jax.experimental.pallas import tpu as pltpu
from jax.sharding import PartitionSpec as P

SWEEPS = 2
MIGRATION_PLANES = 2

LATERAL = 0.015625
RADIAL = 32.0
BUOYANCY = 0.1
PRIOR_WEIGHT = 0.5
CONTRAST_BASALT = 2.3
CONTRAST_MELT = 1.5

BF16_ROWS = 16


def round_up(value, multiple):
    return -(-value // multiple) * multiple


def split_index(index, count):
    if count & (count - 1) == 0:
        return lax.shift_right_logical(index, count.bit_length() - 1), index & (count - 1)
    quotient = lax.div(index, count)
    return quotient, index - quotient * count


def payload_sections(cells_radial):
    pair = MIGRATION_PLANES * cells_radial
    starts = [0, 3 * pair, 6 * pair, 9 * pair, 10 * pair]
    return starts, round_up(10 * pair + 3 * cells_radial, 8)


def spread_row(row):
    return jnp.broadcast_to(row, (BF16_ROWS, row.shape[1])).astype(jnp.bfloat16)


def hot_tiles(index, row_total):
    lane_total = index.shape[1]
    iota = lax.broadcasted_iota(jnp.int32, (BF16_ROWS, lane_total), 0)
    return [
        index == (iota + first).astype(jnp.float32).astype(jnp.bfloat16)
        for first in range(0, row_total, BF16_ROWS)
    ]


def hot_product(loads, high, low, high_rows, low_rows):
    left, right = [], []
    zero = jnp.zeros((BF16_ROWS, high.shape[1]), jnp.bfloat16)
    one = jnp.ones((BF16_ROWS, high.shape[1]), jnp.bfloat16)
    for row in range(high.shape[0]):
        pick = slice(row, row + 1)
        high_masks = hot_tiles(spread_row(high[pick]), high_rows)
        low_masks = hot_tiles(spread_row(low[pick]), low_rows)
        spread = [spread_row(load[pick]) for load in loads]
        left.append(
            jnp.concatenate(
                [jnp.where(mask, load, zero) for load in spread for mask in high_masks], 0
            )
        )
        right.append(jnp.concatenate([jnp.where(mask, one, zero) for mask in low_masks], 0))
    return lax.dot_general(
        jnp.concatenate(left, 1),
        jnp.concatenate(right, 1),
        (((1,), (1,)), ((), ())),
        preferred_element_type=jnp.float32,
    )


def tracer_kernel(
    block_rows,
    counts_hbm,
    values_hbm,
    cells_hbm,
    base_hbm,
    velocity_hbm,
    forcing_hbm,
    stay_ref,
    first_ref,
    second_ref,
    counts,
    values,
    cells,
    base,
    velocity,
    forcing,
    stay_sums,
    moved_sums,
    payload,
    semaphores,
):
    cells_lateral, cells_radial, cells_side = base_hbm.shape
    plane_total = cells_lateral * cells_radial
    moved_planes = MIGRATION_PLANES * cells_radial
    half_side = cells_side // 2
    group_rows, lane_total = values.shape[2:]

    copies = []

    def fetch(source, target):
        copy = pltpu.make_async_copy(source, target, semaphores.at[len(copies)])
        copy.start()
        copies.append(copy)

    fetch(counts_hbm, counts)
    for first_row, rows in ((0, block_rows), (block_rows, group_rows - block_rows)):
        part = pl.ds(first_row, rows)
        fetch(cells_hbm.at[:, part], cells.at[:, part])
        fetch(values_hbm.at[:, :, part], values.at[:, :, part])
    for upward in (0, 1):
        outer = pl.ds((cells_lateral - MIGRATION_PLANES) * upward, MIGRATION_PLANES)
        fetch(base_hbm.at[outer], base.at[upward])
        fetch(velocity_hbm.at[:, outer], velocity.at[upward])
        fetch(forcing_hbm.at[:, pl.ds((cells_lateral - 1) * upward, 1)], forcing.at[upward])

    stay_sums[...] = jnp.zeros_like(stay_sums)
    moved_sums[...] = jnp.zeros_like(moved_sums)

    def loads_of(group, first_row):
        rows = pl.ds(first_row, block_rows)
        shape = (block_rows, lane_total)
        slot = (first_row + lax.broadcasted_iota(jnp.int32, shape, 0)) * lane_total
        slot = slot + lax.broadcasted_iota(jnp.int32, shape, 1)
        weight = jnp.where(
            slot < counts[0, 0, group], 0.5 + values[0, group, rows, :], jnp.float32(0.0)
        )
        loads = [weight, weight * values[1, group, rows, :], weight * values[2, group, rows, :]]
        plane, side = split_index(cells[group, rows, :], cells_side)
        return loads, plane, side

    def step(first_row):
        loads, plane, side = loads_of(1, first_row)
        stay_sums[...] += hot_product(
            loads, plane.astype(jnp.float32), side.astype(jnp.float32), plane_total, cells_side
        )
        for slot, group in enumerate((0, 2)):
            loads, plane, side = loads_of(group, first_row)
            if group == 0:
                plane = plane - (plane_total - moved_planes)
            upper = side >= half_side
            high = jnp.where(upper, plane + moved_planes, plane).astype(jnp.float32)
            low = jnp.where(upper, side - half_side, side).astype(jnp.float32)
            moved_sums[slot] += hot_product(loads, high, low, 2 * moved_planes, half_side)

    for copy in copies[:3]:
        copy.wait()
    step(0)
    for copy in copies[3:5]:
        copy.wait()

    def repeat(index, carried):
        step(pl.multiple_of(index * block_rows, block_rows))
        return carried

    lax.fori_loop(1, group_rows // block_rows, repeat, 0)
    for copy in copies[5:]:
        copy.wait()

    stay_ref[...] = stay_sums[...]
    starts, _ = payload_sections(cells_radial)
    odd = lax.rem(lax.axis_index("lat"), 2)
    for upward in (0, 1):
        place = odd if upward else 1 - odd
        first_plane = cells_lateral - MIGRATION_PLANES if upward else 0
        for q in range(3):
            for half in (0, 1):
                payload[
                    place,
                    pl.ds(starts[0] + q * moved_planes, moved_planes),
                    pl.ds(half * half_side, half_side),
                ] = moved_sums[upward, pl.ds((2 * q + half) * moved_planes, moved_planes), :]
            payload[place, pl.ds(starts[1] + q * moved_planes, moved_planes), :] = stay_sums[
                pl.ds(q * plane_total + first_plane * cells_radial, moved_planes), :
            ]
            for offset in range(MIGRATION_PLANES):
                payload[
                    place,
                    pl.ds(starts[2] + q * moved_planes + offset * cells_radial, cells_radial),
                    :,
                ] = velocity[upward, q, offset]
            payload[place, pl.ds(starts[4] + q * cells_radial, cells_radial), :] = forcing[
                upward, q, 0
            ]
        for offset in range(MIGRATION_PLANES):
            payload[place, pl.ds(starts[3] + offset * cells_radial, cells_radial), :] = base[
                upward, offset
            ]
    first_ref[...] = payload[0]
    second_ref[...] = payload[1]


def tracer_sums(tracer_values, tracer_cell, tracer_count, base_viscosity, velocity, forcing):
    cells_lateral, cells_radial, cells_side = base_viscosity.shape
    plane_total = cells_lateral * cells_radial
    moved_planes = MIGRATION_PLANES * cells_radial
    lane_total = 128
    values = tracer_values.reshape(3, 3, -1, lane_total)
    cells = tracer_cell.reshape(3, -1, lane_total)
    group_rows = cells.shape[1]
    _, payload_rows = payload_sections(cells_radial)
    hbm = pl.BlockSpec(memory_space=pltpu.HBM)
    vmem = pl.BlockSpec(memory_space=pltpu.VMEM)
    payload = jax.ShapeDtypeStruct((payload_rows, cells_side), jnp.float32)
    outer_planes = (MIGRATION_PLANES, cells_radial, cells_side)
    return pl.pallas_call(
        functools.partial(tracer_kernel, 16),
        out_shape=(
            jax.ShapeDtypeStruct((3 * plane_total, cells_side), jnp.float32),
            payload,
            payload,
        ),
        in_specs=[hbm] * 6,
        out_specs=(vmem, vmem, vmem),
        scratch_shapes=[
            pltpu.SMEM(tracer_count.shape, jnp.int32),
            pltpu.VMEM(values.shape, jnp.float32),
            pltpu.VMEM(cells.shape, jnp.int32),
            pltpu.VMEM((2,) + outer_planes, jnp.float32),
            pltpu.VMEM((2, 3) + outer_planes, jnp.float32),
            pltpu.VMEM((2, 3, 1, cells_radial, cells_side), jnp.float32),
            pltpu.VMEM((3 * plane_total, cells_side), jnp.float32),
            pltpu.VMEM((2, 6 * moved_planes, cells_side // 2), jnp.float32),
            pltpu.VMEM((2, payload_rows, cells_side), jnp.float32),
            pltpu.SemaphoreType.DMA((11,)),
        ],
        compiler_params=pltpu.CompilerParams(vmem_limit_bytes=32 * 2**20),
        cost_estimate=pl.CostEstimate(
            flops=6 * group_rows * lane_total * plane_total * cells_side // 8,
            bytes_accessed=4 * (values.size + cells.size),
            transcendentals=0,
        ),
        name="tracer_sums",
    )(
        *(
            pltpu.with_memory_space_constraint(array, pltpu.HBM)
            for array in (tracer_count, values, cells, base_viscosity, velocity, forcing)
        )
    )


def pair_swaps(first, second):
    count = lax.axis_size("lat")
    received = []
    for payload, start in ((second, 1), (first, 0)):
        pairs = [(low, low + 1) for low in range(start, count - 1, 2)]
        received.append(lax.ppermute(payload, "lat", pairs + [(b, a) for a, b in pairs]))
    return received[::-1]


def shift_planes(block, step):
    return pltpu.roll(block, step % block.shape[0], 0)


def shift_side(block, step):
    lane_total = block.shape[1]
    lane = lax.broadcasted_iota(jnp.int32, block.shape, 1)
    inside = lane >= step if step > 0 else lane < lane_total + step
    return jnp.where(inside, pltpu.roll(block, step % lane_total, 1), jnp.float32(0.0))


def neighbours(block):
    return (
        shift_planes(block, 1),
        shift_planes(block, -1),
        shift_side(block, 1),
        shift_side(block, -1),
    )


def total_of(terms):
    result = terms[0]
    for term in terms[1:]:
        result = result + term
    return result


def inside_grid(shape, margin, cells_lateral):
    plane = lax.broadcasted_iota(jnp.int32, shape, 0)
    lateral = lax.axis_index("lat")
    first = jnp.where(lateral == 0, margin, 1)
    last = jnp.where(lateral == lax.axis_size("lat") - 1, margin + cells_lateral, shape[0] - 1)
    return (plane >= first) & (plane < last)


def eliminate_kernel(
    stay_ref,
    second_ref,
    first_ref,
    from_second_ref,
    from_first_ref,
    base_ref,
    velocity_ref,
    forcing_ref,
    composition_ref,
    message_ref,
    parts_ref,
    fields,
):
    cells_lateral, cells_radial, cells_side = base_ref.shape
    margin = MIGRATION_PLANES
    planes = cells_lateral + 2 * margin
    pitch = fields.shape[1] // planes
    moved_planes = margin * cells_radial
    starts, _ = payload_sections(cells_radial)
    odd = lax.rem(lax.axis_index("lat"), 2) == 1
    BASE, VELOCITY, SOURCE = 3, 4, 7

    def sent(upward, start, rows):
        part = pl.ds(start, rows)
        mine_first = odd if not upward else jnp.logical_not(odd)
        return jnp.where(mine_first, first_ref[part, :], second_ref[part, :])

    def arrived(from_above, start, rows):
        part = pl.ds(start, rows)
        is_first = odd if not from_above else jnp.logical_not(odd)
        return jnp.where(is_first, from_first_ref[part, :], from_second_ref[part, :])

    def put(field, plane, value):
        fields[field, pl.ds(plane * pitch, cells_radial), :] = value

    for q in range(3):
        for x in range(cells_lateral):
            mine = stay_ref[pl.ds((q * cells_lateral + x) * cells_radial, cells_radial), :]
            if x < margin:
                row = q * moved_planes + x * cells_radial
                mine = mine + arrived(False, starts[0] + row, cells_radial)
            if x >= cells_lateral - margin:
                row = q * moved_planes + (x - cells_lateral + margin) * cells_radial
                mine = mine + arrived(True, starts[0] + row, cells_radial)
            put(q, margin + x, mine)
            put(VELOCITY + q, margin + x, velocity_ref[q, x])
            put(SOURCE + q, margin + x, forcing_ref[q, x])
        for offset in range(margin):
            row = q * moved_planes + offset * cells_radial
            for above in (False, True):
                plane = offset + (margin + cells_lateral if above else 0)
                put(
                    q,
                    plane,
                    sent(above, starts[0] + row, cells_radial)
                    + arrived(above, starts[1] + row, cells_radial),
                )
                put(VELOCITY + q, plane, arrived(above, starts[2] + row, cells_radial))
        put(
            SOURCE + q,
            margin - 1,
            arrived(False, starts[4] + q * cells_radial, cells_radial),
        )
        put(
            SOURCE + q,
            margin + cells_lateral,
            arrived(True, starts[4] + q * cells_radial, cells_radial),
        )
        for plane in (0, planes - 1):
            put(SOURCE + q, plane, jnp.zeros((cells_radial, cells_side), jnp.float32))
    for x in range(cells_lateral):
        put(BASE, margin + x, base_ref[x])
    for offset in range(margin):
        for above in (False, True):
            plane = offset + (margin + cells_lateral if above else 0)
            put(BASE, plane, arrived(above, starts[3] + offset * cells_radial, cells_radial))

    for plane in range(planes):
        rows = pl.ds(plane * pitch, cells_radial)
        total_weight = fields[0, rows, :] + PRIOR_WEIGHT
        basalt_share = fields[1, rows, :] / total_weight
        melt_share = fields[2, rows, :] / total_weight
        fields[BASE, rows, :] = fields[BASE, rows, :] * jnp.exp(
            CONTRAST_BASALT * basalt_share - CONTRAST_MELT * melt_share
        )
        fields[SOURCE + 2, rows, :] = fields[SOURCE + 2, rows, :] - BUOYANCY * basalt_share
        if margin <= plane < margin + cells_lateral:
            composition_ref[0, plane - margin] = basalt_share
            composition_ref[1, plane - margin] = melt_share

    lower_block = lax.axis_index("rad") == 0

    def radial(field, t):
        row = jnp.where(lower_block, t, cells_radial - 1 - t)
        return fields[field, pl.ds(row, planes, stride=pitch), :]

    shape = (planes, cells_side)
    valid = inside_grid(shape, margin, cells_lateral)
    nothing = jnp.zeros(shape, jnp.float32)
    last = cells_radial - 1
    viscosity = [radial(BASE, t) for t in range(cells_radial)]
    lateral_faces = [
        [LATERAL * 0.5 * (here + there) for there in neighbours(here)] for here in viscosity
    ]
    radial_faces = [RADIAL * 0.5 * viscosity[0]] + [
        RADIAL * 0.5 * (viscosity[t - 1] + viscosity[t]) for t in range(1, cells_radial)
    ]

    excess = total_of(lateral_faces[0]) + radial_faces[0]
    inverse, coupling = [], []
    for t in range(last):
        inverse.append(1.0 / (excess + radial_faces[t + 1]))
        coupling.append(radial_faces[t + 1] * inverse[t])
        excess = total_of(lateral_faces[t + 1]) + coupling[t] * excess

    def lateral_terms(t, around):
        return [face * there for face, there in zip(lateral_faces[t], around)]

    def forward(right_side):
        eliminated = [right_side[0]]
        for t in range(1, cells_radial):
            eliminated.append(right_side[t] + coupling[t - 1] * eliminated[t - 1])
        return eliminated

    def backward(eliminated):
        solved = [nothing]
        for t in range(last - 1, -1, -1):
            solved.append(eliminated[t] * inverse[t] + coupling[t] * solved[-1])
        return solved[::-1]

    response = [jnp.ones(shape, jnp.float32)]
    for t in range(last - 1, -1, -1):
        response.append(coupling[t] * response[-1])
    response = response[::-1]

    message_ref[pl.ds(0, planes), :] = viscosity[last]
    message_ref[pl.ds(planes, planes), :] = excess
    short_start = 5 * planes

    def put_short(index, value):
        message_ref[pl.ds(short_start + index * cells_lateral, cells_lateral), :] = value[
            margin : margin + cells_lateral
        ]

    parts = []
    for q in range(3):
        source = [radial(SOURCE + q, t) for t in range(cells_radial)]
        eliminated = forward(
            [
                total_of([source[t]] + lateral_terms(t, neighbours(radial(VELOCITY + q, t))))
                for t in range(cells_radial)
            ]
        )
        message_ref[pl.ds((2 + q) * planes, planes), :] = eliminated[last]
        particular = [jnp.where(valid, value, 0.0) for value in backward(eliminated)]
        eliminated = forward(
            [
                total_of([source[t]] + lateral_terms(t, neighbours(particular[t])))
                for t in range(cells_radial)
            ]
        )
        put_short(q, eliminated[last])
        parts.append(backward(eliminated))
    around = [neighbours(jnp.where(valid, value, 0.0)) for value in response]
    for side in range(4):
        eliminated = forward([lateral_faces[t][side] * around[t][side] for t in range(cells_radial)])
        put_short(3 + side, eliminated[last])
        parts.append(backward(eliminated))
    parts.append(response)
    for index, part in enumerate(parts):
        for t in range(cells_radial):
            parts_ref[index, t] = part[t]
    unused = short_start + 7 * cells_lateral
    message_ref[pl.ds(unused, message_ref.shape[0] - unused), :] = jnp.zeros(
        (message_ref.shape[0] - unused, cells_side), jnp.float32
    )


def message_rows(cells_lateral):
    planes = cells_lateral + 2 * MIGRATION_PLANES
    return round_up(5 * planes + 7 * cells_lateral + MIGRATION_PLANES, 8)


def eliminate(stay, sent, received, base_viscosity, velocity, forcing):
    cells_lateral, cells_radial, cells_side = base_viscosity.shape
    planes = cells_lateral + 2 * MIGRATION_PLANES
    pitch = round_up(cells_radial, 8)
    vmem = pl.BlockSpec(memory_space=pltpu.VMEM)
    return pl.pallas_call(
        eliminate_kernel,
        out_shape=(
            jax.ShapeDtypeStruct((2,) + base_viscosity.shape, jnp.float32),
            jax.ShapeDtypeStruct((message_rows(cells_lateral), cells_side), jnp.float32),
            jax.ShapeDtypeStruct((8, cells_radial, planes, cells_side), jnp.float32),
        ),
        in_specs=[vmem] * 8,
        out_specs=(vmem, vmem, vmem),
        scratch_shapes=[pltpu.VMEM((10, planes * pitch, cells_side), jnp.float32)],
        compiler_params=pltpu.CompilerParams(vmem_limit_bytes=32 * 2**20),
        name="eliminate",
    )(stay, *sent[::-1], *received[::-1], base_viscosity, velocity, forcing)


def join_kernel(mine_ref, other_ref, parts_ref, smoothed_ref, lines):
    _, cells_lateral, cells_radial, cells_side = smoothed_ref.shape
    margin = MIGRATION_PLANES
    planes = cells_lateral + 2 * margin
    pitch = lines.shape[0] // cells_lateral
    shape = (planes, cells_side)
    valid = inside_grid(shape, margin, cells_lateral)
    lower_block = lax.axis_index("rad") == 0

    def long(ref, index):
        return ref[pl.ds(index * planes, planes), :]

    def short(ref, index):
        return ref[pl.ds(5 * planes + index * cells_lateral - margin, planes), :]

    face = RADIAL * 0.5 * (long(mine_ref, 0) + long(other_ref, 0))
    excess, other_excess = long(mine_ref, 1), long(other_ref, 1)
    scale = 1.0 / (excess * other_excess + face * (excess + other_excess))
    own_weight = (other_excess + face) * scale
    other_weight = (excess + face) * scale
    cross = face * scale
    factors = [short(mine_ref, 3 + side) for side in range(4)]
    other_factors = [short(other_ref, 3 + side) for side in range(4)]
    for q in range(3):
        right, other_right = long(mine_ref, 2 + q), long(other_ref, 2 + q)
        own = jnp.where(valid, own_weight * right + cross * other_right, 0.0)
        other = jnp.where(valid, other_weight * other_right + cross * right, 0.0)
        around, other_around = neighbours(own), neighbours(other)
        right = total_of(
            [short(mine_ref, q)] + [factor * there for factor, there in zip(factors, around)]
        )
        other_right = total_of(
            [short(other_ref, q)]
            + [factor * there for factor, there in zip(other_factors, other_around)]
        )
        final = own_weight * right + cross * other_right
        for t in range(cells_radial):
            value = parts_ref[q, t] + parts_ref[7, t] * final
            for side in range(4):
                value = value + parts_ref[3 + side, t] * around[side]
            row = jnp.where(lower_block, t, cells_radial - 1 - t)
            lines[pl.ds(row, cells_lateral, stride=pitch), :] = value[
                margin : margin + cells_lateral
            ]
        for x in range(cells_lateral):
            smoothed_ref[q, x] = lines[pl.ds(x * pitch, cells_radial), :]


def join(message, other, parts, like):
    cells_lateral, cells_radial, cells_side = like.shape[1:]
    pitch = round_up(cells_radial, 8)
    vmem = pl.BlockSpec(memory_space=pltpu.VMEM)
    return pl.pallas_call(
        join_kernel,
        out_shape=jax.ShapeDtypeStruct(like.shape, jnp.float32),
        in_specs=[vmem] * 3,
        out_specs=vmem,
        scratch_shapes=[pltpu.VMEM((cells_lateral * pitch, cells_side), jnp.float32)],
        compiler_params=pltpu.CompilerParams(vmem_limit_bytes=32 * 2**20),
        name="join",
    )(message, other, parts)


def extended(block, sides, width):
    for axis, dim in sides:
        count = lax.axis_size(axis)
        forward = [(i, i + 1) for i in range(count - 1)]
        backward = [(target, source) for source, target in forward]
        low = lax.ppermute(
            lax.slice_in_dim(block, block.shape[dim] - width, None, axis=dim), axis, forward
        )
        high = lax.ppermute(lax.slice_in_dim(block, 0, width, axis=dim), axis, backward)
        block = jnp.concatenate([low, block, high], axis=dim)
    return block


def block_factor(diagonal, lower_band, upper_band):
    pivots = []
    upper_scaled = []
    for row_index in range(diagonal.shape[1]):
        if row_index == 0:
            pivot_row = diagonal[:, 0]
        else:
            pivot_row = diagonal[:, row_index] - lower_band[:, row_index] * upper_scaled[-1]
        pivots.append(pivot_row)
        upper_scaled.append(upper_band[:, row_index] / pivot_row)
    return (pivots, upper_scaled)


def block_solve(pivots, upper_scaled, lower_band, right_side):
    row_total = len(pivots)
    modified = []
    for row_index in range(row_total):
        if row_index == 0:
            value_row = right_side[:, :, 0] / pivots[0]
        else:
            value_row = (
                right_side[:, :, row_index] - lower_band[:, row_index] * modified[-1]
            ) / pivots[row_index]
        modified.append(value_row)
    solved = [modified[-1]]
    for row_index in range(row_total - 2, -1, -1):
        solved.append(modified[row_index] - upper_scaled[row_index] * solved[-1])
    ordered = solved[::-1]
    return jnp.stack(ordered, 2)


def interface_solve(coefficients):
    column_total = coefficients.shape[2]

    def forward(carried, inputs):
        offset, carried_slope = carried
        left_first, right_first, left_last, right_last, free_first, free_last = inputs
        divisor = 1.0 - left_first * carried_slope
        first_fixed = (free_first + left_first * offset) / divisor
        first_slope = right_first / divisor
        next_offset = free_last + left_last * (offset + carried_slope * first_fixed)
        next_slope = left_last * carried_slope * first_slope + right_last
        return ((next_offset, next_slope), (first_fixed, first_slope, next_offset, next_slope))

    start_state = (
        jnp.zeros((3, column_total), jnp.float32),
        jnp.zeros((column_total,), jnp.float32),
    )
    scan_inputs = (
        coefficients[:, 0],
        coefficients[:, 1],
        coefficients[:, 2],
        coefficients[:, 3],
        coefficients[:, 4:7],
        coefficients[:, 7:10],
    )
    final_state, eliminated = lax.scan(forward, start_state, scan_inputs)

    def backward(first_next, inputs):
        fixed_first, slope_first, fixed_last, slope_last = inputs
        first_value = fixed_first + slope_first * first_next
        last_value = fixed_last + slope_last * first_next
        return (first_value, (first_value, last_value))

    final_first, values_pair = lax.scan(
        backward, jnp.zeros((3, column_total), jnp.float32), eliminated, reverse=True
    )
    first_values, last_values = values_pair
    nothing_row = jnp.zeros((1, 3, column_total), jnp.float32)
    from_below = jnp.concatenate([nothing_row, last_values[:-1]], 0)
    from_above = jnp.concatenate([first_values[1:], nothing_row], 0)
    return jnp.concatenate([from_below, from_above], 1)


def reduced_boundary(interface):
    gathered = lax.all_gather(interface, "rad", axis=0, tiled=True)
    solved = interface_solve(gathered)
    return lax.dynamic_index_in_dim(solved, lax.axis_index("rad"), 0, keepdims=False)


def many_blocks(stay, received, base_viscosity, velocity, forcing):
    cells_lateral, cells_radial, cells_side = base_viscosity.shape
    moved_rows = MIGRATION_PLANES * cells_radial
    odd = lax.rem(lax.axis_index("lat"), 2) == 1
    from_below = jnp.where(odd, received[0], received[1])[: 3 * moved_rows]
    from_above = jnp.where(odd, received[1], received[0])[: 3 * moved_rows]
    stay = stay.reshape(3, cells_lateral * cells_radial, cells_side)
    totals = stay.at[:, :moved_rows].add(from_below.reshape(3, moved_rows, cells_side))
    totals = totals.at[:, -moved_rows:].add(from_above.reshape(3, moved_rows, cells_side))
    grouped = totals.reshape(3, cells_lateral, cells_radial, cells_side)
    total_weight = grouped[0] + PRIOR_WEIGHT
    basalt_share = grouped[1] / total_weight
    melt_share = grouped[2] / total_weight
    viscosity = base_viscosity * jnp.exp(
        CONTRAST_BASALT * basalt_share - CONTRAST_MELT * melt_share
    )
    viscosity_pad = extended(viscosity, (("lat", 0), ("rad", 1)), 1)
    side_pad = jnp.pad(viscosity, ((0, 0), (0, 0), (1, 1)))
    face_west = LATERAL * 0.5 * (viscosity + viscosity_pad[:-2, 1:-1])
    face_east = LATERAL * 0.5 * (viscosity + viscosity_pad[2:, 1:-1])
    face_south = LATERAL * 0.5 * (viscosity + side_pad[:, :, :-2])
    face_north = LATERAL * 0.5 * (viscosity + side_pad[:, :, 2:])
    face_below = RADIAL * 0.5 * (viscosity + viscosity_pad[1:-1, :-2])
    face_above = RADIAL * 0.5 * (viscosity + viscosity_pad[1:-1, 2:])
    diagonal = face_west + face_east + face_south + face_north + face_below + face_above
    source = jnp.concatenate([forcing[:2], (forcing[2] - BUOYANCY * basalt_share)[None]], 0)
    lower_band = -face_below
    upper_band = -face_above
    pivots, upper_scaled = block_factor(diagonal, lower_band, upper_band)
    radial_iota = lax.broadcasted_iota(jnp.int32, viscosity.shape, 1)
    response_side = jnp.stack(
        [
            jnp.where(radial_iota == 0, face_below, jnp.float32(0.0)),
            jnp.where(radial_iota == cells_radial - 1, face_above, jnp.float32(0.0)),
        ]
    )
    response = block_solve(pivots, upper_scaled, lower_band, response_side)
    current = velocity
    for sweep_index in range(SWEEPS):
        velocity_pad = extended(current, (("lat", 1),), 1)
        side_velocity = jnp.pad(current, ((0, 0), (0, 0), (0, 0), (1, 1)))
        right_side = (
            source
            + face_west * velocity_pad[:, :-2]
            + face_east * velocity_pad[:, 2:]
            + face_south * side_velocity[..., :-2]
            + face_north * side_velocity[..., 2:]
        )
        particular = block_solve(pivots, upper_scaled, lower_band, right_side)
        interface = jnp.concatenate(
            [response[:, :, 0], response[:, :, -1], particular[:, :, 0], particular[:, :, -1]], 0
        )
        interface = interface.reshape(1, 10, cells_lateral * cells_side)
        boundary = reduced_boundary(interface).reshape(6, cells_lateral, 1, cells_side)
        current = particular + response[0][None] * boundary[:3] + response[1][None] * boundary[3:]
    composition = jnp.stack([basalt_share, melt_share])
    return (current, composition)

def local(tracer_values, tracer_cell, tracer_count, base_viscosity, velocity, forcing):
    stay, *sent = tracer_sums(
        tracer_values, tracer_cell, tracer_count, base_viscosity, velocity, forcing
    )
    received = pair_swaps(*sent)
    if lax.axis_size("rad") != 2:
        return many_blocks(stay, received, base_viscosity, velocity, forcing)
    composition, message, parts = eliminate(
        stay, sent, received, base_viscosity, velocity, forcing
    )
    other = lax.ppermute(message, "rad", [(0, 1), (1, 0)])
    return join(message, other, parts, velocity), composition


def solution(mesh):
    return jax.shard_map(
        local,
        mesh=mesh,
        in_specs=(
            P("lat", "rad", None, None),
            P("lat", "rad", None),
            P("lat", "rad", None),
            P("lat", "rad", None),
            P(None, "lat", "rad", None),
            P(None, "lat", "rad", None),
        ),
        out_specs=(P(None, "lat", "rad", None), P(None, "lat", "rad", None)),
        check_vma=False,
    )
```

```python
import functools

import jax
import jax.numpy as jnp
from jax import lax
from jax.experimental import pallas as pl
from jax.experimental.pallas import tpu as pltpu
from jax.sharding import PartitionSpec as P

SWEEPS = 2
MIGRATION_PLANES = 2

LATERAL = 0.015625
RADIAL = 32.0
BUOYANCY = 0.1
PRIOR_WEIGHT = 0.5
CONTRAST_BASALT = 2.3
CONTRAST_MELT = 1.5

TILE_ROWS = 8


def round_up(value, multiple):
    return -(-value // multiple) * multiple


def split_index(index, count):
    if count & (count - 1) == 0:
        return lax.shift_right_logical(index, count.bit_length() - 1), index & (count - 1)
    quotient = lax.div(index, count)
    return quotient, index - quotient * count


def payload_sections(cells_radial):
    pair = MIGRATION_PLANES * cells_radial
    starts = [0, 3 * pair, 6 * pair, 9 * pair, 10 * pair]
    return starts, round_up(10 * pair + 3 * cells_radial, 8)


def spread_row(row):
    return jnp.broadcast_to(row, (TILE_ROWS, row.shape[1]))


def hot_tiles(index, row_total):
    iota = lax.broadcasted_iota(jnp.int32, index.shape, 0)
    return [
        index == (iota + first).astype(jnp.float32)
        for first in range(0, row_total, index.shape[0])
    ]


def hot_product(loads, high, low, high_rows, low_rows):
    left, right = [], []
    for row in range(high.shape[0]):
        pick = slice(row, row + 1)
        high_masks = hot_tiles(spread_row(high[pick]), high_rows)
        low_masks = hot_tiles(spread_row(low[pick]), low_rows)
        spread = [spread_row(load[pick]) for load in loads]
        left.append(
            jnp.concatenate(
                [jnp.where(mask, load, 0.0) for load in spread for mask in high_masks], 0
            ).astype(jnp.bfloat16)
        )
        right.append(
            jnp.concatenate([jnp.where(mask, 1.0, 0.0) for mask in low_masks], 0).astype(
                jnp.bfloat16
            )
        )
    return lax.dot_general(
        jnp.concatenate(left, 1),
        jnp.concatenate(right, 1),
        (((1,), (1,)), ((), ())),
        preferred_element_type=jnp.float32,
    )


def has_partners():
    lateral, count = lax.axis_index("lat"), lax.axis_size("lat")
    odd = lax.rem(lateral, 2) == 1
    above, below = lateral + 1 < count, lateral > 0
    return jnp.logical_or(odd, above), jnp.where(odd, above, below)


def tracer_kernel(
    block_rows,
    counts_hbm,
    values_hbm,
    cells_hbm,
    base_hbm,
    velocity_hbm,
    forcing_hbm,
    stay_ref,
    first_ref,
    second_ref,
    counts,
    values,
    cells,
    base,
    velocity,
    forcing,
    stay_sums,
    moved_sums,
    payload,
    semaphores,
):
    cells_lateral, cells_radial, cells_side = base_hbm.shape
    plane_total = cells_lateral * cells_radial
    moved_planes = MIGRATION_PLANES * cells_radial
    half_side = cells_side // 2
    group_rows, lane_total = values.shape[2:]

    copies = []

    def fetch(source, target):
        copy = pltpu.make_async_copy(source, target, semaphores.at[len(copies)])
        copy.start()
        copies.append(copy)

    fetch(counts_hbm, counts)
    for first_row, rows in ((0, block_rows), (block_rows, group_rows - block_rows)):
        part = pl.ds(first_row, rows)
        fetch(cells_hbm.at[:, part], cells.at[:, part])
        fetch(values_hbm.at[:, :, part], values.at[:, :, part])
    for upward in (0, 1):
        outer = pl.ds((cells_lateral - MIGRATION_PLANES) * upward, MIGRATION_PLANES)
        fetch(base_hbm.at[outer], base.at[upward])
        fetch(velocity_hbm.at[:, outer], velocity.at[upward])
        fetch(forcing_hbm.at[:, pl.ds((cells_lateral - 1) * upward, 1)], forcing.at[upward])

    stay_sums[...] = jnp.zeros_like(stay_sums)
    moved_sums[...] = jnp.zeros_like(moved_sums)

    def loads_of(group, first_row):
        rows = pl.ds(first_row, block_rows)
        shape = (block_rows, lane_total)
        slot = (first_row + lax.broadcasted_iota(jnp.int32, shape, 0)) * lane_total
        slot = slot + lax.broadcasted_iota(jnp.int32, shape, 1)
        weight = jnp.where(
            slot < counts[0, 0, group], 0.5 + values[0, group, rows, :], jnp.float32(0.0)
        )
        loads = [weight, weight * values[1, group, rows, :], weight * values[2, group, rows, :]]
        plane, side = split_index(cells[group, rows, :], cells_side)
        return loads, plane, side

    def step(first_row):
        loads, plane, side = loads_of(1, first_row)
        stay_sums[...] += hot_product(
            loads, plane.astype(jnp.float32), side.astype(jnp.float32), plane_total, cells_side
        )
        for slot, group in enumerate((0, 2)):
            loads, plane, side = loads_of(group, first_row)
            if group == 0:
                plane = plane - (plane_total - moved_planes)
            upper = side >= half_side
            high = jnp.where(upper, plane + moved_planes, plane).astype(jnp.float32)
            low = jnp.where(upper, side - half_side, side).astype(jnp.float32)
            moved_sums[slot] += hot_product(loads, high, low, 2 * moved_planes, half_side)

    for copy in copies[:3]:
        copy.wait()
    step(0)
    for copy in copies[3:5]:
        copy.wait()

    def repeat(index, carried):
        step(pl.multiple_of(index * block_rows, block_rows))
        return carried

    lax.fori_loop(1, group_rows // block_rows, repeat, 0)
    for copy in copies[5:]:
        copy.wait()

    stay_ref[...] = stay_sums[...]
    starts, _ = payload_sections(cells_radial)
    odd = lax.rem(lax.axis_index("lat"), 2)
    for upward in (0, 1):
        place = odd if upward else 1 - odd
        first_plane = cells_lateral - MIGRATION_PLANES if upward else 0
        for q in range(3):
            for half in (0, 1):
                payload[
                    place,
                    pl.ds(starts[0] + q * moved_planes, moved_planes),
                    pl.ds(half * half_side, half_side),
                ] = moved_sums[upward, pl.ds((2 * q + half) * moved_planes, moved_planes), :]
            payload[place, pl.ds(starts[1] + q * moved_planes, moved_planes), :] = stay_sums[
                pl.ds(q * plane_total + first_plane * cells_radial, moved_planes), :
            ]
            for offset in range(MIGRATION_PLANES):
                payload[
                    place,
                    pl.ds(starts[2] + q * moved_planes + offset * cells_radial, cells_radial),
                    :,
                ] = velocity[upward, q, offset]
            payload[place, pl.ds(starts[4] + q * cells_radial, cells_radial), :] = forcing[
                upward, q, 0
            ]
        for offset in range(MIGRATION_PLANES):
            payload[place, pl.ds(starts[3] + offset * cells_radial, cells_radial), :] = base[
                upward, offset
            ]
    has_first, has_second = has_partners()
    first_ref[...] = jnp.where(has_first, payload[0], 0.0)
    second_ref[...] = jnp.where(has_second, payload[1], 0.0)


def tracer_sums(tracer_values, tracer_cell, tracer_count, base_viscosity, velocity, forcing):
    cells_lateral, cells_radial, cells_side = base_viscosity.shape
    plane_total = cells_lateral * cells_radial
    moved_planes = MIGRATION_PLANES * cells_radial
    lane_total = 128
    values = tracer_values.reshape(3, 3, -1, lane_total)
    cells = tracer_cell.reshape(3, -1, lane_total)
    group_rows = cells.shape[1]
    _, payload_rows = payload_sections(cells_radial)
    hbm = pl.BlockSpec(memory_space=pltpu.HBM)
    vmem = pl.BlockSpec(memory_space=pltpu.VMEM)
    payload = jax.ShapeDtypeStruct((payload_rows, cells_side), jnp.float32)
    outer_planes = (MIGRATION_PLANES, cells_radial, cells_side)
    return pl.pallas_call(
        functools.partial(tracer_kernel, 16),
        out_shape=(
            jax.ShapeDtypeStruct((3 * plane_total, cells_side), jnp.float32),
            payload,
            payload,
        ),
        in_specs=[hbm] * 6,
        out_specs=(vmem, vmem, vmem),
        scratch_shapes=[
            pltpu.SMEM(tracer_count.shape, jnp.int32),
            pltpu.VMEM(values.shape, jnp.float32),
            pltpu.VMEM(cells.shape, jnp.int32),
            pltpu.VMEM((2,) + outer_planes, jnp.float32),
            pltpu.VMEM((2, 3) + outer_planes, jnp.float32),
            pltpu.VMEM((2, 3, 1, cells_radial, cells_side), jnp.float32),
            pltpu.VMEM((3 * plane_total, cells_side), jnp.float32),
            pltpu.VMEM((2, 6 * moved_planes, cells_side // 2), jnp.float32),
            pltpu.VMEM((2, payload_rows, cells_side), jnp.float32),
            pltpu.SemaphoreType.DMA((11,)),
        ],
        compiler_params=pltpu.CompilerParams(vmem_limit_bytes=32 * 2**20),
        cost_estimate=pl.CostEstimate(
            flops=6 * group_rows * lane_total * plane_total * cells_side // 8,
            bytes_accessed=4 * (values.size + cells.size),
            transcendentals=0,
        ),
        name="tracer_sums",
    )(
        *(
            pltpu.with_memory_space_constraint(array, pltpu.HBM)
            for array in (tracer_count, values, cells, base_viscosity, velocity, forcing)
        )
    )


def pair_swaps(first, second):
    count = lax.axis_size("lat")
    received = []
    for payload, start in ((second, 1), (first, 0)):
        target = list(range(count))
        for low in range(start, count - 1, 2):
            target[low], target[low + 1] = low + 1, low
        received.append(lax.ppermute(payload, "lat", list(enumerate(target))))
    return received[::-1]


def shift_planes(block, step):
    return pltpu.roll(block, step % block.shape[0], 0)


def shift_side(block, step):
    lane_total = block.shape[1]
    lane = lax.broadcasted_iota(jnp.int32, block.shape, 1)
    inside = lane >= step if step > 0 else lane < lane_total + step
    return jnp.where(inside, pltpu.roll(block, step % lane_total, 1), jnp.float32(0.0))


def neighbours(block):
    return (
        shift_planes(block, 1),
        shift_planes(block, -1),
        shift_side(block, 1),
        shift_side(block, -1),
    )


def total_of(terms):
    result = terms[0]
    for term in terms[1:]:
        result = result + term
    return result


def inside_grid(shape, margin, cells_lateral):
    plane = lax.broadcasted_iota(jnp.int32, shape, 0)
    lateral = lax.axis_index("lat")
    first = jnp.where(lateral == 0, margin, 1)
    last = jnp.where(lateral == lax.axis_size("lat") - 1, margin + cells_lateral, shape[0] - 1)
    return (plane >= first) & (plane < last)


def eliminate_kernel(
    stay_ref,
    second_ref,
    first_ref,
    from_second_ref,
    from_first_ref,
    base_ref,
    velocity_ref,
    forcing_ref,
    composition_ref,
    message_ref,
    parts_ref,
    fields,
):
    cells_lateral, cells_radial, cells_side = base_ref.shape
    margin = MIGRATION_PLANES
    planes = cells_lateral + 2 * margin
    pitch = fields.shape[1] // planes
    moved_planes = margin * cells_radial
    starts, _ = payload_sections(cells_radial)
    odd = lax.rem(lax.axis_index("lat"), 2) == 1
    BASE, VELOCITY, SOURCE = 3, 4, 7

    def sent(upward, start, rows):
        part = pl.ds(start, rows)
        mine_first = odd if not upward else jnp.logical_not(odd)
        return jnp.where(mine_first, first_ref[part, :], second_ref[part, :])

    def arrived(from_above, start, rows):
        part = pl.ds(start, rows)
        is_first = odd if not from_above else jnp.logical_not(odd)
        return jnp.where(is_first, from_first_ref[part, :], from_second_ref[part, :])

    def put(field, plane, value):
        fields[field, pl.ds(plane * pitch, cells_radial), :] = value

    for q in range(3):
        for x in range(cells_lateral):
            mine = stay_ref[pl.ds((q * cells_lateral + x) * cells_radial, cells_radial), :]
            if x < margin:
                row = q * moved_planes + x * cells_radial
                mine = mine + arrived(False, starts[0] + row, cells_radial)
            if x >= cells_lateral - margin:
                row = q * moved_planes + (x - cells_lateral + margin) * cells_radial
                mine = mine + arrived(True, starts[0] + row, cells_radial)
            put(q, margin + x, mine)
            put(VELOCITY + q, margin + x, velocity_ref[q, x])
            put(SOURCE + q, margin + x, forcing_ref[q, x])
        for offset in range(margin):
            row = q * moved_planes + offset * cells_radial
            for above in (False, True):
                plane = offset + (margin + cells_lateral if above else 0)
                put(
                    q,
                    plane,
                    sent(above, starts[0] + row, cells_radial)
                    + arrived(above, starts[1] + row, cells_radial),
                )
                put(VELOCITY + q, plane, arrived(above, starts[2] + row, cells_radial))
        put(
            SOURCE + q,
            margin - 1,
            arrived(False, starts[4] + q * cells_radial, cells_radial),
        )
        put(
            SOURCE + q,
            margin + cells_lateral,
            arrived(True, starts[4] + q * cells_radial, cells_radial),
        )
        for plane in (0, planes - 1):
            put(SOURCE + q, plane, jnp.zeros((cells_radial, cells_side), jnp.float32))
    for x in range(cells_lateral):
        put(BASE, margin + x, base_ref[x])
    for offset in range(margin):
        for above in (False, True):
            plane = offset + (margin + cells_lateral if above else 0)
            put(BASE, plane, arrived(above, starts[3] + offset * cells_radial, cells_radial))

    for plane in range(planes):
        rows = pl.ds(plane * pitch, cells_radial)
        total_weight = fields[0, rows, :] + PRIOR_WEIGHT
        basalt_share = fields[1, rows, :] / total_weight
        melt_share = fields[2, rows, :] / total_weight
        fields[BASE, rows, :] = fields[BASE, rows, :] * jnp.exp(
            CONTRAST_BASALT * basalt_share - CONTRAST_MELT * melt_share
        )
        fields[SOURCE + 2, rows, :] = fields[SOURCE + 2, rows, :] - BUOYANCY * basalt_share
        if margin <= plane < margin + cells_lateral:
            composition_ref[0, plane - margin] = basalt_share
            composition_ref[1, plane - margin] = melt_share

    lower_block = lax.axis_index("rad") == 0

    def radial(field, t):
        row = jnp.where(lower_block, t, cells_radial - 1 - t)
        return fields[field, pl.ds(row, planes, stride=pitch), :]

    shape = (planes, cells_side)
    valid = inside_grid(shape, margin, cells_lateral)
    nothing = jnp.zeros(shape, jnp.float32)
    last = cells_radial - 1
    viscosity = [radial(BASE, t) for t in range(cells_radial)]
    lateral_faces = [
        [LATERAL * 0.5 * (here + there) for there in neighbours(here)] for here in viscosity
    ]
    radial_faces = [RADIAL * 0.5 * viscosity[0]] + [
        RADIAL * 0.5 * (viscosity[t - 1] + viscosity[t]) for t in range(1, cells_radial)
    ]

    excess = total_of(lateral_faces[0]) + radial_faces[0]
    inverse, coupling = [], []
    for t in range(last):
        inverse.append(1.0 / (excess + radial_faces[t + 1]))
        coupling.append(radial_faces[t + 1] * inverse[t])
        excess = total_of(lateral_faces[t + 1]) + coupling[t] * excess

    def lateral_terms(t, around):
        return [face * there for face, there in zip(lateral_faces[t], around)]

    def forward(right_side):
        eliminated = [right_side[0]]
        for t in range(1, cells_radial):
            eliminated.append(right_side[t] + coupling[t - 1] * eliminated[t - 1])
        return eliminated

    def backward(eliminated):
        solved = [nothing]
        for t in range(last - 1, -1, -1):
            solved.append(eliminated[t] * inverse[t] + coupling[t] * solved[-1])
        return solved[::-1]

    response = [jnp.ones(shape, jnp.float32)]
    for t in range(last - 1, -1, -1):
        response.append(coupling[t] * response[-1])
    response = response[::-1]

    message_ref[pl.ds(0, planes), :] = viscosity[last]
    message_ref[pl.ds(planes, planes), :] = excess
    short_start = 5 * planes

    def put_short(index, value):
        message_ref[pl.ds(short_start + index * cells_lateral, cells_lateral), :] = value[
            margin : margin + cells_lateral
        ]

    parts = []
    for q in range(3):
        source = [radial(SOURCE + q, t) for t in range(cells_radial)]
        eliminated = forward(
            [
                total_of([source[t]] + lateral_terms(t, neighbours(radial(VELOCITY + q, t))))
                for t in range(cells_radial)
            ]
        )
        message_ref[pl.ds((2 + q) * planes, planes), :] = eliminated[last]
        particular = [jnp.where(valid, value, 0.0) for value in backward(eliminated)]
        eliminated = forward(
            [
                total_of([source[t]] + lateral_terms(t, neighbours(particular[t])))
                for t in range(cells_radial)
            ]
        )
        put_short(q, eliminated[last])
        parts.append(backward(eliminated))
    around = [neighbours(jnp.where(valid, value, 0.0)) for value in response]
    for side in range(4):
        eliminated = forward([lateral_faces[t][side] * around[t][side] for t in range(cells_radial)])
        put_short(3 + side, eliminated[last])
        parts.append(backward(eliminated))
    parts.append(response)
    for index, part in enumerate(parts):
        for t in range(cells_radial):
            parts_ref[index, t] = part[t]
    unused = short_start + 7 * cells_lateral
    message_ref[pl.ds(unused, message_ref.shape[0] - unused), :] = jnp.zeros(
        (message_ref.shape[0] - unused, cells_side), jnp.float32
    )


def message_rows(cells_lateral):
    planes = cells_lateral + 2 * MIGRATION_PLANES
    return round_up(5 * planes + 7 * cells_lateral + MIGRATION_PLANES, 8)


def eliminate(stay, sent, received, base_viscosity, velocity, forcing):
    cells_lateral, cells_radial, cells_side = base_viscosity.shape
    planes = cells_lateral + 2 * MIGRATION_PLANES
    pitch = round_up(cells_radial, 8)
    vmem = pl.BlockSpec(memory_space=pltpu.VMEM)
    return pl.pallas_call(
        eliminate_kernel,
        out_shape=(
            jax.ShapeDtypeStruct((2,) + base_viscosity.shape, jnp.float32),
            jax.ShapeDtypeStruct((message_rows(cells_lateral), cells_side), jnp.float32),
            jax.ShapeDtypeStruct((8, cells_radial, planes, cells_side), jnp.float32),
        ),
        in_specs=[vmem] * 8,
        out_specs=(vmem, vmem, vmem),
        scratch_shapes=[pltpu.VMEM((10, planes * pitch, cells_side), jnp.float32)],
        compiler_params=pltpu.CompilerParams(vmem_limit_bytes=32 * 2**20),
        name="eliminate",
    )(stay, *sent[::-1], *received[::-1], base_viscosity, velocity, forcing)


def join_kernel(mine_ref, other_ref, parts_ref, smoothed_ref, lines):
    _, cells_lateral, cells_radial, cells_side = smoothed_ref.shape
    margin = MIGRATION_PLANES
    planes = cells_lateral + 2 * margin
    pitch = lines.shape[0] // cells_lateral
    shape = (planes, cells_side)
    valid = inside_grid(shape, margin, cells_lateral)
    lower_block = lax.axis_index("rad") == 0

    def long(ref, index):
        return ref[pl.ds(index * planes, planes), :]

    def short(ref, index):
        return ref[pl.ds(5 * planes + index * cells_lateral - margin, planes), :]

    face = RADIAL * 0.5 * (long(mine_ref, 0) + long(other_ref, 0))
    excess, other_excess = long(mine_ref, 1), long(other_ref, 1)
    scale = 1.0 / (excess * other_excess + face * (excess + other_excess))
    own_weight = (other_excess + face) * scale
    other_weight = (excess + face) * scale
    cross = face * scale
    factors = [short(mine_ref, 3 + side) for side in range(4)]
    other_factors = [short(other_ref, 3 + side) for side in range(4)]
    for q in range(3):
        right, other_right = long(mine_ref, 2 + q), long(other_ref, 2 + q)
        own = jnp.where(valid, own_weight * right + cross * other_right, 0.0)
        other = jnp.where(valid, other_weight * other_right + cross * right, 0.0)
        around, other_around = neighbours(own), neighbours(other)
        right = total_of(
            [short(mine_ref, q)] + [factor * there for factor, there in zip(factors, around)]
        )
        other_right = total_of(
            [short(other_ref, q)]
            + [factor * there for factor, there in zip(other_factors, other_around)]
        )
        final = own_weight * right + cross * other_right
        for t in range(cells_radial):
            value = parts_ref[q, t] + parts_ref[7, t] * final
            for side in range(4):
                value = value + parts_ref[3 + side, t] * around[side]
            row = jnp.where(lower_block, t, cells_radial - 1 - t)
            lines[pl.ds(row, cells_lateral, stride=pitch), :] = value[
                margin : margin + cells_lateral
            ]
        for x in range(cells_lateral):
            smoothed_ref[q, x] = lines[pl.ds(x * pitch, cells_radial), :]


def join(message, other, parts, like):
    cells_lateral, cells_radial, cells_side = like.shape[1:]
    pitch = round_up(cells_radial, 8)
    vmem = pl.BlockSpec(memory_space=pltpu.VMEM)
    return pl.pallas_call(
        join_kernel,
        out_shape=jax.ShapeDtypeStruct(like.shape, jnp.float32),
        in_specs=[vmem] * 3,
        out_specs=vmem,
        scratch_shapes=[pltpu.VMEM((cells_lateral * pitch, cells_side), jnp.float32)],
        compiler_params=pltpu.CompilerParams(vmem_limit_bytes=32 * 2**20),
        name="join",
    )(message, other, parts)


def extended(block, sides, width):
    for axis, dim in sides:
        count = lax.axis_size(axis)
        forward = [(i, i + 1) for i in range(count - 1)]
        backward = [(target, source) for source, target in forward]
        low = lax.ppermute(
            lax.slice_in_dim(block, block.shape[dim] - width, None, axis=dim), axis, forward
        )
        high = lax.ppermute(lax.slice_in_dim(block, 0, width, axis=dim), axis, backward)
        block = jnp.concatenate([low, block, high], axis=dim)
    return block


def block_factor(diagonal, lower_band, upper_band):
    pivots = []
    upper_scaled = []
    for row_index in range(diagonal.shape[1]):
        if row_index == 0:
            pivot_row = diagonal[:, 0]
        else:
            pivot_row = diagonal[:, row_index] - lower_band[:, row_index] * upper_scaled[-1]
        pivots.append(pivot_row)
        upper_scaled.append(upper_band[:, row_index] / pivot_row)
    return (pivots, upper_scaled)


def block_solve(pivots, upper_scaled, lower_band, right_side):
    row_total = len(pivots)
    modified = []
    for row_index in range(row_total):
        if row_index == 0:
            value_row = right_side[:, :, 0] / pivots[0]
        else:
            value_row = (
                right_side[:, :, row_index] - lower_band[:, row_index] * modified[-1]
            ) / pivots[row_index]
        modified.append(value_row)
    solved = [modified[-1]]
    for row_index in range(row_total - 2, -1, -1):
        solved.append(modified[row_index] - upper_scaled[row_index] * solved[-1])
    ordered = solved[::-1]
    return jnp.stack(ordered, 2)


def interface_solve(coefficients):
    column_total = coefficients.shape[2]

    def forward(carried, inputs):
        offset, carried_slope = carried
        left_first, right_first, left_last, right_last, free_first, free_last = inputs
        divisor = 1.0 - left_first * carried_slope
        first_fixed = (free_first + left_first * offset) / divisor
        first_slope = right_first / divisor
        next_offset = free_last + left_last * (offset + carried_slope * first_fixed)
        next_slope = left_last * carried_slope * first_slope + right_last
        return ((next_offset, next_slope), (first_fixed, first_slope, next_offset, next_slope))

    start_state = (
        jnp.zeros((3, column_total), jnp.float32),
        jnp.zeros((column_total,), jnp.float32),
    )
    scan_inputs = (
        coefficients[:, 0],
        coefficients[:, 1],
        coefficients[:, 2],
        coefficients[:, 3],
        coefficients[:, 4:7],
        coefficients[:, 7:10],
    )
    final_state, eliminated = lax.scan(forward, start_state, scan_inputs)

    def backward(first_next, inputs):
        fixed_first, slope_first, fixed_last, slope_last = inputs
        first_value = fixed_first + slope_first * first_next
        last_value = fixed_last + slope_last * first_next
        return (first_value, (first_value, last_value))

    final_first, values_pair = lax.scan(
        backward, jnp.zeros((3, column_total), jnp.float32), eliminated, reverse=True
    )
    first_values, last_values = values_pair
    nothing_row = jnp.zeros((1, 3, column_total), jnp.float32)
    from_below = jnp.concatenate([nothing_row, last_values[:-1]], 0)
    from_above = jnp.concatenate([first_values[1:], nothing_row], 0)
    return jnp.concatenate([from_below, from_above], 1)


def reduced_boundary(interface):
    gathered = lax.all_gather(interface, "rad", axis=0, tiled=True)
    solved = interface_solve(gathered)
    return lax.dynamic_index_in_dim(solved, lax.axis_index("rad"), 0, keepdims=False)


def many_blocks(stay, received, base_viscosity, velocity, forcing):
    cells_lateral, cells_radial, cells_side = base_viscosity.shape
    moved_rows = MIGRATION_PLANES * cells_radial
    odd = lax.rem(lax.axis_index("lat"), 2) == 1
    from_below = jnp.where(odd, received[0], received[1])[: 3 * moved_rows]
    from_above = jnp.where(odd, received[1], received[0])[: 3 * moved_rows]
    stay = stay.reshape(3, cells_lateral * cells_radial, cells_side)
    totals = stay.at[:, :moved_rows].add(from_below.reshape(3, moved_rows, cells_side))
    totals = totals.at[:, -moved_rows:].add(from_above.reshape(3, moved_rows, cells_side))
    grouped = totals.reshape(3, cells_lateral, cells_radial, cells_side)
    total_weight = grouped[0] + PRIOR_WEIGHT
    basalt_share = grouped[1] / total_weight
    melt_share = grouped[2] / total_weight
    viscosity = base_viscosity * jnp.exp(
        CONTRAST_BASALT * basalt_share - CONTRAST_MELT * melt_share
    )
    viscosity_pad = extended(viscosity, (("lat", 0), ("rad", 1)), 1)
    side_pad = jnp.pad(viscosity, ((0, 0), (0, 0), (1, 1)))
    face_west = LATERAL * 0.5 * (viscosity + viscosity_pad[:-2, 1:-1])
    face_east = LATERAL * 0.5 * (viscosity + viscosity_pad[2:, 1:-1])
    face_south = LATERAL * 0.5 * (viscosity + side_pad[:, :, :-2])
    face_north = LATERAL * 0.5 * (viscosity + side_pad[:, :, 2:])
    face_below = RADIAL * 0.5 * (viscosity + viscosity_pad[1:-1, :-2])
    face_above = RADIAL * 0.5 * (viscosity + viscosity_pad[1:-1, 2:])
    diagonal = face_west + face_east + face_south + face_north + face_below + face_above
    source = jnp.concatenate([forcing[:2], (forcing[2] - BUOYANCY * basalt_share)[None]], 0)
    lower_band = -face_below
    upper_band = -face_above
    pivots, upper_scaled = block_factor(diagonal, lower_band, upper_band)
    radial_iota = lax.broadcasted_iota(jnp.int32, viscosity.shape, 1)
    response_side = jnp.stack(
        [
            jnp.where(radial_iota == 0, face_below, jnp.float32(0.0)),
            jnp.where(radial_iota == cells_radial - 1, face_above, jnp.float32(0.0)),
        ]
    )
    response = block_solve(pivots, upper_scaled, lower_band, response_side)
    current = velocity
    for sweep_index in range(SWEEPS):
        velocity_pad = extended(current, (("lat", 1),), 1)
        side_velocity = jnp.pad(current, ((0, 0), (0, 0), (0, 0), (1, 1)))
        right_side = (
            source
            + face_west * velocity_pad[:, :-2]
            + face_east * velocity_pad[:, 2:]
            + face_south * side_velocity[..., :-2]
            + face_north * side_velocity[..., 2:]
        )
        particular = block_solve(pivots, upper_scaled, lower_band, right_side)
        interface = jnp.concatenate(
            [response[:, :, 0], response[:, :, -1], particular[:, :, 0], particular[:, :, -1]], 0
        )
        interface = interface.reshape(1, 10, cells_lateral * cells_side)
        boundary = reduced_boundary(interface).reshape(6, cells_lateral, 1, cells_side)
        current = particular + response[0][None] * boundary[:3] + response[1][None] * boundary[3:]
    composition = jnp.stack([basalt_share, melt_share])
    return (current, composition)

def local(tracer_values, tracer_cell, tracer_count, base_viscosity, velocity, forcing):
    stay, *sent = tracer_sums(
        tracer_values, tracer_cell, tracer_count, base_viscosity, velocity, forcing
    )
    received = pair_swaps(*sent)
    if lax.axis_size("rad") != 2:
        return many_blocks(stay, received, base_viscosity, velocity, forcing)
    composition, message, parts = eliminate(
        stay, sent, received, base_viscosity, velocity, forcing
    )
    other = lax.ppermute(message, "rad", [(0, 1), (1, 0)])
    return join(message, other, parts, velocity), composition


def solution(mesh):
    return jax.shard_map(
        local,
        mesh=mesh,
        in_specs=(
            P("lat", "rad", None, None),
            P("lat", "rad", None),
            P("lat", "rad", None),
            P("lat", "rad", None),
            P(None, "lat", "rad", None),
            P(None, "lat", "rad", None),
        ),
        out_specs=(P(None, "lat", "rad", None), P(None, "lat", "rad", None)),
        check_vma=False,
    )
```

```python
import functools

import jax
import jax.numpy as jnp
from jax import lax
from jax.experimental import pallas as pl
from jax.experimental.pallas import tpu as pltpu
from jax.sharding import PartitionSpec as P

SWEEPS = 2
MIGRATION_PLANES = 2

LATERAL = 0.015625
RADIAL = 32.0
BUOYANCY = 0.1
PRIOR_WEIGHT = 0.5
CONTRAST_BASALT = 2.3
CONTRAST_MELT = 1.5

TILE_ROWS = 16


def round_up(value, multiple):
    return -(-value // multiple) * multiple


def split_index(index, count):
    if count & (count - 1) == 0:
        return lax.shift_right_logical(index, count.bit_length() - 1), index & (count - 1)
    quotient = lax.div(index, count)
    return quotient, index - quotient * count


def payload_sections(cells_radial):
    pair = MIGRATION_PLANES * cells_radial
    starts = [0, 3 * pair, 6 * pair, 9 * pair, 10 * pair]
    return starts, round_up(10 * pair + 3 * cells_radial, 8)


def spread_row(row):
    return jnp.broadcast_to(row, (TILE_ROWS, row.shape[1])).astype(jnp.bfloat16)


def hot_tiles(index, row_total):
    iota = lax.broadcasted_iota(jnp.int32, index.shape, 0)
    return [
        index == (iota + first).astype(jnp.float32).astype(jnp.bfloat16)
        for first in range(0, row_total, TILE_ROWS)
    ]


def put_hot(left_ref, right_ref, loads, high, low):
    high_rows, low_rows = left_ref.shape[0] // 3, right_ref.shape[0]
    lane_total = high.shape[1]
    zero = jnp.zeros((TILE_ROWS, lane_total), jnp.bfloat16)
    one = jnp.ones((TILE_ROWS, lane_total), jnp.bfloat16)
    for row in range(high.shape[0]):
        pick = slice(row, row + 1)
        lanes = slice(row * lane_total, (row + 1) * lane_total)
        high_masks = hot_tiles(spread_row(high[pick]), high_rows)
        for q, load in enumerate(loads):
            load = spread_row(load[pick])
            for tile, mask in enumerate(high_masks):
                first = q * high_rows + tile * TILE_ROWS
                left_ref[first : first + TILE_ROWS, lanes] = jnp.where(mask, load, zero)
        for tile, mask in enumerate(hot_tiles(spread_row(low[pick]), low_rows)):
            first = tile * TILE_ROWS
            right_ref[first : first + TILE_ROWS, lanes] = jnp.where(mask, one, zero)


def hot_product(left_ref, right_ref):
    return lax.dot_general(
        left_ref[...],
        right_ref[...],
        (((1,), (1,)), ((), ())),
        preferred_element_type=jnp.float32,
    )


def has_partners():
    lateral, count = lax.axis_index("lat"), lax.axis_size("lat")
    odd = lax.rem(lateral, 2) == 1
    above, below = lateral + 1 < count, lateral > 0
    return jnp.logical_or(odd, above), jnp.where(odd, above, below)


def tracer_kernel(
    block_rows,
    counts_hbm,
    values_hbm,
    cells_hbm,
    base_hbm,
    velocity_hbm,
    forcing_hbm,
    stay_ref,
    first_ref,
    second_ref,
    counts,
    values,
    cells,
    base,
    velocity,
    forcing,
    stay_sums,
    moved_sums,
    payload,
    semaphores,
    *hot,
):
    cells_lateral, cells_radial, cells_side = base_hbm.shape
    plane_total = cells_lateral * cells_radial
    half_planes = plane_total // 2
    moved_planes = MIGRATION_PLANES * cells_radial
    half_side = cells_side // 2
    group_rows, lane_total = values.shape[2:]
    half_rows = stay_sums.shape[0] // 3
    moved_rows = moved_sums.shape[1] // 3
    buffers = (hot[: len(hot) // 2], hot[len(hot) // 2 :])

    copies = []

    def fetch(source, target):
        copy = pltpu.make_async_copy(source, target, semaphores.at[len(copies)])
        copy.start()
        copies.append(copy)

    fetch(counts_hbm, counts)
    for first_row, rows in ((0, block_rows), (block_rows, group_rows - block_rows)):
        part = pl.ds(first_row, rows)
        fetch(cells_hbm.at[:, part], cells.at[:, part])
        fetch(values_hbm.at[:, :, part], values.at[:, :, part])
    for upward in (0, 1):
        outer = pl.ds((cells_lateral - MIGRATION_PLANES) * upward, MIGRATION_PLANES)
        fetch(base_hbm.at[outer], base.at[upward])
        fetch(velocity_hbm.at[:, outer], velocity.at[upward])
        fetch(forcing_hbm.at[:, pl.ds((cells_lateral - 1) * upward, 1)], forcing.at[upward])

    stay_sums[...] = jnp.zeros_like(stay_sums)
    moved_sums[...] = jnp.zeros_like(moved_sums)

    def loads_of(group, first_row):
        rows = pl.ds(first_row, block_rows)
        shape = (block_rows, lane_total)
        slot = (first_row + lax.broadcasted_iota(jnp.int32, shape, 0)) * lane_total
        slot = slot + lax.broadcasted_iota(jnp.int32, shape, 1)
        weight = jnp.where(
            slot < counts[0, 0, group], 0.5 + values[0, group, rows, :], jnp.float32(0.0)
        )
        loads = [weight, weight * values[1, group, rows, :], weight * values[2, group, rows, :]]
        plane, side = split_index(cells[group, rows, :], cells_side)
        return loads, plane, side

    def prepare(buffer, block):
        first_row = block * block_rows
        if not isinstance(block, int):
            first_row = pl.multiple_of(first_row, block_rows)
        loads, plane, side = loads_of(1, first_row)
        upper = plane >= half_planes
        high = jnp.where(upper, plane - half_planes, plane).astype(jnp.float32)
        low = jnp.where(upper, side + cells_side, side).astype(jnp.float32)
        put_hot(buffer[0], buffer[1], loads, high, low)
        for slot, group in enumerate((0, 2)):
            loads, plane, side = loads_of(group, first_row)
            if group == 0:
                plane = plane - (plane_total - moved_planes)
            upper = side >= half_side
            high = jnp.where(upper, plane + moved_planes, plane).astype(jnp.float32)
            low = jnp.where(upper, side - half_side, side).astype(jnp.float32)
            put_hot(buffer[2 + 2 * slot], buffer[3 + 2 * slot], loads, high, low)

    def add(buffer):
        stay_sums[...] += hot_product(buffer[0], buffer[1])
        for slot in (0, 1):
            moved_sums[slot] += hot_product(buffer[2 + 2 * slot], buffer[3 + 2 * slot])

    for copy in copies[:3]:
        copy.wait()
    prepare(buffers[0], 0)
    for copy in copies[3:5]:
        copy.wait()
    blocks = group_rows // block_rows

    def repeat(index, carried):
        prepare(buffers[1], 2 * index + 1)
        add(buffers[0])
        prepare(buffers[0], 2 * index + 2)
        add(buffers[1])
        return carried

    lax.fori_loop(0, (blocks - 1) // 2, repeat, 0)
    if blocks % 2 == 0:
        prepare(buffers[1], blocks - 1)
    add(buffers[0])
    if blocks % 2 == 0:
        add(buffers[1])
    for copy in copies[5:]:
        copy.wait()

    for q in range(3):
        rows = pl.ds(q * half_rows, half_planes)
        for half in (0, 1):
            stay_ref[pl.ds(q * plane_total + half * half_planes, half_planes), :] = stay_sums[
                rows, half * cells_side : (half + 1) * cells_side
            ]
    starts, _ = payload_sections(cells_radial)
    odd = lax.rem(lax.axis_index("lat"), 2)
    for upward in (0, 1):
        place = odd if upward else 1 - odd
        first_plane = cells_lateral - MIGRATION_PLANES if upward else 0
        for q in range(3):
            for half in (0, 1):
                payload[
                    place,
                    pl.ds(starts[0] + q * moved_planes, moved_planes),
                    pl.ds(half * half_side, half_side),
                ] = moved_sums[
                    upward, pl.ds(q * moved_rows + half * moved_planes, moved_planes), :
                ]
            payload[place, pl.ds(starts[1] + q * moved_planes, moved_planes), :] = stay_ref[
                pl.ds(q * plane_total + first_plane * cells_radial, moved_planes), :
            ]
            for offset in range(MIGRATION_PLANES):
                payload[
                    place,
                    pl.ds(starts[2] + q * moved_planes + offset * cells_radial, cells_radial),
                    :,
                ] = velocity[upward, q, offset]
            payload[place, pl.ds(starts[4] + q * cells_radial, cells_radial), :] = forcing[
                upward, q, 0
            ]
        for offset in range(MIGRATION_PLANES):
            payload[place, pl.ds(starts[3] + offset * cells_radial, cells_radial), :] = base[
                upward, offset
            ]
    has_first, has_second = has_partners()
    first_ref[...] = jnp.where(has_first, payload[0], 0.0)
    second_ref[...] = jnp.where(has_second, payload[1], 0.0)


def tracer_sums(tracer_values, tracer_cell, tracer_count, base_viscosity, velocity, forcing):
    cells_lateral, cells_radial, cells_side = base_viscosity.shape
    plane_total = cells_lateral * cells_radial
    moved_planes = MIGRATION_PLANES * cells_radial
    lane_total = 128
    values = tracer_values.reshape(3, 3, -1, lane_total)
    cells = tracer_cell.reshape(3, -1, lane_total)
    group_rows = cells.shape[1]
    _, payload_rows = payload_sections(cells_radial)
    hbm = pl.BlockSpec(memory_space=pltpu.HBM)
    vmem = pl.BlockSpec(memory_space=pltpu.VMEM)
    payload = jax.ShapeDtypeStruct((payload_rows, cells_side), jnp.float32)
    outer_planes = (MIGRATION_PLANES, cells_radial, cells_side)
    half_rows = round_up(plane_total // 2, TILE_ROWS)
    moved_rows = round_up(2 * moved_planes, TILE_ROWS)
    block_rows = 8
    hot = [
        pltpu.VMEM((rows, block_rows * lane_total), jnp.bfloat16)
        for rows in (3 * half_rows, 2 * cells_side) + 2 * (3 * moved_rows, cells_side // 2)
    ]
    return pl.pallas_call(
        functools.partial(tracer_kernel, block_rows),
        out_shape=(
            jax.ShapeDtypeStruct((3 * plane_total, cells_side), jnp.float32),
            payload,
            payload,
        ),
        in_specs=[hbm] * 6,
        out_specs=(vmem, vmem, vmem),
        scratch_shapes=[
            pltpu.SMEM(tracer_count.shape, jnp.int32),
            pltpu.VMEM(values.shape, jnp.float32),
            pltpu.VMEM(cells.shape, jnp.int32),
            pltpu.VMEM((2,) + outer_planes, jnp.float32),
            pltpu.VMEM((2, 3) + outer_planes, jnp.float32),
            pltpu.VMEM((2, 3, 1, cells_radial, cells_side), jnp.float32),
            pltpu.VMEM((3 * half_rows, 2 * cells_side), jnp.float32),
            pltpu.VMEM((2, 3 * moved_rows, cells_side // 2), jnp.float32),
            pltpu.VMEM((2, payload_rows, cells_side), jnp.float32),
            pltpu.SemaphoreType.DMA((11,)),
        ]
        + 2 * hot,
        compiler_params=pltpu.CompilerParams(vmem_limit_bytes=32 * 2**20),
        cost_estimate=pl.CostEstimate(
            flops=6 * group_rows * lane_total * plane_total * cells_side // 8,
            bytes_accessed=4 * (values.size + cells.size),
            transcendentals=0,
        ),
        name="tracer_sums",
    )(
        *(
            pltpu.with_memory_space_constraint(array, pltpu.HBM)
            for array in (tracer_count, values, cells, base_viscosity, velocity, forcing)
        )
    )


def pair_swaps(first, second):
    count = lax.axis_size("lat")
    received = []
    for payload, start in ((second, 1), (first, 0)):
        target = list(range(count))
        for low in range(start, count - 1, 2):
            target[low], target[low + 1] = low + 1, low
        received.append(lax.ppermute(payload, "lat", list(enumerate(target))))
    return received[::-1]


def shift_planes(block, step):
    return pltpu.roll(block, step % block.shape[0], 0)


def shift_side(block, step):
    lane_total = block.shape[1]
    lane = lax.broadcasted_iota(jnp.int32, block.shape, 1)
    inside = lane >= step if step > 0 else lane < lane_total + step
    return jnp.where(inside, pltpu.roll(block, step % lane_total, 1), jnp.float32(0.0))


def neighbours(block):
    return (
        shift_planes(block, 1),
        shift_planes(block, -1),
        shift_side(block, 1),
        shift_side(block, -1),
    )


def total_of(terms):
    result = terms[0]
    for term in terms[1:]:
        result = result + term
    return result


def inside_grid(shape, margin, cells_lateral):
    plane = lax.broadcasted_iota(jnp.int32, shape, 0)
    lateral = lax.axis_index("lat")
    first = jnp.where(lateral == 0, margin, 1)
    last = jnp.where(lateral == lax.axis_size("lat") - 1, margin + cells_lateral, shape[0] - 1)
    return (plane >= first) & (plane < last)


def eliminate_kernel(
    stay_ref,
    second_ref,
    first_ref,
    from_second_ref,
    from_first_ref,
    base_ref,
    velocity_ref,
    forcing_ref,
    composition_ref,
    message_ref,
    parts_ref,
    fields,
):
    cells_lateral, cells_radial, cells_side = base_ref.shape
    margin = MIGRATION_PLANES
    planes = cells_lateral + 2 * margin
    pitch = fields.shape[1] // planes
    moved_planes = margin * cells_radial
    starts, _ = payload_sections(cells_radial)
    odd = lax.rem(lax.axis_index("lat"), 2) == 1
    BASE, VELOCITY, SOURCE = 3, 4, 7

    def sent(upward, start, rows):
        part = pl.ds(start, rows)
        mine_first = odd if not upward else jnp.logical_not(odd)
        return jnp.where(mine_first, first_ref[part, :], second_ref[part, :])

    def arrived(from_above, start, rows):
        part = pl.ds(start, rows)
        is_first = odd if not from_above else jnp.logical_not(odd)
        return jnp.where(is_first, from_first_ref[part, :], from_second_ref[part, :])

    def put(field, plane, value):
        fields[field, pl.ds(plane * pitch, cells_radial), :] = value

    for q in range(3):
        for x in range(cells_lateral):
            mine = stay_ref[pl.ds((q * cells_lateral + x) * cells_radial, cells_radial), :]
            if x < margin:
                row = q * moved_planes + x * cells_radial
                mine = mine + arrived(False, starts[0] + row, cells_radial)
            if x >= cells_lateral - margin:
                row = q * moved_planes + (x - cells_lateral + margin) * cells_radial
                mine = mine + arrived(True, starts[0] + row, cells_radial)
            put(q, margin + x, mine)
            put(VELOCITY + q, margin + x, velocity_ref[q, x])
            put(SOURCE + q, margin + x, forcing_ref[q, x])
        for offset in range(margin):
            row = q * moved_planes + offset * cells_radial
            for above in (False, True):
                plane = offset + (margin + cells_lateral if above else 0)
                put(
                    q,
                    plane,
                    sent(above, starts[0] + row, cells_radial)
                    + arrived(above, starts[1] + row, cells_radial),
                )
                put(VELOCITY + q, plane, arrived(above, starts[2] + row, cells_radial))
        put(
            SOURCE + q,
            margin - 1,
            arrived(False, starts[4] + q * cells_radial, cells_radial),
        )
        put(
            SOURCE + q,
            margin + cells_lateral,
            arrived(True, starts[4] + q * cells_radial, cells_radial),
        )
        for plane in (0, planes - 1):
            put(SOURCE + q, plane, jnp.zeros((cells_radial, cells_side), jnp.float32))
    for x in range(cells_lateral):
        put(BASE, margin + x, base_ref[x])
    for offset in range(margin):
        for above in (False, True):
            plane = offset + (margin + cells_lateral if above else 0)
            put(BASE, plane, arrived(above, starts[3] + offset * cells_radial, cells_radial))

    for plane in range(planes):
        rows = pl.ds(plane * pitch, cells_radial)
        total_weight = fields[0, rows, :] + PRIOR_WEIGHT
        basalt_share = fields[1, rows, :] / total_weight
        melt_share = fields[2, rows, :] / total_weight
        fields[BASE, rows, :] = fields[BASE, rows, :] * jnp.exp(
            CONTRAST_BASALT * basalt_share - CONTRAST_MELT * melt_share
        )
        fields[SOURCE + 2, rows, :] = fields[SOURCE + 2, rows, :] - BUOYANCY * basalt_share
        if margin <= plane < margin + cells_lateral:
            composition_ref[0, plane - margin] = basalt_share
            composition_ref[1, plane - margin] = melt_share

    lower_block = lax.axis_index("rad") == 0

    def radial(field, t):
        row = jnp.where(lower_block, t, cells_radial - 1 - t)
        return fields[field, pl.ds(row, planes, stride=pitch), :]

    shape = (planes, cells_side)
    valid = inside_grid(shape, margin, cells_lateral)
    nothing = jnp.zeros(shape, jnp.float32)
    last = cells_radial - 1
    viscosity = [radial(BASE, t) for t in range(cells_radial)]
    lateral_faces = [
        [LATERAL * 0.5 * (here + there) for there in neighbours(here)] for here in viscosity
    ]
    radial_faces = [RADIAL * 0.5 * viscosity[0]] + [
        RADIAL * 0.5 * (viscosity[t - 1] + viscosity[t]) for t in range(1, cells_radial)
    ]

    excess = total_of(lateral_faces[0]) + radial_faces[0]
    inverse, coupling = [], []
    for t in range(last):
        inverse.append(1.0 / (excess + radial_faces[t + 1]))
        coupling.append(radial_faces[t + 1] * inverse[t])
        excess = total_of(lateral_faces[t + 1]) + coupling[t] * excess

    def lateral_terms(t, around):
        return [face * there for face, there in zip(lateral_faces[t], around)]

    def forward(right_side):
        eliminated = [right_side[0]]
        for t in range(1, cells_radial):
            eliminated.append(right_side[t] + coupling[t - 1] * eliminated[t - 1])
        return eliminated

    def backward(eliminated):
        solved = [nothing]
        for t in range(last - 1, -1, -1):
            solved.append(eliminated[t] * inverse[t] + coupling[t] * solved[-1])
        return solved[::-1]

    response = [jnp.ones(shape, jnp.float32)]
    for t in range(last - 1, -1, -1):
        response.append(coupling[t] * response[-1])
    response = response[::-1]

    message_ref[pl.ds(0, planes), :] = viscosity[last]
    message_ref[pl.ds(planes, planes), :] = excess
    short_start = 5 * planes

    def put_short(index, value):
        message_ref[pl.ds(short_start + index * cells_lateral, cells_lateral), :] = value[
            margin : margin + cells_lateral
        ]

    parts = []
    for q in range(3):
        source = [radial(SOURCE + q, t) for t in range(cells_radial)]
        eliminated = forward(
            [
                total_of([source[t]] + lateral_terms(t, neighbours(radial(VELOCITY + q, t))))
                for t in range(cells_radial)
            ]
        )
        message_ref[pl.ds((2 + q) * planes, planes), :] = eliminated[last]
        particular = [jnp.where(valid, value, 0.0) for value in backward(eliminated)]
        eliminated = forward(
            [
                total_of([source[t]] + lateral_terms(t, neighbours(particular[t])))
                for t in range(cells_radial)
            ]
        )
        put_short(q, eliminated[last])
        parts.append(backward(eliminated))
    around = [neighbours(jnp.where(valid, value, 0.0)) for value in response]
    for side in range(4):
        eliminated = forward([lateral_faces[t][side] * around[t][side] for t in range(cells_radial)])
        put_short(3 + side, eliminated[last])
        parts.append(backward(eliminated))
    parts.append(response)
    for index, part in enumerate(parts):
        for t in range(cells_radial):
            parts_ref[index, t] = part[t]
    unused = short_start + 7 * cells_lateral
    message_ref[pl.ds(unused, message_ref.shape[0] - unused), :] = jnp.zeros(
        (message_ref.shape[0] - unused, cells_side), jnp.float32
    )


def message_rows(cells_lateral):
    planes = cells_lateral + 2 * MIGRATION_PLANES
    return round_up(5 * planes + 7 * cells_lateral + MIGRATION_PLANES, 8)


def eliminate(stay, sent, received, base_viscosity, velocity, forcing):
    cells_lateral, cells_radial, cells_side = base_viscosity.shape
    planes = cells_lateral + 2 * MIGRATION_PLANES
    pitch = round_up(cells_radial, 8)
    vmem = pl.BlockSpec(memory_space=pltpu.VMEM)
    return pl.pallas_call(
        eliminate_kernel,
        out_shape=(
            jax.ShapeDtypeStruct((2,) + base_viscosity.shape, jnp.float32),
            jax.ShapeDtypeStruct((message_rows(cells_lateral), cells_side), jnp.float32),
            jax.ShapeDtypeStruct((8, cells_radial, planes, cells_side), jnp.float32),
        ),
        in_specs=[vmem] * 8,
        out_specs=(vmem, vmem, vmem),
        scratch_shapes=[pltpu.VMEM((10, planes * pitch, cells_side), jnp.float32)],
        compiler_params=pltpu.CompilerParams(vmem_limit_bytes=32 * 2**20),
        name="eliminate",
    )(stay, *sent[::-1], *received[::-1], base_viscosity, velocity, forcing)


def join_kernel(mine_ref, other_ref, parts_ref, smoothed_ref, lines):
    _, cells_lateral, cells_radial, cells_side = smoothed_ref.shape
    margin = MIGRATION_PLANES
    planes = cells_lateral + 2 * margin
    pitch = lines.shape[0] // cells_lateral
    shape = (planes, cells_side)
    valid = inside_grid(shape, margin, cells_lateral)
    lower_block = lax.axis_index("rad") == 0

    def long(ref, index):
        return ref[pl.ds(index * planes, planes), :]

    def short(ref, index):
        return ref[pl.ds(5 * planes + index * cells_lateral - margin, planes), :]

    face = RADIAL * 0.5 * (long(mine_ref, 0) + long(other_ref, 0))
    excess, other_excess = long(mine_ref, 1), long(other_ref, 1)
    scale = 1.0 / (excess * other_excess + face * (excess + other_excess))
    own_weight = (other_excess + face) * scale
    other_weight = (excess + face) * scale
    cross = face * scale
    factors = [short(mine_ref, 3 + side) for side in range(4)]
    other_factors = [short(other_ref, 3 + side) for side in range(4)]
    for q in range(3):
        right, other_right = long(mine_ref, 2 + q), long(other_ref, 2 + q)
        own = jnp.where(valid, own_weight * right + cross * other_right, 0.0)
        other = jnp.where(valid, other_weight * other_right + cross * right, 0.0)
        around, other_around = neighbours(own), neighbours(other)
        right = total_of(
            [short(mine_ref, q)] + [factor * there for factor, there in zip(factors, around)]
        )
        other_right = total_of(
            [short(other_ref, q)]
            + [factor * there for factor, there in zip(other_factors, other_around)]
        )
        final = own_weight * right + cross * other_right
        for t in range(cells_radial):
            value = parts_ref[q, t] + parts_ref[7, t] * final
            for side in range(4):
                value = value + parts_ref[3 + side, t] * around[side]
            row = jnp.where(lower_block, t, cells_radial - 1 - t)
            lines[pl.ds(row, cells_lateral, stride=pitch), :] = value[
                margin : margin + cells_lateral
            ]
        for x in range(cells_lateral):
            smoothed_ref[q, x] = lines[pl.ds(x * pitch, cells_radial), :]


def join(message, other, parts, like):
    cells_lateral, cells_radial, cells_side = like.shape[1:]
    pitch = round_up(cells_radial, 8)
    vmem = pl.BlockSpec(memory_space=pltpu.VMEM)
    return pl.pallas_call(
        join_kernel,
        out_shape=jax.ShapeDtypeStruct(like.shape, jnp.float32),
        in_specs=[vmem] * 3,
        out_specs=vmem,
        scratch_shapes=[pltpu.VMEM((cells_lateral * pitch, cells_side), jnp.float32)],
        compiler_params=pltpu.CompilerParams(vmem_limit_bytes=32 * 2**20),
        name="join",
    )(message, other, parts)


def extended(block, sides, width):
    for axis, dim in sides:
        count = lax.axis_size(axis)
        forward = [(i, i + 1) for i in range(count - 1)]
        backward = [(target, source) for source, target in forward]
        low = lax.ppermute(
            lax.slice_in_dim(block, block.shape[dim] - width, None, axis=dim), axis, forward
        )
        high = lax.ppermute(lax.slice_in_dim(block, 0, width, axis=dim), axis, backward)
        block = jnp.concatenate([low, block, high], axis=dim)
    return block


def block_factor(diagonal, lower_band, upper_band):
    pivots = []
    upper_scaled = []
    for row_index in range(diagonal.shape[1]):
        if row_index == 0:
            pivot_row = diagonal[:, 0]
        else:
            pivot_row = diagonal[:, row_index] - lower_band[:, row_index] * upper_scaled[-1]
        pivots.append(pivot_row)
        upper_scaled.append(upper_band[:, row_index] / pivot_row)
    return (pivots, upper_scaled)


def block_solve(pivots, upper_scaled, lower_band, right_side):
    row_total = len(pivots)
    modified = []
    for row_index in range(row_total):
        if row_index == 0:
            value_row = right_side[:, :, 0] / pivots[0]
        else:
            value_row = (
                right_side[:, :, row_index] - lower_band[:, row_index] * modified[-1]
            ) / pivots[row_index]
        modified.append(value_row)
    solved = [modified[-1]]
    for row_index in range(row_total - 2, -1, -1):
        solved.append(modified[row_index] - upper_scaled[row_index] * solved[-1])
    ordered = solved[::-1]
    return jnp.stack(ordered, 2)


def interface_solve(coefficients):
    column_total = coefficients.shape[2]

    def forward(carried, inputs):
        offset, carried_slope = carried
        left_first, right_first, left_last, right_last, free_first, free_last = inputs
        divisor = 1.0 - left_first * carried_slope
        first_fixed = (free_first + left_first * offset) / divisor
        first_slope = right_first / divisor
        next_offset = free_last + left_last * (offset + carried_slope * first_fixed)
        next_slope = left_last * carried_slope * first_slope + right_last
        return ((next_offset, next_slope), (first_fixed, first_slope, next_offset, next_slope))

    start_state = (
        jnp.zeros((3, column_total), jnp.float32),
        jnp.zeros((column_total,), jnp.float32),
    )
    scan_inputs = (
        coefficients[:, 0],
        coefficients[:, 1],
        coefficients[:, 2],
        coefficients[:, 3],
        coefficients[:, 4:7],
        coefficients[:, 7:10],
    )
    final_state, eliminated = lax.scan(forward, start_state, scan_inputs)

    def backward(first_next, inputs):
        fixed_first, slope_first, fixed_last, slope_last = inputs
        first_value = fixed_first + slope_first * first_next
        last_value = fixed_last + slope_last * first_next
        return (first_value, (first_value, last_value))

    final_first, values_pair = lax.scan(
        backward, jnp.zeros((3, column_total), jnp.float32), eliminated, reverse=True
    )
    first_values, last_values = values_pair
    nothing_row = jnp.zeros((1, 3, column_total), jnp.float32)
    from_below = jnp.concatenate([nothing_row, last_values[:-1]], 0)
    from_above = jnp.concatenate([first_values[1:], nothing_row], 0)
    return jnp.concatenate([from_below, from_above], 1)


def reduced_boundary(interface):
    gathered = lax.all_gather(interface, "rad", axis=0, tiled=True)
    solved = interface_solve(gathered)
    return lax.dynamic_index_in_dim(solved, lax.axis_index("rad"), 0, keepdims=False)


def many_blocks(stay, received, base_viscosity, velocity, forcing):
    cells_lateral, cells_radial, cells_side = base_viscosity.shape
    moved_rows = MIGRATION_PLANES * cells_radial
    odd = lax.rem(lax.axis_index("lat"), 2) == 1
    from_below = jnp.where(odd, received[0], received[1])[: 3 * moved_rows]
    from_above = jnp.where(odd, received[1], received[0])[: 3 * moved_rows]
    stay = stay.reshape(3, cells_lateral * cells_radial, cells_side)
    totals = stay.at[:, :moved_rows].add(from_below.reshape(3, moved_rows, cells_side))
    totals = totals.at[:, -moved_rows:].add(from_above.reshape(3, moved_rows, cells_side))
    grouped = totals.reshape(3, cells_lateral, cells_radial, cells_side)
    total_weight = grouped[0] + PRIOR_WEIGHT
    basalt_share = grouped[1] / total_weight
    melt_share = grouped[2] / total_weight
    viscosity = base_viscosity * jnp.exp(
        CONTRAST_BASALT * basalt_share - CONTRAST_MELT * melt_share
    )
    viscosity_pad = extended(viscosity, (("lat", 0), ("rad", 1)), 1)
    side_pad = jnp.pad(viscosity, ((0, 0), (0, 0), (1, 1)))
    face_west = LATERAL * 0.5 * (viscosity + viscosity_pad[:-2, 1:-1])
    face_east = LATERAL * 0.5 * (viscosity + viscosity_pad[2:, 1:-1])
    face_south = LATERAL * 0.5 * (viscosity + side_pad[:, :, :-2])
    face_north = LATERAL * 0.5 * (viscosity + side_pad[:, :, 2:])
    face_below = RADIAL * 0.5 * (viscosity + viscosity_pad[1:-1, :-2])
    face_above = RADIAL * 0.5 * (viscosity + viscosity_pad[1:-1, 2:])
    diagonal = face_west + face_east + face_south + face_north + face_below + face_above
    source = jnp.concatenate([forcing[:2], (forcing[2] - BUOYANCY * basalt_share)[None]], 0)
    lower_band = -face_below
    upper_band = -face_above
    pivots, upper_scaled = block_factor(diagonal, lower_band, upper_band)
    radial_iota = lax.broadcasted_iota(jnp.int32, viscosity.shape, 1)
    response_side = jnp.stack(
        [
            jnp.where(radial_iota == 0, face_below, jnp.float32(0.0)),
            jnp.where(radial_iota == cells_radial - 1, face_above, jnp.float32(0.0)),
        ]
    )
    response = block_solve(pivots, upper_scaled, lower_band, response_side)
    current = velocity
    for sweep_index in range(SWEEPS):
        velocity_pad = extended(current, (("lat", 1),), 1)
        side_velocity = jnp.pad(current, ((0, 0), (0, 0), (0, 0), (1, 1)))
        right_side = (
            source
            + face_west * velocity_pad[:, :-2]
            + face_east * velocity_pad[:, 2:]
            + face_south * side_velocity[..., :-2]
            + face_north * side_velocity[..., 2:]
        )
        particular = block_solve(pivots, upper_scaled, lower_band, right_side)
        interface = jnp.concatenate(
            [response[:, :, 0], response[:, :, -1], particular[:, :, 0], particular[:, :, -1]], 0
        )
        interface = interface.reshape(1, 10, cells_lateral * cells_side)
        boundary = reduced_boundary(interface).reshape(6, cells_lateral, 1, cells_side)
        current = particular + response[0][None] * boundary[:3] + response[1][None] * boundary[3:]
    composition = jnp.stack([basalt_share, melt_share])
    return (current, composition)

def local(tracer_values, tracer_cell, tracer_count, base_viscosity, velocity, forcing):
    stay, *sent = tracer_sums(
        tracer_values, tracer_cell, tracer_count, base_viscosity, velocity, forcing
    )
    received = pair_swaps(*sent)
    if lax.axis_size("rad") != 2:
        return many_blocks(stay, received, base_viscosity, velocity, forcing)
    composition, message, parts = eliminate(
        stay, sent, received, base_viscosity, velocity, forcing
    )
    other = lax.ppermute(message, "rad", [(0, 1), (1, 0)])
    return join(message, other, parts, velocity), composition


def solution(mesh):
    return jax.shard_map(
        local,
        mesh=mesh,
        in_specs=(
            P("lat", "rad", None, None),
            P("lat", "rad", None),
            P("lat", "rad", None),
            P("lat", "rad", None),
            P(None, "lat", "rad", None),
            P(None, "lat", "rad", None),
        ),
        out_specs=(P(None, "lat", "rad", None), P(None, "lat", "rad", None)),
        check_vma=False,
    )
```

```python
import functools

import jax
import jax.numpy as jnp
from jax import lax
from jax.experimental import pallas as pl
from jax.experimental.pallas import tpu as pltpu
from jax.sharding import PartitionSpec as P

SWEEPS = 2
MIGRATION_PLANES = 2

LATERAL = 0.015625
RADIAL = 32.0
BUOYANCY = 0.1
PRIOR_WEIGHT = 0.5
CONTRAST_BASALT = 2.3
CONTRAST_MELT = 1.5

TILE_ROWS = 16


def round_up(value, multiple):
    return -(-value // multiple) * multiple


def split_index(index, count):
    if count & (count - 1) == 0:
        return lax.shift_right_logical(index, count.bit_length() - 1), index & (count - 1)
    quotient = lax.div(index, count)
    return quotient, index - quotient * count


def payload_sections(cells_radial):
    pair = MIGRATION_PLANES * cells_radial
    starts = [0, 3 * pair, 6 * pair, 9 * pair, 10 * pair]
    return starts, round_up(10 * pair + 3 * cells_radial, 8)


def hot_product(loads, high, low, high_rows, low_lanes):
    block_rows, lane_total = high.shape
    tile = (TILE_ROWS, lane_total)
    zero, one = jnp.zeros(tile, jnp.bfloat16), jnp.ones((lane_total, lane_total), jnp.bfloat16)
    row_number = lax.broadcasted_iota(jnp.int32, tile, 0)
    lane_number = lax.broadcasted_iota(jnp.int32, (lane_total, lane_total), 1)
    turned = jnp.transpose(low)
    left, right = [], []
    for row in range(block_rows):
        pick = slice(row, row + 1)
        index = jnp.broadcast_to(high[pick], tile).astype(jnp.bfloat16)
        masks = [
            index == (row_number + first).astype(jnp.float32).astype(jnp.bfloat16)
            for first in range(0, high_rows, TILE_ROWS)
        ]
        spread = [jnp.broadcast_to(load[pick], tile).astype(jnp.bfloat16) for load in loads]
        left.append(
            jnp.concatenate([jnp.where(mask, load, zero) for load in spread for mask in masks], 0)
        )
        index = jnp.broadcast_to(turned[:, pick], (lane_total, lane_total)).astype(jnp.bfloat16)
        right.append(
            jnp.concatenate(
                [
                    jnp.where(
                        index == (lane_number + first).astype(jnp.float32).astype(jnp.bfloat16),
                        one,
                        jnp.zeros_like(one),
                    )
                    for first in range(0, low_lanes, lane_total)
                ],
                1,
            )
        )
    return jnp.dot(
        jnp.concatenate(left, 1),
        jnp.concatenate(right, 0),
        preferred_element_type=jnp.float32,
    )


def has_partners():
    lateral, count = lax.axis_index("lat"), lax.axis_size("lat")
    odd = lax.rem(lateral, 2) == 1
    above, below = lateral + 1 < count, lateral > 0
    return jnp.logical_or(odd, above), jnp.where(odd, above, below)


def tracer_kernel(
    block_rows,
    counts_hbm,
    values_hbm,
    cells_hbm,
    base_hbm,
    velocity_hbm,
    forcing_hbm,
    stay_ref,
    first_ref,
    second_sums_ref,
    second_fields_ref,
    counts,
    values,
    cells,
    base,
    velocity,
    forcing,
    stay_sums,
    moved_sums,
    payload,
    semaphores,
):
    cells_lateral, cells_radial, cells_side = base_hbm.shape
    plane_total = cells_lateral * cells_radial
    moved_planes = MIGRATION_PLANES * cells_radial
    half_planes = plane_total // 2
    group_rows, lane_total = values.shape[2:]
    half_rows = stay_sums.shape[0] // 3
    moved_rows = moved_sums.shape[1] // 3

    copies = []

    def fetch(source, target):
        copy = pltpu.make_async_copy(source, target, semaphores.at[len(copies)])
        copy.start()
        copies.append(copy)

    fetch(counts_hbm, counts)
    for first_row, rows in ((0, block_rows), (block_rows, group_rows - block_rows)):
        part = pl.ds(first_row, rows)
        fetch(cells_hbm.at[:, part], cells.at[:, part])
        fetch(values_hbm.at[:, :, part], values.at[:, :, part])
    for upward in (0, 1):
        outer = pl.ds((cells_lateral - MIGRATION_PLANES) * upward, MIGRATION_PLANES)
        fetch(base_hbm.at[outer], base.at[upward])
        fetch(velocity_hbm.at[:, outer], velocity.at[upward])
        fetch(forcing_hbm.at[:, pl.ds((cells_lateral - 1) * upward, 1)], forcing.at[upward])

    stay_sums[...] = jnp.zeros_like(stay_sums)
    moved_sums[...] = jnp.zeros_like(moved_sums)

    def loads_of(group, first_row):
        rows = pl.ds(first_row, block_rows)
        shape = (block_rows, lane_total)
        slot = (first_row + lax.broadcasted_iota(jnp.int32, shape, 0)) * lane_total
        slot = slot + lax.broadcasted_iota(jnp.int32, shape, 1)
        weight = jnp.where(
            slot < counts[0, 0, group], 0.5 + values[0, group, rows, :], jnp.float32(0.0)
        )
        loads = [weight, weight * values[1, group, rows, :], weight * values[2, group, rows, :]]
        plane, side = split_index(cells[group, rows, :], cells_side)
        return loads, plane, side

    def step(first_row):
        loads, plane, side = loads_of(1, first_row)
        upper = plane >= half_planes
        high = jnp.where(upper, plane - half_planes, plane).astype(jnp.float32)
        low = jnp.where(upper, side + cells_side, side).astype(jnp.float32)
        stay_sums[...] += hot_product(loads, high, low, half_rows, 2 * cells_side)
        for slot, group in enumerate((0, 2)):
            loads, plane, side = loads_of(group, first_row)
            if group == 0:
                plane = plane - (plane_total - moved_planes)
            moved_sums[slot] += hot_product(
                loads, plane.astype(jnp.float32), side.astype(jnp.float32), moved_rows, cells_side
            )

    for copy in copies[:3]:
        copy.wait()
    step(0)
    for copy in copies[3:5]:
        copy.wait()

    def repeat(index, carried):
        step(pl.multiple_of(index * block_rows, block_rows))
        return carried

    lax.fori_loop(1, group_rows // block_rows, repeat, 0)
    for copy in copies[5:]:
        copy.wait()

    for q in range(3):
        rows = pl.ds(q * half_rows, half_planes)
        for half in (0, 1):
            stay_ref[pl.ds(q * plane_total + half * half_planes, half_planes), :] = stay_sums[
                rows, half * cells_side : (half + 1) * cells_side
            ]
    starts, _ = payload_sections(cells_radial)
    odd = lax.rem(lax.axis_index("lat"), 2)
    for upward in (0, 1):
        place = odd if upward else 1 - odd
        first_plane = cells_lateral - MIGRATION_PLANES if upward else 0
        for q in range(3):
            payload[place, pl.ds(starts[0] + q * moved_planes, moved_planes), :] = moved_sums[
                upward, pl.ds(q * moved_rows, moved_planes), :
            ]
            payload[place, pl.ds(starts[1] + q * moved_planes, moved_planes), :] = stay_ref[
                pl.ds(q * plane_total + first_plane * cells_radial, moved_planes), :
            ]
            for offset in range(MIGRATION_PLANES):
                payload[
                    place,
                    pl.ds(starts[2] + q * moved_planes + offset * cells_radial, cells_radial),
                    :,
                ] = velocity[upward, q, offset]
            payload[place, pl.ds(starts[4] + q * cells_radial, cells_radial), :] = forcing[
                upward, q, 0
            ]
        for offset in range(MIGRATION_PLANES):
            payload[place, pl.ds(starts[3] + offset * cells_radial, cells_radial), :] = base[
                upward, offset
            ]
    has_first, has_second = has_partners()
    first_ref[...] = jnp.where(has_first, payload[0], 0.0)
    second_sums_ref[...] = jnp.where(has_second, payload[1, 0 : starts[2]], 0.0)
    second_fields_ref[...] = jnp.where(has_second, payload[1, starts[2] :], 0.0)


def tracer_sums(tracer_values, tracer_cell, tracer_count, base_viscosity, velocity, forcing):
    cells_lateral, cells_radial, cells_side = base_viscosity.shape
    plane_total = cells_lateral * cells_radial
    moved_planes = MIGRATION_PLANES * cells_radial
    lane_total = 128
    values = tracer_values.reshape(3, 3, -1, lane_total)
    cells = tracer_cell.reshape(3, -1, lane_total)
    group_rows = cells.shape[1]
    starts, payload_rows = payload_sections(cells_radial)
    hbm = pl.BlockSpec(memory_space=pltpu.HBM)
    vmem = pl.BlockSpec(memory_space=pltpu.VMEM)
    payloads = [
        jax.ShapeDtypeStruct((rows, cells_side), jnp.float32)
        for rows in (payload_rows, starts[2], payload_rows - starts[2])
    ]
    outer_planes = (MIGRATION_PLANES, cells_radial, cells_side)
    half_rows = round_up(plane_total // 2, TILE_ROWS)
    moved_rows = round_up(moved_planes, TILE_ROWS)
    return pl.pallas_call(
        functools.partial(tracer_kernel, 16),
        out_shape=(
            jax.ShapeDtypeStruct((3 * plane_total, cells_side), jnp.float32),
            *payloads,
        ),
        in_specs=[hbm] * 6,
        out_specs=(vmem,) * 4,
        scratch_shapes=[
            pltpu.SMEM(tracer_count.shape, jnp.int32),
            pltpu.VMEM(values.shape, jnp.float32),
            pltpu.VMEM(cells.shape, jnp.int32),
            pltpu.VMEM((2,) + outer_planes, jnp.float32),
            pltpu.VMEM((2, 3) + outer_planes, jnp.float32),
            pltpu.VMEM((2, 3, 1, cells_radial, cells_side), jnp.float32),
            pltpu.VMEM((3 * half_rows, 2 * cells_side), jnp.float32),
            pltpu.VMEM((2, 3 * moved_rows, cells_side), jnp.float32),
            pltpu.VMEM((2, payload_rows, cells_side), jnp.float32),
            pltpu.SemaphoreType.DMA((11,)),
        ],
        compiler_params=pltpu.CompilerParams(vmem_limit_bytes=32 * 2**20),
        cost_estimate=pl.CostEstimate(
            flops=6 * group_rows * lane_total * plane_total * cells_side // 8,
            bytes_accessed=4 * (values.size + cells.size),
            transcendentals=0,
        ),
        name="tracer_sums",
    )(
        *(
            pltpu.with_memory_space_constraint(array, pltpu.HBM)
            for array in (tracer_count, values, cells, base_viscosity, velocity, forcing)
        )
    )


def pair_swap(payload, start):
    count = lax.axis_size("lat")
    target = list(range(count))
    for low in range(start, count - 1, 2):
        target[low], target[low + 1] = low + 1, low
    return lax.ppermute(payload, "lat", list(enumerate(target)))


def shift_planes(block, step):
    return pltpu.roll(block, step % block.shape[0], 0)


def shift_side(block, step):
    lane_total = block.shape[1]
    lane = lax.broadcasted_iota(jnp.int32, block.shape, 1)
    inside = lane >= step if step > 0 else lane < lane_total + step
    return jnp.where(inside, pltpu.roll(block, step % lane_total, 1), jnp.float32(0.0))


def neighbours(block):
    return (
        shift_planes(block, 1),
        shift_planes(block, -1),
        shift_side(block, 1),
        shift_side(block, -1),
    )


def total_of(terms):
    result = terms[0]
    for term in terms[1:]:
        result = result + term
    return result


def inside_grid(shape, margin, cells_lateral):
    plane = lax.broadcasted_iota(jnp.int32, shape, 0)
    lateral = lax.axis_index("lat")
    first = jnp.where(lateral == 0, margin, 1)
    last = jnp.where(lateral == lax.axis_size("lat") - 1, margin + cells_lateral, shape[0] - 1)
    return (plane >= first) & (plane < last)


def eliminate_kernel(
    stay_ref,
    second_sums_ref,
    second_fields_ref,
    first_ref,
    from_second_sums_ref,
    from_second_fields_ref,
    from_first_ref,
    base_ref,
    velocity_ref,
    forcing_ref,
    composition_ref,
    message_ref,
    parts_ref,
    fields,
):
    cells_lateral, cells_radial, cells_side = base_ref.shape
    margin = MIGRATION_PLANES
    planes = cells_lateral + 2 * margin
    pitch = fields.shape[1] // planes
    moved_planes = margin * cells_radial
    starts, _ = payload_sections(cells_radial)
    odd = lax.rem(lax.axis_index("lat"), 2) == 1
    BASE, VELOCITY, SOURCE = 3, 4, 7

    def from_second(sums_ref, fields_ref, start, rows):
        if start < starts[2]:
            return sums_ref[pl.ds(start, rows), :]
        return fields_ref[pl.ds(start - starts[2], rows), :]

    def sent(upward, start, rows):
        mine_first = odd if not upward else jnp.logical_not(odd)
        second = from_second(second_sums_ref, second_fields_ref, start, rows)
        return jnp.where(mine_first, first_ref[pl.ds(start, rows), :], second)

    def arrived(from_above, start, rows):
        is_first = odd if not from_above else jnp.logical_not(odd)
        second = from_second(from_second_sums_ref, from_second_fields_ref, start, rows)
        return jnp.where(is_first, from_first_ref[pl.ds(start, rows), :], second)

    def put(field, plane, value):
        fields[field, pl.ds(plane * pitch, cells_radial), :] = value

    for q in range(3):
        for x in range(cells_lateral):
            mine = stay_ref[pl.ds((q * cells_lateral + x) * cells_radial, cells_radial), :]
            if x < margin:
                row = q * moved_planes + x * cells_radial
                mine = mine + arrived(False, starts[0] + row, cells_radial)
            if x >= cells_lateral - margin:
                row = q * moved_planes + (x - cells_lateral + margin) * cells_radial
                mine = mine + arrived(True, starts[0] + row, cells_radial)
            put(q, margin + x, mine)
            put(VELOCITY + q, margin + x, velocity_ref[q, x])
            put(SOURCE + q, margin + x, forcing_ref[q, x])
        for offset in range(margin):
            row = q * moved_planes + offset * cells_radial
            for above in (False, True):
                plane = offset + (margin + cells_lateral if above else 0)
                put(
                    q,
                    plane,
                    sent(above, starts[0] + row, cells_radial)
                    + arrived(above, starts[1] + row, cells_radial),
                )
                put(VELOCITY + q, plane, arrived(above, starts[2] + row, cells_radial))
        put(
            SOURCE + q,
            margin - 1,
            arrived(False, starts[4] + q * cells_radial, cells_radial),
        )
        put(
            SOURCE + q,
            margin + cells_lateral,
            arrived(True, starts[4] + q * cells_radial, cells_radial),
        )
        for plane in (0, planes - 1):
            put(SOURCE + q, plane, jnp.zeros((cells_radial, cells_side), jnp.float32))
    for x in range(cells_lateral):
        put(BASE, margin + x, base_ref[x])
    for offset in range(margin):
        for above in (False, True):
            plane = offset + (margin + cells_lateral if above else 0)
            put(BASE, plane, arrived(above, starts[3] + offset * cells_radial, cells_radial))

    for plane in range(planes):
        rows = pl.ds(plane * pitch, cells_radial)
        total_weight = fields[0, rows, :] + PRIOR_WEIGHT
        basalt_share = fields[1, rows, :] / total_weight
        melt_share = fields[2, rows, :] / total_weight
        fields[BASE, rows, :] = fields[BASE, rows, :] * jnp.exp(
            CONTRAST_BASALT * basalt_share - CONTRAST_MELT * melt_share
        )
        fields[SOURCE + 2, rows, :] = fields[SOURCE + 2, rows, :] - BUOYANCY * basalt_share
        if margin <= plane < margin + cells_lateral:
            composition_ref[0, plane - margin] = basalt_share
            composition_ref[1, plane - margin] = melt_share

    lower_block = lax.axis_index("rad") == 0

    def radial(field, t):
        row = jnp.where(lower_block, t, cells_radial - 1 - t)
        return fields[field, pl.ds(row, planes, stride=pitch), :]

    shape = (planes, cells_side)
    valid = inside_grid(shape, margin, cells_lateral)
    nothing = jnp.zeros(shape, jnp.float32)
    last = cells_radial - 1
    viscosity = [radial(BASE, t) for t in range(cells_radial)]
    lateral_faces = [
        [LATERAL * 0.5 * (here + there) for there in neighbours(here)] for here in viscosity
    ]
    radial_faces = [RADIAL * 0.5 * viscosity[0]] + [
        RADIAL * 0.5 * (viscosity[t - 1] + viscosity[t]) for t in range(1, cells_radial)
    ]

    excess = total_of(lateral_faces[0]) + radial_faces[0]
    inverse, coupling = [], []
    for t in range(last):
        inverse.append(1.0 / (excess + radial_faces[t + 1]))
        coupling.append(radial_faces[t + 1] * inverse[t])
        excess = total_of(lateral_faces[t + 1]) + coupling[t] * excess

    def lateral_terms(t, around):
        return [face * there for face, there in zip(lateral_faces[t], around)]

    def forward(right_side):
        eliminated = [right_side[0]]
        for t in range(1, cells_radial):
            eliminated.append(right_side[t] + coupling[t - 1] * eliminated[t - 1])
        return eliminated

    def backward(eliminated):
        solved = [nothing]
        for t in range(last - 1, -1, -1):
            solved.append(eliminated[t] * inverse[t] + coupling[t] * solved[-1])
        return solved[::-1]

    response = [jnp.ones(shape, jnp.float32)]
    for t in range(last - 1, -1, -1):
        response.append(coupling[t] * response[-1])
    response = response[::-1]

    message_ref[pl.ds(0, planes), :] = viscosity[last]
    message_ref[pl.ds(planes, planes), :] = excess
    short_start = 5 * planes

    def put_short(index, value):
        message_ref[pl.ds(short_start + index * cells_lateral, cells_lateral), :] = value[
            margin : margin + cells_lateral
        ]

    parts = []
    for q in range(3):
        source = [radial(SOURCE + q, t) for t in range(cells_radial)]
        eliminated = forward(
            [
                total_of([source[t]] + lateral_terms(t, neighbours(radial(VELOCITY + q, t))))
                for t in range(cells_radial)
            ]
        )
        message_ref[pl.ds((2 + q) * planes, planes), :] = eliminated[last]
        particular = [jnp.where(valid, value, 0.0) for value in backward(eliminated)]
        eliminated = forward(
            [
                total_of([source[t]] + lateral_terms(t, neighbours(particular[t])))
                for t in range(cells_radial)
            ]
        )
        put_short(q, eliminated[last])
        parts.append(backward(eliminated))
    around = [neighbours(jnp.where(valid, value, 0.0)) for value in response]
    for side in range(4):
        eliminated = forward([lateral_faces[t][side] * around[t][side] for t in range(cells_radial)])
        put_short(3 + side, eliminated[last])
        parts.append(backward(eliminated))
    parts.append(response)
    for index, part in enumerate(parts):
        for t in range(cells_radial):
            parts_ref[index, t] = part[t]
    unused = short_start + 7 * cells_lateral
    message_ref[pl.ds(unused, message_ref.shape[0] - unused), :] = jnp.zeros(
        (message_ref.shape[0] - unused, cells_side), jnp.float32
    )


def message_rows(cells_lateral):
    planes = cells_lateral + 2 * MIGRATION_PLANES
    return round_up(5 * planes + 7 * cells_lateral + MIGRATION_PLANES, 8)


def eliminate(stay, sent, received, base_viscosity, velocity, forcing):
    cells_lateral, cells_radial, cells_side = base_viscosity.shape
    planes = cells_lateral + 2 * MIGRATION_PLANES
    pitch = round_up(cells_radial, 8)
    vmem = pl.BlockSpec(memory_space=pltpu.VMEM)
    return pl.pallas_call(
        eliminate_kernel,
        out_shape=(
            jax.ShapeDtypeStruct((2,) + base_viscosity.shape, jnp.float32),
            jax.ShapeDtypeStruct((message_rows(cells_lateral), cells_side), jnp.float32),
            jax.ShapeDtypeStruct((8, cells_radial, planes, cells_side), jnp.float32),
        ),
        in_specs=[vmem] * 10,
        out_specs=(vmem, vmem, vmem),
        scratch_shapes=[pltpu.VMEM((10, planes * pitch, cells_side), jnp.float32)],
        compiler_params=pltpu.CompilerParams(vmem_limit_bytes=32 * 2**20),
        name="eliminate",
    )(stay, *sent, *received, base_viscosity, velocity, forcing)


def join_kernel(mine_ref, other_ref, parts_ref, smoothed_ref, lines):
    _, cells_lateral, cells_radial, cells_side = smoothed_ref.shape
    margin = MIGRATION_PLANES
    planes = cells_lateral + 2 * margin
    pitch = lines.shape[0] // cells_lateral
    shape = (planes, cells_side)
    valid = inside_grid(shape, margin, cells_lateral)
    lower_block = lax.axis_index("rad") == 0

    def long(ref, index):
        return ref[pl.ds(index * planes, planes), :]

    def short(ref, index):
        return ref[pl.ds(5 * planes + index * cells_lateral - margin, planes), :]

    face = RADIAL * 0.5 * (long(mine_ref, 0) + long(other_ref, 0))
    excess, other_excess = long(mine_ref, 1), long(other_ref, 1)
    scale = 1.0 / (excess * other_excess + face * (excess + other_excess))
    own_weight = (other_excess + face) * scale
    other_weight = (excess + face) * scale
    cross = face * scale
    factors = [short(mine_ref, 3 + side) for side in range(4)]
    other_factors = [short(other_ref, 3 + side) for side in range(4)]
    for q in range(3):
        right, other_right = long(mine_ref, 2 + q), long(other_ref, 2 + q)
        own = jnp.where(valid, own_weight * right + cross * other_right, 0.0)
        other = jnp.where(valid, other_weight * other_right + cross * right, 0.0)
        around, other_around = neighbours(own), neighbours(other)
        right = total_of(
            [short(mine_ref, q)] + [factor * there for factor, there in zip(factors, around)]
        )
        other_right = total_of(
            [short(other_ref, q)]
            + [factor * there for factor, there in zip(other_factors, other_around)]
        )
        final = own_weight * right + cross * other_right
        for t in range(cells_radial):
            value = parts_ref[q, t] + parts_ref[7, t] * final
            for side in range(4):
                value = value + parts_ref[3 + side, t] * around[side]
            row = jnp.where(lower_block, t, cells_radial - 1 - t)
            lines[pl.ds(row, cells_lateral, stride=pitch), :] = value[
                margin : margin + cells_lateral
            ]
        for x in range(cells_lateral):
            smoothed_ref[q, x] = lines[pl.ds(x * pitch, cells_radial), :]


def join(message, other, parts, like):
    cells_lateral, cells_radial, cells_side = like.shape[1:]
    pitch = round_up(cells_radial, 8)
    vmem = pl.BlockSpec(memory_space=pltpu.VMEM)
    return pl.pallas_call(
        join_kernel,
        out_shape=jax.ShapeDtypeStruct(like.shape, jnp.float32),
        in_specs=[vmem] * 3,
        out_specs=vmem,
        scratch_shapes=[pltpu.VMEM((cells_lateral * pitch, cells_side), jnp.float32)],
        compiler_params=pltpu.CompilerParams(vmem_limit_bytes=32 * 2**20),
        name="join",
    )(message, other, parts)


def extended(block, sides, width):
    for axis, dim in sides:
        count = lax.axis_size(axis)
        forward = [(i, i + 1) for i in range(count - 1)]
        backward = [(target, source) for source, target in forward]
        low = lax.ppermute(
            lax.slice_in_dim(block, block.shape[dim] - width, None, axis=dim), axis, forward
        )
        high = lax.ppermute(lax.slice_in_dim(block, 0, width, axis=dim), axis, backward)
        block = jnp.concatenate([low, block, high], axis=dim)
    return block


def block_factor(diagonal, lower_band, upper_band):
    pivots = []
    upper_scaled = []
    for row_index in range(diagonal.shape[1]):
        if row_index == 0:
            pivot_row = diagonal[:, 0]
        else:
            pivot_row = diagonal[:, row_index] - lower_band[:, row_index] * upper_scaled[-1]
        pivots.append(pivot_row)
        upper_scaled.append(upper_band[:, row_index] / pivot_row)
    return (pivots, upper_scaled)


def block_solve(pivots, upper_scaled, lower_band, right_side):
    row_total = len(pivots)
    modified = []
    for row_index in range(row_total):
        if row_index == 0:
            value_row = right_side[:, :, 0] / pivots[0]
        else:
            value_row = (
                right_side[:, :, row_index] - lower_band[:, row_index] * modified[-1]
            ) / pivots[row_index]
        modified.append(value_row)
    solved = [modified[-1]]
    for row_index in range(row_total - 2, -1, -1):
        solved.append(modified[row_index] - upper_scaled[row_index] * solved[-1])
    ordered = solved[::-1]
    return jnp.stack(ordered, 2)


def interface_solve(coefficients):
    column_total = coefficients.shape[2]

    def forward(carried, inputs):
        offset, carried_slope = carried
        left_first, right_first, left_last, right_last, free_first, free_last = inputs
        divisor = 1.0 - left_first * carried_slope
        first_fixed = (free_first + left_first * offset) / divisor
        first_slope = right_first / divisor
        next_offset = free_last + left_last * (offset + carried_slope * first_fixed)
        next_slope = left_last * carried_slope * first_slope + right_last
        return ((next_offset, next_slope), (first_fixed, first_slope, next_offset, next_slope))

    start_state = (
        jnp.zeros((3, column_total), jnp.float32),
        jnp.zeros((column_total,), jnp.float32),
    )
    scan_inputs = (
        coefficients[:, 0],
        coefficients[:, 1],
        coefficients[:, 2],
        coefficients[:, 3],
        coefficients[:, 4:7],
        coefficients[:, 7:10],
    )
    final_state, eliminated = lax.scan(forward, start_state, scan_inputs)

    def backward(first_next, inputs):
        fixed_first, slope_first, fixed_last, slope_last = inputs
        first_value = fixed_first + slope_first * first_next
        last_value = fixed_last + slope_last * first_next
        return (first_value, (first_value, last_value))

    final_first, values_pair = lax.scan(
        backward, jnp.zeros((3, column_total), jnp.float32), eliminated, reverse=True
    )
    first_values, last_values = values_pair
    nothing_row = jnp.zeros((1, 3, column_total), jnp.float32)
    from_below = jnp.concatenate([nothing_row, last_values[:-1]], 0)
    from_above = jnp.concatenate([first_values[1:], nothing_row], 0)
    return jnp.concatenate([from_below, from_above], 1)


def reduced_boundary(interface):
    gathered = lax.all_gather(interface, "rad", axis=0, tiled=True)
    solved = interface_solve(gathered)
    return lax.dynamic_index_in_dim(solved, lax.axis_index("rad"), 0, keepdims=False)


def many_blocks(stay, first, second, base_viscosity, velocity, forcing):
    cells_lateral, cells_radial, cells_side = base_viscosity.shape
    moved_rows = MIGRATION_PLANES * cells_radial
    odd = lax.rem(lax.axis_index("lat"), 2) == 1
    from_below = jnp.where(odd, first[: 3 * moved_rows], second[: 3 * moved_rows])
    from_above = jnp.where(odd, second[: 3 * moved_rows], first[: 3 * moved_rows])
    stay = stay.reshape(3, cells_lateral * cells_radial, cells_side)
    totals = stay.at[:, :moved_rows].add(from_below.reshape(3, moved_rows, cells_side))
    totals = totals.at[:, -moved_rows:].add(from_above.reshape(3, moved_rows, cells_side))
    grouped = totals.reshape(3, cells_lateral, cells_radial, cells_side)
    total_weight = grouped[0] + PRIOR_WEIGHT
    basalt_share = grouped[1] / total_weight
    melt_share = grouped[2] / total_weight
    viscosity = base_viscosity * jnp.exp(
        CONTRAST_BASALT * basalt_share - CONTRAST_MELT * melt_share
    )
    viscosity_pad = extended(viscosity, (("lat", 0), ("rad", 1)), 1)
    side_pad = jnp.pad(viscosity, ((0, 0), (0, 0), (1, 1)))
    face_west = LATERAL * 0.5 * (viscosity + viscosity_pad[:-2, 1:-1])
    face_east = LATERAL * 0.5 * (viscosity + viscosity_pad[2:, 1:-1])
    face_south = LATERAL * 0.5 * (viscosity + side_pad[:, :, :-2])
    face_north = LATERAL * 0.5 * (viscosity + side_pad[:, :, 2:])
    face_below = RADIAL * 0.5 * (viscosity + viscosity_pad[1:-1, :-2])
    face_above = RADIAL * 0.5 * (viscosity + viscosity_pad[1:-1, 2:])
    diagonal = face_west + face_east + face_south + face_north + face_below + face_above
    source = jnp.concatenate([forcing[:2], (forcing[2] - BUOYANCY * basalt_share)[None]], 0)
    lower_band = -face_below
    upper_band = -face_above
    pivots, upper_scaled = block_factor(diagonal, lower_band, upper_band)
    radial_iota = lax.broadcasted_iota(jnp.int32, viscosity.shape, 1)
    response_side = jnp.stack(
        [
            jnp.where(radial_iota == 0, face_below, jnp.float32(0.0)),
            jnp.where(radial_iota == cells_radial - 1, face_above, jnp.float32(0.0)),
        ]
    )
    response = block_solve(pivots, upper_scaled, lower_band, response_side)
    current = velocity
    for sweep_index in range(SWEEPS):
        velocity_pad = extended(current, (("lat", 1),), 1)
        side_velocity = jnp.pad(current, ((0, 0), (0, 0), (0, 0), (1, 1)))
        right_side = (
            source
            + face_west * velocity_pad[:, :-2]
            + face_east * velocity_pad[:, 2:]
            + face_south * side_velocity[..., :-2]
            + face_north * side_velocity[..., 2:]
        )
        particular = block_solve(pivots, upper_scaled, lower_band, right_side)
        interface = jnp.concatenate(
            [response[:, :, 0], response[:, :, -1], particular[:, :, 0], particular[:, :, -1]], 0
        )
        interface = interface.reshape(1, 10, cells_lateral * cells_side)
        boundary = reduced_boundary(interface).reshape(6, cells_lateral, 1, cells_side)
        current = particular + response[0][None] * boundary[:3] + response[1][None] * boundary[3:]
    composition = jnp.stack([basalt_share, melt_share])
    return (current, composition)

def local(tracer_values, tracer_cell, tracer_count, base_viscosity, velocity, forcing):
    stay, first, *second = tracer_sums(
        tracer_values, tracer_cell, tracer_count, base_viscosity, velocity, forcing
    )
    sent = (*second, first)
    received = [pair_swap(payload, start) for payload, start in zip(sent, (1, 1, 0))]
    if lax.axis_size("rad") != 2:
        return many_blocks(stay, received[2], received[0], base_viscosity, velocity, forcing)
    composition, message, parts = eliminate(
        stay, sent, received, base_viscosity, velocity, forcing
    )
    other = lax.ppermute(message, "rad", [(0, 1), (1, 0)])
    return join(message, other, parts, velocity), composition


def solution(mesh):
    return jax.shard_map(
        local,
        mesh=mesh,
        in_specs=(
            P("lat", "rad", None, None),
            P("lat", "rad", None),
            P("lat", "rad", None),
            P("lat", "rad", None),
            P(None, "lat", "rad", None),
            P(None, "lat", "rad", None),
        ),
        out_specs=(P(None, "lat", "rad", None), P(None, "lat", "rad", None)),
        check_vma=False,
    )
```

```python
import functools

import jax
import jax.numpy as jnp
from jax import lax
from jax.experimental import pallas as pl
from jax.experimental.pallas import tpu as pltpu
from jax.sharding import PartitionSpec as P

SWEEPS = 2
MIGRATION_PLANES = 2

LATERAL = 0.015625
RADIAL = 32.0
BUOYANCY = 0.1
PRIOR_WEIGHT = 0.5
CONTRAST_BASALT = 2.3
CONTRAST_MELT = 1.5

TILE_ROWS = 16


def round_up(value, multiple):
    return -(-value // multiple) * multiple


def split_index(index, count):
    if count & (count - 1) == 0:
        return lax.shift_right_logical(index, count.bit_length() - 1), index & (count - 1)
    quotient = lax.div(index, count)
    return quotient, index - quotient * count


def payload_sections(cells_radial):
    pair = MIGRATION_PLANES * cells_radial
    starts = [0, 3 * pair, 6 * pair, 9 * pair, 10 * pair]
    return starts, round_up(10 * pair + 3 * cells_radial, 8)


def spread_row(row):
    return jnp.broadcast_to(row, (TILE_ROWS, row.shape[1])).astype(jnp.bfloat16)


def hot_tiles(index, row_total):
    iota = lax.broadcasted_iota(jnp.int32, index.shape, 0)
    return [
        index == (iota + first).astype(jnp.float32).astype(jnp.bfloat16)
        for first in range(0, row_total, TILE_ROWS)
    ]


def hot_product(loads, high, low, high_rows, low_rows):
    left, right = [], []
    zero = jnp.zeros((TILE_ROWS, high.shape[1]), jnp.bfloat16)
    one = jnp.ones((TILE_ROWS, high.shape[1]), jnp.bfloat16)
    for row in range(high.shape[0]):
        pick = slice(row, row + 1)
        high_masks = hot_tiles(spread_row(high[pick]), high_rows)
        low_masks = hot_tiles(spread_row(low[pick]), low_rows)
        spread = [spread_row(load[pick]) for load in loads]
        left.append(
            jnp.concatenate(
                [jnp.where(mask, load, zero) for load in spread for mask in high_masks], 0
            )
        )
        right.append(jnp.concatenate([jnp.where(mask, one, zero) for mask in low_masks], 0))
    return lax.dot_general(
        jnp.concatenate(left, 1),
        jnp.concatenate(right, 1),
        (((1,), (1,)), ((), ())),
        preferred_element_type=jnp.float32,
    )


def fold_stay(plane, side, plane_total, side_total):
    rows, width = plane_total * 2 // 3, side_total // 2
    other = plane >= rows
    half = side >= width
    high = jnp.where(half, plane - rows + (plane_total - rows), plane - rows)
    low = jnp.where(half, side - width, side) + side_total
    high = jnp.where(other, high, plane)
    low = jnp.where(other, low, side)
    return high.astype(jnp.float32), low.astype(jnp.float32), rows, side_total + width


def unfold_stay(table, q, plane_total, side_total, put):
    rows, width = plane_total * 2 // 3, side_total // 2
    left = plane_total - rows
    put(0, 0, table[pl.ds(q * rows, rows), 0:side_total])
    for half in (0, 1):
        block = table[pl.ds(q * rows + half * left, left), side_total : side_total + width]
        put(rows, half * width, block)


def fold_moved(plane, side, plane_total, side_total):
    rows, width = plane_total * 4 // 3, side_total // 4
    third = plane_total // 3
    part = jnp.where(plane >= third, 1, 0) + jnp.where(plane >= 2 * third, 1, 0)
    other = side >= 3 * width
    high = jnp.where(other, plane_total + plane - part * third, plane)
    low = jnp.where(other, side - 3 * width + part * width, side)
    return high.astype(jnp.float32), low.astype(jnp.float32), rows, 3 * width


def unfold_moved(table, q, plane_total, side_total, put):
    rows, width = plane_total * 4 // 3, side_total // 4
    third = plane_total // 3
    put(0, 0, table[pl.ds(q * rows, plane_total), 0 : 3 * width])
    for part in range(3):
        block = table[
            pl.ds(q * rows + plane_total, third), part * width : (part + 1) * width
        ]
        put(part * third, 3 * width, block)


def has_partners():
    lateral, count = lax.axis_index("lat"), lax.axis_size("lat")
    odd = lax.rem(lateral, 2) == 1
    above, below = lateral + 1 < count, lateral > 0
    return jnp.logical_or(odd, above), jnp.where(odd, above, below)


def tracer_kernel(
    block_rows,
    counts_hbm,
    values_hbm,
    cells_hbm,
    base_hbm,
    velocity_hbm,
    forcing_hbm,
    stay_ref,
    first_ref,
    second_ref,
    counts,
    values,
    cells,
    base,
    velocity,
    forcing,
    stay_sums,
    moved_sums,
    payload,
    semaphores,
):
    cells_lateral, cells_radial, cells_side = base_hbm.shape
    plane_total = cells_lateral * cells_radial
    moved_planes = MIGRATION_PLANES * cells_radial
    group_rows, lane_total = values.shape[2:]

    copies = []

    def fetch(source, target):
        copy = pltpu.make_async_copy(source, target, semaphores.at[len(copies)])
        copy.start()
        copies.append(copy)

    fetch(counts_hbm, counts)
    for first_row, rows in ((0, block_rows), (block_rows, group_rows - block_rows)):
        part = pl.ds(first_row, rows)
        fetch(cells_hbm.at[:, part], cells.at[:, part])
        fetch(values_hbm.at[:, :, part], values.at[:, :, part])
    for upward in (0, 1):
        outer = pl.ds((cells_lateral - MIGRATION_PLANES) * upward, MIGRATION_PLANES)
        fetch(base_hbm.at[outer], base.at[upward])
        fetch(velocity_hbm.at[:, outer], velocity.at[upward])
        fetch(forcing_hbm.at[:, pl.ds((cells_lateral - 1) * upward, 1)], forcing.at[upward])

    stay_sums[...] = jnp.zeros_like(stay_sums)
    moved_sums[...] = jnp.zeros_like(moved_sums)

    def loads_of(group, first_row):
        rows = pl.ds(first_row, block_rows)
        shape = (block_rows, lane_total)
        slot = (first_row + lax.broadcasted_iota(jnp.int32, shape, 0)) * lane_total
        slot = slot + lax.broadcasted_iota(jnp.int32, shape, 1)
        weight = jnp.where(
            slot < counts[0, 0, group], 0.5 + values[0, group, rows, :], jnp.float32(0.0)
        )
        loads = [weight, weight * values[1, group, rows, :], weight * values[2, group, rows, :]]
        plane, side = split_index(cells[group, rows, :], cells_side)
        return loads, plane, side

    def step(first_row):
        loads, plane, side = loads_of(1, first_row)
        stay_sums[...] += hot_product(
            loads, *fold_stay(plane, side, plane_total, cells_side)
        )
        for slot, group in enumerate((0, 2)):
            loads, plane, side = loads_of(group, first_row)
            if group == 0:
                plane = plane - (plane_total - moved_planes)
            moved_sums[slot] += hot_product(
                loads, *fold_moved(plane, side, moved_planes, cells_side)
            )

    for copy in copies[:3]:
        copy.wait()
    step(0)
    for copy in copies[3:5]:
        copy.wait()

    def repeat(index, carried):
        step(pl.multiple_of(index * block_rows, block_rows))
        return carried

    lax.fori_loop(1, group_rows // block_rows, repeat, 0)
    for copy in copies[5:]:
        copy.wait()

    for q in range(3):

        def put_stay(plane, column, block):
            height, width = block.shape
            stay_ref[
                pl.ds(q * plane_total + plane, height), column : column + width
            ] = block

        unfold_stay(stay_sums, q, plane_total, cells_side, put_stay)
    starts, _ = payload_sections(cells_radial)
    odd = lax.rem(lax.axis_index("lat"), 2)
    for upward in (0, 1):
        place = odd if upward else 1 - odd
        first_plane = cells_lateral - MIGRATION_PLANES if upward else 0
        for q in range(3):

            def put_moved(plane, column, block):
                height, width = block.shape
                rows = pl.ds(starts[0] + q * moved_planes + plane, height)
                payload[place, rows, column : column + width] = block

            unfold_moved(moved_sums.at[upward], q, moved_planes, cells_side, put_moved)
            payload[place, pl.ds(starts[1] + q * moved_planes, moved_planes), :] = stay_ref[
                pl.ds(q * plane_total + first_plane * cells_radial, moved_planes), :
            ]
            for offset in range(MIGRATION_PLANES):
                payload[
                    place,
                    pl.ds(starts[2] + q * moved_planes + offset * cells_radial, cells_radial),
                    :,
                ] = velocity[upward, q, offset]
            payload[place, pl.ds(starts[4] + q * cells_radial, cells_radial), :] = forcing[
                upward, q, 0
            ]
        for offset in range(MIGRATION_PLANES):
            payload[place, pl.ds(starts[3] + offset * cells_radial, cells_radial), :] = base[
                upward, offset
            ]
    has_first, has_second = has_partners()
    first_ref[...] = jnp.where(has_first, payload[0], 0.0)
    second_ref[...] = jnp.where(has_second, payload[1], 0.0)


def tracer_sums(tracer_values, tracer_cell, tracer_count, base_viscosity, velocity, forcing):
    cells_lateral, cells_radial, cells_side = base_viscosity.shape
    plane_total = cells_lateral * cells_radial
    moved_planes = MIGRATION_PLANES * cells_radial
    lane_total = 128
    values = tracer_values.reshape(3, 3, -1, lane_total)
    cells = tracer_cell.reshape(3, -1, lane_total)
    group_rows = cells.shape[1]
    _, payload_rows = payload_sections(cells_radial)
    hbm = pl.BlockSpec(memory_space=pltpu.HBM)
    vmem = pl.BlockSpec(memory_space=pltpu.VMEM)
    payload = jax.ShapeDtypeStruct((payload_rows, cells_side), jnp.float32)
    outer_planes = (MIGRATION_PLANES, cells_radial, cells_side)
    stay_table = (2 * plane_total, cells_side * 3 // 2)
    moved_table = (4 * moved_planes, cells_side * 3 // 4)

    return pl.pallas_call(
        functools.partial(tracer_kernel, 16),
        out_shape=(
            jax.ShapeDtypeStruct((3 * plane_total, cells_side), jnp.float32),
            payload,
            payload,
        ),
        in_specs=[hbm] * 6,
        out_specs=(vmem, vmem, vmem),
        scratch_shapes=[
            pltpu.SMEM(tracer_count.shape, jnp.int32),
            pltpu.VMEM(values.shape, jnp.float32),
            pltpu.VMEM(cells.shape, jnp.int32),
            pltpu.VMEM((2,) + outer_planes, jnp.float32),
            pltpu.VMEM((2, 3) + outer_planes, jnp.float32),
            pltpu.VMEM((2, 3, 1, cells_radial, cells_side), jnp.float32),
            pltpu.VMEM(stay_table, jnp.float32),
            pltpu.VMEM((2,) + moved_table, jnp.float32),
            pltpu.VMEM((2, payload_rows, cells_side), jnp.float32),
            pltpu.SemaphoreType.DMA((11,)),
        ],
        compiler_params=pltpu.CompilerParams(vmem_limit_bytes=32 * 2**20),
        cost_estimate=pl.CostEstimate(
            flops=6 * group_rows * lane_total * plane_total * cells_side // 8,
            bytes_accessed=4 * (values.size + cells.size),
            transcendentals=0,
        ),
        name="tracer_sums",
    )(
        *(
            pltpu.with_memory_space_constraint(array, pltpu.HBM)
            for array in (tracer_count, values, cells, base_viscosity, velocity, forcing)
        )
    )


def pair_swaps(first, second):
    count = lax.axis_size("lat")
    received = []
    for payload, start in ((second, 1), (first, 0)):
        target = list(range(count))
        for low in range(start, count - 1, 2):
            target[low], target[low + 1] = low + 1, low
        received.append(lax.ppermute(payload, "lat", list(enumerate(target))))
    return received[::-1]


def shift_planes(block, step):
    return pltpu.roll(block, step % block.shape[0], 0)


def shift_side(block, step):
    lane_total = block.shape[1]
    lane = lax.broadcasted_iota(jnp.int32, block.shape, 1)
    inside = lane >= step if step > 0 else lane < lane_total + step
    return jnp.where(inside, pltpu.roll(block, step % lane_total, 1), jnp.float32(0.0))


def neighbours(block):
    return (
        shift_planes(block, 1),
        shift_planes(block, -1),
        shift_side(block, 1),
        shift_side(block, -1),
    )


def total_of(terms):
    result = terms[0]
    for term in terms[1:]:
        result = result + term
    return result


def inside_grid(shape, margin, cells_lateral):
    plane = lax.broadcasted_iota(jnp.int32, shape, 0)
    lateral = lax.axis_index("lat")
    first = jnp.where(lateral == 0, margin, 1)
    last = jnp.where(lateral == lax.axis_size("lat") - 1, margin + cells_lateral, shape[0] - 1)
    return (plane >= first) & (plane < last)


VISCOSITY, VELOCITY, SOURCE, BLOCK_FIELDS = 3, 4, 7, 10
LONG_FIELDS, SHORT_FIELDS = 5, 7


def message_pieces(cells_lateral):
    margin = MIGRATION_PLANES
    planes = cells_lateral + 2 * margin
    inner = (
        [(1 + 2 * margin, planes - 2 - 4 * margin)],
        [(3 * margin, planes - 6 * margin)],
    )
    edge = (
        [(1, 2 * margin), (planes - 1 - 2 * margin, 2 * margin)],
        [(margin, 2 * margin), (planes - 3 * margin, 2 * margin)],
    )
    return inner, edge


def piece_rows(pieces):
    row, places = 0, []
    for field in range(LONG_FIELDS + SHORT_FIELDS):
        places.append([])
        for first, count in pieces[0 if field < LONG_FIELDS else 1]:
            places[field].append((row, first, count))
            row += count
    return places, round_up(row, 8)


def put_pieces(message_ref, pieces, field, value):
    for row, first, count in piece_rows(pieces)[0][field]:
        message_ref[pl.ds(row, count), :] = value[first : first + count]


def block_place(fields, cells_radial):
    pitch = round_up(cells_radial, 8)

    def put(field, plane, value):
        fields[field, pl.ds(plane * pitch, cells_radial), :] = value

    return put


def put_own(put, stay_ref, base_ref, velocity_ref, forcing_ref):
    cells_lateral, cells_radial, _ = base_ref.shape
    for x in range(cells_lateral):
        plane = MIGRATION_PLANES + x
        put(VISCOSITY, plane, base_ref[x])
        for q in range(3):
            rows = pl.ds((q * cells_lateral + x) * cells_radial, cells_radial)
            put(q, plane, stay_ref[rows, :])
            put(VELOCITY + q, plane, velocity_ref[q, x])
            put(SOURCE + q, plane, forcing_ref[q, x])


def composition_of(fields, cells_radial, plane):
    rows = pl.ds(plane * round_up(cells_radial, 8), cells_radial)
    total_weight = fields[0, rows, :] + PRIOR_WEIGHT
    basalt_share = fields[1, rows, :] / total_weight
    melt_share = fields[2, rows, :] / total_weight
    fields[VISCOSITY, rows, :] = fields[VISCOSITY, rows, :] * jnp.exp(
        CONTRAST_BASALT * basalt_share - CONTRAST_MELT * melt_share
    )
    fields[SOURCE + 2, rows, :] = fields[SOURCE + 2, rows, :] - BUOYANCY * basalt_share
    return basalt_share, melt_share


def solve_lines(fields, planes, cells_radial, valid, keep, keep_part):
    pitch = round_up(cells_radial, 8)
    lower_block = lax.axis_index("rad") == 0

    def radial(field, t):
        row = jnp.where(lower_block, t, cells_radial - 1 - t)
        return fields[field, pl.ds(row, planes, stride=pitch), :]

    last = cells_radial - 1
    viscosity = [radial(VISCOSITY, t) for t in range(cells_radial)]
    lateral_faces = [
        [LATERAL * 0.5 * (here + there) for there in neighbours(here)] for here in viscosity
    ]
    radial_faces = [RADIAL * 0.5 * viscosity[0]] + [
        RADIAL * 0.5 * (viscosity[t - 1] + viscosity[t]) for t in range(1, cells_radial)
    ]

    excess = total_of(lateral_faces[0]) + radial_faces[0]
    inverse, coupling = [], []
    for t in range(last):
        inverse.append(1.0 / (excess + radial_faces[t + 1]))
        coupling.append(radial_faces[t + 1] * inverse[t])
        excess = total_of(lateral_faces[t + 1]) + coupling[t] * excess

    def lateral_terms(t, around):
        return [face * there for face, there in zip(lateral_faces[t], around)]

    def forward(right_side):
        eliminated = [right_side[0]]
        for t in range(1, cells_radial):
            eliminated.append(right_side[t] + coupling[t - 1] * eliminated[t - 1])
        return eliminated

    def backward(eliminated):
        solved = [jnp.zeros_like(excess)]
        for t in range(last - 1, -1, -1):
            solved.append(eliminated[t] * inverse[t] + coupling[t] * solved[-1])
        return solved[::-1]

    response = [jnp.ones_like(excess)]
    for t in range(last - 1, -1, -1):
        response.append(coupling[t] * response[-1])
    response = response[::-1]

    def finish(part, eliminated):
        keep(LONG_FIELDS + part, eliminated[last])
        if keep_part is not None:
            for t, value in enumerate(backward(eliminated)):
                keep_part(part, t, value)

    keep(0, viscosity[last])
    keep(1, excess)
    for q in range(3):
        source = [radial(SOURCE + q, t) for t in range(cells_radial)]
        eliminated = forward(
            [
                total_of([source[t]] + lateral_terms(t, neighbours(radial(VELOCITY + q, t))))
                for t in range(cells_radial)
            ]
        )
        keep(2 + q, eliminated[last])
        particular = [jnp.where(valid, value, 0.0) for value in backward(eliminated)]
        finish(
            q,
            forward(
                [
                    total_of([source[t]] + lateral_terms(t, neighbours(particular[t])))
                    for t in range(cells_radial)
                ]
            ),
        )
    around = [neighbours(jnp.where(valid, value, 0.0)) for value in response]
    for side in range(4):
        finish(
            3 + side,
            forward([lateral_faces[t][side] * around[t][side] for t in range(cells_radial)]),
        )
    if keep_part is not None:
        for t in range(cells_radial):
            keep_part(SHORT_FIELDS, t, response[t])


def inner_kernel(stay_ref, base_ref, velocity_ref, forcing_ref, message_ref, fields):
    cells_lateral, cells_radial, cells_side = base_ref.shape
    margin = MIGRATION_PLANES
    planes = cells_lateral + 2 * margin
    put = block_place(fields, cells_radial)
    outside = jnp.zeros((cells_radial, cells_side), jnp.float32)
    for plane in [*range(margin), *range(margin + cells_lateral, planes)]:
        for field in range(BLOCK_FIELDS):
            put(field, plane, outside)
    put_own(put, stay_ref, base_ref, velocity_ref, forcing_ref)
    for plane in range(2 * margin, planes - 2 * margin):
        composition_of(fields, cells_radial, plane)
    inner, _ = message_pieces(cells_lateral)
    message_ref[...] = jnp.zeros_like(message_ref)
    valid = inside_grid((planes, cells_side), margin, cells_lateral)
    keep = functools.partial(put_pieces, message_ref, inner)
    solve_lines(fields, planes, cells_radial, valid, keep, None)


def edge_kernel(
    stay_ref,
    second_ref,
    first_ref,
    from_second_ref,
    from_first_ref,
    base_ref,
    velocity_ref,
    forcing_ref,
    inner_ref,
    composition_ref,
    mine_ref,
    message_ref,
    parts_ref,
    fields,
):
    cells_lateral, cells_radial, cells_side = base_ref.shape
    margin = MIGRATION_PLANES
    planes = cells_lateral + 2 * margin
    moved_planes = margin * cells_radial
    starts, _ = payload_sections(cells_radial)
    odd = lax.rem(lax.axis_index("lat"), 2) == 1
    put = block_place(fields, cells_radial)

    def sent(upward, start):
        part = pl.ds(start, cells_radial)
        mine_first = odd if not upward else jnp.logical_not(odd)
        return jnp.where(mine_first, first_ref[part, :], second_ref[part, :])

    def arrived(from_above, start):
        part = pl.ds(start, cells_radial)
        is_first = odd if not from_above else jnp.logical_not(odd)
        return jnp.where(is_first, from_first_ref[part, :], from_second_ref[part, :])

    put_own(put, stay_ref, base_ref, velocity_ref, forcing_ref)
    for above in (False, True):
        outer = margin + cells_lateral if above else margin - 1
        beyond = planes - 1 if above else 0
        for offset in range(margin):
            x = offset + (cells_lateral - margin if above else 0)
            plane = offset + (margin + cells_lateral if above else 0)
            shift = offset * cells_radial
            put(VISCOSITY, plane, arrived(above, starts[3] + shift))
            for q in range(3):
                row = q * moved_planes + shift
                rows = pl.ds((q * cells_lateral + x) * cells_radial, cells_radial)
                put(q, margin + x, stay_ref[rows, :] + arrived(above, starts[0] + row))
                put(q, plane, sent(above, starts[0] + row) + arrived(above, starts[1] + row))
                put(VELOCITY + q, plane, arrived(above, starts[2] + row))
        for q in range(3):
            put(SOURCE + q, outer, arrived(above, starts[4] + q * cells_radial))
            put(SOURCE + q, beyond, jnp.zeros((cells_radial, cells_side), jnp.float32))
    for plane in range(planes):
        basalt_share, melt_share = composition_of(fields, cells_radial, plane)
        if margin <= plane < margin + cells_lateral:
            composition_ref[0, plane - margin] = basalt_share
            composition_ref[1, plane - margin] = melt_share

    _, edge = message_pieces(cells_lateral)
    if piece_rows(edge)[0][-1][-1][0] + 2 * margin < message_ref.shape[0]:
        message_ref[...] = jnp.zeros_like(message_ref)

    def keep(field, value):
        mine_ref[field] = value
        put_pieces(message_ref, edge, field, value)

    def keep_part(part, t, value):
        parts_ref[part, t] = value

    valid = inside_grid((planes, cells_side), margin, cells_lateral)
    solve_lines(fields, planes, cells_radial, valid, keep, keep_part)


def eliminate_inner(stay, base_viscosity, velocity, forcing):
    cells_lateral, cells_radial, cells_side = base_viscosity.shape
    planes = cells_lateral + 2 * MIGRATION_PLANES
    vmem = pl.BlockSpec(memory_space=pltpu.VMEM)
    rows = piece_rows(message_pieces(cells_lateral)[0])[1]
    return pl.pallas_call(
        inner_kernel,
        out_shape=jax.ShapeDtypeStruct((rows, cells_side), jnp.float32),
        in_specs=[vmem] * 4,
        out_specs=vmem,
        scratch_shapes=[
            pltpu.VMEM((BLOCK_FIELDS, planes * round_up(cells_radial, 8), cells_side), jnp.float32)
        ],
        compiler_params=pltpu.CompilerParams(vmem_limit_bytes=32 * 2**20),
        name="eliminate_inner",
    )(stay, base_viscosity, velocity, forcing)


def eliminate_edge(stay, sent, received, base_viscosity, velocity, forcing, inner):
    cells_lateral, cells_radial, cells_side = base_viscosity.shape
    planes = cells_lateral + 2 * MIGRATION_PLANES
    vmem = pl.BlockSpec(memory_space=pltpu.VMEM)
    rows = piece_rows(message_pieces(cells_lateral)[1])[1]
    lines = (planes, cells_side)
    return pl.pallas_call(
        edge_kernel,
        out_shape=(
            jax.ShapeDtypeStruct((2,) + base_viscosity.shape, jnp.float32),
            jax.ShapeDtypeStruct((LONG_FIELDS + SHORT_FIELDS,) + lines, jnp.float32),
            jax.ShapeDtypeStruct((rows, cells_side), jnp.float32),
            jax.ShapeDtypeStruct((SHORT_FIELDS + 1, cells_radial) + lines, jnp.float32),
        ),
        in_specs=[vmem] * 8 + [pl.BlockSpec(memory_space=pl.ANY)],
        out_specs=(vmem,) * 4,
        scratch_shapes=[
            pltpu.VMEM((BLOCK_FIELDS, planes * round_up(cells_radial, 8), cells_side), jnp.float32)
        ],
        compiler_params=pltpu.CompilerParams(vmem_limit_bytes=32 * 2**20),
        name="eliminate_edge",
    )(stay, *sent[::-1], *received[::-1], base_viscosity, velocity, forcing, inner)


def join_kernel(mine_ref, inner_ref, edge_ref, parts_ref, smoothed_ref, lines, other_ref):
    _, cells_lateral, cells_radial, cells_side = smoothed_ref.shape
    margin = MIGRATION_PLANES
    planes = cells_lateral + 2 * margin
    pitch = round_up(cells_radial, 8)
    valid = inside_grid((planes, cells_side), margin, cells_lateral)
    lower_block = lax.axis_index("rad") == 0

    other_ref[...] = jnp.zeros_like(other_ref)
    for message_ref, pieces in zip((inner_ref, edge_ref), message_pieces(cells_lateral)):
        for field, places in enumerate(piece_rows(pieces)[0]):
            for row, first, count in places:
                other_ref[field, pl.ds(first, count), :] = message_ref[pl.ds(row, count), :]

    face = RADIAL * 0.5 * (mine_ref[0] + other_ref[0])
    excess, other_excess = mine_ref[1], other_ref[1]
    scale = 1.0 / (excess * other_excess + face * (excess + other_excess))
    own_weight = (other_excess + face) * scale
    other_weight = (excess + face) * scale
    cross = face * scale

    def second_right(ref, q, around):
        terms = [ref[LONG_FIELDS + 3 + side] * there for side, there in enumerate(around)]
        return total_of([ref[LONG_FIELDS + q]] + terms)

    for q in range(3):
        right, other_right = mine_ref[2 + q], other_ref[2 + q]
        own = jnp.where(valid, own_weight * right + cross * other_right, 0.0)
        other = jnp.where(valid, other_weight * other_right + cross * right, 0.0)
        around = neighbours(own)
        right = second_right(mine_ref, q, around)
        other_right = second_right(other_ref, q, neighbours(other))
        final = own_weight * right + cross * other_right
        for t in range(cells_radial):
            value = parts_ref[q, t] + parts_ref[SHORT_FIELDS, t] * final
            for side in range(4):
                value = value + parts_ref[3 + side, t] * around[side]
            row = jnp.where(lower_block, t, cells_radial - 1 - t)
            lines[pl.ds(row, cells_lateral, stride=pitch), :] = value[
                margin : margin + cells_lateral
            ]
        for x in range(cells_lateral):
            smoothed_ref[q, x] = lines[pl.ds(x * pitch, cells_radial), :]


def join(mine, inner, edge, parts, like):
    cells_lateral, cells_radial, cells_side = like.shape[1:]
    vmem = pl.BlockSpec(memory_space=pltpu.VMEM)
    return pl.pallas_call(
        join_kernel,
        out_shape=jax.ShapeDtypeStruct(like.shape, jnp.float32),
        in_specs=[vmem] * 4,
        out_specs=vmem,
        scratch_shapes=[
            pltpu.VMEM((cells_lateral * round_up(cells_radial, 8), cells_side), jnp.float32),
            pltpu.VMEM(mine.shape, jnp.float32),
        ],
        compiler_params=pltpu.CompilerParams(vmem_limit_bytes=32 * 2**20),
        name="join",
    )(mine, inner, edge, parts)


def extended(block, sides, width):
    for axis, dim in sides:
        count = lax.axis_size(axis)
        forward = [(i, i + 1) for i in range(count - 1)]
        backward = [(target, source) for source, target in forward]
        low = lax.ppermute(
            lax.slice_in_dim(block, block.shape[dim] - width, None, axis=dim), axis, forward
        )
        high = lax.ppermute(lax.slice_in_dim(block, 0, width, axis=dim), axis, backward)
        block = jnp.concatenate([low, block, high], axis=dim)
    return block


def block_factor(diagonal, lower_band, upper_band):
    pivots = []
    upper_scaled = []
    for row_index in range(diagonal.shape[1]):
        if row_index == 0:
            pivot_row = diagonal[:, 0]
        else:
            pivot_row = diagonal[:, row_index] - lower_band[:, row_index] * upper_scaled[-1]
        pivots.append(pivot_row)
        upper_scaled.append(upper_band[:, row_index] / pivot_row)
    return (pivots, upper_scaled)


def block_solve(pivots, upper_scaled, lower_band, right_side):
    row_total = len(pivots)
    modified = []
    for row_index in range(row_total):
        if row_index == 0:
            value_row = right_side[:, :, 0] / pivots[0]
        else:
            value_row = (
                right_side[:, :, row_index] - lower_band[:, row_index] * modified[-1]
            ) / pivots[row_index]
        modified.append(value_row)
    solved = [modified[-1]]
    for row_index in range(row_total - 2, -1, -1):
        solved.append(modified[row_index] - upper_scaled[row_index] * solved[-1])
    ordered = solved[::-1]
    return jnp.stack(ordered, 2)


def interface_solve(coefficients):
    column_total = coefficients.shape[2]

    def forward(carried, inputs):
        offset, carried_slope = carried
        left_first, right_first, left_last, right_last, free_first, free_last = inputs
        divisor = 1.0 - left_first * carried_slope
        first_fixed = (free_first + left_first * offset) / divisor
        first_slope = right_first / divisor
        next_offset = free_last + left_last * (offset + carried_slope * first_fixed)
        next_slope = left_last * carried_slope * first_slope + right_last
        return ((next_offset, next_slope), (first_fixed, first_slope, next_offset, next_slope))

    start_state = (
        jnp.zeros((3, column_total), jnp.float32),
        jnp.zeros((column_total,), jnp.float32),
    )
    scan_inputs = (
        coefficients[:, 0],
        coefficients[:, 1],
        coefficients[:, 2],
        coefficients[:, 3],
        coefficients[:, 4:7],
        coefficients[:, 7:10],
    )
    final_state, eliminated = lax.scan(forward, start_state, scan_inputs)

    def backward(first_next, inputs):
        fixed_first, slope_first, fixed_last, slope_last = inputs
        first_value = fixed_first + slope_first * first_next
        last_value = fixed_last + slope_last * first_next
        return (first_value, (first_value, last_value))

    final_first, values_pair = lax.scan(
        backward, jnp.zeros((3, column_total), jnp.float32), eliminated, reverse=True
    )
    first_values, last_values = values_pair
    nothing_row = jnp.zeros((1, 3, column_total), jnp.float32)
    from_below = jnp.concatenate([nothing_row, last_values[:-1]], 0)
    from_above = jnp.concatenate([first_values[1:], nothing_row], 0)
    return jnp.concatenate([from_below, from_above], 1)


def reduced_boundary(interface):
    gathered = lax.all_gather(interface, "rad", axis=0, tiled=True)
    solved = interface_solve(gathered)
    return lax.dynamic_index_in_dim(solved, lax.axis_index("rad"), 0, keepdims=False)


def many_blocks(stay, received, base_viscosity, velocity, forcing):
    cells_lateral, cells_radial, cells_side = base_viscosity.shape
    moved_rows = MIGRATION_PLANES * cells_radial
    odd = lax.rem(lax.axis_index("lat"), 2) == 1
    from_below = jnp.where(odd, received[0], received[1])[: 3 * moved_rows]
    from_above = jnp.where(odd, received[1], received[0])[: 3 * moved_rows]
    stay = stay.reshape(3, cells_lateral * cells_radial, cells_side)
    totals = stay.at[:, :moved_rows].add(from_below.reshape(3, moved_rows, cells_side))
    totals = totals.at[:, -moved_rows:].add(from_above.reshape(3, moved_rows, cells_side))
    grouped = totals.reshape(3, cells_lateral, cells_radial, cells_side)
    total_weight = grouped[0] + PRIOR_WEIGHT
    basalt_share = grouped[1] / total_weight
    melt_share = grouped[2] / total_weight
    viscosity = base_viscosity * jnp.exp(
        CONTRAST_BASALT * basalt_share - CONTRAST_MELT * melt_share
    )
    viscosity_pad = extended(viscosity, (("lat", 0), ("rad", 1)), 1)
    side_pad = jnp.pad(viscosity, ((0, 0), (0, 0), (1, 1)))
    face_west = LATERAL * 0.5 * (viscosity + viscosity_pad[:-2, 1:-1])
    face_east = LATERAL * 0.5 * (viscosity + viscosity_pad[2:, 1:-1])
    face_south = LATERAL * 0.5 * (viscosity + side_pad[:, :, :-2])
    face_north = LATERAL * 0.5 * (viscosity + side_pad[:, :, 2:])
    face_below = RADIAL * 0.5 * (viscosity + viscosity_pad[1:-1, :-2])
    face_above = RADIAL * 0.5 * (viscosity + viscosity_pad[1:-1, 2:])
    diagonal = face_west + face_east + face_south + face_north + face_below + face_above
    source = jnp.concatenate([forcing[:2], (forcing[2] - BUOYANCY * basalt_share)[None]], 0)
    lower_band = -face_below
    upper_band = -face_above
    pivots, upper_scaled = block_factor(diagonal, lower_band, upper_band)
    radial_iota = lax.broadcasted_iota(jnp.int32, viscosity.shape, 1)
    response_side = jnp.stack(
        [
            jnp.where(radial_iota == 0, face_below, jnp.float32(0.0)),
            jnp.where(radial_iota == cells_radial - 1, face_above, jnp.float32(0.0)),
        ]
    )
    response = block_solve(pivots, upper_scaled, lower_band, response_side)
    current = velocity
    for sweep_index in range(SWEEPS):
        velocity_pad = extended(current, (("lat", 1),), 1)
        side_velocity = jnp.pad(current, ((0, 0), (0, 0), (0, 0), (1, 1)))
        right_side = (
            source
            + face_west * velocity_pad[:, :-2]
            + face_east * velocity_pad[:, 2:]
            + face_south * side_velocity[..., :-2]
            + face_north * side_velocity[..., 2:]
        )
        particular = block_solve(pivots, upper_scaled, lower_band, right_side)
        interface = jnp.concatenate(
            [response[:, :, 0], response[:, :, -1], particular[:, :, 0], particular[:, :, -1]], 0
        )
        interface = interface.reshape(1, 10, cells_lateral * cells_side)
        boundary = reduced_boundary(interface).reshape(6, cells_lateral, 1, cells_side)
        current = particular + response[0][None] * boundary[:3] + response[1][None] * boundary[3:]
    composition = jnp.stack([basalt_share, melt_share])
    return (current, composition)

def local(tracer_values, tracer_cell, tracer_count, base_viscosity, velocity, forcing):
    stay, *sent = tracer_sums(
        tracer_values, tracer_cell, tracer_count, base_viscosity, velocity, forcing
    )
    received = pair_swaps(*sent)
    if lax.axis_size("rad") != 2:
        return many_blocks(stay, received, base_viscosity, velocity, forcing)
    inner = eliminate_inner(stay, base_viscosity, velocity, forcing)
    from_inner = lax.ppermute(inner, "rad", [(0, 1), (1, 0)])
    composition, mine, edge, parts = eliminate_edge(
        stay, sent, received, base_viscosity, velocity, forcing, from_inner
    )
    from_edge = lax.ppermute(edge, "rad", [(0, 1), (1, 0)])
    return join(mine, from_inner, from_edge, parts, velocity), composition


def solution(mesh):
    return jax.shard_map(
        local,
        mesh=mesh,
        in_specs=(
            P("lat", "rad", None, None),
            P("lat", "rad", None),
            P("lat", "rad", None),
            P("lat", "rad", None),
            P(None, "lat", "rad", None),
            P(None, "lat", "rad", None),
        ),
        out_specs=(P(None, "lat", "rad", None), P(None, "lat", "rad", None)),
        check_vma=False,
    )
```

```python
import functools

import jax
import jax.numpy as jnp
from jax import lax
from jax.experimental import pallas as pl
from jax.experimental.pallas import tpu as pltpu
from jax.sharding import PartitionSpec as P

SWEEPS = 2
MIGRATION_PLANES = 2

LATERAL = 0.015625
RADIAL = 32.0
BUOYANCY = 0.1
PRIOR_WEIGHT = 0.5
CONTRAST_BASALT = 2.3
CONTRAST_MELT = 1.5

TILE_ROWS = 16


def round_up(value, multiple):
    return -(-value // multiple) * multiple


def split_index(index, count):
    if count & (count - 1) == 0:
        return lax.shift_right_logical(index, count.bit_length() - 1), index & (count - 1)
    quotient = lax.div(index, count)
    return quotient, index - quotient * count


def payload_sections(cells_radial):
    pair = MIGRATION_PLANES * cells_radial
    starts = [0, 3 * pair, 6 * pair, 9 * pair, 10 * pair]
    return starts, round_up(10 * pair + 3 * cells_radial, 8)


def spread_row(row):
    return jnp.broadcast_to(row, (TILE_ROWS, row.shape[1])).astype(jnp.bfloat16)


def hot_tiles(index, row_total):
    iota = lax.broadcasted_iota(jnp.int32, index.shape, 0)
    return [
        index == (iota + first).astype(jnp.float32).astype(jnp.bfloat16)
        for first in range(0, row_total, TILE_ROWS)
    ]


def hot_product(loads, high, low, high_rows, low_rows):
    left, right = [], []
    zero = jnp.zeros((TILE_ROWS, high.shape[1]), jnp.bfloat16)
    one = jnp.ones((TILE_ROWS, high.shape[1]), jnp.bfloat16)
    for row in range(high.shape[0]):
        pick = slice(row, row + 1)
        high_masks = hot_tiles(spread_row(high[pick]), high_rows)
        low_masks = hot_tiles(spread_row(low[pick]), low_rows)
        spread = [spread_row(load[pick]) for load in loads]
        left.append(
            jnp.concatenate(
                [jnp.where(mask, load, zero) for load in spread for mask in high_masks], 0
            )
        )
        right.append(jnp.concatenate([jnp.where(mask, one, zero) for mask in low_masks], 0))
    return lax.dot_general(
        jnp.concatenate(left, 1),
        jnp.concatenate(right, 1),
        (((1,), (1,)), ((), ())),
        preferred_element_type=jnp.float32,
    )


def fold_stay(plane, side, plane_total, side_total):
    rows, width = plane_total * 2 // 3, side_total // 2
    other = plane >= rows
    half = side >= width
    high = jnp.where(half, plane - rows + (plane_total - rows), plane - rows)
    low = jnp.where(half, side - width, side) + side_total
    high = jnp.where(other, high, plane)
    low = jnp.where(other, low, side)
    return high.astype(jnp.float32), low.astype(jnp.float32), rows, side_total + width


def unfold_stay(table, q, plane_total, side_total, put):
    rows, width = plane_total * 2 // 3, side_total // 2
    left = plane_total - rows
    put(0, 0, table[pl.ds(q * rows, rows), 0:side_total])
    for half in (0, 1):
        block = table[pl.ds(q * rows + half * left, left), side_total : side_total + width]
        put(rows, half * width, block)


def fold_moved(plane, side, plane_total, side_total):
    rows, width = plane_total * 4 // 3, side_total // 4
    third = plane_total // 3
    part = jnp.where(plane >= third, 1, 0) + jnp.where(plane >= 2 * third, 1, 0)
    other = side >= 3 * width
    high = jnp.where(other, plane_total + plane - part * third, plane)
    low = jnp.where(other, side - 3 * width + part * width, side)
    return high.astype(jnp.float32), low.astype(jnp.float32), rows, 3 * width


def unfold_moved(table, q, plane_total, side_total, put):
    rows, width = plane_total * 4 // 3, side_total // 4
    third = plane_total // 3
    put(0, 0, table[pl.ds(q * rows, plane_total), 0 : 3 * width])
    for part in range(3):
        block = table[
            pl.ds(q * rows + plane_total, third), part * width : (part + 1) * width
        ]
        put(part * third, 3 * width, block)


def has_partners():
    lateral, count = lax.axis_index("lat"), lax.axis_size("lat")
    odd = lax.rem(lateral, 2) == 1
    above, below = lateral + 1 < count, lateral > 0
    return jnp.logical_or(odd, above), jnp.where(odd, above, below)


def tracer_kernel(
    block_rows,
    counts_hbm,
    values_hbm,
    cells_hbm,
    base_hbm,
    velocity_hbm,
    forcing_hbm,
    stay_ref,
    first_ref,
    second_ref,
    counts,
    values,
    cells,
    base,
    velocity,
    forcing,
    stay_sums,
    moved_sums,
    payload,
    semaphores,
):
    cells_lateral, cells_radial, cells_side = base_hbm.shape
    plane_total = cells_lateral * cells_radial
    moved_planes = MIGRATION_PLANES * cells_radial
    group_rows, lane_total = values.shape[2:]

    copies = []

    def fetch(source, target):
        copy = pltpu.make_async_copy(source, target, semaphores.at[len(copies)])
        copy.start()
        copies.append(copy)

    fetch(counts_hbm, counts)
    for first_row, rows in ((0, block_rows), (block_rows, group_rows - block_rows)):
        part = pl.ds(first_row, rows)
        fetch(cells_hbm.at[:, part], cells.at[:, part])
        fetch(values_hbm.at[:, :, part], values.at[:, :, part])
    for upward in (0, 1):
        outer = pl.ds((cells_lateral - MIGRATION_PLANES) * upward, MIGRATION_PLANES)
        fetch(base_hbm.at[outer], base.at[upward])
        fetch(velocity_hbm.at[:, outer], velocity.at[upward])
        fetch(forcing_hbm.at[:, pl.ds((cells_lateral - 1) * upward, 1)], forcing.at[upward])

    stay_sums[...] = jnp.zeros_like(stay_sums)
    moved_sums[...] = jnp.zeros_like(moved_sums)

    def loads_of(group, first_row):
        rows = pl.ds(first_row, block_rows)
        shape = (block_rows, lane_total)
        slot = (first_row + lax.broadcasted_iota(jnp.int32, shape, 0)) * lane_total
        slot = slot + lax.broadcasted_iota(jnp.int32, shape, 1)
        weight = jnp.where(
            slot < counts[0, 0, group], 0.5 + values[0, group, rows, :], jnp.float32(0.0)
        )
        loads = [weight, weight * values[1, group, rows, :], weight * values[2, group, rows, :]]
        plane, side = split_index(cells[group, rows, :], cells_side)
        return loads, plane, side

    def step(first_row):
        loads, plane, side = loads_of(1, first_row)
        stay_sums[...] += hot_product(
            loads, *fold_stay(plane, side, plane_total, cells_side)
        )
        for slot, group in enumerate((0, 2)):
            loads, plane, side = loads_of(group, first_row)
            if group == 0:
                plane = plane - (plane_total - moved_planes)
            moved_sums[slot] += hot_product(
                loads, *fold_moved(plane, side, moved_planes, cells_side)
            )

    for copy in copies[:3]:
        copy.wait()
    step(0)
    for copy in copies[3:5]:
        copy.wait()

    def repeat(index, carried):
        step(pl.multiple_of(index * block_rows, block_rows))
        return carried

    used = jnp.maximum(jnp.maximum(counts[0, 0, 0], counts[0, 0, 1]), counts[0, 0, 2])
    block_slots = block_rows * lane_total
    blocks = lax.div(used + (block_slots - 1), block_slots)
    lax.fori_loop(1, jnp.minimum(blocks, group_rows // block_rows), repeat, 0)
    for copy in copies[5:]:
        copy.wait()

    for q in range(3):

        def put_stay(plane, column, block):
            height, width = block.shape
            stay_ref[
                pl.ds(q * plane_total + plane, height), column : column + width
            ] = block

        unfold_stay(stay_sums, q, plane_total, cells_side, put_stay)
    starts, _ = payload_sections(cells_radial)
    odd = lax.rem(lax.axis_index("lat"), 2)
    for upward in (0, 1):
        place = odd if upward else 1 - odd
        first_plane = cells_lateral - MIGRATION_PLANES if upward else 0
        for q in range(3):

            def put_moved(plane, column, block):
                height, width = block.shape
                rows = pl.ds(starts[0] + q * moved_planes + plane, height)
                payload[place, rows, column : column + width] = block

            unfold_moved(moved_sums.at[upward], q, moved_planes, cells_side, put_moved)
            payload[place, pl.ds(starts[1] + q * moved_planes, moved_planes), :] = stay_ref[
                pl.ds(q * plane_total + first_plane * cells_radial, moved_planes), :
            ]
            for offset in range(MIGRATION_PLANES):
                payload[
                    place,
                    pl.ds(starts[2] + q * moved_planes + offset * cells_radial, cells_radial),
                    :,
                ] = velocity[upward, q, offset]
            payload[place, pl.ds(starts[4] + q * cells_radial, cells_radial), :] = forcing[
                upward, q, 0
            ]
        for offset in range(MIGRATION_PLANES):
            payload[place, pl.ds(starts[3] + offset * cells_radial, cells_radial), :] = base[
                upward, offset
            ]
    has_first, has_second = has_partners()
    first_ref[...] = jnp.where(has_first, payload[0], 0.0)
    second_ref[...] = jnp.where(has_second, payload[1], 0.0)


def tracer_sums(tracer_values, tracer_cell, tracer_count, base_viscosity, velocity, forcing):
    cells_lateral, cells_radial, cells_side = base_viscosity.shape
    plane_total = cells_lateral * cells_radial
    moved_planes = MIGRATION_PLANES * cells_radial
    lane_total = 128
    values = tracer_values.reshape(3, 3, -1, lane_total)
    cells = tracer_cell.reshape(3, -1, lane_total)
    group_rows = cells.shape[1]
    _, payload_rows = payload_sections(cells_radial)
    hbm = pl.BlockSpec(memory_space=pltpu.HBM)
    vmem = pl.BlockSpec(memory_space=pltpu.VMEM)
    payload = jax.ShapeDtypeStruct((payload_rows, cells_side), jnp.float32)
    outer_planes = (MIGRATION_PLANES, cells_radial, cells_side)
    stay_table = (2 * plane_total, cells_side * 3 // 2)
    moved_table = (4 * moved_planes, cells_side * 3 // 4)

    return pl.pallas_call(
        functools.partial(tracer_kernel, 16),
        out_shape=(
            jax.ShapeDtypeStruct((3 * plane_total, cells_side), jnp.float32),
            payload,
            payload,
        ),
        in_specs=[hbm] * 6,
        out_specs=(vmem, vmem, vmem),
        scratch_shapes=[
            pltpu.SMEM(tracer_count.shape, jnp.int32),
            pltpu.VMEM(values.shape, jnp.float32),
            pltpu.VMEM(cells.shape, jnp.int32),
            pltpu.VMEM((2,) + outer_planes, jnp.float32),
            pltpu.VMEM((2, 3) + outer_planes, jnp.float32),
            pltpu.VMEM((2, 3, 1, cells_radial, cells_side), jnp.float32),
            pltpu.VMEM(stay_table, jnp.float32),
            pltpu.VMEM((2,) + moved_table, jnp.float32),
            pltpu.VMEM((2, payload_rows, cells_side), jnp.float32),
            pltpu.SemaphoreType.DMA((11,)),
        ],
        compiler_params=pltpu.CompilerParams(vmem_limit_bytes=32 * 2**20),
        cost_estimate=pl.CostEstimate(
            flops=6 * group_rows * lane_total * plane_total * cells_side // 8,
            bytes_accessed=4 * (values.size + cells.size),
            transcendentals=0,
        ),
        name="tracer_sums",
    )(
        *(
            pltpu.with_memory_space_constraint(array, pltpu.HBM)
            for array in (tracer_count, values, cells, base_viscosity, velocity, forcing)
        )
    )


def pair_swaps(first, second):
    count = lax.axis_size("lat")
    received = []
    for payload, start in ((first, 0), (second, 1)):
        target = list(range(count))
        for low in range(start, count - 1, 2):
            target[low], target[low + 1] = low + 1, low
        received.append(lax.ppermute(payload, "lat", list(enumerate(target))))
    return received


def shift_planes(block, step):
    return pltpu.roll(block, step % block.shape[0], 0)


def shift_side(block, step):
    lane_total = block.shape[1]
    lane = lax.broadcasted_iota(jnp.int32, block.shape, 1)
    inside = lane >= step if step > 0 else lane < lane_total + step
    return jnp.where(inside, pltpu.roll(block, step % lane_total, 1), jnp.float32(0.0))


def neighbours(block):
    return (
        shift_planes(block, 1),
        shift_planes(block, -1),
        shift_side(block, 1),
        shift_side(block, -1),
    )


def total_of(terms):
    result = terms[0]
    for term in terms[1:]:
        result = result + term
    return result


def inside_grid(shape, margin, cells_lateral):
    plane = lax.broadcasted_iota(jnp.int32, shape, 0)
    lateral = lax.axis_index("lat")
    first = jnp.where(lateral == 0, margin, 1)
    last = jnp.where(lateral == lax.axis_size("lat") - 1, margin + cells_lateral, shape[0] - 1)
    return (plane >= first) & (plane < last)


VISCOSITY, VELOCITY, SOURCE, BLOCK_FIELDS = 3, 4, 7, 10
LONG_FIELDS, SHORT_FIELDS = 5, 7


def message_rows(cells_lateral):
    planes = cells_lateral + 2 * MIGRATION_PLANES
    return round_up(LONG_FIELDS * planes + SHORT_FIELDS * cells_lateral, 8)


def message_part(cells_lateral, field):
    planes = cells_lateral + 2 * MIGRATION_PLANES
    if field < LONG_FIELDS:
        return pl.ds(field * planes, planes), 0, planes
    first = LONG_FIELDS * planes + (field - LONG_FIELDS) * cells_lateral
    return pl.ds(first, cells_lateral), MIGRATION_PLANES, cells_lateral


def block_place(fields, cells_radial):
    pitch = round_up(cells_radial, 8)

    def put(field, plane, value):
        fields[field, pl.ds(plane * pitch, cells_radial), :] = value

    return put


def put_own(put, stay_ref, base_ref, velocity_ref, forcing_ref):
    cells_lateral, cells_radial, _ = base_ref.shape
    for x in range(cells_lateral):
        plane = MIGRATION_PLANES + x
        put(VISCOSITY, plane, base_ref[x])
        for q in range(3):
            rows = pl.ds((q * cells_lateral + x) * cells_radial, cells_radial)
            put(q, plane, stay_ref[rows, :])
            put(VELOCITY + q, plane, velocity_ref[q, x])
            put(SOURCE + q, plane, forcing_ref[q, x])


def composition_of(fields, cells_radial, plane):
    rows = pl.ds(plane * round_up(cells_radial, 8), cells_radial)
    total_weight = fields[0, rows, :] + PRIOR_WEIGHT
    basalt_share = fields[1, rows, :] / total_weight
    melt_share = fields[2, rows, :] / total_weight
    fields[VISCOSITY, rows, :] = fields[VISCOSITY, rows, :] * jnp.exp(
        CONTRAST_BASALT * basalt_share - CONTRAST_MELT * melt_share
    )
    fields[SOURCE + 2, rows, :] = fields[SOURCE + 2, rows, :] - BUOYANCY * basalt_share
    return basalt_share, melt_share


def solve_lines(fields, planes, cells_radial, valid, keep, keep_part):
    pitch = round_up(cells_radial, 8)
    lower_block = lax.axis_index("rad") == 0

    def radial(field, t):
        row = jnp.where(lower_block, t, cells_radial - 1 - t)
        return fields[field, pl.ds(row, planes, stride=pitch), :]

    last = cells_radial - 1
    viscosity = [radial(VISCOSITY, t) for t in range(cells_radial)]
    lateral_faces = [
        [LATERAL * 0.5 * (here + there) for there in neighbours(here)] for here in viscosity
    ]
    radial_faces = [RADIAL * 0.5 * viscosity[0]] + [
        RADIAL * 0.5 * (viscosity[t - 1] + viscosity[t]) for t in range(1, cells_radial)
    ]

    excess = total_of(lateral_faces[0]) + radial_faces[0]
    inverse, coupling = [], []
    for t in range(last):
        inverse.append(1.0 / (excess + radial_faces[t + 1]))
        coupling.append(radial_faces[t + 1] * inverse[t])
        excess = total_of(lateral_faces[t + 1]) + coupling[t] * excess

    def lateral_terms(t, around):
        return [face * there for face, there in zip(lateral_faces[t], around)]

    def forward(right_side):
        eliminated = [right_side[0]]
        for t in range(1, cells_radial):
            eliminated.append(right_side[t] + coupling[t - 1] * eliminated[t - 1])
        return eliminated

    def backward(eliminated):
        solved = [jnp.zeros_like(excess)]
        for t in range(last - 1, -1, -1):
            solved.append(eliminated[t] * inverse[t] + coupling[t] * solved[-1])
        return solved[::-1]

    response = [jnp.ones_like(excess)]
    for t in range(last - 1, -1, -1):
        response.append(coupling[t] * response[-1])
    response = response[::-1]

    def finish(part, eliminated):
        keep(LONG_FIELDS + part, eliminated[last])
        if keep_part is not None:
            for t, value in enumerate(eliminated[:last]):
                keep_part(part, t, value)

    keep(0, viscosity[last])
    keep(1, excess)
    for q in range(3):
        source = [radial(SOURCE + q, t) for t in range(cells_radial)]
        eliminated = forward(
            [
                total_of([source[t]] + lateral_terms(t, neighbours(radial(VELOCITY + q, t))))
                for t in range(cells_radial)
            ]
        )
        keep(2 + q, eliminated[last])
        particular = [jnp.where(valid, value, 0.0) for value in backward(eliminated)]
        finish(
            q,
            forward(
                [
                    total_of([source[t]] + lateral_terms(t, neighbours(particular[t])))
                    for t in range(cells_radial)
                ]
            ),
        )
    around = [neighbours(jnp.where(valid, value, 0.0)) for value in response]
    for side in range(4):
        finish(
            3 + side,
            forward([lateral_faces[t][side] * around[t][side] for t in range(cells_radial)]),
        )
    if keep_part is not None:
        for t in range(last):
            keep_part(SHORT_FIELDS, t, inverse[t])
            keep_part(SHORT_FIELDS + 1, t, coupling[t])


def eliminate_kernel(
    stay_ref,
    first_ref,
    second_ref,
    from_first_ref,
    from_second_ref,
    base_ref,
    velocity_ref,
    forcing_ref,
    composition_ref,
    mine_ref,
    message_ref,
    parts_ref,
    fields,
):
    cells_lateral, cells_radial, cells_side = base_ref.shape
    margin = MIGRATION_PLANES
    planes = cells_lateral + 2 * margin
    moved_planes = margin * cells_radial
    starts, _ = payload_sections(cells_radial)
    odd = lax.rem(lax.axis_index("lat"), 2) == 1
    put = block_place(fields, cells_radial)

    def sent(upward, start):
        part = pl.ds(start, cells_radial)
        mine_first = odd if not upward else jnp.logical_not(odd)
        return jnp.where(mine_first, first_ref[part, :], second_ref[part, :])

    def arrived(from_above, start):
        part = pl.ds(start, cells_radial)
        is_first = odd if not from_above else jnp.logical_not(odd)
        return jnp.where(is_first, from_first_ref[part, :], from_second_ref[part, :])

    put_own(put, stay_ref, base_ref, velocity_ref, forcing_ref)
    for above in (False, True):
        outer = margin + cells_lateral if above else margin - 1
        beyond = planes - 1 if above else 0
        for offset in range(margin):
            x = offset + (cells_lateral - margin if above else 0)
            plane = offset + (margin + cells_lateral if above else 0)
            shift = offset * cells_radial
            put(VISCOSITY, plane, arrived(above, starts[3] + shift))
            for q in range(3):
                row = q * moved_planes + shift
                rows = pl.ds((q * cells_lateral + x) * cells_radial, cells_radial)
                put(q, margin + x, stay_ref[rows, :] + arrived(above, starts[0] + row))
                put(q, plane, sent(above, starts[0] + row) + arrived(above, starts[1] + row))
                put(VELOCITY + q, plane, arrived(above, starts[2] + row))
        for q in range(3):
            put(SOURCE + q, outer, arrived(above, starts[4] + q * cells_radial))
            put(SOURCE + q, beyond, jnp.zeros((cells_radial, cells_side), jnp.float32))
    for plane in range(planes):
        basalt_share, melt_share = composition_of(fields, cells_radial, plane)
        if margin <= plane < margin + cells_lateral:
            composition_ref[0, plane - margin] = basalt_share
            composition_ref[1, plane - margin] = melt_share

    unused = LONG_FIELDS * planes + SHORT_FIELDS * cells_lateral
    if unused < message_ref.shape[0]:
        message_ref[unused:, :] = jnp.zeros((message_ref.shape[0] - unused, cells_side), jnp.float32)

    def keep(field, value):
        rows, first, count = message_part(cells_lateral, field)
        mine_ref[field] = value
        message_ref[rows, :] = value[first : first + count]

    def keep_part(part, t, value):
        parts_ref[part, t] = value

    valid = inside_grid((planes, cells_side), margin, cells_lateral)
    solve_lines(fields, planes, cells_radial, valid, keep, keep_part)


def eliminate(stay, sent, received, base_viscosity, velocity, forcing):
    cells_lateral, cells_radial, cells_side = base_viscosity.shape
    planes = cells_lateral + 2 * MIGRATION_PLANES
    vmem = pl.BlockSpec(memory_space=pltpu.VMEM)
    lines = (planes, cells_side)
    return pl.pallas_call(
        eliminate_kernel,
        out_shape=(
            jax.ShapeDtypeStruct((2,) + base_viscosity.shape, jnp.float32),
            jax.ShapeDtypeStruct((LONG_FIELDS + SHORT_FIELDS,) + lines, jnp.float32),
            jax.ShapeDtypeStruct((message_rows(cells_lateral), cells_side), jnp.float32),
            jax.ShapeDtypeStruct((SHORT_FIELDS + 2, cells_radial - 1) + lines, jnp.float32),
        ),
        in_specs=[vmem] * 8,
        out_specs=(vmem,) * 4,
        scratch_shapes=[
            pltpu.VMEM((BLOCK_FIELDS, planes * round_up(cells_radial, 8), cells_side), jnp.float32)
        ],
        compiler_params=pltpu.CompilerParams(vmem_limit_bytes=32 * 2**20),
        name="eliminate",
    )(stay, *sent, *received, base_viscosity, velocity, forcing)


def join_kernel(mine_ref, message_ref, parts_ref, smoothed_ref, lines, other_ref):
    _, cells_lateral, cells_radial, cells_side = smoothed_ref.shape
    margin = MIGRATION_PLANES
    planes = cells_lateral + 2 * margin
    pitch = round_up(cells_radial, 8)
    valid = inside_grid((planes, cells_side), margin, cells_lateral)
    lower_block = lax.axis_index("rad") == 0

    other_ref[LONG_FIELDS:] = jnp.zeros_like(other_ref[LONG_FIELDS:])
    for field in range(LONG_FIELDS + SHORT_FIELDS):
        rows, first, count = message_part(cells_lateral, field)
        other_ref[field, pl.ds(first, count), :] = message_ref[rows, :]

    face = RADIAL * 0.5 * (mine_ref[0] + other_ref[0])
    excess, other_excess = mine_ref[1], other_ref[1]
    scale = 1.0 / (excess * other_excess + face * (excess + other_excess))
    own_weight = (other_excess + face) * scale
    other_weight = (excess + face) * scale
    cross = face * scale

    def second_right(ref, q, around):
        terms = [ref[LONG_FIELDS + 3 + side] * there for side, there in enumerate(around)]
        return total_of([ref[LONG_FIELDS + q]] + terms)

    for q in range(3):
        right, other_right = mine_ref[2 + q], other_ref[2 + q]
        own = jnp.where(valid, own_weight * right + cross * other_right, 0.0)
        other = jnp.where(valid, other_weight * other_right + cross * right, 0.0)
        around = neighbours(own)
        right = second_right(mine_ref, q, around)
        other_right = second_right(other_ref, q, neighbours(other))
        value = own_weight * right + cross * other_right
        for t in range(cells_radial - 1, -1, -1):
            if t < cells_radial - 1:
                terms = [parts_ref[3 + side, t] * there for side, there in enumerate(around)]
                right = total_of([parts_ref[q, t]] + terms)
                value = right * parts_ref[SHORT_FIELDS, t] + parts_ref[SHORT_FIELDS + 1, t] * value
            row = jnp.where(lower_block, t, cells_radial - 1 - t)
            lines[pl.ds(row, cells_lateral, stride=pitch), :] = value[
                margin : margin + cells_lateral
            ]
        for x in range(cells_lateral):
            smoothed_ref[q, x] = lines[pl.ds(x * pitch, cells_radial), :]


def join(mine, message, parts, like):
    cells_lateral, cells_radial, cells_side = like.shape[1:]
    vmem = pl.BlockSpec(memory_space=pltpu.VMEM)
    return pl.pallas_call(
        join_kernel,
        out_shape=jax.ShapeDtypeStruct(like.shape, jnp.float32),
        in_specs=[vmem] * 3,
        out_specs=vmem,
        scratch_shapes=[
            pltpu.VMEM((cells_lateral * round_up(cells_radial, 8), cells_side), jnp.float32),
            pltpu.VMEM(mine.shape, jnp.float32),
        ],
        compiler_params=pltpu.CompilerParams(vmem_limit_bytes=32 * 2**20),
        name="join",
    )(mine, message, parts)


def extended(block, sides, width):
    for axis, dim in sides:
        count = lax.axis_size(axis)
        forward = [(i, i + 1) for i in range(count - 1)]
        backward = [(target, source) for source, target in forward]
        low = lax.ppermute(
            lax.slice_in_dim(block, block.shape[dim] - width, None, axis=dim), axis, forward
        )
        high = lax.ppermute(lax.slice_in_dim(block, 0, width, axis=dim), axis, backward)
        block = jnp.concatenate([low, block, high], axis=dim)
    return block


def block_factor(diagonal, lower_band, upper_band):
    pivots = []
    upper_scaled = []
    for row_index in range(diagonal.shape[1]):
        if row_index == 0:
            pivot_row = diagonal[:, 0]
        else:
            pivot_row = diagonal[:, row_index] - lower_band[:, row_index] * upper_scaled[-1]
        pivots.append(pivot_row)
        upper_scaled.append(upper_band[:, row_index] / pivot_row)
    return (pivots, upper_scaled)


def block_solve(pivots, upper_scaled, lower_band, right_side):
    row_total = len(pivots)
    modified = []
    for row_index in range(row_total):
        if row_index == 0:
            value_row = right_side[:, :, 0] / pivots[0]
        else:
            value_row = (
                right_side[:, :, row_index] - lower_band[:, row_index] * modified[-1]
            ) / pivots[row_index]
        modified.append(value_row)
    solved = [modified[-1]]
    for row_index in range(row_total - 2, -1, -1):
        solved.append(modified[row_index] - upper_scaled[row_index] * solved[-1])
    ordered = solved[::-1]
    return jnp.stack(ordered, 2)


def interface_solve(coefficients):
    column_total = coefficients.shape[2]

    def forward(carried, inputs):
        offset, carried_slope = carried
        left_first, right_first, left_last, right_last, free_first, free_last = inputs
        divisor = 1.0 - left_first * carried_slope
        first_fixed = (free_first + left_first * offset) / divisor
        first_slope = right_first / divisor
        next_offset = free_last + left_last * (offset + carried_slope * first_fixed)
        next_slope = left_last * carried_slope * first_slope + right_last
        return ((next_offset, next_slope), (first_fixed, first_slope, next_offset, next_slope))

    start_state = (
        jnp.zeros((3, column_total), jnp.float32),
        jnp.zeros((column_total,), jnp.float32),
    )
    scan_inputs = (
        coefficients[:, 0],
        coefficients[:, 1],
        coefficients[:, 2],
        coefficients[:, 3],
        coefficients[:, 4:7],
        coefficients[:, 7:10],
    )
    final_state, eliminated = lax.scan(forward, start_state, scan_inputs)

    def backward(first_next, inputs):
        fixed_first, slope_first, fixed_last, slope_last = inputs
        first_value = fixed_first + slope_first * first_next
        last_value = fixed_last + slope_last * first_next
        return (first_value, (first_value, last_value))

    final_first, values_pair = lax.scan(
        backward, jnp.zeros((3, column_total), jnp.float32), eliminated, reverse=True
    )
    first_values, last_values = values_pair
    nothing_row = jnp.zeros((1, 3, column_total), jnp.float32)
    from_below = jnp.concatenate([nothing_row, last_values[:-1]], 0)
    from_above = jnp.concatenate([first_values[1:], nothing_row], 0)
    return jnp.concatenate([from_below, from_above], 1)


def reduced_boundary(interface):
    gathered = lax.all_gather(interface, "rad", axis=0, tiled=True)
    solved = interface_solve(gathered)
    return lax.dynamic_index_in_dim(solved, lax.axis_index("rad"), 0, keepdims=False)


def many_blocks(stay, received, base_viscosity, velocity, forcing):
    cells_lateral, cells_radial, cells_side = base_viscosity.shape
    moved_rows = MIGRATION_PLANES * cells_radial
    odd = lax.rem(lax.axis_index("lat"), 2) == 1
    from_below = jnp.where(odd, received[0], received[1])[: 3 * moved_rows]
    from_above = jnp.where(odd, received[1], received[0])[: 3 * moved_rows]
    stay = stay.reshape(3, cells_lateral * cells_radial, cells_side)
    totals = stay.at[:, :moved_rows].add(from_below.reshape(3, moved_rows, cells_side))
    totals = totals.at[:, -moved_rows:].add(from_above.reshape(3, moved_rows, cells_side))
    grouped = totals.reshape(3, cells_lateral, cells_radial, cells_side)
    total_weight = grouped[0] + PRIOR_WEIGHT
    basalt_share = grouped[1] / total_weight
    melt_share = grouped[2] / total_weight
    viscosity = base_viscosity * jnp.exp(
        CONTRAST_BASALT * basalt_share - CONTRAST_MELT * melt_share
    )
    viscosity_pad = extended(viscosity, (("lat", 0), ("rad", 1)), 1)
    side_pad = jnp.pad(viscosity, ((0, 0), (0, 0), (1, 1)))
    face_west = LATERAL * 0.5 * (viscosity + viscosity_pad[:-2, 1:-1])
    face_east = LATERAL * 0.5 * (viscosity + viscosity_pad[2:, 1:-1])
    face_south = LATERAL * 0.5 * (viscosity + side_pad[:, :, :-2])
    face_north = LATERAL * 0.5 * (viscosity + side_pad[:, :, 2:])
    face_below = RADIAL * 0.5 * (viscosity + viscosity_pad[1:-1, :-2])
    face_above = RADIAL * 0.5 * (viscosity + viscosity_pad[1:-1, 2:])
    diagonal = face_west + face_east + face_south + face_north + face_below + face_above
    source = jnp.concatenate([forcing[:2], (forcing[2] - BUOYANCY * basalt_share)[None]], 0)
    lower_band = -face_below
    upper_band = -face_above
    pivots, upper_scaled = block_factor(diagonal, lower_band, upper_band)
    radial_iota = lax.broadcasted_iota(jnp.int32, viscosity.shape, 1)
    response_side = jnp.stack(
        [
            jnp.where(radial_iota == 0, face_below, jnp.float32(0.0)),
            jnp.where(radial_iota == cells_radial - 1, face_above, jnp.float32(0.0)),
        ]
    )
    response = block_solve(pivots, upper_scaled, lower_band, response_side)
    current = velocity
    for sweep_index in range(SWEEPS):
        velocity_pad = extended(current, (("lat", 1),), 1)
        side_velocity = jnp.pad(current, ((0, 0), (0, 0), (0, 0), (1, 1)))
        right_side = (
            source
            + face_west * velocity_pad[:, :-2]
            + face_east * velocity_pad[:, 2:]
            + face_south * side_velocity[..., :-2]
            + face_north * side_velocity[..., 2:]
        )
        particular = block_solve(pivots, upper_scaled, lower_band, right_side)
        interface = jnp.concatenate(
            [response[:, :, 0], response[:, :, -1], particular[:, :, 0], particular[:, :, -1]], 0
        )
        interface = interface.reshape(1, 10, cells_lateral * cells_side)
        boundary = reduced_boundary(interface).reshape(6, cells_lateral, 1, cells_side)
        current = particular + response[0][None] * boundary[:3] + response[1][None] * boundary[3:]
    composition = jnp.stack([basalt_share, melt_share])
    return (current, composition)

def local(tracer_values, tracer_cell, tracer_count, base_viscosity, velocity, forcing):
    stay, *sent = tracer_sums(
        tracer_values, tracer_cell, tracer_count, base_viscosity, velocity, forcing
    )
    received = pair_swaps(*sent)
    if lax.axis_size("rad") != 2:
        return many_blocks(stay, received, base_viscosity, velocity, forcing)
    composition, mine, message, parts = eliminate(
        stay, sent, received, base_viscosity, velocity, forcing
    )
    other = lax.ppermute(message, "rad", [(0, 1), (1, 0)])
    return join(mine, other, parts, velocity), composition


def solution(mesh):
    return jax.shard_map(
        local,
        mesh=mesh,
        in_specs=(
            P("lat", "rad", None, None),
            P("lat", "rad", None),
            P("lat", "rad", None),
            P("lat", "rad", None),
            P(None, "lat", "rad", None),
            P(None, "lat", "rad", None),
        ),
        out_specs=(P(None, "lat", "rad", None), P(None, "lat", "rad", None)),
        check_vma=False,
    )
```

```python
import functools

import jax
import jax.numpy as jnp
from jax import lax
from jax.experimental import pallas as pl
from jax.experimental.pallas import tpu as pltpu
from jax.sharding import PartitionSpec as P

SWEEPS = 2
MIGRATION_PLANES = 2

LATERAL = 0.015625
RADIAL = 32.0
BUOYANCY = 0.1
PRIOR_WEIGHT = 0.5
CONTRAST_BASALT = 2.3
CONTRAST_MELT = 1.5

TILE_ROWS = 16


def round_up(value, multiple):
    return -(-value // multiple) * multiple


def split_index(index, count):
    if count & (count - 1) == 0:
        return lax.shift_right_logical(index, count.bit_length() - 1), index & (count - 1)
    quotient = lax.div(index, count)
    return quotient, index - quotient * count


def payload_sections(cells_radial):
    pair = MIGRATION_PLANES * cells_radial
    starts = [0, 3 * pair, 6 * pair, 9 * pair, 10 * pair]
    return starts, round_up(10 * pair + 3 * cells_radial, 8)


def spread_row(row):
    return jnp.broadcast_to(row, (TILE_ROWS, row.shape[1])).astype(jnp.bfloat16)


def hot_tiles(index, row_total):
    iota = lax.broadcasted_iota(jnp.int32, index.shape, 0)
    return [
        index == (iota + first).astype(jnp.float32).astype(jnp.bfloat16)
        for first in range(0, row_total, TILE_ROWS)
    ]


def hot_product(loads, high, low, high_rows, low_rows):
    left, right = [], []
    zero = jnp.zeros((TILE_ROWS, high.shape[1]), jnp.bfloat16)
    one = jnp.ones((TILE_ROWS, high.shape[1]), jnp.bfloat16)
    for row in range(high.shape[0]):
        pick = slice(row, row + 1)
        high_masks = hot_tiles(spread_row(high[pick]), high_rows)
        low_masks = hot_tiles(spread_row(low[pick]), low_rows)
        spread = [spread_row(load[pick]) for load in loads]
        left.append(
            jnp.concatenate(
                [jnp.where(mask, load, zero) for load in spread for mask in high_masks], 0
            )
        )
        right.append(jnp.concatenate([jnp.where(mask, one, zero) for mask in low_masks], 0))
    return lax.dot_general(
        jnp.concatenate(left, 1),
        jnp.concatenate(right, 1),
        (((1,), (1,)), ((), ())),
        preferred_element_type=jnp.float32,
    )


def fold_stay(plane, side, plane_total, side_total):
    rows, width = plane_total * 2 // 3, side_total // 2
    other = plane >= rows
    half = side >= width
    high = jnp.where(half, plane - rows + (plane_total - rows), plane - rows)
    low = jnp.where(half, side - width, side) + side_total
    high = jnp.where(other, high, plane)
    low = jnp.where(other, low, side)
    return high.astype(jnp.float32), low.astype(jnp.float32), rows, side_total + width


def unfold_stay(table, q, plane_total, side_total, put):
    rows, width = plane_total * 2 // 3, side_total // 2
    left = plane_total - rows
    put(0, 0, table[pl.ds(q * rows, rows), 0:side_total])
    for half in (0, 1):
        block = table[pl.ds(q * rows + half * left, left), side_total : side_total + width]
        put(rows, half * width, block)


def fold_moved(plane, side, plane_total, side_total):
    rows, width = plane_total * 4 // 3, side_total // 4
    third = plane_total // 3
    part = jnp.where(plane >= third, 1, 0) + jnp.where(plane >= 2 * third, 1, 0)
    other = side >= 3 * width
    high = jnp.where(other, plane_total + plane - part * third, plane)
    low = jnp.where(other, side - 3 * width + part * width, side)
    return high.astype(jnp.float32), low.astype(jnp.float32), rows, 3 * width


def unfold_moved(table, q, plane_total, side_total, put):
    rows, width = plane_total * 4 // 3, side_total // 4
    third = plane_total // 3
    put(0, 0, table[pl.ds(q * rows, plane_total), 0 : 3 * width])
    for part in range(3):
        block = table[
            pl.ds(q * rows + plane_total, third), part * width : (part + 1) * width
        ]
        put(part * third, 3 * width, block)


def has_partners():
    lateral, count = lax.axis_index("lat"), lax.axis_size("lat")
    odd = lax.rem(lateral, 2) == 1
    above, below = lateral + 1 < count, lateral > 0
    return jnp.logical_or(odd, above), jnp.where(odd, above, below)


def tracer_kernel(
    block_rows,
    counts_hbm,
    values_hbm,
    cells_hbm,
    base_hbm,
    velocity_hbm,
    forcing_hbm,
    stay_ref,
    first_ref,
    second_ref,
    counts,
    values,
    cells,
    base,
    velocity,
    forcing,
    stay_sums,
    moved_sums,
    payload,
    semaphores,
):
    cells_lateral, cells_radial, cells_side = base_hbm.shape
    plane_total = cells_lateral * cells_radial
    moved_planes = MIGRATION_PLANES * cells_radial
    group_rows, lane_total = values.shape[2:]

    copies = []

    def fetch(source, target):
        copy = pltpu.make_async_copy(source, target, semaphores.at[len(copies)])
        copy.start()
        copies.append(copy)

    fetch(counts_hbm, counts)
    for first_row, rows in ((0, block_rows), (block_rows, group_rows - block_rows)):
        part = pl.ds(first_row, rows)
        fetch(cells_hbm.at[:, part], cells.at[:, part])
        fetch(values_hbm.at[:, :, part], values.at[:, :, part])
    for upward in (0, 1):
        outer = pl.ds((cells_lateral - MIGRATION_PLANES) * upward, MIGRATION_PLANES)
        fetch(base_hbm.at[outer], base.at[upward])
        fetch(velocity_hbm.at[:, outer], velocity.at[upward])
        fetch(forcing_hbm.at[:, pl.ds((cells_lateral - 1) * upward, 1)], forcing.at[upward])

    stay_sums[...] = jnp.zeros_like(stay_sums)
    moved_sums[...] = jnp.zeros_like(moved_sums)

    def loads_of(group, first_row):
        rows = pl.ds(first_row, block_rows)
        shape = (block_rows, lane_total)
        slot = (first_row + lax.broadcasted_iota(jnp.int32, shape, 0)) * lane_total
        slot = slot + lax.broadcasted_iota(jnp.int32, shape, 1)
        weight = jnp.where(
            slot < counts[0, 0, group], 0.5 + values[0, group, rows, :], jnp.float32(0.0)
        )
        loads = [weight, weight * values[1, group, rows, :], weight * values[2, group, rows, :]]
        plane, side = split_index(cells[group, rows, :], cells_side)
        return loads, plane, side

    def step(first_row):
        loads, plane, side = loads_of(1, first_row)
        stay_sums[...] += hot_product(
            loads, *fold_stay(plane, side, plane_total, cells_side)
        )
        for slot, group in enumerate((0, 2)):
            loads, plane, side = loads_of(group, first_row)
            if group == 0:
                plane = plane - (plane_total - moved_planes)
            moved_sums[slot] += hot_product(
                loads, *fold_moved(plane, side, moved_planes, cells_side)
            )

    for copy in copies[:3]:
        copy.wait()
    step(0)
    for copy in copies[3:5]:
        copy.wait()

    def repeat(index, carried):
        step(pl.multiple_of(index * block_rows, block_rows))
        return carried

    used = jnp.maximum(jnp.maximum(counts[0, 0, 0], counts[0, 0, 1]), counts[0, 0, 2])
    block_slots = block_rows * lane_total
    blocks = lax.div(used + (block_slots - 1), block_slots)
    lax.fori_loop(1, jnp.minimum(blocks, group_rows // block_rows), repeat, 0)
    for copy in copies[5:]:
        copy.wait()

    for q in range(3):

        def put_stay(plane, column, block):
            height, width = block.shape
            stay_ref[
                pl.ds(q * plane_total + plane, height), column : column + width
            ] = block

        unfold_stay(stay_sums, q, plane_total, cells_side, put_stay)
    starts, _ = payload_sections(cells_radial)
    odd = lax.rem(lax.axis_index("lat"), 2)
    for upward in (0, 1):
        place = odd if upward else 1 - odd
        first_plane = cells_lateral - MIGRATION_PLANES if upward else 0
        for q in range(3):

            def put_moved(plane, column, block):
                height, width = block.shape
                rows = pl.ds(starts[0] + q * moved_planes + plane, height)
                payload[place, rows, column : column + width] = block

            unfold_moved(moved_sums.at[upward], q, moved_planes, cells_side, put_moved)
            payload[place, pl.ds(starts[1] + q * moved_planes, moved_planes), :] = stay_ref[
                pl.ds(q * plane_total + first_plane * cells_radial, moved_planes), :
            ]
            for offset in range(MIGRATION_PLANES):
                payload[
                    place,
                    pl.ds(starts[2] + q * moved_planes + offset * cells_radial, cells_radial),
                    :,
                ] = velocity[upward, q, offset]
            payload[place, pl.ds(starts[4] + q * cells_radial, cells_radial), :] = forcing[
                upward, q, 0
            ]
        for offset in range(MIGRATION_PLANES):
            payload[place, pl.ds(starts[3] + offset * cells_radial, cells_radial), :] = base[
                upward, offset
            ]
    has_first, has_second = has_partners()
    first_ref[...] = jnp.where(has_first, payload[0], 0.0)
    second_ref[...] = jnp.where(has_second, payload[1], 0.0)


def tracer_sums(tracer_values, tracer_cell, tracer_count, base_viscosity, velocity, forcing):
    cells_lateral, cells_radial, cells_side = base_viscosity.shape
    plane_total = cells_lateral * cells_radial
    moved_planes = MIGRATION_PLANES * cells_radial
    lane_total = 128
    values = tracer_values.reshape(3, 3, -1, lane_total)
    cells = tracer_cell.reshape(3, -1, lane_total)
    group_rows = cells.shape[1]
    _, payload_rows = payload_sections(cells_radial)
    hbm = pl.BlockSpec(memory_space=pltpu.HBM)
    vmem = pl.BlockSpec(memory_space=pltpu.VMEM)
    payload = jax.ShapeDtypeStruct((payload_rows, cells_side), jnp.float32)
    outer_planes = (MIGRATION_PLANES, cells_radial, cells_side)
    stay_table = (2 * plane_total, cells_side * 3 // 2)
    moved_table = (4 * moved_planes, cells_side * 3 // 4)

    return pl.pallas_call(
        functools.partial(tracer_kernel, 32),
        out_shape=(
            jax.ShapeDtypeStruct((3 * plane_total, cells_side), jnp.float32),
            payload,
            payload,
        ),
        in_specs=[hbm] * 6,
        out_specs=(vmem, vmem, vmem),
        scratch_shapes=[
            pltpu.SMEM(tracer_count.shape, jnp.int32),
            pltpu.VMEM(values.shape, jnp.float32),
            pltpu.VMEM(cells.shape, jnp.int32),
            pltpu.VMEM((2,) + outer_planes, jnp.float32),
            pltpu.VMEM((2, 3) + outer_planes, jnp.float32),
            pltpu.VMEM((2, 3, 1, cells_radial, cells_side), jnp.float32),
            pltpu.VMEM(stay_table, jnp.float32),
            pltpu.VMEM((2,) + moved_table, jnp.float32),
            pltpu.VMEM((2, payload_rows, cells_side), jnp.float32),
            pltpu.SemaphoreType.DMA((11,)),
        ],
        compiler_params=pltpu.CompilerParams(vmem_limit_bytes=32 * 2**20),
        cost_estimate=pl.CostEstimate(
            flops=6 * group_rows * lane_total * plane_total * cells_side // 8,
            bytes_accessed=4 * (values.size + cells.size),
            transcendentals=0,
        ),
        name="tracer_sums",
    )(
        *(
            pltpu.with_memory_space_constraint(array, pltpu.HBM)
            for array in (tracer_count, values, cells, base_viscosity, velocity, forcing)
        )
    )


def pair_swaps(first, second):
    count = lax.axis_size("lat")
    received = []
    for payload, start in ((second, 1), (first, 0)):
        target = list(range(count))
        for low in range(start, count - 1, 2):
            target[low], target[low + 1] = low + 1, low
        received.append(lax.ppermute(payload, "lat", list(enumerate(target))))
    return received[::-1]


def shift_planes(block, step):
    return pltpu.roll(block, step % block.shape[0], 0)


def shift_side(block, step):
    return pltpu.roll(block, step % block.shape[1], 1)


def neighbours(block):
    return (
        shift_planes(block, 1),
        shift_planes(block, -1),
        shift_side(block, 1),
        shift_side(block, -1),
    )


def inside_side(values):
    lane = lax.broadcasted_iota(jnp.int32, values[2].shape, 1)
    lower = jnp.where(lane > 0, values[2], 0.0)
    upper = jnp.where(lane < lane.shape[1] - 1, values[3], 0.0)
    return values[0], values[1], lower, upper


def total_of(terms):
    result = terms[0]
    for term in terms[1:]:
        result = result + term
    return result


def inside_grid(shape, margin, cells_lateral):
    plane = lax.broadcasted_iota(jnp.int32, shape, 0)
    lateral = lax.axis_index("lat")
    first = jnp.where(lateral == 0, margin, 1)
    last = jnp.where(lateral == lax.axis_size("lat") - 1, margin + cells_lateral, shape[0] - 1)
    return (plane >= first) & (plane < last)


VISCOSITY, VELOCITY, SOURCE, BLOCK_FIELDS = 3, 4, 7, 10
LONG_FIELDS, SHORT_FIELDS = 5, 7


def message_rows(cells_lateral):
    planes = cells_lateral + 2 * MIGRATION_PLANES
    return round_up(LONG_FIELDS * planes + SHORT_FIELDS * cells_lateral, 8)


def message_part(cells_lateral, field):
    planes = cells_lateral + 2 * MIGRATION_PLANES
    if field < LONG_FIELDS:
        return pl.ds(field * planes, planes), 0, planes
    first = LONG_FIELDS * planes + (field - LONG_FIELDS) * cells_lateral
    return pl.ds(first, cells_lateral), MIGRATION_PLANES, cells_lateral


def block_place(fields, cells_radial):
    pitch = round_up(cells_radial, 8)

    def put(field, plane, value):
        fields[field, pl.ds(plane * pitch, cells_radial), :] = value

    return put


def put_own(put, stay_ref, base_ref, velocity_ref, forcing_ref):
    cells_lateral, cells_radial, _ = base_ref.shape
    for x in range(cells_lateral):
        plane = MIGRATION_PLANES + x
        put(VISCOSITY, plane, base_ref[x])
        for q in range(3):
            rows = pl.ds((q * cells_lateral + x) * cells_radial, cells_radial)
            put(q, plane, stay_ref[rows, :])
            put(VELOCITY + q, plane, velocity_ref[q, x])
            put(SOURCE + q, plane, forcing_ref[q, x])


def composition_of(fields, cells_radial, plane):
    rows = pl.ds(plane * round_up(cells_radial, 8), cells_radial)
    total_weight = fields[0, rows, :] + PRIOR_WEIGHT
    basalt_share = fields[1, rows, :] / total_weight
    melt_share = fields[2, rows, :] / total_weight
    fields[VISCOSITY, rows, :] = fields[VISCOSITY, rows, :] * jnp.exp(
        CONTRAST_BASALT * basalt_share - CONTRAST_MELT * melt_share
    )
    fields[SOURCE + 2, rows, :] = fields[SOURCE + 2, rows, :] - BUOYANCY * basalt_share
    return basalt_share, melt_share


def solve_lines(fields, planes, cells_radial, valid, keep, keep_part):
    pitch = round_up(cells_radial, 8)
    lower_block = lax.axis_index("rad") == 0

    def radial(field, t):
        row = jnp.where(lower_block, t, cells_radial - 1 - t)
        return fields[field, pl.ds(row, planes, stride=pitch), :]

    last = cells_radial - 1
    viscosity = [radial(VISCOSITY, t) for t in range(cells_radial)]
    lateral_faces, lateral_sums = [], []
    for here in viscosity:
        faces = [LATERAL * 0.5 * (here + there) for there in inside_side(neighbours(here))]
        lateral_sums.append(total_of(faces))
        lateral_faces.append(inside_side(faces))
    radial_faces = [RADIAL * 0.5 * viscosity[0]] + [
        RADIAL * 0.5 * (viscosity[t - 1] + viscosity[t]) for t in range(1, cells_radial)
    ]

    excess = lateral_sums[0] + radial_faces[0]
    inverse, coupling = [], []
    for t in range(last):
        inverse.append(1.0 / (excess + radial_faces[t + 1]))
        coupling.append(radial_faces[t + 1] * inverse[t])
        excess = lateral_sums[t + 1] + coupling[t] * excess

    def lateral_terms(t, around):
        return [face * there for face, there in zip(lateral_faces[t], around)]

    def forward(right_side):
        eliminated = [right_side[0]]
        for t in range(1, cells_radial):
            eliminated.append(right_side[t] + coupling[t - 1] * eliminated[t - 1])
        return eliminated

    def backward(eliminated):
        solved = [jnp.zeros_like(excess)]
        for t in range(last - 1, -1, -1):
            solved.append(eliminated[t] * inverse[t] + coupling[t] * solved[-1])
        return solved[::-1]

    response = [jnp.ones_like(excess)]
    for t in range(last - 1, -1, -1):
        response.append(coupling[t] * response[-1])
    response = response[::-1]

    def finish(part, eliminated):
        keep(LONG_FIELDS + part, eliminated[last])
        if keep_part is not None:
            for t, value in enumerate(eliminated[:last]):
                keep_part(part, t, value)

    keep(0, viscosity[last])
    keep(1, excess)
    for q in range(3):
        source = [radial(SOURCE + q, t) for t in range(cells_radial)]
        eliminated = forward(
            [
                total_of([source[t]] + lateral_terms(t, neighbours(radial(VELOCITY + q, t))))
                for t in range(cells_radial)
            ]
        )
        keep(2 + q, eliminated[last])
        particular = [jnp.where(valid, value, 0.0) for value in backward(eliminated)]
        finish(
            q,
            forward(
                [
                    total_of([source[t]] + lateral_terms(t, neighbours(particular[t])))
                    for t in range(cells_radial)
                ]
            ),
        )
    around = [neighbours(jnp.where(valid, value, 0.0)) for value in response]
    for side in range(4):
        finish(
            3 + side,
            forward([lateral_faces[t][side] * around[t][side] for t in range(cells_radial)]),
        )
    if keep_part is not None:
        for t in range(last):
            keep_part(SHORT_FIELDS, t, inverse[t])
            keep_part(SHORT_FIELDS + 1, t, coupling[t])


def eliminate_kernel(
    stay_ref,
    second_ref,
    first_ref,
    from_second_ref,
    from_first_ref,
    base_ref,
    velocity_ref,
    forcing_ref,
    composition_ref,
    mine_ref,
    message_ref,
    parts_ref,
    fields,
):
    cells_lateral, cells_radial, cells_side = base_ref.shape
    margin = MIGRATION_PLANES
    planes = cells_lateral + 2 * margin
    moved_planes = margin * cells_radial
    starts, _ = payload_sections(cells_radial)
    odd = lax.rem(lax.axis_index("lat"), 2) == 1
    put = block_place(fields, cells_radial)

    def sent(upward, start):
        part = pl.ds(start, cells_radial)
        mine_first = odd if not upward else jnp.logical_not(odd)
        return jnp.where(mine_first, first_ref[part, :], second_ref[part, :])

    def arrived(from_above, start):
        part = pl.ds(start, cells_radial)
        is_first = odd if not from_above else jnp.logical_not(odd)
        return jnp.where(is_first, from_first_ref[part, :], from_second_ref[part, :])

    put_own(put, stay_ref, base_ref, velocity_ref, forcing_ref)
    for above in (False, True):
        outer = margin + cells_lateral if above else margin - 1
        beyond = planes - 1 if above else 0
        for offset in range(margin):
            x = offset + (cells_lateral - margin if above else 0)
            plane = offset + (margin + cells_lateral if above else 0)
            shift = offset * cells_radial
            put(VISCOSITY, plane, arrived(above, starts[3] + shift))
            for q in range(3):
                row = q * moved_planes + shift
                rows = pl.ds((q * cells_lateral + x) * cells_radial, cells_radial)
                put(q, margin + x, stay_ref[rows, :] + arrived(above, starts[0] + row))
                put(q, plane, sent(above, starts[0] + row) + arrived(above, starts[1] + row))
                put(VELOCITY + q, plane, arrived(above, starts[2] + row))
        for q in range(3):
            put(SOURCE + q, outer, arrived(above, starts[4] + q * cells_radial))
            put(SOURCE + q, beyond, jnp.zeros((cells_radial, cells_side), jnp.float32))
    for plane in range(planes):
        basalt_share, melt_share = composition_of(fields, cells_radial, plane)
        if margin <= plane < margin + cells_lateral:
            composition_ref[0, plane - margin] = basalt_share
            composition_ref[1, plane - margin] = melt_share

    unused = LONG_FIELDS * planes + SHORT_FIELDS * cells_lateral
    if unused < message_ref.shape[0]:
        message_ref[unused:, :] = jnp.zeros((message_ref.shape[0] - unused, cells_side), jnp.float32)

    def keep(field, value):
        rows, first, count = message_part(cells_lateral, field)
        mine_ref[field] = value
        message_ref[rows, :] = value[first : first + count]

    def keep_part(part, t, value):
        parts_ref[part, t] = value

    valid = inside_grid((planes, cells_side), margin, cells_lateral)
    solve_lines(fields, planes, cells_radial, valid, keep, keep_part)


def eliminate(stay, sent, received, base_viscosity, velocity, forcing):
    cells_lateral, cells_radial, cells_side = base_viscosity.shape
    planes = cells_lateral + 2 * MIGRATION_PLANES
    vmem = pl.BlockSpec(memory_space=pltpu.VMEM)
    lines = (planes, cells_side)
    return pl.pallas_call(
        eliminate_kernel,
        out_shape=(
            jax.ShapeDtypeStruct((2,) + base_viscosity.shape, jnp.float32),
            jax.ShapeDtypeStruct((LONG_FIELDS + SHORT_FIELDS,) + lines, jnp.float32),
            jax.ShapeDtypeStruct((message_rows(cells_lateral), cells_side), jnp.float32),
            jax.ShapeDtypeStruct((SHORT_FIELDS + 2, cells_radial - 1) + lines, jnp.float32),
        ),
        in_specs=[vmem] * 8,
        out_specs=(vmem,) * 4,
        scratch_shapes=[
            pltpu.VMEM((BLOCK_FIELDS, planes * round_up(cells_radial, 8), cells_side), jnp.float32)
        ],
        compiler_params=pltpu.CompilerParams(vmem_limit_bytes=32 * 2**20),
        name="eliminate",
    )(stay, *sent[::-1], *received[::-1], base_viscosity, velocity, forcing)


def join_kernel(mine_ref, message_ref, parts_ref, smoothed_ref, lines, other_ref):
    _, cells_lateral, cells_radial, cells_side = smoothed_ref.shape
    margin = MIGRATION_PLANES
    planes = cells_lateral + 2 * margin
    pitch = round_up(cells_radial, 8)
    valid = inside_grid((planes, cells_side), margin, cells_lateral)
    lower_block = lax.axis_index("rad") == 0

    other_ref[LONG_FIELDS:] = jnp.zeros_like(other_ref[LONG_FIELDS:])
    for field in range(LONG_FIELDS + SHORT_FIELDS):
        rows, first, count = message_part(cells_lateral, field)
        other_ref[field, pl.ds(first, count), :] = message_ref[rows, :]

    face = RADIAL * 0.5 * (mine_ref[0] + other_ref[0])
    excess, other_excess = mine_ref[1], other_ref[1]
    scale = 1.0 / (excess * other_excess + face * (excess + other_excess))
    own_weight = (other_excess + face) * scale
    other_weight = (excess + face) * scale
    cross = face * scale

    def second_right(ref, q, around):
        terms = [ref[LONG_FIELDS + 3 + side] * there for side, there in enumerate(around)]
        return total_of([ref[LONG_FIELDS + q]] + terms)

    for q in range(3):
        right, other_right = mine_ref[2 + q], other_ref[2 + q]
        own = jnp.where(valid, own_weight * right + cross * other_right, 0.0)
        other = jnp.where(valid, other_weight * other_right + cross * right, 0.0)
        around = neighbours(own)
        right = second_right(mine_ref, q, around)
        other_right = second_right(other_ref, q, neighbours(other))
        value = own_weight * right + cross * other_right
        for t in range(cells_radial - 1, -1, -1):
            if t < cells_radial - 1:
                terms = [parts_ref[3 + side, t] * there for side, there in enumerate(around)]
                right = total_of([parts_ref[q, t]] + terms)
                value = right * parts_ref[SHORT_FIELDS, t] + parts_ref[SHORT_FIELDS + 1, t] * value
            row = jnp.where(lower_block, t, cells_radial - 1 - t)
            lines[pl.ds(row, cells_lateral, stride=pitch), :] = value[
                margin : margin + cells_lateral
            ]
        for x in range(cells_lateral):
            smoothed_ref[q, x] = lines[pl.ds(x * pitch, cells_radial), :]


def join(mine, message, parts, like):
    cells_lateral, cells_radial, cells_side = like.shape[1:]
    vmem = pl.BlockSpec(memory_space=pltpu.VMEM)
    return pl.pallas_call(
        join_kernel,
        out_shape=jax.ShapeDtypeStruct(like.shape, jnp.float32),
        in_specs=[vmem] * 3,
        out_specs=vmem,
        scratch_shapes=[
            pltpu.VMEM((cells_lateral * round_up(cells_radial, 8), cells_side), jnp.float32),
            pltpu.VMEM(mine.shape, jnp.float32),
        ],
        compiler_params=pltpu.CompilerParams(vmem_limit_bytes=32 * 2**20),
        name="join",
    )(mine, message, parts)


def extended(block, sides, width):
    for axis, dim in sides:
        count = lax.axis_size(axis)
        forward = [(i, i + 1) for i in range(count - 1)]
        backward = [(target, source) for source, target in forward]
        low = lax.ppermute(
            lax.slice_in_dim(block, block.shape[dim] - width, None, axis=dim), axis, forward
        )
        high = lax.ppermute(lax.slice_in_dim(block, 0, width, axis=dim), axis, backward)
        block = jnp.concatenate([low, block, high], axis=dim)
    return block


def block_factor(diagonal, lower_band, upper_band):
    pivots = []
    upper_scaled = []
    for row_index in range(diagonal.shape[1]):
        if row_index == 0:
            pivot_row = diagonal[:, 0]
        else:
            pivot_row = diagonal[:, row_index] - lower_band[:, row_index] * upper_scaled[-1]
        pivots.append(pivot_row)
        upper_scaled.append(upper_band[:, row_index] / pivot_row)
    return (pivots, upper_scaled)


def block_solve(pivots, upper_scaled, lower_band, right_side):
    row_total = len(pivots)
    modified = []
    for row_index in range(row_total):
        if row_index == 0:
            value_row = right_side[:, :, 0] / pivots[0]
        else:
            value_row = (
                right_side[:, :, row_index] - lower_band[:, row_index] * modified[-1]
            ) / pivots[row_index]
        modified.append(value_row)
    solved = [modified[-1]]
    for row_index in range(row_total - 2, -1, -1):
        solved.append(modified[row_index] - upper_scaled[row_index] * solved[-1])
    ordered = solved[::-1]
    return jnp.stack(ordered, 2)


def interface_solve(coefficients):
    column_total = coefficients.shape[2]

    def forward(carried, inputs):
        offset, carried_slope = carried
        left_first, right_first, left_last, right_last, free_first, free_last = inputs
        divisor = 1.0 - left_first * carried_slope
        first_fixed = (free_first + left_first * offset) / divisor
        first_slope = right_first / divisor
        next_offset = free_last + left_last * (offset + carried_slope * first_fixed)
        next_slope = left_last * carried_slope * first_slope + right_last
        return ((next_offset, next_slope), (first_fixed, first_slope, next_offset, next_slope))

    start_state = (
        jnp.zeros((3, column_total), jnp.float32),
        jnp.zeros((column_total,), jnp.float32),
    )
    scan_inputs = (
        coefficients[:, 0],
        coefficients[:, 1],
        coefficients[:, 2],
        coefficients[:, 3],
        coefficients[:, 4:7],
        coefficients[:, 7:10],
    )
    final_state, eliminated = lax.scan(forward, start_state, scan_inputs)

    def backward(first_next, inputs):
        fixed_first, slope_first, fixed_last, slope_last = inputs
        first_value = fixed_first + slope_first * first_next
        last_value = fixed_last + slope_last * first_next
        return (first_value, (first_value, last_value))

    final_first, values_pair = lax.scan(
        backward, jnp.zeros((3, column_total), jnp.float32), eliminated, reverse=True
    )
    first_values, last_values = values_pair
    nothing_row = jnp.zeros((1, 3, column_total), jnp.float32)
    from_below = jnp.concatenate([nothing_row, last_values[:-1]], 0)
    from_above = jnp.concatenate([first_values[1:], nothing_row], 0)
    return jnp.concatenate([from_below, from_above], 1)


def reduced_boundary(interface):
    gathered = lax.all_gather(interface, "rad", axis=0, tiled=True)
    solved = interface_solve(gathered)
    return lax.dynamic_index_in_dim(solved, lax.axis_index("rad"), 0, keepdims=False)


def many_blocks(stay, received, base_viscosity, velocity, forcing):
    cells_lateral, cells_radial, cells_side = base_viscosity.shape
    moved_rows = MIGRATION_PLANES * cells_radial
    odd = lax.rem(lax.axis_index("lat"), 2) == 1
    from_below = jnp.where(odd, received[0], received[1])[: 3 * moved_rows]
    from_above = jnp.where(odd, received[1], received[0])[: 3 * moved_rows]
    stay = stay.reshape(3, cells_lateral * cells_radial, cells_side)
    totals = stay.at[:, :moved_rows].add(from_below.reshape(3, moved_rows, cells_side))
    totals = totals.at[:, -moved_rows:].add(from_above.reshape(3, moved_rows, cells_side))
    grouped = totals.reshape(3, cells_lateral, cells_radial, cells_side)
    total_weight = grouped[0] + PRIOR_WEIGHT
    basalt_share = grouped[1] / total_weight
    melt_share = grouped[2] / total_weight
    viscosity = base_viscosity * jnp.exp(
        CONTRAST_BASALT * basalt_share - CONTRAST_MELT * melt_share
    )
    viscosity_pad = extended(viscosity, (("lat", 0), ("rad", 1)), 1)
    side_pad = jnp.pad(viscosity, ((0, 0), (0, 0), (1, 1)))
    face_west = LATERAL * 0.5 * (viscosity + viscosity_pad[:-2, 1:-1])
    face_east = LATERAL * 0.5 * (viscosity + viscosity_pad[2:, 1:-1])
    face_south = LATERAL * 0.5 * (viscosity + side_pad[:, :, :-2])
    face_north = LATERAL * 0.5 * (viscosity + side_pad[:, :, 2:])
    face_below = RADIAL * 0.5 * (viscosity + viscosity_pad[1:-1, :-2])
    face_above = RADIAL * 0.5 * (viscosity + viscosity_pad[1:-1, 2:])
    diagonal = face_west + face_east + face_south + face_north + face_below + face_above
    source = jnp.concatenate([forcing[:2], (forcing[2] - BUOYANCY * basalt_share)[None]], 0)
    lower_band = -face_below
    upper_band = -face_above
    pivots, upper_scaled = block_factor(diagonal, lower_band, upper_band)
    radial_iota = lax.broadcasted_iota(jnp.int32, viscosity.shape, 1)
    response_side = jnp.stack(
        [
            jnp.where(radial_iota == 0, face_below, jnp.float32(0.0)),
            jnp.where(radial_iota == cells_radial - 1, face_above, jnp.float32(0.0)),
        ]
    )
    response = block_solve(pivots, upper_scaled, lower_band, response_side)
    current = velocity
    for sweep_index in range(SWEEPS):
        velocity_pad = extended(current, (("lat", 1),), 1)
        side_velocity = jnp.pad(current, ((0, 0), (0, 0), (0, 0), (1, 1)))
        right_side = (
            source
            + face_west * velocity_pad[:, :-2]
            + face_east * velocity_pad[:, 2:]
            + face_south * side_velocity[..., :-2]
            + face_north * side_velocity[..., 2:]
        )
        particular = block_solve(pivots, upper_scaled, lower_band, right_side)
        interface = jnp.concatenate(
            [response[:, :, 0], response[:, :, -1], particular[:, :, 0], particular[:, :, -1]], 0
        )
        interface = interface.reshape(1, 10, cells_lateral * cells_side)
        boundary = reduced_boundary(interface).reshape(6, cells_lateral, 1, cells_side)
        current = particular + response[0][None] * boundary[:3] + response[1][None] * boundary[3:]
    composition = jnp.stack([basalt_share, melt_share])
    return (current, composition)

def local(tracer_values, tracer_cell, tracer_count, base_viscosity, velocity, forcing):
    stay, *sent = tracer_sums(
        tracer_values, tracer_cell, tracer_count, base_viscosity, velocity, forcing
    )
    received = pair_swaps(*sent)
    if lax.axis_size("rad") != 2:
        return many_blocks(stay, received, base_viscosity, velocity, forcing)
    composition, mine, message, parts = eliminate(
        stay, sent, received, base_viscosity, velocity, forcing
    )
    other = lax.ppermute(message, "rad", [(0, 1), (1, 0)])
    return join(mine, other, parts, velocity), composition


def solution(mesh):
    return jax.shard_map(
        local,
        mesh=mesh,
        in_specs=(
            P("lat", "rad", None, None),
            P("lat", "rad", None),
            P("lat", "rad", None),
            P("lat", "rad", None),
            P(None, "lat", "rad", None),
            P(None, "lat", "rad", None),
        ),
        out_specs=(P(None, "lat", "rad", None), P(None, "lat", "rad", None)),
        check_vma=False,
    )
```

```python
import functools

import jax
import jax.numpy as jnp
from jax import lax
from jax.experimental import pallas as pl
from jax.experimental.pallas import tpu as pltpu
from jax.sharding import PartitionSpec as P

SWEEPS = 2
MIGRATION_PLANES = 2

LATERAL = 0.015625
RADIAL = 32.0
BUOYANCY = 0.1
PRIOR_WEIGHT = 0.5
CONTRAST_BASALT = 2.3
CONTRAST_MELT = 1.5

TILE_ROWS = 16


def round_up(value, multiple):
    return -(-value // multiple) * multiple


def split_index(index, count):
    if count & (count - 1) == 0:
        return lax.shift_right_logical(index, count.bit_length() - 1), index & (count - 1)
    quotient = lax.div(index, count)
    return quotient, index - quotient * count


def payload_sections(cells_radial):
    pair = MIGRATION_PLANES * cells_radial
    starts = [0, 3 * pair, 6 * pair, 9 * pair, 10 * pair]
    return starts, round_up(10 * pair + 3 * cells_radial, 8)


def spread_row(row):
    return jnp.broadcast_to(row, (TILE_ROWS, row.shape[1])).astype(jnp.bfloat16)


def hot_tiles(index, row_total):
    iota = lax.broadcasted_iota(jnp.int32, index.shape, 0)
    return [
        index == (iota + first).astype(jnp.float32).astype(jnp.bfloat16)
        for first in range(0, row_total, TILE_ROWS)
    ]


def hot_product(loads, high, low, high_rows, low_rows):
    left, right = [], []
    high, low = high.astype(jnp.float32), low.astype(jnp.float32)
    zero = jnp.zeros((TILE_ROWS, high.shape[1]), jnp.bfloat16)
    one = jnp.ones((TILE_ROWS, high.shape[1]), jnp.bfloat16)
    for row in range(high.shape[0]):
        pick = slice(row, row + 1)
        high_masks = hot_tiles(spread_row(high[pick]), high_rows)
        low_masks = hot_tiles(spread_row(low[pick]), low_rows)
        spread = [spread_row(load[pick]) for load in loads]
        left.append(
            jnp.concatenate(
                [jnp.where(mask, load, zero) for load in spread for mask in high_masks], 0
            )
        )
        right.append(jnp.concatenate([jnp.where(mask, one, zero) for mask in low_masks], 0))
    return lax.dot_general(
        jnp.concatenate(left, 1),
        jnp.concatenate(right, 1),
        (((1,), (1,)), ((), ())),
        preferred_element_type=jnp.float32,
    )


def edge_row(plane, plane_total, moved_total):
    inner = (plane >= moved_total) & (plane < plane_total - moved_total)
    last = plane - (plane_total - 2 * moved_total)
    return jnp.where(inner, 2 * moved_total, jnp.where(plane < moved_total, plane, last))


def fold_moved(plane, side, plane_total, side_total):
    width, third = side_total // 4, plane_total // 3
    part = jnp.where(plane >= third, 1, 0) + jnp.where(plane >= 2 * third, 1, 0)
    other = side >= 3 * width
    high = jnp.where(other, plane_total + plane - part * third, plane)
    low = jnp.where(other, side - 3 * width + part * width, side)
    return high, low, plane_total + third, 3 * width


def unfold_moved(table, q, plane_total, side_total, put):
    width, third = side_total // 4, plane_total // 3
    rows = plane_total + third
    put(0, 0, table[pl.ds(q * rows, plane_total), 0 : 3 * width])
    for part in range(3):
        block = table[
            pl.ds(q * rows + plane_total, third), part * width : (part + 1) * width
        ]
        put(part * third, 3 * width, block)


def tracer_block(counts, values, cells, group, place, first_row, block_rows, cells_side):
    rows = pl.ds(first_row, block_rows)
    lane_total = cells.shape[2]
    shape = (block_rows, lane_total)
    slot = (first_row + lax.broadcasted_iota(jnp.int32, shape, 0)) * lane_total
    slot = slot + lax.broadcasted_iota(jnp.int32, shape, 1)
    weight = jnp.where(
        slot < counts[0, 0, group], 0.5 + values[0, place, rows, :], jnp.float32(0.0)
    )
    loads = [weight, weight * values[1, place, rows, :], weight * values[2, place, rows, :]]
    plane, side = split_index(cells[place, rows, :], cells_side)
    return loads, plane, side


def for_used_blocks(used, group_rows, block_rows, lane_total, late_copies, step):
    block_slots = block_rows * lane_total
    blocks = lax.div(used + (block_slots - 1), block_slots)
    blocks = jnp.clip(blocks, 1, group_rows // block_rows)

    def wait_late():
        for copy in late_copies:
            copy.wait()

    def repeat(index, carried):
        pl.when(index == 1)(wait_late)
        step(pl.multiple_of(index * block_rows, block_rows))
        return carried

    lax.fori_loop(0, blocks, repeat, 0)
    pl.when(blocks == 1)(wait_late)


class Fetches:
    def __init__(self, semaphores):
        self.semaphores = semaphores
        self.copies = []

    def start(self, source, target):
        copy = pltpu.make_async_copy(source, target, self.semaphores.at[len(self.copies)])
        copy.start()
        self.copies.append(copy)

    def wait(self, first, last):
        for copy in self.copies[first:last]:
            copy.wait()


def has_partners():
    lateral, count = lax.axis_index("lat"), lax.axis_size("lat")
    odd = lax.rem(lateral, 2) == 1
    above, below = lateral + 1 < count, lateral > 0
    return jnp.logical_or(odd, above), jnp.where(odd, above, below)


def outgoing_kernel(
    block_rows,
    counts_hbm,
    values_hbm,
    cells_hbm,
    base_hbm,
    velocity_hbm,
    forcing_hbm,
    edge_ref,
    first_ref,
    second_ref,
    counts,
    values,
    cells,
    base,
    velocity,
    forcing,
    edge_sums,
    moved_sums,
    payload,
    semaphores,
):
    cells_lateral, cells_radial, cells_side = base_hbm.shape
    plane_total = cells_lateral * cells_radial
    moved_planes = MIGRATION_PLANES * cells_radial
    group_rows, lane_total = values.shape[2:]

    fetches = Fetches(semaphores)
    fetches.start(counts_hbm, counts)
    for first_row, rows in ((0, block_rows), (block_rows, group_rows - block_rows)):
        part = pl.ds(first_row, rows)
        fetches.start(cells_hbm.at[:, part], cells.at[:, part])
        fetches.start(values_hbm.at[:, :, part], values.at[:, :, part])
    for upward in (0, 1):
        outer = pl.ds((cells_lateral - MIGRATION_PLANES) * upward, MIGRATION_PLANES)
        fetches.start(base_hbm.at[outer], base.at[upward])
        fetches.start(velocity_hbm.at[:, outer], velocity.at[upward])
        outermost = pl.ds((cells_lateral - 1) * upward, 1)
        fetches.start(forcing_hbm.at[:, outermost], forcing.at[upward])

    edge_sums[...] = jnp.zeros_like(edge_sums)
    moved_sums[...] = jnp.zeros_like(moved_sums)

    def step(first_row):
        loads, plane, side = tracer_block(
            counts, values, cells, 1, 1, first_row, block_rows, cells_side
        )
        row = edge_row(plane, plane_total, moved_planes)
        edge_sums[...] += hot_product(loads, row, side, 2 * moved_planes, cells_side)
        for slot, group in enumerate((0, 2)):
            loads, plane, side = tracer_block(
                counts, values, cells, group, group, first_row, block_rows, cells_side
            )
            if group == 0:
                plane = plane - (plane_total - moved_planes)
            moved_sums[slot] += hot_product(
                loads, *fold_moved(plane, side, moved_planes, cells_side)
            )

    fetches.wait(0, 3)
    used = jnp.maximum(jnp.maximum(counts[0, 0, 0], counts[0, 0, 1]), counts[0, 0, 2])
    for_used_blocks(used, group_rows, block_rows, lane_total, fetches.copies[3:5], step)
    fetches.wait(5, None)

    edge_ref[...] = edge_sums[...]
    starts, _ = payload_sections(cells_radial)
    odd = lax.rem(lax.axis_index("lat"), 2)
    for upward in (0, 1):
        place = odd if upward else 1 - odd
        for q in range(3):

            def put_moved(plane, column, block):
                height, width = block.shape
                rows = pl.ds(starts[0] + q * moved_planes + plane, height)
                payload[place, rows, column : column + width] = block

            unfold_moved(moved_sums.at[upward], q, moved_planes, cells_side, put_moved)
            payload[place, pl.ds(starts[1] + q * moved_planes, moved_planes), :] = edge_sums[
                pl.ds((2 * q + upward) * moved_planes, moved_planes), :
            ]
            for offset in range(MIGRATION_PLANES):
                payload[
                    place,
                    pl.ds(starts[2] + q * moved_planes + offset * cells_radial, cells_radial),
                    :,
                ] = velocity[upward, q, offset]
            payload[place, pl.ds(starts[4] + q * cells_radial, cells_radial), :] = forcing[
                upward, q, 0
            ]
        for offset in range(MIGRATION_PLANES):
            payload[place, pl.ds(starts[3] + offset * cells_radial, cells_radial), :] = base[
                upward, offset
            ]
    has_first, has_second = has_partners()
    first_ref[...] = jnp.where(has_first, payload[0], 0.0)
    second_ref[...] = jnp.where(has_second, payload[1], 0.0)


def inner_kernel(
    block_rows,
    moved_planes,
    counts_hbm,
    values_hbm,
    cells_hbm,
    inner_ref,
    counts,
    values,
    cells,
    semaphores,
):
    cells_side = inner_ref.shape[1]
    inner_planes = inner_ref.shape[0] // 3
    group_rows, lane_total = values.shape[2:]
    fetches = Fetches(semaphores)
    fetches.start(counts_hbm, counts)
    for first_row, rows in ((0, block_rows), (block_rows, group_rows - block_rows)):
        part = pl.ds(first_row, rows)
        fetches.start(cells_hbm.at[1:2, part], cells.at[:, part])
        fetches.start(values_hbm.at[:, 1:2, part], values.at[:, :, part])
    inner_ref[...] = jnp.zeros_like(inner_ref)

    def step(first_row):
        loads, plane, side = tracer_block(
            counts, values, cells, 1, 0, first_row, block_rows, cells_side
        )
        inner_ref[...] += hot_product(loads, plane - moved_planes, side, inner_planes, cells_side)

    fetches.wait(0, 3)
    for_used_blocks(
        counts[0, 0, 1], group_rows, block_rows, lane_total, fetches.copies[3:5], step
    )


BLOCK_ROWS = 32


def dense_tracers(tracer_values, tracer_cell):
    lane_total = 128
    return tracer_values.reshape(3, 3, -1, lane_total), tracer_cell.reshape(3, -1, lane_total)


def outgoing_sums(tracer_count, values, cells, base_viscosity, velocity, forcing):
    cells_lateral, cells_radial, cells_side = base_viscosity.shape
    moved_planes = MIGRATION_PLANES * cells_radial
    group_rows, lane_total = cells.shape[1:]
    block_rows = min(BLOCK_ROWS, group_rows // 2)
    _, payload_rows = payload_sections(cells_radial)
    hbm = pl.BlockSpec(memory_space=pltpu.HBM)
    vmem = pl.BlockSpec(memory_space=pltpu.VMEM)
    payload = jax.ShapeDtypeStruct((payload_rows, cells_side), jnp.float32)
    edge = (6 * moved_planes, cells_side)
    outer_planes = (MIGRATION_PLANES, cells_radial, cells_side)
    return pl.pallas_call(
        functools.partial(outgoing_kernel, block_rows),
        out_shape=(jax.ShapeDtypeStruct(edge, jnp.float32), payload, payload),
        in_specs=[hbm] * 6,
        out_specs=(vmem, vmem, vmem),
        scratch_shapes=[
            pltpu.SMEM(tracer_count.shape, jnp.int32),
            pltpu.VMEM(values.shape, jnp.float32),
            pltpu.VMEM(cells.shape, jnp.int32),
            pltpu.VMEM((2,) + outer_planes, jnp.float32),
            pltpu.VMEM((2, 3) + outer_planes, jnp.float32),
            pltpu.VMEM((2, 3, 1, cells_radial, cells_side), jnp.float32),
            pltpu.VMEM(edge, jnp.float32),
            pltpu.VMEM((2, 4 * moved_planes, cells_side * 3 // 4), jnp.float32),
            pltpu.VMEM((2, payload_rows, cells_side), jnp.float32),
            pltpu.SemaphoreType.DMA((11,)),
        ],
        compiler_params=pltpu.CompilerParams(vmem_limit_bytes=32 * 2**20),
        cost_estimate=pl.CostEstimate(
            flops=30 * group_rows * lane_total * moved_planes * cells_side,
            bytes_accessed=4 * (values.size + cells.size),
            transcendentals=0,
        ),
        name="outgoing_sums",
    )(
        *(
            pltpu.with_memory_space_constraint(array, pltpu.HBM)
            for array in (tracer_count, values, cells, base_viscosity, velocity, forcing)
        )
    )


def inner_sums(tracer_count, values, cells, base_viscosity):
    cells_lateral, cells_radial, cells_side = base_viscosity.shape
    moved_planes = MIGRATION_PLANES * cells_radial
    inner_planes = cells_lateral * cells_radial - 2 * moved_planes
    group_rows, lane_total = cells.shape[1:]
    block_rows = min(BLOCK_ROWS, group_rows // 2)
    return pl.pallas_call(
        functools.partial(inner_kernel, block_rows, moved_planes),
        out_shape=jax.ShapeDtypeStruct((3 * inner_planes, cells_side), jnp.float32),
        in_specs=[pl.BlockSpec(memory_space=pltpu.HBM)] * 3,
        out_specs=pl.BlockSpec(memory_space=pltpu.VMEM),
        scratch_shapes=[
            pltpu.SMEM(tracer_count.shape, jnp.int32),
            pltpu.VMEM((3, 1, group_rows, lane_total), jnp.float32),
            pltpu.VMEM((1, group_rows, lane_total), jnp.int32),
            pltpu.SemaphoreType.DMA((5,)),
        ],
        compiler_params=pltpu.CompilerParams(vmem_limit_bytes=32 * 2**20),
        cost_estimate=pl.CostEstimate(
            flops=6 * group_rows * lane_total * inner_planes * cells_side,
            bytes_accessed=4 * (values.size + cells.size) // 3,
            transcendentals=0,
        ),
        name="inner_sums",
    )(
        *(
            pltpu.with_memory_space_constraint(array, pltpu.HBM)
            for array in (tracer_count, values, cells)
        )
    )


def pair_swaps(first, second):
    count = lax.axis_size("lat")
    received = []
    for payload, start in ((second, 1), (first, 0)):
        target = list(range(count))
        for low in range(start, count - 1, 2):
            target[low], target[low + 1] = low + 1, low
        received.append(lax.ppermute(payload, "lat", list(enumerate(target))))
    return received[::-1]


def shift_planes(block, step):
    return pltpu.roll(block, step % block.shape[0], 0)


def shift_side(block, step):
    return pltpu.roll(block, step % block.shape[1], 1)


def neighbours(block):
    return (
        shift_planes(block, 1),
        shift_planes(block, -1),
        shift_side(block, 1),
        shift_side(block, -1),
    )


def inside_side(values):
    lane = lax.broadcasted_iota(jnp.int32, values[2].shape, 1)
    lower = jnp.where(lane > 0, values[2], 0.0)
    upper = jnp.where(lane < lane.shape[1] - 1, values[3], 0.0)
    return values[0], values[1], lower, upper


def total_of(terms):
    result = terms[0]
    for term in terms[1:]:
        result = result + term
    return result


def inside_grid(shape, margin, cells_lateral):
    plane = lax.broadcasted_iota(jnp.int32, shape, 0)
    lateral = lax.axis_index("lat")
    first = jnp.where(lateral == 0, margin, 1)
    last = jnp.where(lateral == lax.axis_size("lat") - 1, margin + cells_lateral, shape[0] - 1)
    return (plane >= first) & (plane < last)


VISCOSITY, VELOCITY, SOURCE, BLOCK_FIELDS = 3, 4, 7, 10
LONG_FIELDS, SHORT_FIELDS = 5, 7


def message_rows(cells_lateral):
    planes = cells_lateral + 2 * MIGRATION_PLANES
    return round_up(LONG_FIELDS * planes + SHORT_FIELDS * cells_lateral, 8)


def message_part(cells_lateral, field):
    planes = cells_lateral + 2 * MIGRATION_PLANES
    if field < LONG_FIELDS:
        return pl.ds(field * planes, planes), 0, planes
    first = LONG_FIELDS * planes + (field - LONG_FIELDS) * cells_lateral
    return pl.ds(first, cells_lateral), MIGRATION_PLANES, cells_lateral


def block_place(fields, cells_radial):
    pitch = round_up(cells_radial, 8)

    def put(field, plane, value):
        fields[field, pl.ds(plane * pitch, cells_radial), :] = value

    return put


def put_own(put, inner_ref, base_ref, velocity_ref, forcing_ref):
    cells_lateral, cells_radial, _ = base_ref.shape
    inner = range(MIGRATION_PLANES, cells_lateral - MIGRATION_PLANES)
    for x in range(cells_lateral):
        plane = MIGRATION_PLANES + x
        put(VISCOSITY, plane, base_ref[x])
        for q in range(3):
            if x in inner:
                row = (q * len(inner) + x - MIGRATION_PLANES) * cells_radial
                put(q, plane, inner_ref[pl.ds(row, cells_radial), :])
            put(VELOCITY + q, plane, velocity_ref[q, x])
            put(SOURCE + q, plane, forcing_ref[q, x])


def composition_of(fields, cells_radial, plane):
    rows = pl.ds(plane * round_up(cells_radial, 8), cells_radial)
    total_weight = fields[0, rows, :] + PRIOR_WEIGHT
    basalt_share = fields[1, rows, :] / total_weight
    melt_share = fields[2, rows, :] / total_weight
    fields[VISCOSITY, rows, :] = fields[VISCOSITY, rows, :] * jnp.exp(
        CONTRAST_BASALT * basalt_share - CONTRAST_MELT * melt_share
    )
    fields[SOURCE + 2, rows, :] = fields[SOURCE + 2, rows, :] - BUOYANCY * basalt_share
    return basalt_share, melt_share


def solve_lines(fields, planes, cells_radial, valid, keep, keep_part):
    pitch = round_up(cells_radial, 8)
    lower_block = lax.axis_index("rad") == 0

    def radial(field, t):
        row = jnp.where(lower_block, t, cells_radial - 1 - t)
        return fields[field, pl.ds(row, planes, stride=pitch), :]

    last = cells_radial - 1
    viscosity = [radial(VISCOSITY, t) for t in range(cells_radial)]
    lateral_faces, lateral_sums = [], []
    for here in viscosity:
        faces = [LATERAL * 0.5 * (here + there) for there in inside_side(neighbours(here))]
        lateral_sums.append(total_of(faces))
        lateral_faces.append(inside_side(faces))
    radial_faces = [RADIAL * 0.5 * viscosity[0]] + [
        RADIAL * 0.5 * (viscosity[t - 1] + viscosity[t]) for t in range(1, cells_radial)
    ]

    excess = lateral_sums[0] + radial_faces[0]
    inverse, coupling = [], []
    for t in range(last):
        inverse.append(1.0 / (excess + radial_faces[t + 1]))
        coupling.append(radial_faces[t + 1] * inverse[t])
        excess = lateral_sums[t + 1] + coupling[t] * excess

    def lateral_terms(t, around):
        return [face * there for face, there in zip(lateral_faces[t], around)]

    def forward(right_side):
        eliminated = [right_side[0]]
        for t in range(1, cells_radial):
            eliminated.append(right_side[t] + coupling[t - 1] * eliminated[t - 1])
        return eliminated

    def backward(eliminated):
        solved = [jnp.zeros_like(excess)]
        for t in range(last - 1, -1, -1):
            solved.append(eliminated[t] * inverse[t] + coupling[t] * solved[-1])
        return solved[::-1]

    response = [jnp.ones_like(excess)]
    for t in range(last - 1, -1, -1):
        response.append(coupling[t] * response[-1])
    response = response[::-1]

    def finish(part, eliminated):
        keep(LONG_FIELDS + part, eliminated[last])
        if keep_part is not None:
            for t, value in enumerate(eliminated[:last]):
                keep_part(part, t, value)

    keep(0, viscosity[last])
    keep(1, excess)
    for q in range(3):
        source = [radial(SOURCE + q, t) for t in range(cells_radial)]
        eliminated = forward(
            [
                total_of([source[t]] + lateral_terms(t, neighbours(radial(VELOCITY + q, t))))
                for t in range(cells_radial)
            ]
        )
        keep(2 + q, eliminated[last])
        particular = [jnp.where(valid, value, 0.0) for value in backward(eliminated)]
        finish(
            q,
            forward(
                [
                    total_of([source[t]] + lateral_terms(t, neighbours(particular[t])))
                    for t in range(cells_radial)
                ]
            ),
        )
    around = [neighbours(jnp.where(valid, value, 0.0)) for value in response]
    for side in range(4):
        finish(
            3 + side,
            forward([lateral_faces[t][side] * around[t][side] for t in range(cells_radial)]),
        )
    if keep_part is not None:
        for t in range(last):
            keep_part(SHORT_FIELDS, t, inverse[t])
            keep_part(SHORT_FIELDS + 1, t, coupling[t])


def eliminate_kernel(
    inner_ref,
    edge_ref,
    second_ref,
    first_ref,
    from_second_ref,
    from_first_ref,
    base_ref,
    velocity_ref,
    forcing_ref,
    composition_ref,
    mine_ref,
    message_ref,
    parts_ref,
    fields,
):
    cells_lateral, cells_radial, cells_side = base_ref.shape
    margin = MIGRATION_PLANES
    planes = cells_lateral + 2 * margin
    moved_planes = margin * cells_radial
    starts, _ = payload_sections(cells_radial)
    odd = lax.rem(lax.axis_index("lat"), 2) == 1
    put = block_place(fields, cells_radial)

    def sent(upward, start):
        part = pl.ds(start, cells_radial)
        mine_first = odd if not upward else jnp.logical_not(odd)
        return jnp.where(mine_first, first_ref[part, :], second_ref[part, :])

    def arrived(from_above, start):
        part = pl.ds(start, cells_radial)
        is_first = odd if not from_above else jnp.logical_not(odd)
        return jnp.where(is_first, from_first_ref[part, :], from_second_ref[part, :])

    put_own(put, inner_ref, base_ref, velocity_ref, forcing_ref)
    for above in (False, True):
        outer = margin + cells_lateral if above else margin - 1
        beyond = planes - 1 if above else 0
        for offset in range(margin):
            x = offset + (cells_lateral - margin if above else 0)
            plane = offset + (margin + cells_lateral if above else 0)
            shift = offset * cells_radial
            put(VISCOSITY, plane, arrived(above, starts[3] + shift))
            for q in range(3):
                row = q * moved_planes + shift
                rows = pl.ds((2 * q + int(above)) * moved_planes + shift, cells_radial)
                put(q, margin + x, edge_ref[rows, :] + arrived(above, starts[0] + row))
                put(q, plane, sent(above, starts[0] + row) + arrived(above, starts[1] + row))
                put(VELOCITY + q, plane, arrived(above, starts[2] + row))
        for q in range(3):
            put(SOURCE + q, outer, arrived(above, starts[4] + q * cells_radial))
            put(SOURCE + q, beyond, jnp.zeros((cells_radial, cells_side), jnp.float32))
    for plane in range(planes):
        basalt_share, melt_share = composition_of(fields, cells_radial, plane)
        if margin <= plane < margin + cells_lateral:
            composition_ref[0, plane - margin] = basalt_share
            composition_ref[1, plane - margin] = melt_share

    unused = LONG_FIELDS * planes + SHORT_FIELDS * cells_lateral
    if unused < message_ref.shape[0]:
        message_ref[unused:, :] = jnp.zeros((message_ref.shape[0] - unused, cells_side), jnp.float32)

    def keep(field, value):
        rows, first, count = message_part(cells_lateral, field)
        mine_ref[field] = value
        message_ref[rows, :] = value[first : first + count]

    def keep_part(part, t, value):
        parts_ref[part, t] = value

    valid = inside_grid((planes, cells_side), margin, cells_lateral)
    solve_lines(fields, planes, cells_radial, valid, keep, keep_part)


def eliminate(inner, edge, sent, received, base_viscosity, velocity, forcing):
    cells_lateral, cells_radial, cells_side = base_viscosity.shape
    planes = cells_lateral + 2 * MIGRATION_PLANES
    vmem = pl.BlockSpec(memory_space=pltpu.VMEM)
    lines = (planes, cells_side)
    return pl.pallas_call(
        eliminate_kernel,
        out_shape=(
            jax.ShapeDtypeStruct((2,) + base_viscosity.shape, jnp.float32),
            jax.ShapeDtypeStruct((LONG_FIELDS + SHORT_FIELDS,) + lines, jnp.float32),
            jax.ShapeDtypeStruct((message_rows(cells_lateral), cells_side), jnp.float32),
            jax.ShapeDtypeStruct((SHORT_FIELDS + 2, cells_radial - 1) + lines, jnp.float32),
        ),
        in_specs=[vmem] * 9,
        out_specs=(vmem,) * 4,
        scratch_shapes=[
            pltpu.VMEM((BLOCK_FIELDS, planes * round_up(cells_radial, 8), cells_side), jnp.float32)
        ],
        compiler_params=pltpu.CompilerParams(vmem_limit_bytes=32 * 2**20),
        name="eliminate",
    )(inner, edge, *sent[::-1], *received[::-1], base_viscosity, velocity, forcing)


def join_kernel(mine_ref, message_ref, parts_ref, smoothed_ref, lines, other_ref):
    _, cells_lateral, cells_radial, cells_side = smoothed_ref.shape
    margin = MIGRATION_PLANES
    planes = cells_lateral + 2 * margin
    pitch = round_up(cells_radial, 8)
    valid = inside_grid((planes, cells_side), margin, cells_lateral)
    lower_block = lax.axis_index("rad") == 0

    other_ref[LONG_FIELDS:] = jnp.zeros_like(other_ref[LONG_FIELDS:])
    for field in range(LONG_FIELDS + SHORT_FIELDS):
        rows, first, count = message_part(cells_lateral, field)
        other_ref[field, pl.ds(first, count), :] = message_ref[rows, :]

    face = RADIAL * 0.5 * (mine_ref[0] + other_ref[0])
    excess, other_excess = mine_ref[1], other_ref[1]
    scale = 1.0 / (excess * other_excess + face * (excess + other_excess))
    own_weight = (other_excess + face) * scale
    other_weight = (excess + face) * scale
    cross = face * scale

    def second_right(ref, q, around):
        terms = [ref[LONG_FIELDS + 3 + side] * there for side, there in enumerate(around)]
        return total_of([ref[LONG_FIELDS + q]] + terms)

    for q in range(3):
        right, other_right = mine_ref[2 + q], other_ref[2 + q]
        own = jnp.where(valid, own_weight * right + cross * other_right, 0.0)
        other = jnp.where(valid, other_weight * other_right + cross * right, 0.0)
        around = neighbours(own)
        right = second_right(mine_ref, q, around)
        other_right = second_right(other_ref, q, neighbours(other))
        value = own_weight * right + cross * other_right
        for t in range(cells_radial - 1, -1, -1):
            if t < cells_radial - 1:
                terms = [parts_ref[3 + side, t] * there for side, there in enumerate(around)]
                right = total_of([parts_ref[q, t]] + terms)
                value = right * parts_ref[SHORT_FIELDS, t] + parts_ref[SHORT_FIELDS + 1, t] * value
            row = jnp.where(lower_block, t, cells_radial - 1 - t)
            lines[pl.ds(row, cells_lateral, stride=pitch), :] = value[
                margin : margin + cells_lateral
            ]
        for x in range(cells_lateral):
            smoothed_ref[q, x] = lines[pl.ds(x * pitch, cells_radial), :]


def join(mine, message, parts, like):
    cells_lateral, cells_radial, cells_side = like.shape[1:]
    vmem = pl.BlockSpec(memory_space=pltpu.VMEM)
    return pl.pallas_call(
        join_kernel,
        out_shape=jax.ShapeDtypeStruct(like.shape, jnp.float32),
        in_specs=[vmem] * 3,
        out_specs=vmem,
        scratch_shapes=[
            pltpu.VMEM((cells_lateral * round_up(cells_radial, 8), cells_side), jnp.float32),
            pltpu.VMEM(mine.shape, jnp.float32),
        ],
        compiler_params=pltpu.CompilerParams(vmem_limit_bytes=32 * 2**20),
        name="join",
    )(mine, message, parts)


def extended(block, sides, width):
    for axis, dim in sides:
        count = lax.axis_size(axis)
        forward = [(i, i + 1) for i in range(count - 1)]
        backward = [(target, source) for source, target in forward]
        low = lax.ppermute(
            lax.slice_in_dim(block, block.shape[dim] - width, None, axis=dim), axis, forward
        )
        high = lax.ppermute(lax.slice_in_dim(block, 0, width, axis=dim), axis, backward)
        block = jnp.concatenate([low, block, high], axis=dim)
    return block


def block_factor(diagonal, lower_band, upper_band):
    pivots = []
    upper_scaled = []
    for row_index in range(diagonal.shape[1]):
        if row_index == 0:
            pivot_row = diagonal[:, 0]
        else:
            pivot_row = diagonal[:, row_index] - lower_band[:, row_index] * upper_scaled[-1]
        pivots.append(pivot_row)
        upper_scaled.append(upper_band[:, row_index] / pivot_row)
    return (pivots, upper_scaled)


def block_solve(pivots, upper_scaled, lower_band, right_side):
    row_total = len(pivots)
    modified = []
    for row_index in range(row_total):
        if row_index == 0:
            value_row = right_side[:, :, 0] / pivots[0]
        else:
            value_row = (
                right_side[:, :, row_index] - lower_band[:, row_index] * modified[-1]
            ) / pivots[row_index]
        modified.append(value_row)
    solved = [modified[-1]]
    for row_index in range(row_total - 2, -1, -1):
        solved.append(modified[row_index] - upper_scaled[row_index] * solved[-1])
    ordered = solved[::-1]
    return jnp.stack(ordered, 2)


def interface_solve(coefficients):
    column_total = coefficients.shape[2]

    def forward(carried, inputs):
        offset, carried_slope = carried
        left_first, right_first, left_last, right_last, free_first, free_last = inputs
        divisor = 1.0 - left_first * carried_slope
        first_fixed = (free_first + left_first * offset) / divisor
        first_slope = right_first / divisor
        next_offset = free_last + left_last * (offset + carried_slope * first_fixed)
        next_slope = left_last * carried_slope * first_slope + right_last
        return ((next_offset, next_slope), (first_fixed, first_slope, next_offset, next_slope))

    start_state = (
        jnp.zeros((3, column_total), jnp.float32),
        jnp.zeros((column_total,), jnp.float32),
    )
    scan_inputs = (
        coefficients[:, 0],
        coefficients[:, 1],
        coefficients[:, 2],
        coefficients[:, 3],
        coefficients[:, 4:7],
        coefficients[:, 7:10],
    )
    final_state, eliminated = lax.scan(forward, start_state, scan_inputs)

    def backward(first_next, inputs):
        fixed_first, slope_first, fixed_last, slope_last = inputs
        first_value = fixed_first + slope_first * first_next
        last_value = fixed_last + slope_last * first_next
        return (first_value, (first_value, last_value))

    final_first, values_pair = lax.scan(
        backward, jnp.zeros((3, column_total), jnp.float32), eliminated, reverse=True
    )
    first_values, last_values = values_pair
    nothing_row = jnp.zeros((1, 3, column_total), jnp.float32)
    from_below = jnp.concatenate([nothing_row, last_values[:-1]], 0)
    from_above = jnp.concatenate([first_values[1:], nothing_row], 0)
    return jnp.concatenate([from_below, from_above], 1)


def reduced_boundary(interface):
    gathered = lax.all_gather(interface, "rad", axis=0, tiled=True)
    solved = interface_solve(gathered)
    return lax.dynamic_index_in_dim(solved, lax.axis_index("rad"), 0, keepdims=False)


def many_blocks(inner, edge, received, base_viscosity, velocity, forcing):
    cells_lateral, cells_radial, cells_side = base_viscosity.shape
    moved_rows = MIGRATION_PLANES * cells_radial
    odd = lax.rem(lax.axis_index("lat"), 2) == 1
    from_below = jnp.where(odd, received[0], received[1])[: 3 * moved_rows]
    from_above = jnp.where(odd, received[1], received[0])[: 3 * moved_rows]
    edge = edge.reshape(3, 2, moved_rows, cells_side)
    totals = jnp.concatenate(
        [
            edge[:, 0] + from_below.reshape(3, moved_rows, cells_side),
            inner.reshape(3, -1, cells_side),
            edge[:, 1] + from_above.reshape(3, moved_rows, cells_side),
        ],
        1,
    )
    grouped = totals.reshape(3, cells_lateral, cells_radial, cells_side)
    total_weight = grouped[0] + PRIOR_WEIGHT
    basalt_share = grouped[1] / total_weight
    melt_share = grouped[2] / total_weight
    viscosity = base_viscosity * jnp.exp(
        CONTRAST_BASALT * basalt_share - CONTRAST_MELT * melt_share
    )
    viscosity_pad = extended(viscosity, (("lat", 0), ("rad", 1)), 1)
    side_pad = jnp.pad(viscosity, ((0, 0), (0, 0), (1, 1)))
    face_west = LATERAL * 0.5 * (viscosity + viscosity_pad[:-2, 1:-1])
    face_east = LATERAL * 0.5 * (viscosity + viscosity_pad[2:, 1:-1])
    face_south = LATERAL * 0.5 * (viscosity + side_pad[:, :, :-2])
    face_north = LATERAL * 0.5 * (viscosity + side_pad[:, :, 2:])
    face_below = RADIAL * 0.5 * (viscosity + viscosity_pad[1:-1, :-2])
    face_above = RADIAL * 0.5 * (viscosity + viscosity_pad[1:-1, 2:])
    diagonal = face_west + face_east + face_south + face_north + face_below + face_above
    source = jnp.concatenate([forcing[:2], (forcing[2] - BUOYANCY * basalt_share)[None]], 0)
    lower_band = -face_below
    upper_band = -face_above
    pivots, upper_scaled = block_factor(diagonal, lower_band, upper_band)
    radial_iota = lax.broadcasted_iota(jnp.int32, viscosity.shape, 1)
    response_side = jnp.stack(
        [
            jnp.where(radial_iota == 0, face_below, jnp.float32(0.0)),
            jnp.where(radial_iota == cells_radial - 1, face_above, jnp.float32(0.0)),
        ]
    )
    response = block_solve(pivots, upper_scaled, lower_band, response_side)
    current = velocity
    for sweep_index in range(SWEEPS):
        velocity_pad = extended(current, (("lat", 1),), 1)
        side_velocity = jnp.pad(current, ((0, 0), (0, 0), (0, 0), (1, 1)))
        right_side = (
            source
            + face_west * velocity_pad[:, :-2]
            + face_east * velocity_pad[:, 2:]
            + face_south * side_velocity[..., :-2]
            + face_north * side_velocity[..., 2:]
        )
        particular = block_solve(pivots, upper_scaled, lower_band, right_side)
        interface = jnp.concatenate(
            [response[:, :, 0], response[:, :, -1], particular[:, :, 0], particular[:, :, -1]], 0
        )
        interface = interface.reshape(1, 10, cells_lateral * cells_side)
        boundary = reduced_boundary(interface).reshape(6, cells_lateral, 1, cells_side)
        current = particular + response[0][None] * boundary[:3] + response[1][None] * boundary[3:]
    composition = jnp.stack([basalt_share, melt_share])
    return (current, composition)

def local(tracer_values, tracer_cell, tracer_count, base_viscosity, velocity, forcing):
    values, cells = dense_tracers(tracer_values, tracer_cell)
    edge, *sent = outgoing_sums(
        tracer_count, values, cells, base_viscosity, velocity, forcing
    )
    received = pair_swaps(*sent)
    inner = inner_sums(tracer_count, values, cells, base_viscosity)
    if lax.axis_size("rad") != 2:
        return many_blocks(inner, edge, received, base_viscosity, velocity, forcing)
    composition, mine, message, parts = eliminate(
        inner, edge, sent, received, base_viscosity, velocity, forcing
    )
    other = lax.ppermute(message, "rad", [(0, 1), (1, 0)])
    return join(mine, other, parts, velocity), composition


def solution(mesh):
    return jax.shard_map(
        local,
        mesh=mesh,
        in_specs=(
            P("lat", "rad", None, None),
            P("lat", "rad", None),
            P("lat", "rad", None),
            P("lat", "rad", None),
            P(None, "lat", "rad", None),
            P(None, "lat", "rad", None),
        ),
        out_specs=(P(None, "lat", "rad", None), P(None, "lat", "rad", None)),
        check_vma=False,
    )
```

```python
import functools

import jax
import jax.numpy as jnp
from jax import lax
from jax.experimental import pallas as pl
from jax.experimental.pallas import tpu as pltpu
from jax.sharding import PartitionSpec as P

SWEEPS = 2
MIGRATION_PLANES = 2

LATERAL = 0.015625
RADIAL = 32.0
BUOYANCY = 0.1
PRIOR_WEIGHT = 0.5
CONTRAST_BASALT = 2.3
CONTRAST_MELT = 1.5

TILE_ROWS = 16


def round_up(value, multiple):
    return -(-value // multiple) * multiple


def split_index(index, count):
    if count & (count - 1) == 0:
        return lax.shift_right_logical(index, count.bit_length() - 1), index & (count - 1)
    quotient = lax.div(index, count)
    return quotient, index - quotient * count


def payload_sections(cells_radial):
    pair = MIGRATION_PLANES * cells_radial
    starts = [0, 3 * pair, 6 * pair, 9 * pair, 10 * pair]
    return starts, round_up(10 * pair + 3 * cells_radial, 8)


def spread_row(row):
    return jnp.broadcast_to(row, (TILE_ROWS, row.shape[1])).astype(jnp.bfloat16)


def hot_tiles(index, row_total):
    iota = lax.broadcasted_iota(jnp.int32, index.shape, 0)
    return [
        index == (iota + first).astype(jnp.float32).astype(jnp.bfloat16)
        for first in range(0, row_total, TILE_ROWS)
    ]


def hot_product(loads, high, low, high_rows, low_rows):
    left, right = [], []
    high, low = high.astype(jnp.float32), low.astype(jnp.float32)
    zero = jnp.zeros((TILE_ROWS, high.shape[1]), jnp.bfloat16)
    one = jnp.ones((TILE_ROWS, high.shape[1]), jnp.bfloat16)
    for row in range(high.shape[0]):
        pick = slice(row, row + 1)
        high_masks = hot_tiles(spread_row(high[pick]), high_rows)
        low_masks = hot_tiles(spread_row(low[pick]), low_rows)
        spread = [spread_row(load[pick]) for load in loads]
        left.append(
            jnp.concatenate(
                [jnp.where(mask, load, zero) for load in spread for mask in high_masks], 0
            )
        )
        right.append(jnp.concatenate([jnp.where(mask, one, zero) for mask in low_masks], 0))
    return lax.dot_general(
        jnp.concatenate(left, 1),
        jnp.concatenate(right, 1),
        (((1,), (1,)), ((), ())),
        preferred_element_type=jnp.float32,
    )


def edge_row(plane, plane_total, moved_total):
    inner = (plane >= moved_total) & (plane < plane_total - moved_total)
    last = plane - (plane_total - 2 * moved_total)
    return jnp.where(inner, 2 * moved_total, jnp.where(plane < moved_total, plane, last))


def fold_moved(plane, side, plane_total, side_total):
    width, third = side_total // 4, plane_total // 3
    part = jnp.where(plane >= third, 1, 0) + jnp.where(plane >= 2 * third, 1, 0)
    other = side >= 3 * width
    high = jnp.where(other, plane_total + plane - part * third, plane)
    low = jnp.where(other, side - 3 * width + part * width, side)
    return high, low, plane_total + third, 3 * width


def unfold_moved(table, q, plane_total, side_total, put):
    width, third = side_total // 4, plane_total // 3
    rows = plane_total + third
    put(0, 0, table[pl.ds(q * rows, plane_total), 0 : 3 * width])
    for part in range(3):
        block = table[
            pl.ds(q * rows + plane_total, third), part * width : (part + 1) * width
        ]
        put(part * third, 3 * width, block)


def tracer_block(count, values, cells, first_row, block_rows, cells_side):
    rows = pl.ds(first_row, block_rows)
    lane_total = cells.shape[1]
    shape = (block_rows, lane_total)
    slot = (first_row + lax.broadcasted_iota(jnp.int32, shape, 0)) * lane_total
    slot = slot + lax.broadcasted_iota(jnp.int32, shape, 1)
    weight = jnp.where(slot < count, 0.5 + values[0, rows, :], jnp.float32(0.0))
    loads = [weight, weight * values[1, rows, :], weight * values[2, rows, :]]
    plane, side = split_index(cells[rows, :], cells_side)
    return loads, plane, side


def for_used_blocks(used, group_rows, block_rows, lane_total, late_copies, step):
    block_slots = block_rows * lane_total
    blocks = lax.div(used + (block_slots - 1), block_slots)
    blocks = jnp.clip(blocks, 1, group_rows // block_rows)

    def wait_late():
        for copy in late_copies:
            copy.wait()

    def repeat(index, carried):
        pl.when(index == 1)(wait_late)
        step(pl.multiple_of(index * block_rows, block_rows))
        return carried

    lax.fori_loop(0, blocks, repeat, 0)
    pl.when(blocks == 1)(wait_late)


VISCOSITY, VELOCITY, SOURCE, LINE_FIELDS = 0, 1, 4, 7


def composition_of(cell_sums, base):
    scale = 1.0 / (cell_sums[0] + PRIOR_WEIGHT)
    basalt_share, melt_share = cell_sums[1] * scale, cell_sums[2] * scale
    weakening = jnp.exp(CONTRAST_BASALT * basalt_share - CONTRAST_MELT * melt_share)
    return basalt_share, melt_share, base * weakening


def outward_row(t, cells_radial):
    return jnp.where(lax.axis_index("rad") == 0, t, cells_radial - 1 - t)


class Fetches:
    def __init__(self, semaphores):
        self.semaphores = semaphores
        self.copies = []

    def start(self, source, target):
        copy = pltpu.make_async_copy(source, target, self.semaphores.at[len(self.copies)])
        copy.start()
        self.copies.append(copy)

    def wait(self, first, last):
        for copy in self.copies[first:last]:
            copy.wait()


def has_partners():
    lateral, count = lax.axis_index("lat"), lax.axis_size("lat")
    odd = lax.rem(lateral, 2) == 1
    above, below = lateral + 1 < count, lateral > 0
    return jnp.logical_or(odd, above), jnp.where(odd, above, below)


def outgoing_kernel(
    block_rows,
    counts_hbm,
    values_hbm,
    cells_hbm,
    base_hbm,
    velocity_hbm,
    forcing_hbm,
    edge_ref,
    first_ref,
    second_ref,
    stay_values,
    stay_cells,
    counts,
    lower_values,
    lower_cells,
    upper_values,
    upper_cells,
    base,
    velocity,
    forcing,
    moved_sums,
    semaphores,
):
    cells_lateral, cells_radial, cells_side = base_hbm.shape
    plane_total = cells_lateral * cells_radial
    moved_planes = MIGRATION_PLANES * cells_radial
    group_rows, lane_total = stay_cells.shape
    groups = (
        (lower_values, lower_cells),
        (stay_values, stay_cells),
        (upper_values, upper_cells),
    )

    fetches = Fetches(semaphores)
    fetches.start(counts_hbm, counts)
    for first_row, rows in ((0, block_rows), (block_rows, group_rows - block_rows)):
        part = pl.ds(first_row, rows)
        for group, (values, cells) in enumerate(groups):
            fetches.start(cells_hbm.at[group, part], cells.at[part])
            fetches.start(values_hbm.at[:, group, part], values.at[:, part])
    for upward in (0, 1):
        outer = pl.ds((cells_lateral - MIGRATION_PLANES) * upward, MIGRATION_PLANES)
        fetches.start(base_hbm.at[outer], base.at[upward])
        fetches.start(velocity_hbm.at[:, outer], velocity.at[upward])
        outermost = pl.ds((cells_lateral - 1) * upward, 1)
        fetches.start(forcing_hbm.at[:, outermost], forcing.at[upward])

    edge_ref[...] = jnp.zeros_like(edge_ref)
    moved_sums[...] = jnp.zeros_like(moved_sums)

    def step(first_row):
        def block_of(group):
            values, cells = groups[group]
            count = counts[0, 0, group]
            return tracer_block(count, values, cells, first_row, block_rows, cells_side)

        loads, plane, side = block_of(1)
        row = edge_row(plane, plane_total, moved_planes)
        edge_ref[...] += hot_product(loads, row, side, 2 * moved_planes, cells_side)
        for slot, group in enumerate((0, 2)):
            loads, plane, side = block_of(group)
            if group == 0:
                plane = plane - (plane_total - moved_planes)
            moved_sums[slot] += hot_product(
                loads, *fold_moved(plane, side, moved_planes, cells_side)
            )

    fetches.wait(0, 7)
    used = jnp.maximum(jnp.maximum(counts[0, 0, 0], counts[0, 0, 1]), counts[0, 0, 2])
    for_used_blocks(used, group_rows, block_rows, lane_total, fetches.copies[7:13], step)
    fetches.wait(13, None)

    starts, rows_total = payload_sections(cells_radial)
    unused = starts[4] + 3 * cells_radial

    def fill(payload, upward):
        for q in range(3):

            def put_moved(plane, column, block):
                height, width = block.shape
                rows = pl.ds(starts[0] + q * moved_planes + plane, height)
                payload[rows, column : column + width] = block

            unfold_moved(moved_sums.at[upward], q, moved_planes, cells_side, put_moved)
            payload[pl.ds(starts[1] + q * moved_planes, moved_planes), :] = edge_ref[
                pl.ds((2 * q + upward) * moved_planes, moved_planes), :
            ]
            for offset in range(MIGRATION_PLANES):
                row = starts[2] + q * moved_planes + offset * cells_radial
                payload[pl.ds(row, cells_radial), :] = velocity[upward, q, offset]
            row = starts[4] + q * cells_radial
            payload[pl.ds(row, cells_radial), :] = forcing[upward, q, 0]
        for offset in range(MIGRATION_PLANES):
            row = starts[3] + offset * cells_radial
            payload[pl.ds(row, cells_radial), :] = base[upward, offset]
        if unused < rows_total:
            payload[unused:, :] = jnp.zeros((rows_total - unused, cells_side), jnp.float32)

    odd = lax.rem(lax.axis_index("lat"), 2) == 1

    @pl.when(odd)
    def _():
        fill(first_ref, 0)
        fill(second_ref, 1)

    @pl.when(jnp.logical_not(odd))
    def _():
        fill(first_ref, 1)
        fill(second_ref, 0)

    for payload, exists in zip((first_ref, second_ref), has_partners()):

        @pl.when(jnp.logical_not(exists))
        def _():
            payload[...] = jnp.zeros_like(payload)


def inner_kernel(
    block_rows,
    counts_ref,
    values_ref,
    cells_ref,
    base_ref,
    velocity_ref,
    forcing_ref,
    composition_ref,
    lines_ref,
    sums,
    fields,
):
    cells_lateral, cells_radial, cells_side = base_ref.shape
    margin = MIGRATION_PLANES
    planes = cells_lateral + 2 * margin
    pitch = round_up(cells_radial, 8)
    moved_planes = margin * cells_radial
    inner_planes = sums.shape[0] // 3
    group_rows, lane_total = cells_ref.shape
    count = counts_ref[0, 0, 1]
    sums[...] = jnp.zeros_like(sums)

    def step(first_row):
        loads, plane, side = tracer_block(
            count, values_ref, cells_ref, first_row, block_rows, cells_side
        )
        sums[...] += hot_product(loads, plane - moved_planes, side, inner_planes, cells_side)

    for_used_blocks(count, group_rows, block_rows, lane_total, [], step)

    nothing = jnp.zeros((cells_radial, cells_side), jnp.float32)
    for plane in range(planes):
        x = plane - margin
        rows = pl.ds(plane * pitch, cells_radial)
        own, inner = 0 <= x < cells_lateral, margin <= x < cells_lateral - margin
        viscosity = nothing
        source = [forcing_ref[q, x] if own else nothing for q in range(3)]
        if inner:
            row = (x - margin) * cells_radial
            cell_sums = [sums[pl.ds(q * inner_planes + row, cells_radial), :] for q in range(3)]
            basalt_share, melt_share, viscosity = composition_of(cell_sums, base_ref[x])
            source[2] = source[2] - BUOYANCY * basalt_share
            composition_ref[0, x - margin] = basalt_share
            composition_ref[1, x - margin] = melt_share
        fields[VISCOSITY, rows, :] = viscosity
        for q in range(3):
            fields[VELOCITY + q, rows, :] = velocity_ref[q, x] if own else nothing
            fields[SOURCE + q, rows, :] = source[q]
    for field in range(LINE_FIELDS):
        for t in range(cells_radial):
            row = outward_row(t, cells_radial)
            lines_ref[field, t] = fields[field, pl.ds(row, planes, stride=pitch), :]


BLOCK_ROWS = 32


def dense_tracers(tracer_values, tracer_cell):
    lane_total = 128
    return tracer_values.reshape(3, 3, -1, lane_total), tracer_cell.reshape(3, -1, lane_total)


def outgoing_sums(tracer_count, values, cells, base_viscosity, velocity, forcing):
    cells_lateral, cells_radial, cells_side = base_viscosity.shape
    moved_planes = MIGRATION_PLANES * cells_radial
    group_rows, lane_total = cells.shape[1:]
    block_rows = min(BLOCK_ROWS, group_rows // 2)
    _, payload_rows = payload_sections(cells_radial)
    hbm = pl.BlockSpec(memory_space=pltpu.HBM)
    vmem = pl.BlockSpec(memory_space=pltpu.VMEM)
    payload = jax.ShapeDtypeStruct((payload_rows, cells_side), jnp.float32)
    group = ((3, group_rows, lane_total), jnp.float32), ((group_rows, lane_total), jnp.int32)
    outer_planes = (MIGRATION_PLANES, cells_radial, cells_side)
    return pl.pallas_call(
        functools.partial(outgoing_kernel, block_rows),
        out_shape=(
            jax.ShapeDtypeStruct((6 * moved_planes, cells_side), jnp.float32),
            payload,
            payload,
            *(jax.ShapeDtypeStruct(*array) for array in group),
        ),
        in_specs=[hbm] * 6,
        out_specs=(vmem,) * 5,
        scratch_shapes=[
            pltpu.SMEM(tracer_count.shape, jnp.int32),
            *(pltpu.VMEM(*array) for array in group + group),
            pltpu.VMEM((2,) + outer_planes, jnp.float32),
            pltpu.VMEM((2, 3) + outer_planes, jnp.float32),
            pltpu.VMEM((2, 3, 1, cells_radial, cells_side), jnp.float32),
            pltpu.VMEM((2, 4 * moved_planes, cells_side * 3 // 4), jnp.float32),
            pltpu.SemaphoreType.DMA((19,)),
        ],
        compiler_params=pltpu.CompilerParams(vmem_limit_bytes=32 * 2**20),
        cost_estimate=pl.CostEstimate(
            flops=30 * group_rows * lane_total * moved_planes * cells_side,
            bytes_accessed=4 * (values.size + cells.size),
            transcendentals=0,
        ),
        name="outgoing_sums",
    )(
        *(
            pltpu.with_memory_space_constraint(array, pltpu.HBM)
            for array in (tracer_count, values, cells, base_viscosity, velocity, forcing)
        )
    )


def inner_lines(tracer_count, values, cells, base_viscosity, velocity, forcing):
    cells_lateral, cells_radial, cells_side = base_viscosity.shape
    planes = cells_lateral + 2 * MIGRATION_PLANES
    inner = cells_lateral - 2 * MIGRATION_PLANES
    group_rows, lane_total = cells.shape
    block_rows = min(BLOCK_ROWS, group_rows // 2)
    vmem = pl.BlockSpec(memory_space=pltpu.VMEM)
    return pl.pallas_call(
        functools.partial(inner_kernel, block_rows),
        out_shape=(
            jax.ShapeDtypeStruct((2, inner, cells_radial, cells_side), jnp.float32),
            jax.ShapeDtypeStruct((LINE_FIELDS, cells_radial, planes, cells_side), jnp.float32),
        ),
        in_specs=[pl.BlockSpec(memory_space=pltpu.SMEM)] + [vmem] * 5,
        out_specs=(vmem, vmem),
        scratch_shapes=[
            pltpu.VMEM((3 * inner * cells_radial, cells_side), jnp.float32),
            pltpu.VMEM((LINE_FIELDS, planes * round_up(cells_radial, 8), cells_side), jnp.float32),
        ],
        compiler_params=pltpu.CompilerParams(vmem_limit_bytes=32 * 2**20),
        cost_estimate=pl.CostEstimate(
            flops=6 * group_rows * lane_total * inner * cells_radial * cells_side,
            bytes_accessed=4 * (values.size + cells.size),
            transcendentals=0,
        ),
        name="inner_lines",
    )(tracer_count, values, cells, base_viscosity, velocity, forcing)


def pair_swaps(first, second):
    count = lax.axis_size("lat")
    received = []
    for payload, start in ((second, 1), (first, 0)):
        target = list(range(count))
        for low in range(start, count - 1, 2):
            target[low], target[low + 1] = low + 1, low
        received.append(lax.ppermute(payload, "lat", list(enumerate(target))))
    return received[::-1]


def shift_planes(block, step):
    return pltpu.roll(block, step % block.shape[0], 0)


def shift_side(block, step):
    return pltpu.roll(block, step % block.shape[1], 1)


def neighbours(block):
    return (
        shift_planes(block, 1),
        shift_planes(block, -1),
        shift_side(block, 1),
        shift_side(block, -1),
    )


def inside_side(values):
    lane = lax.broadcasted_iota(jnp.int32, values[2].shape, 1)
    lower = jnp.where(lane > 0, values[2], 0.0)
    upper = jnp.where(lane < lane.shape[1] - 1, values[3], 0.0)
    return values[0], values[1], lower, upper


def total_of(terms):
    result = terms[0]
    for term in terms[1:]:
        result = result + term
    return result


def inside_grid(shape, margin, cells_lateral):
    plane = lax.broadcasted_iota(jnp.int32, shape, 0)
    lateral = lax.axis_index("lat")
    first = jnp.where(lateral == 0, margin, 1)
    last = jnp.where(lateral == lax.axis_size("lat") - 1, margin + cells_lateral, shape[0] - 1)
    return (plane >= first) & (plane < last)


LONG_FIELDS, SHORT_FIELDS = 5, 7


def message_rows(cells_lateral):
    planes = cells_lateral + 2 * MIGRATION_PLANES
    return round_up(LONG_FIELDS * planes + SHORT_FIELDS * cells_lateral, 8)


def message_part(cells_lateral, field):
    planes = cells_lateral + 2 * MIGRATION_PLANES
    if field < LONG_FIELDS:
        return pl.ds(field * planes, planes), 0, planes
    first = LONG_FIELDS * planes + (field - LONG_FIELDS) * cells_lateral
    return pl.ds(first, cells_lateral), MIGRATION_PLANES, cells_lateral


def solve_lines(radial, cells_radial, valid, keep, keep_part):
    last = cells_radial - 1
    viscosity = [radial(VISCOSITY, t) for t in range(cells_radial)]
    lateral_faces, lateral_sums = [], []
    for here in viscosity:
        faces = [LATERAL * 0.5 * (here + there) for there in inside_side(neighbours(here))]
        lateral_sums.append(total_of(faces))
        lateral_faces.append(inside_side(faces))
    radial_faces = [RADIAL * 0.5 * viscosity[0]] + [
        RADIAL * 0.5 * (viscosity[t - 1] + viscosity[t]) for t in range(1, cells_radial)
    ]

    excess = lateral_sums[0] + radial_faces[0]
    inverse, coupling = [], []
    for t in range(last):
        inverse.append(1.0 / (excess + radial_faces[t + 1]))
        coupling.append(radial_faces[t + 1] * inverse[t])
        excess = lateral_sums[t + 1] + coupling[t] * excess

    def lateral_terms(t, around):
        return [face * there for face, there in zip(lateral_faces[t], around)]

    def forward(right_side):
        eliminated = [right_side[0]]
        for t in range(1, cells_radial):
            eliminated.append(right_side[t] + coupling[t - 1] * eliminated[t - 1])
        return eliminated

    def backward(eliminated):
        solved = [jnp.zeros_like(excess)]
        for t in range(last - 1, -1, -1):
            solved.append(eliminated[t] * inverse[t] + coupling[t] * solved[-1])
        return solved[::-1]

    response = [jnp.ones_like(excess)]
    for t in range(last - 1, -1, -1):
        response.append(coupling[t] * response[-1])
    response = response[::-1]

    def finish(part, eliminated):
        keep(LONG_FIELDS + part, eliminated[last])
        for t, value in enumerate(eliminated[:last]):
            keep_part(part, t, value)

    keep(0, viscosity[last])
    keep(1, excess)
    for q in range(3):
        source = [radial(SOURCE + q, t) for t in range(cells_radial)]
        eliminated = forward(
            [
                total_of([source[t]] + lateral_terms(t, neighbours(radial(VELOCITY + q, t))))
                for t in range(cells_radial)
            ]
        )
        keep(2 + q, eliminated[last])
        particular = [jnp.where(valid, value, 0.0) for value in backward(eliminated)]
        finish(
            q,
            forward(
                [
                    total_of([source[t]] + lateral_terms(t, neighbours(particular[t])))
                    for t in range(cells_radial)
                ]
            ),
        )
    around = [neighbours(jnp.where(valid, value, 0.0)) for value in response]
    for side in range(4):
        finish(
            3 + side,
            forward([lateral_faces[t][side] * around[t][side] for t in range(cells_radial)]),
        )
    for t in range(last):
        keep_part(SHORT_FIELDS, t, inverse[t])
        keep_part(SHORT_FIELDS + 1, t, coupling[t])


def eliminate_kernel(
    inner_ref,
    lines_ref,
    edge_ref,
    second_ref,
    first_ref,
    from_second_ref,
    from_first_ref,
    base_ref,
    forcing_ref,
    composition_ref,
    mine_ref,
    message_ref,
    parts_ref,
    fields,
):
    cells_lateral, cells_radial, cells_side = base_ref.shape
    margin = MIGRATION_PLANES
    planes = cells_lateral + 2 * margin
    pitch = round_up(cells_radial, 8)
    moved_planes = margin * cells_radial
    starts, _ = payload_sections(cells_radial)
    odd = lax.rem(lax.axis_index("lat"), 2) == 1

    def sent(upward, start):
        part = pl.ds(start, cells_radial)
        mine_first = odd if not upward else jnp.logical_not(odd)
        return jnp.where(mine_first, first_ref[part, :], second_ref[part, :])

    def arrived(from_above, start):
        part = pl.ds(start, cells_radial)
        is_first = odd if not from_above else jnp.logical_not(odd)
        return jnp.where(is_first, from_first_ref[part, :], from_second_ref[part, :])

    outer = 2 * margin

    def put(field, slot, value):
        fields[field, pl.ds(slot * pitch, cells_radial), :] = value

    for above in (False, True):
        for offset in range(margin):
            shift = offset * cells_radial
            halo = offset + (outer + margin if above else 0)
            own = offset + (outer if above else margin)
            x = offset + (cells_lateral - margin if above else 0)
            halo_sums, own_sums = [], []
            for q in range(3):
                row = q * moved_planes + shift
                rows = pl.ds((2 * q + int(above)) * moved_planes + shift, cells_radial)
                own_sums.append(edge_ref[rows, :] + arrived(above, starts[0] + row))
                halo_sums.append(sent(above, starts[0] + row) + arrived(above, starts[1] + row))
                put(VELOCITY + q, halo, arrived(above, starts[2] + row))
            basalt_share, melt_share, viscosity = composition_of(own_sums, base_ref[x])
            composition_ref[0, x] = basalt_share
            composition_ref[1, x] = melt_share
            put(VISCOSITY, own, viscosity)
            put(SOURCE + 2, own, forcing_ref[2, x] - BUOYANCY * basalt_share)
            basalt_share, _, viscosity = composition_of(
                halo_sums, arrived(above, starts[3] + shift)
            )
            put(VISCOSITY, halo, viscosity)
            beside = offset == (0 if above else margin - 1)
            for q in range(3):
                source = jnp.zeros_like(viscosity)
                if beside:
                    source = arrived(above, starts[4] + q * cells_radial)
                    if q == 2:
                        source = source - BUOYANCY * basalt_share
                put(SOURCE + q, halo, source)
    for x in range(margin, cells_lateral - margin):
        for q in range(2):
            composition_ref[q, x] = inner_ref[q, x - margin]

    def radial(field, t):
        replaced = outer if field in (VISCOSITY, SOURCE + 2) else margin
        plane = lax.broadcasted_iota(jnp.int32, (planes, cells_side), 0)
        own = (plane >= replaced) & (plane < planes - replaced)
        row = outward_row(t, cells_radial)
        edges = fields[field, pl.ds(row, 2 * outer, stride=pitch), :]
        if 2 * outer * 2 == planes:
            edges = jnp.concatenate([edges, edges], 0)
        else:
            gap = jnp.zeros((planes - 2 * outer, cells_side), jnp.float32)
            edges = jnp.concatenate([edges[:outer], gap, edges[outer:]], 0)
        return jnp.where(own, lines_ref[field, t], edges)

    unused = LONG_FIELDS * planes + SHORT_FIELDS * cells_lateral
    if unused < message_ref.shape[0]:
        message_ref[unused:, :] = jnp.zeros((message_ref.shape[0] - unused, cells_side), jnp.float32)

    def keep(field, value):
        rows, first, count = message_part(cells_lateral, field)
        mine_ref[field] = value
        message_ref[rows, :] = value[first : first + count]

    def keep_part(part, t, value):
        parts_ref[part, t] = value

    valid = inside_grid((planes, cells_side), margin, cells_lateral)
    solve_lines(radial, cells_radial, valid, keep, keep_part)


def eliminate(inner, lines, edge, sent, received, base_viscosity, forcing):
    cells_lateral, cells_radial, cells_side = base_viscosity.shape
    planes = cells_lateral + 2 * MIGRATION_PLANES
    vmem = pl.BlockSpec(memory_space=pltpu.VMEM)
    line = (planes, cells_side)
    return pl.pallas_call(
        eliminate_kernel,
        out_shape=(
            jax.ShapeDtypeStruct((2,) + base_viscosity.shape, jnp.float32),
            jax.ShapeDtypeStruct((LONG_FIELDS + SHORT_FIELDS,) + line, jnp.float32),
            jax.ShapeDtypeStruct((message_rows(cells_lateral), cells_side), jnp.float32),
            jax.ShapeDtypeStruct((SHORT_FIELDS + 2, cells_radial - 1) + line, jnp.float32),
        ),
        in_specs=[vmem] * 9,
        out_specs=(vmem,) * 4,
        scratch_shapes=[
            pltpu.VMEM(
                (LINE_FIELDS, 4 * MIGRATION_PLANES * round_up(cells_radial, 8), cells_side),
                jnp.float32,
            )
        ],
        compiler_params=pltpu.CompilerParams(vmem_limit_bytes=32 * 2**20),
        name="eliminate",
    )(inner, lines, edge, *sent[::-1], *received[::-1], base_viscosity, forcing)


def join_kernel(mine_ref, message_ref, parts_ref, smoothed_ref, lines, other_ref):
    _, cells_lateral, cells_radial, cells_side = smoothed_ref.shape
    margin = MIGRATION_PLANES
    planes = cells_lateral + 2 * margin
    pitch = round_up(cells_radial, 8)
    valid = inside_grid((planes, cells_side), margin, cells_lateral)

    other_ref[LONG_FIELDS:] = jnp.zeros_like(other_ref[LONG_FIELDS:])
    for field in range(LONG_FIELDS + SHORT_FIELDS):
        rows, first, count = message_part(cells_lateral, field)
        other_ref[field, pl.ds(first, count), :] = message_ref[rows, :]

    face = RADIAL * 0.5 * (mine_ref[0] + other_ref[0])
    excess, other_excess = mine_ref[1], other_ref[1]
    scale = 1.0 / (excess * other_excess + face * (excess + other_excess))
    own_weight = (other_excess + face) * scale
    other_weight = (excess + face) * scale
    cross = face * scale

    def second_right(ref, q, around):
        terms = [ref[LONG_FIELDS + 3 + side] * there for side, there in enumerate(around)]
        return total_of([ref[LONG_FIELDS + q]] + terms)

    for q in range(3):
        right, other_right = mine_ref[2 + q], other_ref[2 + q]
        own = jnp.where(valid, own_weight * right + cross * other_right, 0.0)
        other = jnp.where(valid, other_weight * other_right + cross * right, 0.0)
        around = neighbours(own)
        right = second_right(mine_ref, q, around)
        other_right = second_right(other_ref, q, neighbours(other))
        value = own_weight * right + cross * other_right
        for t in range(cells_radial - 1, -1, -1):
            if t < cells_radial - 1:
                terms = [parts_ref[3 + side, t] * there for side, there in enumerate(around)]
                right = total_of([parts_ref[q, t]] + terms)
                value = right * parts_ref[SHORT_FIELDS, t] + parts_ref[SHORT_FIELDS + 1, t] * value
            row = outward_row(t, cells_radial)
            lines[pl.ds(row, cells_lateral, stride=pitch), :] = value[
                margin : margin + cells_lateral
            ]
        for x in range(cells_lateral):
            smoothed_ref[q, x] = lines[pl.ds(x * pitch, cells_radial), :]


def join(mine, message, parts, like):
    cells_lateral, cells_radial, cells_side = like.shape[1:]
    vmem = pl.BlockSpec(memory_space=pltpu.VMEM)
    return pl.pallas_call(
        join_kernel,
        out_shape=jax.ShapeDtypeStruct(like.shape, jnp.float32),
        in_specs=[vmem] * 3,
        out_specs=vmem,
        scratch_shapes=[
            pltpu.VMEM((cells_lateral * round_up(cells_radial, 8), cells_side), jnp.float32),
            pltpu.VMEM(mine.shape, jnp.float32),
        ],
        compiler_params=pltpu.CompilerParams(vmem_limit_bytes=32 * 2**20),
        name="join",
    )(mine, message, parts)


def extended(block, sides, width):
    for axis, dim in sides:
        count = lax.axis_size(axis)
        forward = [(i, i + 1) for i in range(count - 1)]
        backward = [(target, source) for source, target in forward]
        low = lax.ppermute(
            lax.slice_in_dim(block, block.shape[dim] - width, None, axis=dim), axis, forward
        )
        high = lax.ppermute(lax.slice_in_dim(block, 0, width, axis=dim), axis, backward)
        block = jnp.concatenate([low, block, high], axis=dim)
    return block


def block_factor(diagonal, lower_band, upper_band):
    pivots = []
    upper_scaled = []
    for row_index in range(diagonal.shape[1]):
        if row_index == 0:
            pivot_row = diagonal[:, 0]
        else:
            pivot_row = diagonal[:, row_index] - lower_band[:, row_index] * upper_scaled[-1]
        pivots.append(pivot_row)
        upper_scaled.append(upper_band[:, row_index] / pivot_row)
    return (pivots, upper_scaled)


def block_solve(pivots, upper_scaled, lower_band, right_side):
    row_total = len(pivots)
    modified = []
    for row_index in range(row_total):
        if row_index == 0:
            value_row = right_side[:, :, 0] / pivots[0]
        else:
            value_row = (
                right_side[:, :, row_index] - lower_band[:, row_index] * modified[-1]
            ) / pivots[row_index]
        modified.append(value_row)
    solved = [modified[-1]]
    for row_index in range(row_total - 2, -1, -1):
        solved.append(modified[row_index] - upper_scaled[row_index] * solved[-1])
    ordered = solved[::-1]
    return jnp.stack(ordered, 2)


def interface_solve(coefficients):
    column_total = coefficients.shape[2]

    def forward(carried, inputs):
        offset, carried_slope = carried
        left_first, right_first, left_last, right_last, free_first, free_last = inputs
        divisor = 1.0 - left_first * carried_slope
        first_fixed = (free_first + left_first * offset) / divisor
        first_slope = right_first / divisor
        next_offset = free_last + left_last * (offset + carried_slope * first_fixed)
        next_slope = left_last * carried_slope * first_slope + right_last
        return ((next_offset, next_slope), (first_fixed, first_slope, next_offset, next_slope))

    start_state = (
        jnp.zeros((3, column_total), jnp.float32),
        jnp.zeros((column_total,), jnp.float32),
    )
    scan_inputs = (
        coefficients[:, 0],
        coefficients[:, 1],
        coefficients[:, 2],
        coefficients[:, 3],
        coefficients[:, 4:7],
        coefficients[:, 7:10],
    )
    final_state, eliminated = lax.scan(forward, start_state, scan_inputs)

    def backward(first_next, inputs):
        fixed_first, slope_first, fixed_last, slope_last = inputs
        first_value = fixed_first + slope_first * first_next
        last_value = fixed_last + slope_last * first_next
        return (first_value, (first_value, last_value))

    final_first, values_pair = lax.scan(
        backward, jnp.zeros((3, column_total), jnp.float32), eliminated, reverse=True
    )
    first_values, last_values = values_pair
    nothing_row = jnp.zeros((1, 3, column_total), jnp.float32)
    from_below = jnp.concatenate([nothing_row, last_values[:-1]], 0)
    from_above = jnp.concatenate([first_values[1:], nothing_row], 0)
    return jnp.concatenate([from_below, from_above], 1)


def reduced_boundary(interface):
    gathered = lax.all_gather(interface, "rad", axis=0, tiled=True)
    solved = interface_solve(gathered)
    return lax.dynamic_index_in_dim(solved, lax.axis_index("rad"), 0, keepdims=False)


def many_blocks(values, cells, count, edge, received, base_viscosity, velocity, forcing):
    cells_lateral, cells_radial, cells_side = base_viscosity.shape
    moved_rows = MIGRATION_PLANES * cells_radial
    odd = lax.rem(lax.axis_index("lat"), 2) == 1
    from_below = jnp.where(odd, received[0], received[1])[: 3 * moved_rows]
    from_above = jnp.where(odd, received[1], received[0])[: 3 * moved_rows]
    edge = edge.reshape(3, 2, moved_rows, cells_side)
    below = edge[:, 0] + from_below.reshape(3, moved_rows, cells_side)
    above = edge[:, 1] + from_above.reshape(3, moved_rows, cells_side)
    shares = [
        (sums[1:] / (sums[0] + PRIOR_WEIGHT)).reshape(2, -1, cells_radial, cells_side)
        for sums in (below, above)
    ]
    inner, _ = inner_lines(count, values, cells, base_viscosity, velocity, forcing)
    basalt_share, melt_share = jnp.concatenate([shares[0], inner, shares[1]], 1)
    viscosity = base_viscosity * jnp.exp(
        CONTRAST_BASALT * basalt_share - CONTRAST_MELT * melt_share
    )
    viscosity_pad = extended(viscosity, (("lat", 0), ("rad", 1)), 1)
    side_pad = jnp.pad(viscosity, ((0, 0), (0, 0), (1, 1)))
    face_west = LATERAL * 0.5 * (viscosity + viscosity_pad[:-2, 1:-1])
    face_east = LATERAL * 0.5 * (viscosity + viscosity_pad[2:, 1:-1])
    face_south = LATERAL * 0.5 * (viscosity + side_pad[:, :, :-2])
    face_north = LATERAL * 0.5 * (viscosity + side_pad[:, :, 2:])
    face_below = RADIAL * 0.5 * (viscosity + viscosity_pad[1:-1, :-2])
    face_above = RADIAL * 0.5 * (viscosity + viscosity_pad[1:-1, 2:])
    diagonal = face_west + face_east + face_south + face_north + face_below + face_above
    source = jnp.concatenate([forcing[:2], (forcing[2] - BUOYANCY * basalt_share)[None]], 0)
    lower_band = -face_below
    upper_band = -face_above
    pivots, upper_scaled = block_factor(diagonal, lower_band, upper_band)
    radial_iota = lax.broadcasted_iota(jnp.int32, viscosity.shape, 1)
    response_side = jnp.stack(
        [
            jnp.where(radial_iota == 0, face_below, jnp.float32(0.0)),
            jnp.where(radial_iota == cells_radial - 1, face_above, jnp.float32(0.0)),
        ]
    )
    response = block_solve(pivots, upper_scaled, lower_band, response_side)
    current = velocity
    for sweep_index in range(SWEEPS):
        velocity_pad = extended(current, (("lat", 1),), 1)
        side_velocity = jnp.pad(current, ((0, 0), (0, 0), (0, 0), (1, 1)))
        right_side = (
            source
            + face_west * velocity_pad[:, :-2]
            + face_east * velocity_pad[:, 2:]
            + face_south * side_velocity[..., :-2]
            + face_north * side_velocity[..., 2:]
        )
        particular = block_solve(pivots, upper_scaled, lower_band, right_side)
        interface = jnp.concatenate(
            [response[:, :, 0], response[:, :, -1], particular[:, :, 0], particular[:, :, -1]], 0
        )
        interface = interface.reshape(1, 10, cells_lateral * cells_side)
        boundary = reduced_boundary(interface).reshape(6, cells_lateral, 1, cells_side)
        current = particular + response[0][None] * boundary[:3] + response[1][None] * boundary[3:]
    composition = jnp.stack([basalt_share, melt_share])
    return (current, composition)

def local(tracer_values, tracer_cell, tracer_count, base_viscosity, velocity, forcing):
    values, cells = dense_tracers(tracer_values, tracer_cell)
    edge, first, second, values, cells = outgoing_sums(
        tracer_count, values, cells, base_viscosity, velocity, forcing
    )
    sent = first, second
    received = pair_swaps(first, second)
    if lax.axis_size("rad") != 2:
        return many_blocks(
            values, cells, tracer_count, edge, received, base_viscosity, velocity, forcing
        )
    inner, lines = inner_lines(tracer_count, values, cells, base_viscosity, velocity, forcing)
    composition, mine, message, parts = eliminate(
        inner, lines, edge, sent, received, base_viscosity, forcing
    )
    other = lax.ppermute(message, "rad", [(0, 1), (1, 0)])
    return join(mine, other, parts, velocity), composition


def solution(mesh):
    return jax.shard_map(
        local,
        mesh=mesh,
        in_specs=(
            P("lat", "rad", None, None),
            P("lat", "rad", None),
            P("lat", "rad", None),
            P("lat", "rad", None),
            P(None, "lat", "rad", None),
            P(None, "lat", "rad", None),
        ),
        out_specs=(P(None, "lat", "rad", None), P(None, "lat", "rad", None)),
        check_vma=False,
    )
```

```python
import functools

import jax
import jax.numpy as jnp
from jax import lax
from jax.experimental import pallas as pl
from jax.experimental.pallas import tpu as pltpu
from jax.sharding import PartitionSpec as P

SWEEPS = 2
MIGRATION_PLANES = 2

LATERAL = 0.015625
RADIAL = 32.0
BUOYANCY = 0.1
PRIOR_WEIGHT = 0.5
CONTRAST_BASALT = 2.3
CONTRAST_MELT = 1.5

TILE_ROWS = 16


def round_up(value, multiple):
    return -(-value // multiple) * multiple


def split_index(index, count):
    if count & (count - 1) == 0:
        return lax.shift_right_logical(index, count.bit_length() - 1), index & (count - 1)
    quotient = lax.div(index, count)
    return quotient, index - quotient * count


def payload_sections(cells_radial):
    pair = MIGRATION_PLANES * cells_radial
    starts = [0, 3 * pair, 6 * pair, 9 * pair, 10 * pair]
    return starts, round_up(10 * pair + 3 * cells_radial, 8)


def spread_row(row):
    return jnp.broadcast_to(row, (TILE_ROWS, row.shape[1])).astype(jnp.bfloat16)


def hot_tiles(index, row_total):
    iota = lax.broadcasted_iota(jnp.int32, index.shape, 0)
    return [
        index == (iota + first).astype(jnp.float32).astype(jnp.bfloat16)
        for first in range(0, row_total, TILE_ROWS)
    ]


def hot_product(loads, high, low, high_rows, low_rows):
    left, right = [], []
    high, low = high.astype(jnp.float32), low.astype(jnp.float32)
    zero = jnp.zeros((TILE_ROWS, high.shape[1]), jnp.bfloat16)
    one = jnp.ones((TILE_ROWS, high.shape[1]), jnp.bfloat16)
    for row in range(high.shape[0]):
        pick = slice(row, row + 1)
        high_masks = hot_tiles(spread_row(high[pick]), high_rows)
        low_masks = hot_tiles(spread_row(low[pick]), low_rows)
        spread = [spread_row(load[pick]) for load in loads]
        left.append(
            jnp.concatenate(
                [jnp.where(mask, load, zero) for load in spread for mask in high_masks], 0
            )
        )
        right.append(jnp.concatenate([jnp.where(mask, one, zero) for mask in low_masks], 0))
    return lax.dot_general(
        jnp.concatenate(left, 1),
        jnp.concatenate(right, 1),
        (((1,), (1,)), ((), ())),
        preferred_element_type=jnp.float32,
    )


def edge_row(plane, plane_total, moved_total):
    inner = (plane >= moved_total) & (plane < plane_total - moved_total)
    last = plane - (plane_total - 2 * moved_total)
    return jnp.where(inner, -plane_total, jnp.where(plane < moved_total, plane, last))


def fold(plane, side, plane_total, side_total):
    rows, width = plane_total * 2 // 3, side_total // 2
    other = plane >= rows
    half = side >= width
    high = jnp.where(half, plane + (plane_total - 2 * rows), plane - rows)
    low = jnp.where(half, side - width, side) + side_total
    high = jnp.where(other, high, plane)
    low = jnp.where(other, low, side)
    return high, low, rows, side_total + width


def unfold(table, q, plane_total, side_total, put):
    rows, width = plane_total * 2 // 3, side_total // 2
    left = plane_total - rows
    put(0, 0, table[pl.ds(q * rows, rows), 0:side_total])
    for half in (0, 1):
        block = table[pl.ds(q * rows + half * left, left), side_total : side_total + width]
        put(rows, half * width, block)


def tracer_block(count, values, cells, first_row, block_rows, cells_side):
    rows = pl.ds(first_row, block_rows)
    lane_total = cells.shape[1]
    shape = (block_rows, lane_total)
    slot = (first_row + lax.broadcasted_iota(jnp.int32, shape, 0)) * lane_total
    slot = slot + lax.broadcasted_iota(jnp.int32, shape, 1)
    weight = jnp.where(slot < count, 0.5 + values[0, rows, :], jnp.float32(0.0))
    loads = [weight, weight * values[1, rows, :], weight * values[2, rows, :]]
    plane, side = split_index(cells[rows, :], cells_side)
    return loads, plane, side


def for_used_blocks(used, group_rows, block_rows, lane_total, late_copies, step):
    block_slots = block_rows * lane_total
    blocks = lax.div(used + (block_slots - 1), block_slots)
    blocks = jnp.clip(blocks, 1, group_rows // block_rows)

    def wait_late():
        for copy in late_copies:
            copy.wait()

    def repeat(index, carried):
        pl.when(index == 1)(wait_late)
        step(pl.multiple_of(index * block_rows, block_rows))
        return carried

    lax.fori_loop(0, blocks, repeat, 0)
    pl.when(blocks == 1)(wait_late)


VISCOSITY, VELOCITY, SOURCE, LINE_FIELDS = 0, 1, 4, 7


def composition_of(cell_sums, base):
    scale = 1.0 / (cell_sums[0] + PRIOR_WEIGHT)
    basalt_share, melt_share = cell_sums[1] * scale, cell_sums[2] * scale
    weakening = jnp.exp(CONTRAST_BASALT * basalt_share - CONTRAST_MELT * melt_share)
    return basalt_share, melt_share, base * weakening


def outward_row(t, cells_radial):
    return jnp.where(lax.axis_index("rad") == 0, t, cells_radial - 1 - t)


class Fetches:
    def __init__(self, semaphores):
        self.semaphores = semaphores
        self.copies = []

    def start(self, source, target):
        copy = pltpu.make_async_copy(source, target, self.semaphores.at[len(self.copies)])
        copy.start()
        self.copies.append(copy)

    def wait(self, first, last):
        for copy in self.copies[first:last]:
            copy.wait()


def has_partners():
    lateral, count = lax.axis_index("lat"), lax.axis_size("lat")
    odd = lax.rem(lateral, 2) == 1
    above, below = lateral + 1 < count, lateral > 0
    return jnp.logical_or(odd, above), jnp.where(odd, above, below)


def outgoing_kernel(
    block_rows,
    counts_hbm,
    values_hbm,
    cells_hbm,
    base_hbm,
    velocity_hbm,
    forcing_hbm,
    edge_ref,
    first_ref,
    second_ref,
    stay_values,
    stay_cells,
    counts,
    lower_values,
    lower_cells,
    upper_values,
    upper_cells,
    base,
    velocity,
    forcing,
    edge_sums,
    moved_sums,
    semaphores,
):
    cells_lateral, cells_radial, cells_side = base_hbm.shape
    plane_total = cells_lateral * cells_radial
    moved_planes = MIGRATION_PLANES * cells_radial
    group_rows, lane_total = stay_cells.shape
    groups = (
        (lower_values, lower_cells),
        (stay_values, stay_cells),
        (upper_values, upper_cells),
    )

    fetches = Fetches(semaphores)
    fetches.start(counts_hbm, counts)
    for first_row, rows in ((0, block_rows), (block_rows, group_rows - block_rows)):
        part = pl.ds(first_row, rows)
        for group, (values, cells) in enumerate(groups):
            fetches.start(cells_hbm.at[group, part], cells.at[part])
            fetches.start(values_hbm.at[:, group, part], values.at[:, part])
    for upward in (0, 1):
        outer = pl.ds((cells_lateral - MIGRATION_PLANES) * upward, MIGRATION_PLANES)
        fetches.start(base_hbm.at[outer], base.at[upward])
        fetches.start(velocity_hbm.at[:, outer], velocity.at[upward])
        outermost = pl.ds((cells_lateral - 1) * upward, 1)
        fetches.start(forcing_hbm.at[:, outermost], forcing.at[upward])

    edge_sums[...] = jnp.zeros_like(edge_sums)
    moved_sums[...] = jnp.zeros_like(moved_sums)

    def step(first_row):
        def block_of(group):
            values, cells = groups[group]
            count = counts[0, 0, group]
            return tracer_block(count, values, cells, first_row, block_rows, cells_side)

        loads, plane, side = block_of(1)
        row = edge_row(plane, plane_total, moved_planes)
        edge_sums[...] += hot_product(loads, *fold(row, side, 2 * moved_planes, cells_side))
        for slot, group in enumerate((0, 2)):
            loads, plane, side = block_of(group)
            if group == 0:
                plane = plane - (plane_total - moved_planes)
            moved_sums[slot] += hot_product(
                loads, *fold(plane, side, moved_planes, cells_side)
            )

    fetches.wait(0, 7)
    used = jnp.maximum(jnp.maximum(counts[0, 0, 0], counts[0, 0, 1]), counts[0, 0, 2])
    for_used_blocks(used, group_rows, block_rows, lane_total, fetches.copies[7:13], step)
    fetches.wait(13, None)

    for q in range(3):

        def put_edge(plane, column, block):
            height, width = block.shape
            rows = pl.ds(2 * q * moved_planes + plane, height)
            edge_ref[rows, column : column + width] = block

        unfold(edge_sums, q, 2 * moved_planes, cells_side, put_edge)

    starts, rows_total = payload_sections(cells_radial)
    unused = starts[4] + 3 * cells_radial

    def fill(payload, upward):
        for q in range(3):

            def put_moved(plane, column, block):
                height, width = block.shape
                rows = pl.ds(starts[0] + q * moved_planes + plane, height)
                payload[rows, column : column + width] = block

            unfold(moved_sums.at[upward], q, moved_planes, cells_side, put_moved)
            payload[pl.ds(starts[1] + q * moved_planes, moved_planes), :] = edge_ref[
                pl.ds((2 * q + upward) * moved_planes, moved_planes), :
            ]
            for offset in range(MIGRATION_PLANES):
                row = starts[2] + q * moved_planes + offset * cells_radial
                payload[pl.ds(row, cells_radial), :] = velocity[upward, q, offset]
            row = starts[4] + q * cells_radial
            payload[pl.ds(row, cells_radial), :] = forcing[upward, q, 0]
        for offset in range(MIGRATION_PLANES):
            row = starts[3] + offset * cells_radial
            payload[pl.ds(row, cells_radial), :] = base[upward, offset]
        if unused < rows_total:
            payload[unused:, :] = jnp.zeros((rows_total - unused, cells_side), jnp.float32)

    odd = lax.rem(lax.axis_index("lat"), 2) == 1

    @pl.when(odd)
    def _():
        fill(first_ref, 0)
        fill(second_ref, 1)

    @pl.when(jnp.logical_not(odd))
    def _():
        fill(first_ref, 1)
        fill(second_ref, 0)

    for payload, exists in zip((first_ref, second_ref), has_partners()):

        @pl.when(jnp.logical_not(exists))
        def _():
            payload[...] = jnp.zeros_like(payload)


def inner_kernel(
    block_rows,
    counts_hbm,
    values_ref,
    cells_ref,
    base_ref,
    velocity_ref,
    forcing_ref,
    composition_ref,
    lines_ref,
    counts,
    sums,
    fields,
    semaphores,
):
    cells_lateral, cells_radial, cells_side = base_ref.shape
    margin = MIGRATION_PLANES
    planes = cells_lateral + 2 * margin
    pitch = round_up(cells_radial, 8)
    moved_planes = margin * cells_radial
    inner = cells_lateral - 2 * margin
    half_planes = inner * cells_radial // 2
    group_rows, lane_total = cells_ref.shape
    fetches = Fetches(semaphores)
    fetches.start(counts_hbm, counts)
    sums[...] = jnp.zeros_like(sums)

    nothing = jnp.zeros((cells_radial, cells_side), jnp.float32)

    def put(field, plane, value):
        fields[field, pl.ds(plane * pitch, cells_radial), :] = value

    def lay_out(those):
        for field in those:
            for t in range(cells_radial):
                row = outward_row(t, cells_radial)
                lines_ref[field, t] = fields[field, pl.ds(row, planes, stride=pitch), :]

    for plane in range(planes):
        x = plane - margin
        own = 0 <= x < cells_lateral
        for q in range(3):
            put(VELOCITY + q, plane, velocity_ref[q, x] if own else nothing)
        for q in range(2):
            put(SOURCE + q, plane, forcing_ref[q, x] if own else nothing)
    late = VISCOSITY, SOURCE + 2
    lay_out(field for field in range(LINE_FIELDS) if field not in late)

    def step(first_row):
        loads, plane, side = tracer_block(
            count, values_ref, cells_ref, first_row, block_rows, cells_side
        )
        plane = plane - moved_planes
        upper = plane >= half_planes
        high = jnp.where(upper, plane - half_planes, plane)
        low = jnp.where(upper, side + cells_side, side)
        sums[...] += hot_product(loads, high, low, half_planes, 2 * cells_side)

    fetches.wait(0, None)
    count = counts[0, 0, 1]
    for_used_blocks(count, group_rows, block_rows, lane_total, [], step)

    for plane in range(planes):
        x = plane - 2 * margin
        viscosity, source = nothing, nothing
        if 0 <= x < inner:
            half, row = divmod(x * cells_radial, half_planes)
            columns = slice(half * cells_side, (half + 1) * cells_side)
            cell_sums = [sums[pl.ds(q * half_planes + row, cells_radial), columns] for q in range(3)]
            basalt_share, melt_share, viscosity = composition_of(cell_sums, base_ref[x + margin])
            source = forcing_ref[2, x + margin] - BUOYANCY * basalt_share
            composition_ref[0, x] = basalt_share
            composition_ref[1, x] = melt_share
        put(VISCOSITY, plane, viscosity)
        put(SOURCE + 2, plane, source)
    lay_out(late)


BLOCK_ROWS = 64


def dense_tracers(tracer_values, tracer_cell):
    lane_total = 128
    return tracer_values.reshape(3, 3, -1, lane_total), tracer_cell.reshape(3, -1, lane_total)


def outgoing_sums(tracer_count, values, cells, base_viscosity, velocity, forcing):
    cells_lateral, cells_radial, cells_side = base_viscosity.shape
    moved_planes = MIGRATION_PLANES * cells_radial
    group_rows, lane_total = cells.shape[1:]
    block_rows = min(BLOCK_ROWS, group_rows // 2)
    _, payload_rows = payload_sections(cells_radial)
    hbm = pl.BlockSpec(memory_space=pltpu.HBM)
    vmem = pl.BlockSpec(memory_space=pltpu.VMEM)
    payload = jax.ShapeDtypeStruct((payload_rows, cells_side), jnp.float32)
    group = ((3, group_rows, lane_total), jnp.float32), ((group_rows, lane_total), jnp.int32)
    outer_planes = (MIGRATION_PLANES, cells_radial, cells_side)
    return pl.pallas_call(
        functools.partial(outgoing_kernel, block_rows),
        out_shape=(
            jax.ShapeDtypeStruct((6 * moved_planes, cells_side), jnp.float32),
            payload,
            payload,
            *(jax.ShapeDtypeStruct(*array) for array in group),
        ),
        in_specs=[hbm] * 6,
        out_specs=(vmem,) * 5,
        scratch_shapes=[
            pltpu.SMEM(tracer_count.shape, jnp.int32),
            *(pltpu.VMEM(*array) for array in group + group),
            pltpu.VMEM((2,) + outer_planes, jnp.float32),
            pltpu.VMEM((2, 3) + outer_planes, jnp.float32),
            pltpu.VMEM((2, 3, 1, cells_radial, cells_side), jnp.float32),
            pltpu.VMEM((4 * moved_planes, cells_side * 3 // 2), jnp.float32),
            pltpu.VMEM((2, 2 * moved_planes, cells_side * 3 // 2), jnp.float32),
            pltpu.SemaphoreType.DMA((19,)),
        ],
        compiler_params=pltpu.CompilerParams(vmem_limit_bytes=32 * 2**20),
        cost_estimate=pl.CostEstimate(
            flops=30 * group_rows * lane_total * moved_planes * cells_side,
            bytes_accessed=4 * (values.size + cells.size),
            transcendentals=0,
        ),
        name="outgoing_sums",
    )(
        *(
            pltpu.with_memory_space_constraint(array, pltpu.HBM)
            for array in (tracer_count, values, cells, base_viscosity, velocity, forcing)
        )
    )


def inner_lines(tracer_count, values, cells, base_viscosity, velocity, forcing):
    cells_lateral, cells_radial, cells_side = base_viscosity.shape
    planes = cells_lateral + 2 * MIGRATION_PLANES
    inner = cells_lateral - 2 * MIGRATION_PLANES
    group_rows, lane_total = cells.shape
    block_rows = min(BLOCK_ROWS, group_rows // 2)
    vmem = pl.BlockSpec(memory_space=pltpu.VMEM)
    return pl.pallas_call(
        functools.partial(inner_kernel, block_rows),
        out_shape=(
            jax.ShapeDtypeStruct((2, inner, cells_radial, cells_side), jnp.float32),
            jax.ShapeDtypeStruct((LINE_FIELDS, cells_radial, planes, cells_side), jnp.float32),
        ),
        in_specs=[pl.BlockSpec(memory_space=pltpu.HBM)] + [vmem] * 5,
        out_specs=(vmem, vmem),
        scratch_shapes=[
            pltpu.SMEM(tracer_count.shape, jnp.int32),
            pltpu.VMEM((3 * inner * cells_radial // 2, 2 * cells_side), jnp.float32),
            pltpu.VMEM((LINE_FIELDS, planes * round_up(cells_radial, 8), cells_side), jnp.float32),
            pltpu.SemaphoreType.DMA((1,)),
        ],
        compiler_params=pltpu.CompilerParams(vmem_limit_bytes=32 * 2**20),
        cost_estimate=pl.CostEstimate(
            flops=6 * group_rows * lane_total * inner * cells_radial * cells_side,
            bytes_accessed=4 * (values.size + cells.size),
            transcendentals=0,
        ),
        name="inner_lines",
    )(
        pltpu.with_memory_space_constraint(tracer_count, pltpu.HBM),
        values,
        cells,
        base_viscosity,
        velocity,
        forcing,
    )


def pair_swaps(first, second):
    count = lax.axis_size("lat")
    received = []
    for payload, start in ((second, 1), (first, 0)):
        target = list(range(count))
        for low in range(start, count - 1, 2):
            target[low], target[low + 1] = low + 1, low
        received.append(lax.ppermute(payload, "lat", list(enumerate(target))))
    return received[::-1]


def shift_planes(block, step):
    return pltpu.roll(block, step % block.shape[0], 0)


def shift_side(block, step):
    return pltpu.roll(block, step % block.shape[1], 1)


def neighbours(block):
    return (
        shift_planes(block, 1),
        shift_planes(block, -1),
        shift_side(block, 1),
        shift_side(block, -1),
    )


def inside_side(values):
    lane = lax.broadcasted_iota(jnp.int32, values[2].shape, 1)
    lower = jnp.where(lane > 0, values[2], 0.0)
    upper = jnp.where(lane < lane.shape[1] - 1, values[3], 0.0)
    return values[0], values[1], lower, upper


def total_of(terms):
    result = terms[0]
    for term in terms[1:]:
        result = result + term
    return result


def inside_grid(shape, margin, cells_lateral):
    plane = lax.broadcasted_iota(jnp.int32, shape, 0)
    lateral = lax.axis_index("lat")
    first = jnp.where(lateral == 0, margin, 1)
    last = jnp.where(lateral == lax.axis_size("lat") - 1, margin + cells_lateral, shape[0] - 1)
    return (plane >= first) & (plane < last)


LONG_FIELDS, SHORT_FIELDS = 5, 7


def message_rows(cells_lateral):
    planes = cells_lateral + 2 * MIGRATION_PLANES
    return round_up(LONG_FIELDS * planes + SHORT_FIELDS * cells_lateral, 8)


def message_part(cells_lateral, field):
    planes = cells_lateral + 2 * MIGRATION_PLANES
    if field < LONG_FIELDS:
        return pl.ds(field * planes, planes), 0, planes
    first = LONG_FIELDS * planes + (field - LONG_FIELDS) * cells_lateral
    return pl.ds(first, cells_lateral), MIGRATION_PLANES, cells_lateral


def solve_lines(radial, cells_radial, valid, keep, keep_part):
    last = cells_radial - 1
    viscosity = [radial(VISCOSITY, t) for t in range(cells_radial)]
    lateral_faces, lateral_sums = [], []
    for here in viscosity:
        faces = [LATERAL * 0.5 * (here + there) for there in inside_side(neighbours(here))]
        lateral_sums.append(total_of(faces))
        lateral_faces.append(inside_side(faces))
    radial_faces = [RADIAL * 0.5 * viscosity[0]] + [
        RADIAL * 0.5 * (viscosity[t - 1] + viscosity[t]) for t in range(1, cells_radial)
    ]

    excess = lateral_sums[0] + radial_faces[0]
    inverse, coupling = [], []
    for t in range(last):
        inverse.append(1.0 / (excess + radial_faces[t + 1]))
        coupling.append(radial_faces[t + 1] * inverse[t])
        excess = lateral_sums[t + 1] + coupling[t] * excess

    def lateral_terms(t, around):
        return [face * there for face, there in zip(lateral_faces[t], around)]

    def forward(right_side):
        eliminated = [right_side[0]]
        for t in range(1, cells_radial):
            eliminated.append(right_side[t] + coupling[t - 1] * eliminated[t - 1])
        return eliminated

    def backward(eliminated):
        solved = [jnp.zeros_like(excess)]
        for t in range(last - 1, -1, -1):
            solved.append(eliminated[t] * inverse[t] + coupling[t] * solved[-1])
        return solved[::-1]

    response = [jnp.ones_like(excess)]
    for t in range(last - 1, -1, -1):
        response.append(coupling[t] * response[-1])
    response = response[::-1]

    def finish(part, eliminated):
        keep(LONG_FIELDS + part, eliminated[last])
        for t, value in enumerate(eliminated[:last]):
            keep_part(part, t, value)

    keep(0, viscosity[last])
    keep(1, excess)
    for q in range(3):
        source = [radial(SOURCE + q, t) for t in range(cells_radial)]
        eliminated = forward(
            [
                total_of([source[t]] + lateral_terms(t, neighbours(radial(VELOCITY + q, t))))
                for t in range(cells_radial)
            ]
        )
        keep(2 + q, eliminated[last])
        particular = [jnp.where(valid, value, 0.0) for value in backward(eliminated)]
        finish(
            q,
            forward(
                [
                    total_of([source[t]] + lateral_terms(t, neighbours(particular[t])))
                    for t in range(cells_radial)
                ]
            ),
        )
    around = [neighbours(jnp.where(valid, value, 0.0)) for value in response]
    for side in range(4):
        finish(
            3 + side,
            forward([lateral_faces[t][side] * around[t][side] for t in range(cells_radial)]),
        )
    for t in range(last):
        keep_part(SHORT_FIELDS, t, inverse[t])
        keep_part(SHORT_FIELDS + 1, t, coupling[t])


def eliminate_kernel(
    inner_ref,
    lines_ref,
    edge_ref,
    second_ref,
    first_ref,
    from_second_ref,
    from_first_ref,
    base_ref,
    forcing_ref,
    composition_ref,
    mine_ref,
    message_ref,
    parts_ref,
    fields,
):
    cells_lateral, cells_radial, cells_side = base_ref.shape
    margin = MIGRATION_PLANES
    planes = cells_lateral + 2 * margin
    pitch = round_up(cells_radial, 8)
    moved_planes = margin * cells_radial
    starts, _ = payload_sections(cells_radial)
    odd = lax.rem(lax.axis_index("lat"), 2) == 1

    def sent(upward, start):
        part = pl.ds(start, cells_radial)
        mine_first = odd if not upward else jnp.logical_not(odd)
        return jnp.where(mine_first, first_ref[part, :], second_ref[part, :])

    def arrived(from_above, start):
        part = pl.ds(start, cells_radial)
        is_first = odd if not from_above else jnp.logical_not(odd)
        return jnp.where(is_first, from_first_ref[part, :], from_second_ref[part, :])

    outer = 2 * margin

    def put(field, slot, value):
        fields[field, pl.ds(slot * pitch, cells_radial), :] = value

    for above in (False, True):
        for offset in range(margin):
            shift = offset * cells_radial
            halo = offset + (outer + margin if above else 0)
            own = offset + (outer if above else margin)
            x = offset + (cells_lateral - margin if above else 0)
            halo_sums, own_sums = [], []
            for q in range(3):
                row = q * moved_planes + shift
                rows = pl.ds((2 * q + int(above)) * moved_planes + shift, cells_radial)
                own_sums.append(edge_ref[rows, :] + arrived(above, starts[0] + row))
                halo_sums.append(sent(above, starts[0] + row) + arrived(above, starts[1] + row))
                put(VELOCITY + q, halo, arrived(above, starts[2] + row))
            basalt_share, melt_share, viscosity = composition_of(own_sums, base_ref[x])
            composition_ref[0, x] = basalt_share
            composition_ref[1, x] = melt_share
            put(VISCOSITY, own, viscosity)
            put(SOURCE + 2, own, forcing_ref[2, x] - BUOYANCY * basalt_share)
            basalt_share, _, viscosity = composition_of(
                halo_sums, arrived(above, starts[3] + shift)
            )
            put(VISCOSITY, halo, viscosity)
            beside = offset == (0 if above else margin - 1)
            for q in range(3):
                source = jnp.zeros_like(viscosity)
                if beside:
                    source = arrived(above, starts[4] + q * cells_radial)
                    if q == 2:
                        source = source - BUOYANCY * basalt_share
                put(SOURCE + q, halo, source)
    for x in range(margin, cells_lateral - margin):
        for q in range(2):
            composition_ref[q, x] = inner_ref[q, x - margin]

    def radial(field, t):
        replaced = outer if field in (VISCOSITY, SOURCE + 2) else margin
        plane = lax.broadcasted_iota(jnp.int32, (planes, cells_side), 0)
        own = (plane >= replaced) & (plane < planes - replaced)
        row = outward_row(t, cells_radial)
        edges = fields[field, pl.ds(row, 2 * outer, stride=pitch), :]
        if 2 * outer * 2 == planes:
            edges = jnp.concatenate([edges, edges], 0)
        else:
            gap = jnp.zeros((planes - 2 * outer, cells_side), jnp.float32)
            edges = jnp.concatenate([edges[:outer], gap, edges[outer:]], 0)
        return jnp.where(own, lines_ref[field, t], edges)

    unused = LONG_FIELDS * planes + SHORT_FIELDS * cells_lateral
    if unused < message_ref.shape[0]:
        message_ref[unused:, :] = jnp.zeros((message_ref.shape[0] - unused, cells_side), jnp.float32)

    def keep(field, value):
        rows, first, count = message_part(cells_lateral, field)
        mine_ref[field] = value
        message_ref[rows, :] = value[first : first + count]

    def keep_part(part, t, value):
        parts_ref[part, t] = value

    valid = inside_grid((planes, cells_side), margin, cells_lateral)
    solve_lines(radial, cells_radial, valid, keep, keep_part)


def eliminate(inner, lines, edge, sent, received, base_viscosity, forcing):
    cells_lateral, cells_radial, cells_side = base_viscosity.shape
    planes = cells_lateral + 2 * MIGRATION_PLANES
    vmem = pl.BlockSpec(memory_space=pltpu.VMEM)
    line = (planes, cells_side)
    return pl.pallas_call(
        eliminate_kernel,
        out_shape=(
            jax.ShapeDtypeStruct((2,) + base_viscosity.shape, jnp.float32),
            jax.ShapeDtypeStruct((LONG_FIELDS + SHORT_FIELDS,) + line, jnp.float32),
            jax.ShapeDtypeStruct((message_rows(cells_lateral), cells_side), jnp.float32),
            jax.ShapeDtypeStruct((SHORT_FIELDS + 2, cells_radial - 1) + line, jnp.float32),
        ),
        in_specs=[vmem] * 9,
        out_specs=(vmem,) * 4,
        scratch_shapes=[
            pltpu.VMEM(
                (LINE_FIELDS, 4 * MIGRATION_PLANES * round_up(cells_radial, 8), cells_side),
                jnp.float32,
            )
        ],
        compiler_params=pltpu.CompilerParams(vmem_limit_bytes=32 * 2**20),
        name="eliminate",
    )(inner, lines, edge, *sent[::-1], *received[::-1], base_viscosity, forcing)


def join_kernel(mine_ref, message_ref, parts_ref, smoothed_ref, lines, other_ref):
    _, cells_lateral, cells_radial, cells_side = smoothed_ref.shape
    margin = MIGRATION_PLANES
    planes = cells_lateral + 2 * margin
    pitch = round_up(cells_radial, 8)
    valid = inside_grid((planes, cells_side), margin, cells_lateral)

    other_ref[LONG_FIELDS:] = jnp.zeros_like(other_ref[LONG_FIELDS:])
    for field in range(LONG_FIELDS + SHORT_FIELDS):
        rows, first, count = message_part(cells_lateral, field)
        other_ref[field, pl.ds(first, count), :] = message_ref[rows, :]

    face = RADIAL * 0.5 * (mine_ref[0] + other_ref[0])
    excess, other_excess = mine_ref[1], other_ref[1]
    scale = 1.0 / (excess * other_excess + face * (excess + other_excess))
    own_weight = (other_excess + face) * scale
    other_weight = (excess + face) * scale
    cross = face * scale

    def second_right(ref, q, around):
        terms = [ref[LONG_FIELDS + 3 + side] * there for side, there in enumerate(around)]
        return total_of([ref[LONG_FIELDS + q]] + terms)

    for q in range(3):
        right, other_right = mine_ref[2 + q], other_ref[2 + q]
        own = jnp.where(valid, own_weight * right + cross * other_right, 0.0)
        other = jnp.where(valid, other_weight * other_right + cross * right, 0.0)
        around = neighbours(own)
        right = second_right(mine_ref, q, around)
        other_right = second_right(other_ref, q, neighbours(other))
        value = own_weight * right + cross * other_right
        for t in range(cells_radial - 1, -1, -1):
            if t < cells_radial - 1:
                terms = [parts_ref[3 + side, t] * there for side, there in enumerate(around)]
                right = total_of([parts_ref[q, t]] + terms)
                value = right * parts_ref[SHORT_FIELDS, t] + parts_ref[SHORT_FIELDS + 1, t] * value
            row = outward_row(t, cells_radial)
            lines[pl.ds(row, cells_lateral, stride=pitch), :] = value[
                margin : margin + cells_lateral
            ]
        for x in range(cells_lateral):
            smoothed_ref[q, x] = lines[pl.ds(x * pitch, cells_radial), :]


def join(mine, message, parts, like):
    cells_lateral, cells_radial, cells_side = like.shape[1:]
    vmem = pl.BlockSpec(memory_space=pltpu.VMEM)
    return pl.pallas_call(
        join_kernel,
        out_shape=jax.ShapeDtypeStruct(like.shape, jnp.float32),
        in_specs=[vmem] * 3,
        out_specs=vmem,
        scratch_shapes=[
            pltpu.VMEM((cells_lateral * round_up(cells_radial, 8), cells_side), jnp.float32),
            pltpu.VMEM(mine.shape, jnp.float32),
        ],
        compiler_params=pltpu.CompilerParams(vmem_limit_bytes=32 * 2**20),
        name="join",
    )(mine, message, parts)


def extended(block, sides, width):
    for axis, dim in sides:
        count = lax.axis_size(axis)
        forward = [(i, i + 1) for i in range(count - 1)]
        backward = [(target, source) for source, target in forward]
        low = lax.ppermute(
            lax.slice_in_dim(block, block.shape[dim] - width, None, axis=dim), axis, forward
        )
        high = lax.ppermute(lax.slice_in_dim(block, 0, width, axis=dim), axis, backward)
        block = jnp.concatenate([low, block, high], axis=dim)
    return block


def block_factor(diagonal, lower_band, upper_band):
    pivots = []
    upper_scaled = []
    for row_index in range(diagonal.shape[1]):
        if row_index == 0:
            pivot_row = diagonal[:, 0]
        else:
            pivot_row = diagonal[:, row_index] - lower_band[:, row_index] * upper_scaled[-1]
        pivots.append(pivot_row)
        upper_scaled.append(upper_band[:, row_index] / pivot_row)
    return (pivots, upper_scaled)


def block_solve(pivots, upper_scaled, lower_band, right_side):
    row_total = len(pivots)
    modified = []
    for row_index in range(row_total):
        if row_index == 0:
            value_row = right_side[:, :, 0] / pivots[0]
        else:
            value_row = (
                right_side[:, :, row_index] - lower_band[:, row_index] * modified[-1]
            ) / pivots[row_index]
        modified.append(value_row)
    solved = [modified[-1]]
    for row_index in range(row_total - 2, -1, -1):
        solved.append(modified[row_index] - upper_scaled[row_index] * solved[-1])
    ordered = solved[::-1]
    return jnp.stack(ordered, 2)


def interface_solve(coefficients):
    column_total = coefficients.shape[2]

    def forward(carried, inputs):
        offset, carried_slope = carried
        left_first, right_first, left_last, right_last, free_first, free_last = inputs
        divisor = 1.0 - left_first * carried_slope
        first_fixed = (free_first + left_first * offset) / divisor
        first_slope = right_first / divisor
        next_offset = free_last + left_last * (offset + carried_slope * first_fixed)
        next_slope = left_last * carried_slope * first_slope + right_last
        return ((next_offset, next_slope), (first_fixed, first_slope, next_offset, next_slope))

    start_state = (
        jnp.zeros((3, column_total), jnp.float32),
        jnp.zeros((column_total,), jnp.float32),
    )
    scan_inputs = (
        coefficients[:, 0],
        coefficients[:, 1],
        coefficients[:, 2],
        coefficients[:, 3],
        coefficients[:, 4:7],
        coefficients[:, 7:10],
    )
    final_state, eliminated = lax.scan(forward, start_state, scan_inputs)

    def backward(first_next, inputs):
        fixed_first, slope_first, fixed_last, slope_last = inputs
        first_value = fixed_first + slope_first * first_next
        last_value = fixed_last + slope_last * first_next
        return (first_value, (first_value, last_value))

    final_first, values_pair = lax.scan(
        backward, jnp.zeros((3, column_total), jnp.float32), eliminated, reverse=True
    )
    first_values, last_values = values_pair
    nothing_row = jnp.zeros((1, 3, column_total), jnp.float32)
    from_below = jnp.concatenate([nothing_row, last_values[:-1]], 0)
    from_above = jnp.concatenate([first_values[1:], nothing_row], 0)
    return jnp.concatenate([from_below, from_above], 1)


def reduced_boundary(interface):
    gathered = lax.all_gather(interface, "rad", axis=0, tiled=True)
    solved = interface_solve(gathered)
    return lax.dynamic_index_in_dim(solved, lax.axis_index("rad"), 0, keepdims=False)


def many_blocks(values, cells, count, edge, received, base_viscosity, velocity, forcing):
    cells_lateral, cells_radial, cells_side = base_viscosity.shape
    moved_rows = MIGRATION_PLANES * cells_radial
    odd = lax.rem(lax.axis_index("lat"), 2) == 1
    from_below = jnp.where(odd, received[0], received[1])[: 3 * moved_rows]
    from_above = jnp.where(odd, received[1], received[0])[: 3 * moved_rows]
    edge = edge.reshape(3, 2, moved_rows, cells_side)
    below = edge[:, 0] + from_below.reshape(3, moved_rows, cells_side)
    above = edge[:, 1] + from_above.reshape(3, moved_rows, cells_side)
    shares = [
        (sums[1:] / (sums[0] + PRIOR_WEIGHT)).reshape(2, -1, cells_radial, cells_side)
        for sums in (below, above)
    ]
    inner, _ = inner_lines(count, values, cells, base_viscosity, velocity, forcing)
    basalt_share, melt_share = jnp.concatenate([shares[0], inner, shares[1]], 1)
    viscosity = base_viscosity * jnp.exp(
        CONTRAST_BASALT * basalt_share - CONTRAST_MELT * melt_share
    )
    viscosity_pad = extended(viscosity, (("lat", 0), ("rad", 1)), 1)
    side_pad = jnp.pad(viscosity, ((0, 0), (0, 0), (1, 1)))
    face_west = LATERAL * 0.5 * (viscosity + viscosity_pad[:-2, 1:-1])
    face_east = LATERAL * 0.5 * (viscosity + viscosity_pad[2:, 1:-1])
    face_south = LATERAL * 0.5 * (viscosity + side_pad[:, :, :-2])
    face_north = LATERAL * 0.5 * (viscosity + side_pad[:, :, 2:])
    face_below = RADIAL * 0.5 * (viscosity + viscosity_pad[1:-1, :-2])
    face_above = RADIAL * 0.5 * (viscosity + viscosity_pad[1:-1, 2:])
    diagonal = face_west + face_east + face_south + face_north + face_below + face_above
    source = jnp.concatenate([forcing[:2], (forcing[2] - BUOYANCY * basalt_share)[None]], 0)
    lower_band = -face_below
    upper_band = -face_above
    pivots, upper_scaled = block_factor(diagonal, lower_band, upper_band)
    radial_iota = lax.broadcasted_iota(jnp.int32, viscosity.shape, 1)
    response_side = jnp.stack(
        [
            jnp.where(radial_iota == 0, face_below, jnp.float32(0.0)),
            jnp.where(radial_iota == cells_radial - 1, face_above, jnp.float32(0.0)),
        ]
    )
    response = block_solve(pivots, upper_scaled, lower_band, response_side)
    current = velocity
    for sweep_index in range(SWEEPS):
        velocity_pad = extended(current, (("lat", 1),), 1)
        side_velocity = jnp.pad(current, ((0, 0), (0, 0), (0, 0), (1, 1)))
        right_side = (
            source
            + face_west * velocity_pad[:, :-2]
            + face_east * velocity_pad[:, 2:]
            + face_south * side_velocity[..., :-2]
            + face_north * side_velocity[..., 2:]
        )
        particular = block_solve(pivots, upper_scaled, lower_band, right_side)
        interface = jnp.concatenate(
            [response[:, :, 0], response[:, :, -1], particular[:, :, 0], particular[:, :, -1]], 0
        )
        interface = interface.reshape(1, 10, cells_lateral * cells_side)
        boundary = reduced_boundary(interface).reshape(6, cells_lateral, 1, cells_side)
        current = particular + response[0][None] * boundary[:3] + response[1][None] * boundary[3:]
    composition = jnp.stack([basalt_share, melt_share])
    return (current, composition)

def local(tracer_values, tracer_cell, tracer_count, base_viscosity, velocity, forcing):
    values, cells = dense_tracers(tracer_values, tracer_cell)
    edge, first, second, values, cells = outgoing_sums(
        tracer_count, values, cells, base_viscosity, velocity, forcing
    )
    sent = first, second
    received = pair_swaps(first, second)
    if lax.axis_size("rad") != 2:
        return many_blocks(
            values, cells, tracer_count, edge, received, base_viscosity, velocity, forcing
        )
    inner, lines = inner_lines(tracer_count, values, cells, base_viscosity, velocity, forcing)
    composition, mine, message, parts = eliminate(
        inner, lines, edge, sent, received, base_viscosity, forcing
    )
    other = lax.ppermute(message, "rad", [(0, 1), (1, 0)])
    return join(mine, other, parts, velocity), composition


def solution(mesh):
    return jax.shard_map(
        local,
        mesh=mesh,
        in_specs=(
            P("lat", "rad", None, None),
            P("lat", "rad", None),
            P("lat", "rad", None),
            P("lat", "rad", None),
            P(None, "lat", "rad", None),
            P(None, "lat", "rad", None),
        ),
        out_specs=(P(None, "lat", "rad", None), P(None, "lat", "rad", None)),
        check_vma=False,
    )
```

```python
import functools

import jax
import jax.numpy as jnp
from jax import lax
from jax.experimental import pallas as pl
from jax.experimental.pallas import tpu as pltpu
from jax.sharding import PartitionSpec as P

SWEEPS = 2
MIGRATION_PLANES = 2

LATERAL = 0.015625
RADIAL = 32.0
BUOYANCY = 0.1
PRIOR_WEIGHT = 0.5
CONTRAST_BASALT = 2.3
CONTRAST_MELT = 1.5

TILE_ROWS = 16


def round_up(value, multiple):
    return -(-value // multiple) * multiple


def split_index(index, count):
    if count & (count - 1) == 0:
        return lax.shift_right_logical(index, count.bit_length() - 1), index & (count - 1)
    quotient = lax.div(index, count)
    return quotient, index - quotient * count


def payload_sections(cells_radial):
    pair = MIGRATION_PLANES * cells_radial
    starts = [0, 3 * pair, 6 * pair, 9 * pair, 10 * pair]
    return starts, round_up(10 * pair + 3 * cells_radial, 8)


def spread_row(row):
    return jnp.broadcast_to(row, (TILE_ROWS, row.shape[1])).astype(jnp.bfloat16)


def hot_tiles(index, row_total):
    iota = lax.broadcasted_iota(jnp.int32, index.shape, 0)
    return [
        index == (iota + first).astype(jnp.float32).astype(jnp.bfloat16)
        for first in range(0, row_total, TILE_ROWS)
    ]


def hot_product(loads, high, low, high_rows, low_rows):
    left, right = [], []
    high, low = high.astype(jnp.float32), low.astype(jnp.float32)
    zero = jnp.zeros((TILE_ROWS, high.shape[1]), jnp.bfloat16)
    one = jnp.ones((TILE_ROWS, high.shape[1]), jnp.bfloat16)
    for row in range(high.shape[0]):
        pick = slice(row, row + 1)
        high_masks = hot_tiles(spread_row(high[pick]), high_rows)
        low_masks = hot_tiles(spread_row(low[pick]), low_rows)
        spread = [spread_row(load[pick]) for load in loads]
        left.append(
            jnp.concatenate(
                [jnp.where(mask, load, zero) for load in spread for mask in high_masks], 0
            )
        )
        right.append(jnp.concatenate([jnp.where(mask, one, zero) for mask in low_masks], 0))
    return lax.dot_general(
        jnp.concatenate(left, 1),
        jnp.concatenate(right, 1),
        (((1,), (1,)), ((), ())),
        preferred_element_type=jnp.float32,
    )


def edge_row(plane, plane_total, moved_total):
    inner = (plane >= moved_total) & (plane < plane_total - moved_total)
    last = plane - (plane_total - 2 * moved_total)
    return jnp.where(inner, -plane_total, jnp.where(plane < moved_total, plane, last))


def fold_moved(plane, side, plane_total, side_total):
    width, third = side_total // 4, plane_total // 3
    part = jnp.where(plane >= third, 1, 0) + jnp.where(plane >= 2 * third, 1, 0)
    other = side >= 3 * width
    high = jnp.where(other, plane_total + plane - part * third, plane)
    low = jnp.where(other, side - 3 * width + part * width, side)
    return high, low, plane_total + third, 3 * width


def unfold_moved(table, q, plane_total, side_total, put):
    width, third = side_total // 4, plane_total // 3
    rows = plane_total + third
    put(0, 0, table[pl.ds(q * rows, plane_total), 0 : 3 * width])
    for part in range(3):
        block = table[
            pl.ds(q * rows + plane_total, third), part * width : (part + 1) * width
        ]
        put(part * third, 3 * width, block)


def fold_inner(plane, side, plane_total, side_total):
    rows, width = plane_total * 5 // 6, side_total // 4
    part, rest = split_index(side, width)
    other = plane >= rows
    high = jnp.where(other, plane - rows + part * (plane_total - rows), plane)
    high = jnp.where(plane < plane_total, high, -1)
    low = jnp.where(other, side_total + rest, side)
    return high, low, rows, side_total + width


def unfold_inner(table, q, plane_total, side_total, put):
    rows, width = plane_total * 5 // 6, side_total // 4
    left = plane_total - rows
    put(0, 0, table[pl.ds(q * rows, rows), 0:side_total])
    for part in range(4):
        block = table[pl.ds(q * rows + part * left, left), side_total : side_total + width]
        put(rows, part * width, block)


def tracer_block(count, values, cells, first_row, block_rows, cells_side):
    rows = pl.ds(first_row, block_rows)
    lane_total = cells.shape[1]
    shape = (block_rows, lane_total)
    slot = (first_row + lax.broadcasted_iota(jnp.int32, shape, 0)) * lane_total
    slot = slot + lax.broadcasted_iota(jnp.int32, shape, 1)
    weight = jnp.where(slot < count, 0.5 + values[0, rows, :], jnp.float32(0.0))
    loads = [weight, weight * values[1, rows, :], weight * values[2, rows, :]]
    plane, side = split_index(cells[rows, :], cells_side)
    return loads, plane, side


def for_used_blocks(used, group_rows, block_rows, lane_total, late_copies, step):
    block_slots = block_rows * lane_total
    blocks = lax.div(used + (block_slots - 1), block_slots)
    blocks = jnp.clip(blocks, 1, group_rows // block_rows)

    def wait_late():
        for copy in late_copies:
            copy.wait()

    def repeat(index, carried):
        pl.when(index == 1)(wait_late)
        step(pl.multiple_of(index * block_rows, block_rows))
        return carried

    lax.fori_loop(0, blocks, repeat, 0)
    pl.when(blocks == 1)(wait_late)


VISCOSITY, VELOCITY, SOURCE, LINE_FIELDS = 0, 1, 4, 7


def composition_of(cell_sums, base):
    scale = 1.0 / (cell_sums[0] + PRIOR_WEIGHT)
    basalt_share, melt_share = cell_sums[1] * scale, cell_sums[2] * scale
    weakening = jnp.exp(CONTRAST_BASALT * basalt_share - CONTRAST_MELT * melt_share)
    return basalt_share, melt_share, base * weakening


def outward_row(t, cells_radial):
    return jnp.where(lax.axis_index("rad") == 0, t, cells_radial - 1 - t)


class Fetches:
    def __init__(self, semaphores):
        self.semaphores = semaphores
        self.copies = []

    def start(self, source, target):
        copy = pltpu.make_async_copy(source, target, self.semaphores.at[len(self.copies)])
        copy.start()
        self.copies.append(copy)

    def wait(self, first, last):
        for copy in self.copies[first:last]:
            copy.wait()


def has_partners():
    lateral, count = lax.axis_index("lat"), lax.axis_size("lat")
    odd = lax.rem(lateral, 2) == 1
    above, below = lateral + 1 < count, lateral > 0
    return jnp.logical_or(odd, above), jnp.where(odd, above, below)


def outgoing_kernel(
    block_rows,
    counts_hbm,
    values_hbm,
    cells_hbm,
    base_hbm,
    velocity_hbm,
    forcing_hbm,
    edge_ref,
    first_ref,
    second_ref,
    stay_values,
    stay_cells,
    counts,
    lower_values,
    lower_cells,
    upper_values,
    upper_cells,
    base,
    velocity,
    forcing,
    moved_sums,
    semaphores,
):
    cells_lateral, cells_radial, cells_side = base_hbm.shape
    plane_total = cells_lateral * cells_radial
    moved_planes = MIGRATION_PLANES * cells_radial
    group_rows, lane_total = stay_cells.shape
    groups = (
        (lower_values, lower_cells),
        (stay_values, stay_cells),
        (upper_values, upper_cells),
    )

    fetches = Fetches(semaphores)
    fetches.start(counts_hbm, counts)
    for first_row, rows in ((0, block_rows), (block_rows, group_rows - block_rows)):
        part = pl.ds(first_row, rows)
        for group, (values, cells) in enumerate(groups):
            fetches.start(cells_hbm.at[group, part], cells.at[part])
            fetches.start(values_hbm.at[:, group, part], values.at[:, part])
    for upward in (0, 1):
        outer = pl.ds((cells_lateral - MIGRATION_PLANES) * upward, MIGRATION_PLANES)
        fetches.start(base_hbm.at[outer], base.at[upward])
        fetches.start(velocity_hbm.at[:, outer], velocity.at[upward])
        outermost = pl.ds((cells_lateral - 1) * upward, 1)
        fetches.start(forcing_hbm.at[:, outermost], forcing.at[upward])

    edge_ref[...] = jnp.zeros_like(edge_ref)
    moved_sums[...] = jnp.zeros_like(moved_sums)

    def step(first_row):
        def block_of(group):
            values, cells = groups[group]
            count = counts[0, 0, group]
            return tracer_block(count, values, cells, first_row, block_rows, cells_side)

        loads, plane, side = block_of(1)
        row = edge_row(plane, plane_total, moved_planes)
        edge_ref[...] += hot_product(loads, row, side, 2 * moved_planes, cells_side)
        for slot, group in enumerate((0, 2)):
            loads, plane, side = block_of(group)
            if group == 0:
                plane = plane - (plane_total - moved_planes)
            moved_sums[slot] += hot_product(
                loads, *fold_moved(plane, side, moved_planes, cells_side)
            )

    fetches.wait(0, 7)
    used = jnp.maximum(jnp.maximum(counts[0, 0, 0], counts[0, 0, 1]), counts[0, 0, 2])
    for_used_blocks(used, group_rows, block_rows, lane_total, fetches.copies[7:13], step)
    fetches.wait(13, None)

    starts, rows_total = payload_sections(cells_radial)
    unused = starts[4] + 3 * cells_radial

    def fill(payload, upward):
        for q in range(3):

            def put_moved(plane, column, block):
                height, width = block.shape
                rows = pl.ds(starts[0] + q * moved_planes + plane, height)
                payload[rows, column : column + width] = block

            unfold_moved(moved_sums.at[upward], q, moved_planes, cells_side, put_moved)
            payload[pl.ds(starts[1] + q * moved_planes, moved_planes), :] = edge_ref[
                pl.ds((2 * q + upward) * moved_planes, moved_planes), :
            ]
            for offset in range(MIGRATION_PLANES):
                row = starts[2] + q * moved_planes + offset * cells_radial
                payload[pl.ds(row, cells_radial), :] = velocity[upward, q, offset]
            row = starts[4] + q * cells_radial
            payload[pl.ds(row, cells_radial), :] = forcing[upward, q, 0]
        for offset in range(MIGRATION_PLANES):
            row = starts[3] + offset * cells_radial
            payload[pl.ds(row, cells_radial), :] = base[upward, offset]
        if unused < rows_total:
            payload[unused:, :] = jnp.zeros((rows_total - unused, cells_side), jnp.float32)

    odd = lax.rem(lax.axis_index("lat"), 2) == 1

    @pl.when(odd)
    def _():
        fill(first_ref, 0)
        fill(second_ref, 1)

    @pl.when(jnp.logical_not(odd))
    def _():
        fill(first_ref, 1)
        fill(second_ref, 0)

    for payload, exists in zip((first_ref, second_ref), has_partners()):

        @pl.when(jnp.logical_not(exists))
        def _():
            payload[...] = jnp.zeros_like(payload)


def inner_kernel(
    block_rows,
    counts_hbm,
    values_ref,
    cells_ref,
    base_ref,
    velocity_ref,
    forcing_ref,
    composition_ref,
    lines_ref,
    counts,
    table,
    sums,
    fields,
    semaphores,
):
    cells_lateral, cells_radial, cells_side = base_ref.shape
    margin = MIGRATION_PLANES
    planes = cells_lateral + 2 * margin
    pitch = round_up(cells_radial, 8)
    moved_planes = margin * cells_radial
    inner = cells_lateral - 2 * margin
    inner_planes = inner * cells_radial
    group_rows, lane_total = cells_ref.shape
    fetches = Fetches(semaphores)
    fetches.start(counts_hbm, counts)
    table[...] = jnp.zeros_like(table)

    nothing = jnp.zeros((cells_radial, cells_side), jnp.float32)

    def put(field, plane, value):
        fields[field, pl.ds(plane * pitch, cells_radial), :] = value

    def lay_out(those):
        for field in those:
            for t in range(cells_radial):
                row = outward_row(t, cells_radial)
                lines_ref[field, t] = fields[field, pl.ds(row, planes, stride=pitch), :]

    for plane in range(planes):
        x = plane - margin
        own = 0 <= x < cells_lateral
        for q in range(3):
            put(VELOCITY + q, plane, velocity_ref[q, x] if own else nothing)
        for q in range(2):
            put(SOURCE + q, plane, forcing_ref[q, x] if own else nothing)
    late = VISCOSITY, SOURCE + 2
    lay_out(field for field in range(LINE_FIELDS) if field not in late)

    def step(first_row):
        loads, plane, side = tracer_block(
            count, values_ref, cells_ref, first_row, block_rows, cells_side
        )
        table[...] += hot_product(
            loads, *fold_inner(plane - moved_planes, side, inner_planes, cells_side)
        )

    fetches.wait(0, None)
    count = counts[0, 0, 1]
    for_used_blocks(count, group_rows, block_rows, lane_total, [], step)

    for q in range(3):

        def put_sums(plane, column, block):
            height, width = block.shape
            sums[q, pl.ds(plane, height), column : column + width] = block

        unfold_inner(table, q, inner_planes, cells_side, put_sums)
    for plane in range(planes):
        x = plane - 2 * margin
        viscosity, source = nothing, nothing
        if 0 <= x < inner:
            rows = pl.ds(x * cells_radial, cells_radial)
            cell_sums = [sums[q, rows, :] for q in range(3)]
            basalt_share, melt_share, viscosity = composition_of(cell_sums, base_ref[x + margin])
            source = forcing_ref[2, x + margin] - BUOYANCY * basalt_share
            composition_ref[0, x] = basalt_share
            composition_ref[1, x] = melt_share
        put(VISCOSITY, plane, viscosity)
        put(SOURCE + 2, plane, source)
    lay_out(late)


BLOCK_ROWS = 64


def dense_tracers(tracer_values, tracer_cell):
    lane_total = 128
    return tracer_values.reshape(3, 3, -1, lane_total), tracer_cell.reshape(3, -1, lane_total)


def outgoing_sums(tracer_count, values, cells, base_viscosity, velocity, forcing):
    cells_lateral, cells_radial, cells_side = base_viscosity.shape
    moved_planes = MIGRATION_PLANES * cells_radial
    group_rows, lane_total = cells.shape[1:]
    block_rows = min(BLOCK_ROWS, group_rows // 2)
    _, payload_rows = payload_sections(cells_radial)
    hbm = pl.BlockSpec(memory_space=pltpu.HBM)
    vmem = pl.BlockSpec(memory_space=pltpu.VMEM)
    payload = jax.ShapeDtypeStruct((payload_rows, cells_side), jnp.float32)
    group = ((3, group_rows, lane_total), jnp.float32), ((group_rows, lane_total), jnp.int32)
    outer_planes = (MIGRATION_PLANES, cells_radial, cells_side)
    return pl.pallas_call(
        functools.partial(outgoing_kernel, block_rows),
        out_shape=(
            jax.ShapeDtypeStruct((6 * moved_planes, cells_side), jnp.float32),
            payload,
            payload,
            *(jax.ShapeDtypeStruct(*array) for array in group),
        ),
        in_specs=[hbm] * 6,
        out_specs=(vmem,) * 5,
        scratch_shapes=[
            pltpu.SMEM(tracer_count.shape, jnp.int32),
            *(pltpu.VMEM(*array) for array in group + group),
            pltpu.VMEM((2,) + outer_planes, jnp.float32),
            pltpu.VMEM((2, 3) + outer_planes, jnp.float32),
            pltpu.VMEM((2, 3, 1, cells_radial, cells_side), jnp.float32),
            pltpu.VMEM((2, 4 * moved_planes, cells_side * 3 // 4), jnp.float32),
            pltpu.SemaphoreType.DMA((19,)),
        ],
        compiler_params=pltpu.CompilerParams(vmem_limit_bytes=32 * 2**20),
        cost_estimate=pl.CostEstimate(
            flops=30 * group_rows * lane_total * moved_planes * cells_side,
            bytes_accessed=4 * (values.size + cells.size),
            transcendentals=0,
        ),
        name="outgoing_sums",
    )(
        *(
            pltpu.with_memory_space_constraint(array, pltpu.HBM)
            for array in (tracer_count, values, cells, base_viscosity, velocity, forcing)
        )
    )


def inner_lines(tracer_count, values, cells, base_viscosity, velocity, forcing):
    cells_lateral, cells_radial, cells_side = base_viscosity.shape
    planes = cells_lateral + 2 * MIGRATION_PLANES
    inner = cells_lateral - 2 * MIGRATION_PLANES
    inner_planes = inner * cells_radial
    group_rows, lane_total = cells.shape
    block_rows = min(BLOCK_ROWS, group_rows // 2)
    vmem = pl.BlockSpec(memory_space=pltpu.VMEM)
    return pl.pallas_call(
        functools.partial(inner_kernel, block_rows),
        out_shape=(
            jax.ShapeDtypeStruct((2, inner, cells_radial, cells_side), jnp.float32),
            jax.ShapeDtypeStruct((LINE_FIELDS, cells_radial, planes, cells_side), jnp.float32),
        ),
        in_specs=[pl.BlockSpec(memory_space=pltpu.HBM)] + [vmem] * 5,
        out_specs=(vmem, vmem),
        scratch_shapes=[
            pltpu.SMEM(tracer_count.shape, jnp.int32),
            pltpu.VMEM((3 * (inner_planes * 5 // 6), cells_side * 5 // 4), jnp.float32),
            pltpu.VMEM((3, inner_planes, cells_side), jnp.float32),
            pltpu.VMEM((LINE_FIELDS, planes * round_up(cells_radial, 8), cells_side), jnp.float32),
            pltpu.SemaphoreType.DMA((1,)),
        ],
        compiler_params=pltpu.CompilerParams(vmem_limit_bytes=32 * 2**20),
        cost_estimate=pl.CostEstimate(
            flops=6 * group_rows * lane_total * inner * cells_radial * cells_side,
            bytes_accessed=4 * (values.size + cells.size),
            transcendentals=0,
        ),
        name="inner_lines",
    )(
        pltpu.with_memory_space_constraint(tracer_count, pltpu.HBM),
        values,
        cells,
        base_viscosity,
        velocity,
        forcing,
    )


def pair_swaps(first, second):
    count = lax.axis_size("lat")
    received = []
    for payload, start in ((second, 1), (first, 0)):
        target = list(range(count))
        for low in range(start, count - 1, 2):
            target[low], target[low + 1] = low + 1, low
        received.append(lax.ppermute(payload, "lat", list(enumerate(target))))
    return received[::-1]


def shift_planes(block, step):
    return pltpu.roll(block, step % block.shape[0], 0)


def shift_side(block, step):
    return pltpu.roll(block, step % block.shape[1], 1)


def neighbours(block):
    return (
        shift_planes(block, 1),
        shift_planes(block, -1),
        shift_side(block, 1),
        shift_side(block, -1),
    )


def inside_side(values):
    lane = lax.broadcasted_iota(jnp.int32, values[2].shape, 1)
    lower = jnp.where(lane > 0, values[2], 0.0)
    upper = jnp.where(lane < lane.shape[1] - 1, values[3], 0.0)
    return values[0], values[1], lower, upper


def total_of(terms):
    result = terms[0]
    for term in terms[1:]:
        result = result + term
    return result


def inside_grid(shape, margin, cells_lateral):
    plane = lax.broadcasted_iota(jnp.int32, shape, 0)
    lateral = lax.axis_index("lat")
    first = jnp.where(lateral == 0, margin, 1)
    last = jnp.where(lateral == lax.axis_size("lat") - 1, margin + cells_lateral, shape[0] - 1)
    return (plane >= first) & (plane < last)


LONG_FIELDS, SHORT_FIELDS = 5, 7


def message_rows(cells_lateral):
    planes = cells_lateral + 2 * MIGRATION_PLANES
    return round_up(LONG_FIELDS * planes + SHORT_FIELDS * cells_lateral, 8)


def message_part(cells_lateral, field):
    planes = cells_lateral + 2 * MIGRATION_PLANES
    if field < LONG_FIELDS:
        return pl.ds(field * planes, planes), 0, planes
    first = LONG_FIELDS * planes + (field - LONG_FIELDS) * cells_lateral
    return pl.ds(first, cells_lateral), MIGRATION_PLANES, cells_lateral


def solve_lines(radial, cells_radial, valid, keep, keep_part):
    last = cells_radial - 1
    viscosity = [radial(VISCOSITY, t) for t in range(cells_radial)]
    lateral_faces, lateral_sums = [], []
    for here in viscosity:
        faces = [LATERAL * 0.5 * (here + there) for there in inside_side(neighbours(here))]
        lateral_sums.append(total_of(faces))
        lateral_faces.append(inside_side(faces))
    radial_faces = [RADIAL * 0.5 * viscosity[0]] + [
        RADIAL * 0.5 * (viscosity[t - 1] + viscosity[t]) for t in range(1, cells_radial)
    ]

    excess = lateral_sums[0] + radial_faces[0]
    inverse, coupling = [], []
    for t in range(last):
        inverse.append(1.0 / (excess + radial_faces[t + 1]))
        coupling.append(radial_faces[t + 1] * inverse[t])
        excess = lateral_sums[t + 1] + coupling[t] * excess

    def lateral_terms(t, around):
        return [face * there for face, there in zip(lateral_faces[t], around)]

    def forward(right_side):
        eliminated = [right_side[0]]
        for t in range(1, cells_radial):
            eliminated.append(right_side[t] + coupling[t - 1] * eliminated[t - 1])
        return eliminated

    def backward(eliminated):
        solved = [jnp.zeros_like(excess)]
        for t in range(last - 1, -1, -1):
            solved.append(eliminated[t] * inverse[t] + coupling[t] * solved[-1])
        return solved[::-1]

    response = [jnp.ones_like(excess)]
    for t in range(last - 1, -1, -1):
        response.append(coupling[t] * response[-1])
    response = response[::-1]

    def finish(part, eliminated):
        keep(LONG_FIELDS + part, eliminated[last])
        for t, value in enumerate(eliminated[:last]):
            keep_part(part, t, value)

    keep(0, viscosity[last])
    keep(1, excess)
    for q in range(3):
        source = [radial(SOURCE + q, t) for t in range(cells_radial)]
        eliminated = forward(
            [
                total_of([source[t]] + lateral_terms(t, neighbours(radial(VELOCITY + q, t))))
                for t in range(cells_radial)
            ]
        )
        keep(2 + q, eliminated[last])
        particular = [jnp.where(valid, value, 0.0) for value in backward(eliminated)]
        finish(
            q,
            forward(
                [
                    total_of([source[t]] + lateral_terms(t, neighbours(particular[t])))
                    for t in range(cells_radial)
                ]
            ),
        )
    around = [neighbours(jnp.where(valid, value, 0.0)) for value in response]
    for side in range(4):
        finish(
            3 + side,
            forward([lateral_faces[t][side] * around[t][side] for t in range(cells_radial)]),
        )
    for t in range(last):
        keep_part(SHORT_FIELDS, t, inverse[t])
        keep_part(SHORT_FIELDS + 1, t, coupling[t])


def eliminate_kernel(
    inner_ref,
    lines_ref,
    edge_ref,
    second_ref,
    first_ref,
    from_second_ref,
    from_first_ref,
    base_ref,
    forcing_ref,
    composition_ref,
    mine_ref,
    message_ref,
    parts_ref,
    fields,
):
    cells_lateral, cells_radial, cells_side = base_ref.shape
    margin = MIGRATION_PLANES
    planes = cells_lateral + 2 * margin
    pitch = round_up(cells_radial, 8)
    moved_planes = margin * cells_radial
    starts, _ = payload_sections(cells_radial)
    odd = lax.rem(lax.axis_index("lat"), 2) == 1

    def sent(upward, start):
        part = pl.ds(start, cells_radial)
        mine_first = odd if not upward else jnp.logical_not(odd)
        return jnp.where(mine_first, first_ref[part, :], second_ref[part, :])

    def arrived(from_above, start):
        part = pl.ds(start, cells_radial)
        is_first = odd if not from_above else jnp.logical_not(odd)
        return jnp.where(is_first, from_first_ref[part, :], from_second_ref[part, :])

    outer = 2 * margin

    def put(field, slot, value):
        fields[field, pl.ds(slot * pitch, cells_radial), :] = value

    for above in (False, True):
        for offset in range(margin):
            shift = offset * cells_radial
            halo = offset + (outer + margin if above else 0)
            own = offset + (outer if above else margin)
            x = offset + (cells_lateral - margin if above else 0)
            halo_sums, own_sums = [], []
            for q in range(3):
                row = q * moved_planes + shift
                rows = pl.ds((2 * q + int(above)) * moved_planes + shift, cells_radial)
                own_sums.append(edge_ref[rows, :] + arrived(above, starts[0] + row))
                halo_sums.append(sent(above, starts[0] + row) + arrived(above, starts[1] + row))
                put(VELOCITY + q, halo, arrived(above, starts[2] + row))
            basalt_share, melt_share, viscosity = composition_of(own_sums, base_ref[x])
            composition_ref[0, x] = basalt_share
            composition_ref[1, x] = melt_share
            put(VISCOSITY, own, viscosity)
            put(SOURCE + 2, own, forcing_ref[2, x] - BUOYANCY * basalt_share)
            basalt_share, _, viscosity = composition_of(
                halo_sums, arrived(above, starts[3] + shift)
            )
            put(VISCOSITY, halo, viscosity)
            beside = offset == (0 if above else margin - 1)
            for q in range(3):
                source = jnp.zeros_like(viscosity)
                if beside:
                    source = arrived(above, starts[4] + q * cells_radial)
                    if q == 2:
                        source = source - BUOYANCY * basalt_share
                put(SOURCE + q, halo, source)
    for x in range(margin, cells_lateral - margin):
        for q in range(2):
            composition_ref[q, x] = inner_ref[q, x - margin]

    def radial(field, t):
        replaced = outer if field in (VISCOSITY, SOURCE + 2) else margin
        plane = lax.broadcasted_iota(jnp.int32, (planes, cells_side), 0)
        own = (plane >= replaced) & (plane < planes - replaced)
        row = outward_row(t, cells_radial)
        edges = fields[field, pl.ds(row, 2 * outer, stride=pitch), :]
        if 2 * outer * 2 == planes:
            edges = jnp.concatenate([edges, edges], 0)
        else:
            gap = jnp.zeros((planes - 2 * outer, cells_side), jnp.float32)
            edges = jnp.concatenate([edges[:outer], gap, edges[outer:]], 0)
        return jnp.where(own, lines_ref[field, t], edges)

    unused = LONG_FIELDS * planes + SHORT_FIELDS * cells_lateral
    if unused < message_ref.shape[0]:
        message_ref[unused:, :] = jnp.zeros((message_ref.shape[0] - unused, cells_side), jnp.float32)

    def keep(field, value):
        rows, first, count = message_part(cells_lateral, field)
        mine_ref[field] = value
        message_ref[rows, :] = value[first : first + count]

    def keep_part(part, t, value):
        parts_ref[part, t] = value

    valid = inside_grid((planes, cells_side), margin, cells_lateral)
    solve_lines(radial, cells_radial, valid, keep, keep_part)


def eliminate(inner, lines, edge, sent, received, base_viscosity, forcing):
    cells_lateral, cells_radial, cells_side = base_viscosity.shape
    planes = cells_lateral + 2 * MIGRATION_PLANES
    vmem = pl.BlockSpec(memory_space=pltpu.VMEM)
    line = (planes, cells_side)
    return pl.pallas_call(
        eliminate_kernel,
        out_shape=(
            jax.ShapeDtypeStruct((2,) + base_viscosity.shape, jnp.float32),
            jax.ShapeDtypeStruct((LONG_FIELDS + SHORT_FIELDS,) + line, jnp.float32),
            jax.ShapeDtypeStruct((message_rows(cells_lateral), cells_side), jnp.float32),
            jax.ShapeDtypeStruct((SHORT_FIELDS + 2, cells_radial - 1) + line, jnp.float32),
        ),
        in_specs=[vmem] * 9,
        out_specs=(vmem,) * 4,
        scratch_shapes=[
            pltpu.VMEM(
                (LINE_FIELDS, 4 * MIGRATION_PLANES * round_up(cells_radial, 8), cells_side),
                jnp.float32,
            )
        ],
        compiler_params=pltpu.CompilerParams(vmem_limit_bytes=32 * 2**20),
        name="eliminate",
    )(inner, lines, edge, *sent[::-1], *received[::-1], base_viscosity, forcing)


def join_kernel(mine_ref, message_ref, parts_ref, smoothed_ref, lines, other_ref):
    _, cells_lateral, cells_radial, cells_side = smoothed_ref.shape
    margin = MIGRATION_PLANES
    planes = cells_lateral + 2 * margin
    pitch = round_up(cells_radial, 8)
    valid = inside_grid((planes, cells_side), margin, cells_lateral)

    other_ref[LONG_FIELDS:] = jnp.zeros_like(other_ref[LONG_FIELDS:])
    for field in range(LONG_FIELDS + SHORT_FIELDS):
        rows, first, count = message_part(cells_lateral, field)
        other_ref[field, pl.ds(first, count), :] = message_ref[rows, :]

    face = RADIAL * 0.5 * (mine_ref[0] + other_ref[0])
    excess, other_excess = mine_ref[1], other_ref[1]
    scale = 1.0 / (excess * other_excess + face * (excess + other_excess))
    own_weight = (other_excess + face) * scale
    other_weight = (excess + face) * scale
    cross = face * scale

    def second_right(ref, q, around):
        terms = [ref[LONG_FIELDS + 3 + side] * there for side, there in enumerate(around)]
        return total_of([ref[LONG_FIELDS + q]] + terms)

    for q in range(3):
        right, other_right = mine_ref[2 + q], other_ref[2 + q]
        own = jnp.where(valid, own_weight * right + cross * other_right, 0.0)
        other = jnp.where(valid, other_weight * other_right + cross * right, 0.0)
        around = neighbours(own)
        right = second_right(mine_ref, q, around)
        other_right = second_right(other_ref, q, neighbours(other))
        value = own_weight * right + cross * other_right
        for t in range(cells_radial - 1, -1, -1):
            if t < cells_radial - 1:
                terms = [parts_ref[3 + side, t] * there for side, there in enumerate(around)]
                right = total_of([parts_ref[q, t]] + terms)
                value = right * parts_ref[SHORT_FIELDS, t] + parts_ref[SHORT_FIELDS + 1, t] * value
            row = outward_row(t, cells_radial)
            lines[pl.ds(row, cells_lateral, stride=pitch), :] = value[
                margin : margin + cells_lateral
            ]
        for x in range(cells_lateral):
            smoothed_ref[q, x] = lines[pl.ds(x * pitch, cells_radial), :]


def join(mine, message, parts, like):
    cells_lateral, cells_radial, cells_side = like.shape[1:]
    vmem = pl.BlockSpec(memory_space=pltpu.VMEM)
    return pl.pallas_call(
        join_kernel,
        out_shape=jax.ShapeDtypeStruct(like.shape, jnp.float32),
        in_specs=[vmem] * 3,
        out_specs=vmem,
        scratch_shapes=[
            pltpu.VMEM((cells_lateral * round_up(cells_radial, 8), cells_side), jnp.float32),
            pltpu.VMEM(mine.shape, jnp.float32),
        ],
        compiler_params=pltpu.CompilerParams(vmem_limit_bytes=32 * 2**20),
        name="join",
    )(mine, message, parts)


def extended(block, sides, width):
    for axis, dim in sides:
        count = lax.axis_size(axis)
        forward = [(i, i + 1) for i in range(count - 1)]
        backward = [(target, source) for source, target in forward]
        low = lax.ppermute(
            lax.slice_in_dim(block, block.shape[dim] - width, None, axis=dim), axis, forward
        )
        high = lax.ppermute(lax.slice_in_dim(block, 0, width, axis=dim), axis, backward)
        block = jnp.concatenate([low, block, high], axis=dim)
    return block


def block_factor(diagonal, lower_band, upper_band):
    pivots = []
    upper_scaled = []
    for row_index in range(diagonal.shape[1]):
        if row_index == 0:
            pivot_row = diagonal[:, 0]
        else:
            pivot_row = diagonal[:, row_index] - lower_band[:, row_index] * upper_scaled[-1]
        pivots.append(pivot_row)
        upper_scaled.append(upper_band[:, row_index] / pivot_row)
    return (pivots, upper_scaled)


def block_solve(pivots, upper_scaled, lower_band, right_side):
    row_total = len(pivots)
    modified = []
    for row_index in range(row_total):
        if row_index == 0:
            value_row = right_side[:, :, 0] / pivots[0]
        else:
            value_row = (
                right_side[:, :, row_index] - lower_band[:, row_index] * modified[-1]
            ) / pivots[row_index]
        modified.append(value_row)
    solved = [modified[-1]]
    for row_index in range(row_total - 2, -1, -1):
        solved.append(modified[row_index] - upper_scaled[row_index] * solved[-1])
    ordered = solved[::-1]
    return jnp.stack(ordered, 2)


def interface_solve(coefficients):
    column_total = coefficients.shape[2]

    def forward(carried, inputs):
        offset, carried_slope = carried
        left_first, right_first, left_last, right_last, free_first, free_last = inputs
        divisor = 1.0 - left_first * carried_slope
        first_fixed = (free_first + left_first * offset) / divisor
        first_slope = right_first / divisor
        next_offset = free_last + left_last * (offset + carried_slope * first_fixed)
        next_slope = left_last * carried_slope * first_slope + right_last
        return ((next_offset, next_slope), (first_fixed, first_slope, next_offset, next_slope))

    start_state = (
        jnp.zeros((3, column_total), jnp.float32),
        jnp.zeros((column_total,), jnp.float32),
    )
    scan_inputs = (
        coefficients[:, 0],
        coefficients[:, 1],
        coefficients[:, 2],
        coefficients[:, 3],
        coefficients[:, 4:7],
        coefficients[:, 7:10],
    )
    final_state, eliminated = lax.scan(forward, start_state, scan_inputs)

    def backward(first_next, inputs):
        fixed_first, slope_first, fixed_last, slope_last = inputs
        first_value = fixed_first + slope_first * first_next
        last_value = fixed_last + slope_last * first_next
        return (first_value, (first_value, last_value))

    final_first, values_pair = lax.scan(
        backward, jnp.zeros((3, column_total), jnp.float32), eliminated, reverse=True
    )
    first_values, last_values = values_pair
    nothing_row = jnp.zeros((1, 3, column_total), jnp.float32)
    from_below = jnp.concatenate([nothing_row, last_values[:-1]], 0)
    from_above = jnp.concatenate([first_values[1:], nothing_row], 0)
    return jnp.concatenate([from_below, from_above], 1)


def reduced_boundary(interface):
    gathered = lax.all_gather(interface, "rad", axis=0, tiled=True)
    solved = interface_solve(gathered)
    return lax.dynamic_index_in_dim(solved, lax.axis_index("rad"), 0, keepdims=False)


def many_blocks(values, cells, count, edge, received, base_viscosity, velocity, forcing):
    cells_lateral, cells_radial, cells_side = base_viscosity.shape
    moved_rows = MIGRATION_PLANES * cells_radial
    odd = lax.rem(lax.axis_index("lat"), 2) == 1
    from_below = jnp.where(odd, received[0], received[1])[: 3 * moved_rows]
    from_above = jnp.where(odd, received[1], received[0])[: 3 * moved_rows]
    edge = edge.reshape(3, 2, moved_rows, cells_side)
    below = edge[:, 0] + from_below.reshape(3, moved_rows, cells_side)
    above = edge[:, 1] + from_above.reshape(3, moved_rows, cells_side)
    shares = [
        (sums[1:] / (sums[0] + PRIOR_WEIGHT)).reshape(2, -1, cells_radial, cells_side)
        for sums in (below, above)
    ]
    inner, _ = inner_lines(count, values, cells, base_viscosity, velocity, forcing)
    basalt_share, melt_share = jnp.concatenate([shares[0], inner, shares[1]], 1)
    viscosity = base_viscosity * jnp.exp(
        CONTRAST_BASALT * basalt_share - CONTRAST_MELT * melt_share
    )
    viscosity_pad = extended(viscosity, (("lat", 0), ("rad", 1)), 1)
    side_pad = jnp.pad(viscosity, ((0, 0), (0, 0), (1, 1)))
    face_west = LATERAL * 0.5 * (viscosity + viscosity_pad[:-2, 1:-1])
    face_east = LATERAL * 0.5 * (viscosity + viscosity_pad[2:, 1:-1])
    face_south = LATERAL * 0.5 * (viscosity + side_pad[:, :, :-2])
    face_north = LATERAL * 0.5 * (viscosity + side_pad[:, :, 2:])
    face_below = RADIAL * 0.5 * (viscosity + viscosity_pad[1:-1, :-2])
    face_above = RADIAL * 0.5 * (viscosity + viscosity_pad[1:-1, 2:])
    diagonal = face_west + face_east + face_south + face_north + face_below + face_above
    source = jnp.concatenate([forcing[:2], (forcing[2] - BUOYANCY * basalt_share)[None]], 0)
    lower_band = -face_below
    upper_band = -face_above
    pivots, upper_scaled = block_factor(diagonal, lower_band, upper_band)
    radial_iota = lax.broadcasted_iota(jnp.int32, viscosity.shape, 1)
    response_side = jnp.stack(
        [
            jnp.where(radial_iota == 0, face_below, jnp.float32(0.0)),
            jnp.where(radial_iota == cells_radial - 1, face_above, jnp.float32(0.0)),
        ]
    )
    response = block_solve(pivots, upper_scaled, lower_band, response_side)
    current = velocity
    for sweep_index in range(SWEEPS):
        velocity_pad = extended(current, (("lat", 1),), 1)
        side_velocity = jnp.pad(current, ((0, 0), (0, 0), (0, 0), (1, 1)))
        right_side = (
            source
            + face_west * velocity_pad[:, :-2]
            + face_east * velocity_pad[:, 2:]
            + face_south * side_velocity[..., :-2]
            + face_north * side_velocity[..., 2:]
        )
        particular = block_solve(pivots, upper_scaled, lower_band, right_side)
        interface = jnp.concatenate(
            [response[:, :, 0], response[:, :, -1], particular[:, :, 0], particular[:, :, -1]], 0
        )
        interface = interface.reshape(1, 10, cells_lateral * cells_side)
        boundary = reduced_boundary(interface).reshape(6, cells_lateral, 1, cells_side)
        current = particular + response[0][None] * boundary[:3] + response[1][None] * boundary[3:]
    composition = jnp.stack([basalt_share, melt_share])
    return (current, composition)

def local(tracer_values, tracer_cell, tracer_count, base_viscosity, velocity, forcing):
    values, cells = dense_tracers(tracer_values, tracer_cell)
    edge, first, second, values, cells = outgoing_sums(
        tracer_count, values, cells, base_viscosity, velocity, forcing
    )
    sent = first, second
    received = pair_swaps(first, second)
    if lax.axis_size("rad") != 2:
        return many_blocks(
            values, cells, tracer_count, edge, received, base_viscosity, velocity, forcing
        )
    inner, lines = inner_lines(tracer_count, values, cells, base_viscosity, velocity, forcing)
    composition, mine, message, parts = eliminate(
        inner, lines, edge, sent, received, base_viscosity, forcing
    )
    other = lax.ppermute(message, "rad", [(0, 1), (1, 0)])
    return join(mine, other, parts, velocity), composition


def solution(mesh):
    return jax.shard_map(
        local,
        mesh=mesh,
        in_specs=(
            P("lat", "rad", None, None),
            P("lat", "rad", None),
            P("lat", "rad", None),
            P("lat", "rad", None),
            P(None, "lat", "rad", None),
            P(None, "lat", "rad", None),
        ),
        out_specs=(P(None, "lat", "rad", None), P(None, "lat", "rad", None)),
        check_vma=False,
    )
```

```python
import functools

import jax
import jax.numpy as jnp
from jax import lax
from jax.experimental import pallas as pl
from jax.experimental.pallas import tpu as pltpu
from jax.sharding import PartitionSpec as P

SWEEPS = 2
MIGRATION_PLANES = 2

LATERAL = 0.015625
RADIAL = 32.0
BUOYANCY = 0.1
PRIOR_WEIGHT = 0.5
CONTRAST_BASALT = 2.3
CONTRAST_MELT = 1.5

TILE_ROWS = 16


def round_up(value, multiple):
    return -(-value // multiple) * multiple


def split_index(index, count):
    if count & (count - 1) == 0:
        return lax.shift_right_logical(index, count.bit_length() - 1), index & (count - 1)
    quotient = lax.div(index, count)
    return quotient, index - quotient * count


def payload_sections(cells_radial):
    pair = MIGRATION_PLANES * cells_radial
    starts = [0, 3 * pair, 6 * pair, 9 * pair, 10 * pair]
    return starts, round_up(10 * pair + 3 * cells_radial, 8)


def spread_row(row):
    return jnp.broadcast_to(row, (TILE_ROWS, row.shape[1])).astype(jnp.bfloat16)


def hot_tiles(index, row_total):
    iota = lax.broadcasted_iota(jnp.int32, index.shape, 0)
    return [
        index == (iota + first).astype(jnp.float32).astype(jnp.bfloat16)
        for first in range(0, row_total, TILE_ROWS)
    ]


def hot_product(loads, high, low, high_rows, low_rows):
    left, right = [], []
    high, low = high.astype(jnp.float32), low.astype(jnp.float32)
    zero = jnp.zeros((TILE_ROWS, high.shape[1]), jnp.bfloat16)
    one = jnp.ones((TILE_ROWS, high.shape[1]), jnp.bfloat16)
    for row in range(high.shape[0]):
        pick = slice(row, row + 1)
        high_masks = hot_tiles(spread_row(high[pick]), high_rows)
        low_masks = hot_tiles(spread_row(low[pick]), low_rows)
        spread = [spread_row(load[pick]) for load in loads]
        left.append(
            jnp.concatenate(
                [jnp.where(mask, load, zero) for load in spread for mask in high_masks], 0
            )
        )
        right.append(jnp.concatenate([jnp.where(mask, one, zero) for mask in low_masks], 0))
    return lax.dot_general(
        jnp.concatenate(left, 1),
        jnp.concatenate(right, 1),
        (((1,), (1,)), ((), ())),
        preferred_element_type=jnp.float32,
    )


def edge_row(plane, plane_total, moved_total):
    inner = (plane >= moved_total) & (plane < plane_total - moved_total)
    last = plane - (plane_total - 2 * moved_total)
    return jnp.where(inner, -plane_total, jnp.where(plane < moved_total, plane, last))


def fold_moved(plane, side, plane_total, side_total):
    width, third = side_total // 4, plane_total // 3
    part = jnp.where(plane >= third, 1, 0) + jnp.where(plane >= 2 * third, 1, 0)
    other = side >= 3 * width
    high = jnp.where(other, plane_total + plane - part * third, plane)
    low = jnp.where(other, side - 3 * width + part * width, side)
    return high, low, plane_total + third, 3 * width


def unfold_moved(table, q, plane_total, side_total, put):
    width, third = side_total // 4, plane_total // 3
    rows = plane_total + third
    put(0, 0, table[pl.ds(q * rows, plane_total), 0 : 3 * width])
    for part in range(3):
        block = table[
            pl.ds(q * rows + plane_total, third), part * width : (part + 1) * width
        ]
        put(part * third, 3 * width, block)


def fold_inner(plane, side, plane_total, side_total):
    rows, width = plane_total * 5 // 6, side_total // 4
    part, rest = split_index(side, width)
    other = plane >= rows
    high = jnp.where(other, plane - rows + part * (plane_total - rows), plane)
    high = jnp.where(plane < plane_total, high, -1)
    low = jnp.where(other, side_total + rest, side)
    return high, low, rows, side_total + width


def unfold_inner(table, q, plane_total, side_total, put):
    rows, width = plane_total * 5 // 6, side_total // 4
    left = plane_total - rows
    put(0, 0, table[pl.ds(q * rows, rows), 0:side_total])
    for part in range(4):
        block = table[pl.ds(q * rows + part * left, left), side_total : side_total + width]
        put(rows, part * width, block)


def tracer_block(count, values, cells, group, first_row, block_rows, cells_side):
    rows = pl.ds(first_row, block_rows)
    lane_total = cells.shape[2]
    shape = (block_rows, lane_total)
    slot = (first_row + lax.broadcasted_iota(jnp.int32, shape, 0)) * lane_total
    slot = slot + lax.broadcasted_iota(jnp.int32, shape, 1)
    weight = jnp.where(slot < count, 0.5 + values[0, group, rows, :], jnp.float32(0.0))
    loads = [weight, weight * values[1, group, rows, :], weight * values[2, group, rows, :]]
    plane, side = split_index(cells[group, rows, :], cells_side)
    return loads, plane, side


def for_used_blocks(used, group_rows, block_rows, lane_total, late_copies, step):
    block_slots = block_rows * lane_total
    blocks = lax.div(used + (block_slots - 1), block_slots)
    blocks = jnp.clip(blocks, 1, group_rows // block_rows)

    def wait_late():
        for copy in late_copies:
            copy.wait()

    def repeat(index, carried):
        pl.when(index == 1)(wait_late)
        step(pl.multiple_of(index * block_rows, block_rows))
        return carried

    lax.fori_loop(0, blocks, repeat, 0)
    pl.when(blocks == 1)(wait_late)


VISCOSITY, VELOCITY, SOURCE, LINE_FIELDS = 0, 1, 4, 7


def composition_of(cell_sums, base):
    scale = 1.0 / (cell_sums[0] + PRIOR_WEIGHT)
    basalt_share, melt_share = cell_sums[1] * scale, cell_sums[2] * scale
    weakening = jnp.exp(CONTRAST_BASALT * basalt_share - CONTRAST_MELT * melt_share)
    return basalt_share, melt_share, base * weakening


def outward_row(t, cells_radial):
    return jnp.where(lax.axis_index("rad") == 0, t, cells_radial - 1 - t)


class Fetches:
    def __init__(self, semaphores):
        self.semaphores = semaphores
        self.copies = []

    def start(self, source, target):
        copy = pltpu.make_async_copy(source, target, self.semaphores.at[len(self.copies)])
        copy.start()
        self.copies.append(copy)

    def wait(self, first, last):
        for copy in self.copies[first:last]:
            copy.wait()


def has_partners():
    lateral, count = lax.axis_index("lat"), lax.axis_size("lat")
    odd = lax.rem(lateral, 2) == 1
    above, below = lateral + 1 < count, lateral > 0
    return jnp.logical_or(odd, above), jnp.where(odd, above, below)


def outgoing_kernel(
    block_rows,
    counts_hbm,
    values_hbm,
    cells_hbm,
    base_hbm,
    velocity_hbm,
    forcing_hbm,
    edge_ref,
    first_ref,
    second_ref,
    count_ref,
    values,
    cells,
    counts,
    base,
    velocity,
    forcing,
    edge_sums,
    moved_sums,
    semaphores,
):
    cells_lateral, cells_radial, cells_side = base_hbm.shape
    plane_total = cells_lateral * cells_radial
    moved_planes = MIGRATION_PLANES * cells_radial
    group_rows, lane_total = cells.shape[1:]

    fetches = Fetches(semaphores)
    fetches.start(counts_hbm, counts)
    for first_row, rows in ((0, block_rows), (block_rows, group_rows - block_rows)):
        part = pl.ds(first_row, rows)
        fetches.start(cells_hbm.at[:, part], cells.at[:, part])
        fetches.start(values_hbm.at[:, :, part], values.at[:, :, part])
    for upward in (0, 1):
        outer = pl.ds((cells_lateral - MIGRATION_PLANES) * upward, MIGRATION_PLANES)
        fetches.start(base_hbm.at[outer], base.at[upward])
        fetches.start(velocity_hbm.at[:, outer], velocity.at[upward])
        outermost = pl.ds((cells_lateral - 1) * upward, 1)
        fetches.start(forcing_hbm.at[:, outermost], forcing.at[upward])

    edge_sums[...] = jnp.zeros_like(edge_sums)
    moved_sums[...] = jnp.zeros_like(moved_sums)

    def step(first_row):
        def block_of(group):
            count = counts[0, 0, group]
            return tracer_block(count, values, cells, group, first_row, block_rows, cells_side)

        loads, plane, side = block_of(1)
        row = edge_row(plane, plane_total, moved_planes)
        edge_sums[...] += hot_product(
            loads, *fold_moved(row, side, 2 * moved_planes, cells_side)
        )
        for slot, group in enumerate((0, 2)):
            loads, plane, side = block_of(group)
            if group == 0:
                plane = plane - (plane_total - moved_planes)
            moved_sums[slot] += hot_product(
                loads, *fold_moved(plane, side, moved_planes, cells_side)
            )

    fetches.wait(0, 3)
    count_ref[...] = jnp.full(count_ref.shape, counts[0, 0, 1], jnp.int32).astype(jnp.float32)
    used = jnp.maximum(jnp.maximum(counts[0, 0, 0], counts[0, 0, 1]), counts[0, 0, 2])
    for_used_blocks(used, group_rows, block_rows, lane_total, fetches.copies[3:5], step)
    fetches.wait(5, None)

    for q in range(3):

        def put_edge(plane, column, block):
            height, width = block.shape
            rows = pl.ds(2 * q * moved_planes + plane, height)
            edge_ref[rows, column : column + width] = block

        unfold_moved(edge_sums, q, 2 * moved_planes, cells_side, put_edge)

    starts, rows_total = payload_sections(cells_radial)
    unused = starts[4] + 3 * cells_radial

    def fill(payload, upward):
        for q in range(3):

            def put_moved(plane, column, block):
                height, width = block.shape
                rows = pl.ds(starts[0] + q * moved_planes + plane, height)
                payload[rows, column : column + width] = block

            unfold_moved(moved_sums.at[upward], q, moved_planes, cells_side, put_moved)
            payload[pl.ds(starts[1] + q * moved_planes, moved_planes), :] = edge_ref[
                pl.ds((2 * q + upward) * moved_planes, moved_planes), :
            ]
            for offset in range(MIGRATION_PLANES):
                row = starts[2] + q * moved_planes + offset * cells_radial
                payload[pl.ds(row, cells_radial), :] = velocity[upward, q, offset]
            row = starts[4] + q * cells_radial
            payload[pl.ds(row, cells_radial), :] = forcing[upward, q, 0]
        for offset in range(MIGRATION_PLANES):
            row = starts[3] + offset * cells_radial
            payload[pl.ds(row, cells_radial), :] = base[upward, offset]
        if unused < rows_total:
            payload[unused:, :] = jnp.zeros((rows_total - unused, cells_side), jnp.float32)

    odd = lax.rem(lax.axis_index("lat"), 2) == 1

    @pl.when(odd)
    def _():
        fill(first_ref, 0)
        fill(second_ref, 1)

    @pl.when(jnp.logical_not(odd))
    def _():
        fill(first_ref, 1)
        fill(second_ref, 0)

    for payload, exists in zip((first_ref, second_ref), has_partners()):

        @pl.when(jnp.logical_not(exists))
        def _():
            payload[...] = jnp.zeros_like(payload)


def inner_kernel(
    block_rows,
    count_ref,
    values_ref,
    cells_ref,
    base_hbm,
    velocity_hbm,
    forcing_hbm,
    composition_ref,
    lines_ref,
    outer_ref,
    table,
    sums,
    fields,
    base,
    velocity,
    forcing,
    semaphores,
):
    cells_lateral, cells_radial, cells_side = base.shape
    margin = MIGRATION_PLANES
    planes = cells_lateral + 2 * margin
    pitch = round_up(cells_radial, 8)
    moved_planes = margin * cells_radial
    inner = cells_lateral - 2 * margin
    inner_planes = inner * cells_radial
    group_rows, lane_total = cells_ref.shape[1:]
    fetches = Fetches(semaphores)
    fetches.start(velocity_hbm, velocity)
    fetches.start(forcing_hbm, forcing)
    fetches.start(base_hbm, base)
    table[...] = jnp.zeros_like(table)

    nothing = jnp.zeros((cells_radial, cells_side), jnp.float32)

    def put(field, plane, value):
        fields[field, pl.ds(plane * pitch, cells_radial), :] = value

    def lay_out(those):
        for field in those:
            for t in range(cells_radial):
                row = outward_row(t, cells_radial)
                lines_ref[field, t] = fields[field, pl.ds(row, planes, stride=pitch), :]

    def step(first_row):
        loads, plane, side = tracer_block(
            count, values_ref, cells_ref, 1, first_row, block_rows, cells_side
        )
        table[...] += hot_product(
            loads, *fold_inner(plane - moved_planes, side, inner_planes, cells_side)
        )

    count = jnp.max(count_ref[...]).astype(jnp.int32)
    for_used_blocks(count, group_rows, block_rows, lane_total, [], step)

    fetches.wait(0, None)
    for plane in range(planes):
        x = plane - margin
        own = 0 <= x < cells_lateral
        for q in range(3):
            put(VELOCITY + q, plane, velocity[q, x] if own else nothing)
        for q in range(2):
            put(SOURCE + q, plane, forcing[q, x] if own else nothing)
    late = VISCOSITY, SOURCE + 2
    lay_out(field for field in range(LINE_FIELDS) if field not in late)

    for q in range(3):

        def put_sums(plane, column, block):
            height, width = block.shape
            sums[q, pl.ds(plane, height), column : column + width] = block

        unfold_inner(table, q, inner_planes, cells_side, put_sums)
    for plane in range(planes):
        x = plane - 2 * margin
        viscosity, source = nothing, nothing
        if 0 <= x < inner:
            rows = pl.ds(x * cells_radial, cells_radial)
            cell_sums = [sums[q, rows, :] for q in range(3)]
            basalt_share, melt_share, viscosity = composition_of(cell_sums, base[x + margin])
            source = forcing[2, x + margin] - BUOYANCY * basalt_share
            composition_ref[0, x] = basalt_share
            composition_ref[1, x] = melt_share
        put(VISCOSITY, plane, viscosity)
        put(SOURCE + 2, plane, source)
    lay_out(late)
    for offset in range(margin):
        for place, x in ((offset, offset), (margin + offset, cells_lateral - margin + offset)):
            outer_ref[0, place] = base[x]
            outer_ref[1, place] = forcing[2, x]


BLOCK_ROWS = 64


def dense_tracers(tracer_values, tracer_cell):
    lane_total = 128
    return tracer_values.reshape(3, 3, -1, lane_total), tracer_cell.reshape(3, -1, lane_total)


def outgoing_sums(tracer_count, values, cells, base_viscosity, velocity, forcing):
    cells_lateral, cells_radial, cells_side = base_viscosity.shape
    moved_planes = MIGRATION_PLANES * cells_radial
    group_rows, lane_total = cells.shape[1:]
    block_rows = min(BLOCK_ROWS, group_rows // 2)
    _, payload_rows = payload_sections(cells_radial)
    hbm = pl.BlockSpec(memory_space=pltpu.HBM)
    vmem = pl.BlockSpec(memory_space=pltpu.VMEM)
    payload = jax.ShapeDtypeStruct((payload_rows, cells_side), jnp.float32)
    outer_planes = (MIGRATION_PLANES, cells_radial, cells_side)
    return pl.pallas_call(
        functools.partial(outgoing_kernel, block_rows),
        out_shape=(
            jax.ShapeDtypeStruct((6 * moved_planes, cells_side), jnp.float32),
            payload,
            payload,
            jax.ShapeDtypeStruct((8, lane_total), jnp.float32),
            jax.ShapeDtypeStruct(values.shape, jnp.float32),
            jax.ShapeDtypeStruct(cells.shape, jnp.int32),
        ),
        in_specs=[hbm] * 6,
        out_specs=(vmem,) * 6,
        scratch_shapes=[
            pltpu.SMEM(tracer_count.shape, jnp.int32),
            pltpu.VMEM((2,) + outer_planes, jnp.float32),
            pltpu.VMEM((2, 3) + outer_planes, jnp.float32),
            pltpu.VMEM((2, 3, 1, cells_radial, cells_side), jnp.float32),
            pltpu.VMEM((8 * moved_planes, cells_side * 3 // 4), jnp.float32),
            pltpu.VMEM((2, 4 * moved_planes, cells_side * 3 // 4), jnp.float32),
            pltpu.SemaphoreType.DMA((11,)),
        ],
        compiler_params=pltpu.CompilerParams(vmem_limit_bytes=32 * 2**20),
        cost_estimate=pl.CostEstimate(
            flops=30 * group_rows * lane_total * moved_planes * cells_side,
            bytes_accessed=4 * (values.size + cells.size),
            transcendentals=0,
        ),
        name="outgoing_sums",
    )(
        *(
            pltpu.with_memory_space_constraint(array, pltpu.HBM)
            for array in (tracer_count, values, cells, base_viscosity, velocity, forcing)
        )
    )


def inner_lines(count, values, cells, base_viscosity, velocity, forcing):
    cells_lateral, cells_radial, cells_side = base_viscosity.shape
    planes = cells_lateral + 2 * MIGRATION_PLANES
    inner = cells_lateral - 2 * MIGRATION_PLANES
    inner_planes = inner * cells_radial
    group_rows, lane_total = cells.shape[1:]
    block_rows = min(BLOCK_ROWS, group_rows // 2)
    vmem = pl.BlockSpec(memory_space=pltpu.VMEM)
    return pl.pallas_call(
        functools.partial(inner_kernel, block_rows),
        out_shape=(
            jax.ShapeDtypeStruct((2, inner, cells_radial, cells_side), jnp.float32),
            jax.ShapeDtypeStruct((LINE_FIELDS, cells_radial, planes, cells_side), jnp.float32),
            jax.ShapeDtypeStruct(
                (2, 2 * MIGRATION_PLANES, cells_radial, cells_side), jnp.float32
            ),
        ),
        in_specs=[vmem] * 3 + [pl.BlockSpec(memory_space=pltpu.HBM)] * 3,
        out_specs=(vmem,) * 3,
        scratch_shapes=[
            pltpu.VMEM((3 * (inner_planes * 5 // 6), cells_side * 5 // 4), jnp.float32),
            pltpu.VMEM((3, inner_planes, cells_side), jnp.float32),
            pltpu.VMEM((LINE_FIELDS, planes * round_up(cells_radial, 8), cells_side), jnp.float32),
            pltpu.VMEM(base_viscosity.shape, jnp.float32),
            pltpu.VMEM(velocity.shape, jnp.float32),
            pltpu.VMEM(forcing.shape, jnp.float32),
            pltpu.SemaphoreType.DMA((3,)),
        ],
        compiler_params=pltpu.CompilerParams(vmem_limit_bytes=32 * 2**20),
        cost_estimate=pl.CostEstimate(
            flops=6 * group_rows * lane_total * inner * cells_radial * cells_side,
            bytes_accessed=4 * (values.size + cells.size),
            transcendentals=0,
        ),
        name="inner_lines",
    )(
        count,
        values,
        cells,
        *(
            pltpu.with_memory_space_constraint(array, pltpu.HBM)
            for array in (base_viscosity, velocity, forcing)
        ),
    )


def pair_swaps(first, second):
    count = lax.axis_size("lat")
    received = []
    for payload, start in ((second, 1), (first, 0)):
        target = list(range(count))
        for low in range(start, count - 1, 2):
            target[low], target[low + 1] = low + 1, low
        received.append(lax.ppermute(payload, "lat", list(enumerate(target))))
    return received[::-1]


def shift_planes(block, step):
    return pltpu.roll(block, step % block.shape[0], 0)


def shift_side(block, step):
    return pltpu.roll(block, step % block.shape[1], 1)


def neighbours(block):
    return (
        shift_planes(block, 1),
        shift_planes(block, -1),
        shift_side(block, 1),
        shift_side(block, -1),
    )


def inside_side(values):
    lane = lax.broadcasted_iota(jnp.int32, values[2].shape, 1)
    lower = jnp.where(lane > 0, values[2], 0.0)
    upper = jnp.where(lane < lane.shape[1] - 1, values[3], 0.0)
    return values[0], values[1], lower, upper


def total_of(terms):
    result = terms[0]
    for term in terms[1:]:
        result = result + term
    return result


def inside_grid(shape, margin, cells_lateral):
    plane = lax.broadcasted_iota(jnp.int32, shape, 0)
    lateral = lax.axis_index("lat")
    first = jnp.where(lateral == 0, margin, 1)
    last = jnp.where(lateral == lax.axis_size("lat") - 1, margin + cells_lateral, shape[0] - 1)
    return (plane >= first) & (plane < last)


LONG_FIELDS, SHORT_FIELDS = 5, 7


def message_rows(cells_lateral):
    planes = cells_lateral + 2 * MIGRATION_PLANES
    return round_up(LONG_FIELDS * planes + SHORT_FIELDS * cells_lateral + MIGRATION_PLANES, 8)


def message_part(cells_lateral, field):
    planes = cells_lateral + 2 * MIGRATION_PLANES
    if field < LONG_FIELDS:
        return pl.ds(field * planes, planes), 0, planes
    first = LONG_FIELDS * planes + (field - LONG_FIELDS) * cells_lateral
    return pl.ds(first, cells_lateral), MIGRATION_PLANES, cells_lateral


def solve_lines(radial, cells_radial, valid, keep, keep_part):
    last = cells_radial - 1
    viscosity = [radial(VISCOSITY, t) for t in range(cells_radial)]
    lateral_faces, lateral_sums = [], []
    for here in viscosity:
        faces = [LATERAL * 0.5 * (here + there) for there in inside_side(neighbours(here))]
        lateral_sums.append(total_of(faces))
        lateral_faces.append(inside_side(faces))
    radial_faces = [RADIAL * 0.5 * viscosity[0]] + [
        RADIAL * 0.5 * (viscosity[t - 1] + viscosity[t]) for t in range(1, cells_radial)
    ]

    excess = lateral_sums[0] + radial_faces[0]
    inverse, coupling = [], []
    for t in range(last):
        inverse.append(1.0 / (excess + radial_faces[t + 1]))
        coupling.append(radial_faces[t + 1] * inverse[t])
        excess = lateral_sums[t + 1] + coupling[t] * excess

    def lateral_terms(t, around):
        return [face * there for face, there in zip(lateral_faces[t], around)]

    def forward(right_side):
        eliminated = [right_side[0]]
        for t in range(1, cells_radial):
            eliminated.append(right_side[t] + coupling[t - 1] * eliminated[t - 1])
        return eliminated

    def backward(eliminated):
        solved = [jnp.zeros_like(excess)]
        for t in range(last - 1, -1, -1):
            solved.append(eliminated[t] * inverse[t] + coupling[t] * solved[-1])
        return solved[::-1]

    response = [jnp.ones_like(excess)]
    for t in range(last - 1, -1, -1):
        response.append(coupling[t] * response[-1])
    response = response[::-1]

    def finish(part, eliminated):
        keep(LONG_FIELDS + part, eliminated[last])
        for t, value in enumerate(eliminated[:last]):
            keep_part(part, t, value)

    keep(0, viscosity[last])
    keep(1, excess)
    for q in range(3):
        source = [radial(SOURCE + q, t) for t in range(cells_radial)]
        eliminated = forward(
            [
                total_of([source[t]] + lateral_terms(t, neighbours(radial(VELOCITY + q, t))))
                for t in range(cells_radial)
            ]
        )
        keep(2 + q, eliminated[last])
        particular = [jnp.where(valid, value, 0.0) for value in backward(eliminated)]
        finish(
            q,
            forward(
                [
                    total_of([source[t]] + lateral_terms(t, neighbours(particular[t])))
                    for t in range(cells_radial)
                ]
            ),
        )
    around = [neighbours(jnp.where(valid, value, 0.0)) for value in response]
    for side in range(4):
        finish(
            3 + side,
            forward([lateral_faces[t][side] * around[t][side] for t in range(cells_radial)]),
        )
    for t in range(last):
        keep_part(SHORT_FIELDS, t, inverse[t])
        keep_part(SHORT_FIELDS + 1, t, coupling[t])


def eliminate_kernel(
    inner_ref,
    lines_ref,
    edge_ref,
    second_ref,
    first_ref,
    from_second_ref,
    from_first_ref,
    outer_ref,
    composition_ref,
    mine_ref,
    message_ref,
    parts_ref,
    fields,
):
    _, cells_lateral, cells_radial, cells_side = composition_ref.shape
    margin = MIGRATION_PLANES
    planes = cells_lateral + 2 * margin
    pitch = round_up(cells_radial, 8)
    moved_planes = margin * cells_radial
    starts, _ = payload_sections(cells_radial)
    odd = lax.rem(lax.axis_index("lat"), 2) == 1

    def sent(upward, start):
        part = pl.ds(start, cells_radial)
        mine_first = odd if not upward else jnp.logical_not(odd)
        return jnp.where(mine_first, first_ref[part, :], second_ref[part, :])

    def arrived(from_above, start):
        part = pl.ds(start, cells_radial)
        is_first = odd if not from_above else jnp.logical_not(odd)
        return jnp.where(is_first, from_first_ref[part, :], from_second_ref[part, :])

    outer = 2 * margin

    def put(field, slot, value):
        fields[field, pl.ds(slot * pitch, cells_radial), :] = value

    for above in (False, True):
        for offset in range(margin):
            shift = offset * cells_radial
            halo = offset + (outer + margin if above else 0)
            own = offset + (outer if above else margin)
            x = offset + (cells_lateral - margin if above else 0)
            place = offset + (margin if above else 0)
            halo_sums, own_sums = [], []
            for q in range(3):
                row = q * moved_planes + shift
                rows = pl.ds((2 * q + int(above)) * moved_planes + shift, cells_radial)
                own_sums.append(edge_ref[rows, :] + arrived(above, starts[0] + row))
                halo_sums.append(sent(above, starts[0] + row) + arrived(above, starts[1] + row))
                put(VELOCITY + q, halo, arrived(above, starts[2] + row))
            basalt_share, melt_share, viscosity = composition_of(own_sums, outer_ref[0, place])
            composition_ref[0, x] = basalt_share
            composition_ref[1, x] = melt_share
            put(VISCOSITY, own, viscosity)
            put(SOURCE + 2, own, outer_ref[1, place] - BUOYANCY * basalt_share)
            basalt_share, _, viscosity = composition_of(
                halo_sums, arrived(above, starts[3] + shift)
            )
            put(VISCOSITY, halo, viscosity)
            beside = offset == (0 if above else margin - 1)
            for q in range(3):
                source = jnp.zeros_like(viscosity)
                if beside:
                    source = arrived(above, starts[4] + q * cells_radial)
                    if q == 2:
                        source = source - BUOYANCY * basalt_share
                put(SOURCE + q, halo, source)
    for x in range(margin, cells_lateral - margin):
        for q in range(2):
            composition_ref[q, x] = inner_ref[q, x - margin]

    def radial(field, t):
        replaced = outer if field in (VISCOSITY, SOURCE + 2) else margin
        plane = lax.broadcasted_iota(jnp.int32, (planes, cells_side), 0)
        own = (plane >= replaced) & (plane < planes - replaced)
        row = outward_row(t, cells_radial)
        edges = fields[field, pl.ds(row, 2 * outer, stride=pitch), :]
        if 2 * outer * 2 == planes:
            edges = jnp.concatenate([edges, edges], 0)
        else:
            gap = jnp.zeros((planes - 2 * outer, cells_side), jnp.float32)
            edges = jnp.concatenate([edges[:outer], gap, edges[outer:]], 0)
        return jnp.where(own, lines_ref[field, t], edges)

    unused = LONG_FIELDS * planes + SHORT_FIELDS * cells_lateral
    if unused < message_ref.shape[0]:
        message_ref[unused:, :] = jnp.zeros((message_ref.shape[0] - unused, cells_side), jnp.float32)

    def keep(field, value):
        rows, first, count = message_part(cells_lateral, field)
        mine_ref[field] = value
        message_ref[rows, :] = value[first : first + count]

    def keep_part(part, t, value):
        parts_ref[part, t] = value

    valid = inside_grid((planes, cells_side), margin, cells_lateral)
    solve_lines(radial, cells_radial, valid, keep, keep_part)


def eliminate(inner, lines, outer, edge, sent, received, cells_lateral):
    cells_radial, cells_side = inner.shape[2:]
    planes = cells_lateral + 2 * MIGRATION_PLANES
    vmem = pl.BlockSpec(memory_space=pltpu.VMEM)
    line = (planes, cells_side)
    return pl.pallas_call(
        eliminate_kernel,
        out_shape=(
            jax.ShapeDtypeStruct((2, cells_lateral, cells_radial, cells_side), jnp.float32),
            jax.ShapeDtypeStruct((LONG_FIELDS + SHORT_FIELDS,) + line, jnp.float32),
            jax.ShapeDtypeStruct((message_rows(cells_lateral), cells_side), jnp.float32),
            jax.ShapeDtypeStruct((SHORT_FIELDS + 2, cells_radial - 1) + line, jnp.float32),
        ),
        in_specs=[vmem] * 8,
        out_specs=(vmem,) * 4,
        scratch_shapes=[
            pltpu.VMEM(
                (LINE_FIELDS, 4 * MIGRATION_PLANES * round_up(cells_radial, 8), cells_side),
                jnp.float32,
            )
        ],
        compiler_params=pltpu.CompilerParams(vmem_limit_bytes=32 * 2**20),
        name="eliminate",
    )(inner, lines, edge, *sent[::-1], *received[::-1], outer)


def join_kernel(mine_ref, message_ref, parts_ref, smoothed_ref, lines):
    _, cells_lateral, cells_radial, cells_side = smoothed_ref.shape
    margin = MIGRATION_PLANES
    planes = cells_lateral + 2 * margin
    pitch = round_up(cells_radial, 8)
    valid = inside_grid((planes, cells_side), margin, cells_lateral)

    def mine(field):
        return mine_ref[field]

    def other(field):
        rows, first, _ = message_part(cells_lateral, field)
        return message_ref[pl.ds(rows.start - first, planes), :]

    face = RADIAL * 0.5 * (mine(0) + other(0))
    excess, other_excess = mine(1), other(1)
    scale = 1.0 / (excess * other_excess + face * (excess + other_excess))
    own_weight = (other_excess + face) * scale
    other_weight = (excess + face) * scale
    cross = face * scale

    def second_right(field_of, q, around):
        terms = [field_of(LONG_FIELDS + 3 + side) * there for side, there in enumerate(around)]
        return total_of([field_of(LONG_FIELDS + q)] + terms)

    around, values = [], []
    for q in range(3):
        right, other_right = mine(2 + q), other(2 + q)
        own = jnp.where(valid, own_weight * right + cross * other_right, 0.0)
        beyond = jnp.where(valid, other_weight * other_right + cross * right, 0.0)
        around.append(neighbours(own))
        right = second_right(mine, q, around[q])
        other_right = second_right(other, q, neighbours(beyond))
        values.append(own_weight * right + cross * other_right)
    for t in range(cells_radial - 1, -1, -1):
        row = outward_row(t, cells_radial)
        if t < cells_radial - 1:
            factors = [parts_ref[3 + side, t] for side in range(4)]
            inverse, coupling = parts_ref[SHORT_FIELDS, t], parts_ref[SHORT_FIELDS + 1, t]
        for q in range(3):
            if t < cells_radial - 1:
                terms = [factor * there for factor, there in zip(factors, around[q])]
                right = total_of([parts_ref[q, t]] + terms)
                values[q] = right * inverse + coupling * values[q]
            lines[q, pl.ds(row, cells_lateral, stride=pitch), :] = values[q][
                margin : margin + cells_lateral
            ]
    for q in range(3):
        for x in range(cells_lateral):
            smoothed_ref[q, x] = lines[q, pl.ds(x * pitch, cells_radial), :]


def join(mine, message, parts, like):
    cells_lateral, cells_radial, cells_side = like.shape[1:]
    vmem = pl.BlockSpec(memory_space=pltpu.VMEM)
    return pl.pallas_call(
        join_kernel,
        out_shape=jax.ShapeDtypeStruct(like.shape, jnp.float32),
        in_specs=[vmem] * 3,
        out_specs=vmem,
        scratch_shapes=[
            pltpu.VMEM((3, cells_lateral * round_up(cells_radial, 8), cells_side), jnp.float32),
        ],
        compiler_params=pltpu.CompilerParams(vmem_limit_bytes=32 * 2**20),
        name="join",
    )(mine, message, parts)


def extended(block, sides, width):
    for axis, dim in sides:
        count = lax.axis_size(axis)
        forward = [(i, i + 1) for i in range(count - 1)]
        backward = [(target, source) for source, target in forward]
        low = lax.ppermute(
            lax.slice_in_dim(block, block.shape[dim] - width, None, axis=dim), axis, forward
        )
        high = lax.ppermute(lax.slice_in_dim(block, 0, width, axis=dim), axis, backward)
        block = jnp.concatenate([low, block, high], axis=dim)
    return block


def block_factor(diagonal, lower_band, upper_band):
    pivots = []
    upper_scaled = []
    for row_index in range(diagonal.shape[1]):
        if row_index == 0:
            pivot_row = diagonal[:, 0]
        else:
            pivot_row = diagonal[:, row_index] - lower_band[:, row_index] * upper_scaled[-1]
        pivots.append(pivot_row)
        upper_scaled.append(upper_band[:, row_index] / pivot_row)
    return (pivots, upper_scaled)


def block_solve(pivots, upper_scaled, lower_band, right_side):
    row_total = len(pivots)
    modified = []
    for row_index in range(row_total):
        if row_index == 0:
            value_row = right_side[:, :, 0] / pivots[0]
        else:
            value_row = (
                right_side[:, :, row_index] - lower_band[:, row_index] * modified[-1]
            ) / pivots[row_index]
        modified.append(value_row)
    solved = [modified[-1]]
    for row_index in range(row_total - 2, -1, -1):
        solved.append(modified[row_index] - upper_scaled[row_index] * solved[-1])
    ordered = solved[::-1]
    return jnp.stack(ordered, 2)


def interface_solve(coefficients):
    column_total = coefficients.shape[2]

    def forward(carried, inputs):
        offset, carried_slope = carried
        left_first, right_first, left_last, right_last, free_first, free_last = inputs
        divisor = 1.0 - left_first * carried_slope
        first_fixed = (free_first + left_first * offset) / divisor
        first_slope = right_first / divisor
        next_offset = free_last + left_last * (offset + carried_slope * first_fixed)
        next_slope = left_last * carried_slope * first_slope + right_last
        return ((next_offset, next_slope), (first_fixed, first_slope, next_offset, next_slope))

    start_state = (
        jnp.zeros((3, column_total), jnp.float32),
        jnp.zeros((column_total,), jnp.float32),
    )
    scan_inputs = (
        coefficients[:, 0],
        coefficients[:, 1],
        coefficients[:, 2],
        coefficients[:, 3],
        coefficients[:, 4:7],
        coefficients[:, 7:10],
    )
    final_state, eliminated = lax.scan(forward, start_state, scan_inputs)

    def backward(first_next, inputs):
        fixed_first, slope_first, fixed_last, slope_last = inputs
        first_value = fixed_first + slope_first * first_next
        last_value = fixed_last + slope_last * first_next
        return (first_value, (first_value, last_value))

    final_first, values_pair = lax.scan(
        backward, jnp.zeros((3, column_total), jnp.float32), eliminated, reverse=True
    )
    first_values, last_values = values_pair
    nothing_row = jnp.zeros((1, 3, column_total), jnp.float32)
    from_below = jnp.concatenate([nothing_row, last_values[:-1]], 0)
    from_above = jnp.concatenate([first_values[1:], nothing_row], 0)
    return jnp.concatenate([from_below, from_above], 1)


def reduced_boundary(interface):
    gathered = lax.all_gather(interface, "rad", axis=0, tiled=True)
    solved = interface_solve(gathered)
    return lax.dynamic_index_in_dim(solved, lax.axis_index("rad"), 0, keepdims=False)


def many_blocks(values, cells, count, edge, received, base_viscosity, velocity, forcing):
    cells_lateral, cells_radial, cells_side = base_viscosity.shape
    moved_rows = MIGRATION_PLANES * cells_radial
    odd = lax.rem(lax.axis_index("lat"), 2) == 1
    from_below = jnp.where(odd, received[0], received[1])[: 3 * moved_rows]
    from_above = jnp.where(odd, received[1], received[0])[: 3 * moved_rows]
    edge = edge.reshape(3, 2, moved_rows, cells_side)
    below = edge[:, 0] + from_below.reshape(3, moved_rows, cells_side)
    above = edge[:, 1] + from_above.reshape(3, moved_rows, cells_side)
    shares = [
        (sums[1:] / (sums[0] + PRIOR_WEIGHT)).reshape(2, -1, cells_radial, cells_side)
        for sums in (below, above)
    ]
    inner, _, _ = inner_lines(count, values, cells, base_viscosity, velocity, forcing)
    basalt_share, melt_share = jnp.concatenate([shares[0], inner, shares[1]], 1)
    viscosity = base_viscosity * jnp.exp(
        CONTRAST_BASALT * basalt_share - CONTRAST_MELT * melt_share
    )
    viscosity_pad = extended(viscosity, (("lat", 0), ("rad", 1)), 1)
    side_pad = jnp.pad(viscosity, ((0, 0), (0, 0), (1, 1)))
    face_west = LATERAL * 0.5 * (viscosity + viscosity_pad[:-2, 1:-1])
    face_east = LATERAL * 0.5 * (viscosity + viscosity_pad[2:, 1:-1])
    face_south = LATERAL * 0.5 * (viscosity + side_pad[:, :, :-2])
    face_north = LATERAL * 0.5 * (viscosity + side_pad[:, :, 2:])
    face_below = RADIAL * 0.5 * (viscosity + viscosity_pad[1:-1, :-2])
    face_above = RADIAL * 0.5 * (viscosity + viscosity_pad[1:-1, 2:])
    diagonal = face_west + face_east + face_south + face_north + face_below + face_above
    source = jnp.concatenate([forcing[:2], (forcing[2] - BUOYANCY * basalt_share)[None]], 0)
    lower_band = -face_below
    upper_band = -face_above
    pivots, upper_scaled = block_factor(diagonal, lower_band, upper_band)
    radial_iota = lax.broadcasted_iota(jnp.int32, viscosity.shape, 1)
    response_side = jnp.stack(
        [
            jnp.where(radial_iota == 0, face_below, jnp.float32(0.0)),
            jnp.where(radial_iota == cells_radial - 1, face_above, jnp.float32(0.0)),
        ]
    )
    response = block_solve(pivots, upper_scaled, lower_band, response_side)
    current = velocity
    for sweep_index in range(SWEEPS):
        velocity_pad = extended(current, (("lat", 1),), 1)
        side_velocity = jnp.pad(current, ((0, 0), (0, 0), (0, 0), (1, 1)))
        right_side = (
            source
            + face_west * velocity_pad[:, :-2]
            + face_east * velocity_pad[:, 2:]
            + face_south * side_velocity[..., :-2]
            + face_north * side_velocity[..., 2:]
        )
        particular = block_solve(pivots, upper_scaled, lower_band, right_side)
        interface = jnp.concatenate(
            [response[:, :, 0], response[:, :, -1], particular[:, :, 0], particular[:, :, -1]], 0
        )
        interface = interface.reshape(1, 10, cells_lateral * cells_side)
        boundary = reduced_boundary(interface).reshape(6, cells_lateral, 1, cells_side)
        current = particular + response[0][None] * boundary[:3] + response[1][None] * boundary[3:]
    composition = jnp.stack([basalt_share, melt_share])
    return (current, composition)

def local(tracer_values, tracer_cell, tracer_count, base_viscosity, velocity, forcing):
    values, cells = dense_tracers(tracer_values, tracer_cell)
    edge, first, second, count, values, cells = outgoing_sums(
        tracer_count, values, cells, base_viscosity, velocity, forcing
    )
    sent = first, second
    received = pair_swaps(first, second)
    if lax.axis_size("rad") != 2:
        return many_blocks(
            values, cells, count, edge, received, base_viscosity, velocity, forcing
        )
    inner, lines, outer = inner_lines(count, values, cells, base_viscosity, velocity, forcing)
    composition, mine, message, parts = eliminate(
        inner, lines, outer, edge, sent, received, base_viscosity.shape[0]
    )
    other = lax.ppermute(message, "rad", [(0, 1), (1, 0)])
    return join(mine, other, parts, velocity), composition


def solution(mesh):
    return jax.shard_map(
        local,
        mesh=mesh,
        in_specs=(
            P("lat", "rad", None, None),
            P("lat", "rad", None),
            P("lat", "rad", None),
            P("lat", "rad", None),
            P(None, "lat", "rad", None),
            P(None, "lat", "rad", None),
        ),
        out_specs=(P(None, "lat", "rad", None), P(None, "lat", "rad", None)),
        check_vma=False,
    )
```

```python
import functools

import jax
import jax.numpy as jnp
from jax import lax
from jax.experimental import pallas as pl
from jax.experimental.pallas import tpu as pltpu
from jax.sharding import PartitionSpec as P

SWEEPS = 2
MIGRATION_PLANES = 2

LATERAL = 0.015625
RADIAL = 32.0
BUOYANCY = 0.1
PRIOR_WEIGHT = 0.5
CONTRAST_BASALT = 2.3
CONTRAST_MELT = 1.5

TILE_ROWS = 16


def round_up(value, multiple):
    return -(-value // multiple) * multiple


def split_index(index, count):
    if count & (count - 1) == 0:
        return lax.shift_right_logical(index, count.bit_length() - 1), index & (count - 1)
    quotient = lax.div(index, count)
    return quotient, index - quotient * count


def payload_sections(cells_radial):
    pair = MIGRATION_PLANES * cells_radial
    starts = [0, 3 * pair, 6 * pair, 9 * pair, 10 * pair]
    return starts, round_up(10 * pair + 3 * cells_radial, 8)


def spread_row(row):
    return jnp.broadcast_to(row, (TILE_ROWS, row.shape[1])).astype(jnp.bfloat16)


def hot_tiles(index, row_total):
    iota = lax.broadcasted_iota(jnp.int32, index.shape, 0)
    return [
        index == (iota + first).astype(jnp.float32).astype(jnp.bfloat16)
        for first in range(0, row_total, TILE_ROWS)
    ]


def hot_product(loads, high, low, high_rows, low_rows):
    left, right = [], []
    high, low = high.astype(jnp.float32), low.astype(jnp.float32)
    tile = (TILE_ROWS, high.shape[1])
    zero, one = jnp.zeros(tile, jnp.bfloat16), jnp.ones(tile, jnp.bfloat16)
    half = TILE_ROWS // 2
    whole_rows = high_rows // TILE_ROWS * TILE_ROWS
    number = lax.broadcasted_iota(jnp.int32, tile, 0)
    in_lower = number.astype(jnp.float32).astype(jnp.bfloat16) < half
    left_number = jnp.where(number < half, number, number - half) + whole_rows
    left_number = left_number.astype(jnp.float32).astype(jnp.bfloat16)
    for row in range(high.shape[0]):
        pick = slice(row, row + 1)
        index = spread_row(high[pick])
        high_masks = hot_tiles(index, whole_rows)
        low_masks = hot_tiles(spread_row(low[pick]), low_rows)
        spread = [spread_row(load[pick]) for load in loads]
        tiles = [jnp.where(mask, load, zero) for load in spread for mask in high_masks]
        if whole_rows < high_rows:
            mask = index == left_number
            for pair in ((spread[0], spread[1]), (spread[2], zero)):
                tiles.append(jnp.where(mask, jnp.where(in_lower, *pair), zero))
        left.append(jnp.concatenate(tiles, 0))
        right.append(jnp.concatenate([jnp.where(mask, one, zero) for mask in low_masks], 0))
    return lax.dot_general(
        jnp.concatenate(left, 1),
        jnp.concatenate(right, 1),
        (((1,), (1,)), ((), ())),
        preferred_element_type=jnp.float32,
    )


def hot_rows(high_rows, q):
    whole_rows = high_rows // TILE_ROWS * TILE_ROWS
    places = [(q * whole_rows, 0, whole_rows)]
    if whole_rows < high_rows:
        half = TILE_ROWS // 2
        places.append((3 * whole_rows + q * half, whole_rows, half))
    return places


def hot_shape(high_rows, low_rows):
    return round_up(3 * high_rows, TILE_ROWS), low_rows


def edge_row(plane, plane_total, moved_total):
    inner = (plane >= moved_total) & (plane < plane_total - moved_total)
    last = plane - (plane_total - 2 * moved_total)
    return jnp.where(inner, -plane_total, jnp.where(plane < moved_total, plane, last))


def fold_inner(plane, side, plane_total, side_total):
    rows, width = plane_total * 5 // 6, side_total // 4
    part, rest = split_index(side, width)
    other = plane >= rows
    high = jnp.where(other, plane - rows + part * (plane_total - rows), plane)
    high = jnp.where(plane < plane_total, high, -1)
    low = jnp.where(other, side_total + rest, side)
    return high, low, rows, side_total + width


def unfold_inner(table, q, plane_total, side_total, put):
    rows, width = plane_total * 5 // 6, side_total // 4
    left = plane_total - rows
    put(0, 0, table[pl.ds(q * rows, rows), 0:side_total])
    for part in range(4):
        block = table[pl.ds(q * rows + part * left, left), side_total : side_total + width]
        put(rows, part * width, block)


def tracer_block(count, values, cells, group, first_row, block_rows, cells_side):
    rows = pl.ds(first_row, block_rows)
    lane_total = cells.shape[2]
    shape = (block_rows, lane_total)
    slot = (first_row + lax.broadcasted_iota(jnp.int32, shape, 0)) * lane_total
    slot = slot + lax.broadcasted_iota(jnp.int32, shape, 1)
    weight = jnp.where(slot < count, 0.5 + values[0, group, rows, :], jnp.float32(0.0))
    loads = [weight, weight * values[1, group, rows, :], weight * values[2, group, rows, :]]
    plane, side = split_index(cells[group, rows, :], cells_side)
    return loads, plane, side


def for_used_blocks(used, group_rows, block_rows, lane_total, late_copies, step):
    block_slots = block_rows * lane_total
    blocks = lax.div(used + (block_slots - 1), block_slots)
    blocks = jnp.clip(blocks, 1, group_rows // block_rows)

    def wait_late():
        for copy in late_copies:
            copy.wait()

    def repeat(index, carried):
        pl.when(index == 1)(wait_late)
        step(pl.multiple_of(index * block_rows, block_rows))
        return carried

    lax.fori_loop(0, blocks, repeat, 0)
    pl.when(blocks == 1)(wait_late)


VISCOSITY, VELOCITY, SOURCE, LINE_FIELDS = 0, 1, 4, 7


def composition_of(cell_sums, base):
    scale = 1.0 / (cell_sums[0] + PRIOR_WEIGHT)
    basalt_share, melt_share = cell_sums[1] * scale, cell_sums[2] * scale
    weakening = jnp.exp(CONTRAST_BASALT * basalt_share - CONTRAST_MELT * melt_share)
    return basalt_share, melt_share, base * weakening


def outward_row(t, cells_radial):
    return jnp.where(lax.axis_index("rad") == 0, t, cells_radial - 1 - t)


class Fetches:
    def __init__(self, semaphores):
        self.semaphores = semaphores
        self.copies = []

    def start(self, source, target):
        copy = pltpu.make_async_copy(source, target, self.semaphores.at[len(self.copies)])
        copy.start()
        self.copies.append(copy)

    def wait(self, first, last):
        for copy in self.copies[first:last]:
            copy.wait()


def has_partners():
    lateral, count = lax.axis_index("lat"), lax.axis_size("lat")
    odd = lax.rem(lateral, 2) == 1
    above, below = lateral + 1 < count, lateral > 0
    return jnp.logical_or(odd, above), jnp.where(odd, above, below)


def outgoing_kernel(
    block_rows,
    counts_hbm,
    values_hbm,
    cells_hbm,
    base_hbm,
    velocity_hbm,
    forcing_hbm,
    edge_ref,
    first_ref,
    second_ref,
    count_ref,
    values,
    cells,
    counts,
    base,
    velocity,
    forcing,
    edge_sums,
    moved_sums,
    semaphores,
):
    cells_lateral, cells_radial, cells_side = base_hbm.shape
    plane_total = cells_lateral * cells_radial
    moved_planes = MIGRATION_PLANES * cells_radial
    group_rows, lane_total = cells.shape[1:]

    fetches = Fetches(semaphores)
    fetches.start(counts_hbm, counts)
    part = pl.ds(0, block_rows)
    fetches.start(cells_hbm.at[:, part], cells.at[:, part])
    for q in range(3):
        fetches.start(values_hbm.at[q, :, part], values.at[q, :, part])
    part = pl.ds(block_rows, group_rows - block_rows)
    fetches.start(cells_hbm.at[:, part], cells.at[:, part])
    fetches.start(values_hbm.at[:, :, part], values.at[:, :, part])
    for upward in (0, 1):
        outer = pl.ds((cells_lateral - MIGRATION_PLANES) * upward, MIGRATION_PLANES)
        fetches.start(base_hbm.at[outer], base.at[upward])
        fetches.start(velocity_hbm.at[:, outer], velocity.at[upward])
        outermost = pl.ds((cells_lateral - 1) * upward, 1)
        fetches.start(forcing_hbm.at[:, outermost], forcing.at[upward])

    edge_sums[...] = jnp.zeros_like(edge_sums)
    moved_sums[...] = jnp.zeros_like(moved_sums)

    def step(first_row):
        def block_of(group):
            count = counts[0, 0, group]
            return tracer_block(count, values, cells, group, first_row, block_rows, cells_side)

        loads, plane, side = block_of(1)
        row = edge_row(plane, plane_total, moved_planes)
        edge_sums[...] += hot_product(loads, row, side, 2 * moved_planes, cells_side)
        for slot, group in enumerate((0, 2)):
            loads, plane, side = block_of(group)
            if group == 0:
                plane = plane - (plane_total - moved_planes)
            moved_sums[slot] += hot_product(loads, plane, side, moved_planes, cells_side)

    fetches.wait(0, 5)
    count_ref[...] = jnp.full(count_ref.shape, counts[0, 0, 1], jnp.int32).astype(jnp.float32)
    used = jnp.maximum(jnp.maximum(counts[0, 0, 0], counts[0, 0, 1]), counts[0, 0, 2])
    for_used_blocks(used, group_rows, block_rows, lane_total, fetches.copies[5:7], step)
    fetches.wait(7, None)

    for q in range(3):
        for row, plane, count in hot_rows(2 * moved_planes, q):
            target = pl.ds(2 * q * moved_planes + plane, count)
            edge_ref[target, :] = edge_sums[pl.ds(row, count), :]

    starts, rows_total = payload_sections(cells_radial)
    unused = starts[4] + 3 * cells_radial

    def fill(payload, upward):
        for q in range(3):
            for row, plane, count in hot_rows(moved_planes, q):
                target = pl.ds(starts[0] + q * moved_planes + plane, count)
                payload[target, :] = moved_sums[upward, pl.ds(row, count), :]
            payload[pl.ds(starts[1] + q * moved_planes, moved_planes), :] = edge_ref[
                pl.ds((2 * q + upward) * moved_planes, moved_planes), :
            ]
            for offset in range(MIGRATION_PLANES):
                row = starts[2] + q * moved_planes + offset * cells_radial
                payload[pl.ds(row, cells_radial), :] = velocity[upward, q, offset]
            row = starts[4] + q * cells_radial
            payload[pl.ds(row, cells_radial), :] = forcing[upward, q, 0]
        for offset in range(MIGRATION_PLANES):
            row = starts[3] + offset * cells_radial
            payload[pl.ds(row, cells_radial), :] = base[upward, offset]
        if unused < rows_total:
            payload[unused:, :] = jnp.zeros((rows_total - unused, cells_side), jnp.float32)

    odd = lax.rem(lax.axis_index("lat"), 2) == 1

    @pl.when(odd)
    def _():
        fill(first_ref, 0)
        fill(second_ref, 1)

    @pl.when(jnp.logical_not(odd))
    def _():
        fill(first_ref, 1)
        fill(second_ref, 0)

    for payload, exists in zip((first_ref, second_ref), has_partners()):

        @pl.when(jnp.logical_not(exists))
        def _():
            payload[...] = jnp.zeros_like(payload)


def inner_kernel(
    block_rows,
    count_ref,
    values_ref,
    cells_ref,
    base_hbm,
    velocity_hbm,
    forcing_hbm,
    composition_ref,
    lines_ref,
    outer_ref,
    table,
    sums,
    fields,
    base,
    velocity,
    forcing,
    semaphores,
):
    cells_lateral, cells_radial, cells_side = base.shape
    margin = MIGRATION_PLANES
    planes = cells_lateral + 2 * margin
    pitch = round_up(cells_radial, 8)
    moved_planes = margin * cells_radial
    inner = cells_lateral - 2 * margin
    inner_planes = inner * cells_radial
    group_rows, lane_total = cells_ref.shape[1:]
    fetches = Fetches(semaphores)
    fetches.start(velocity_hbm, velocity)
    fetches.start(forcing_hbm, forcing)
    fetches.start(base_hbm, base)
    table[...] = jnp.zeros_like(table)

    nothing = jnp.zeros((cells_radial, cells_side), jnp.float32)

    def put(field, plane, value):
        fields[field, pl.ds(plane * pitch, cells_radial), :] = value

    def lay_out(those):
        for field in those:
            for t in range(cells_radial):
                row = outward_row(t, cells_radial)
                lines_ref[field, t] = fields[field, pl.ds(row, planes, stride=pitch), :]

    def step(first_row):
        loads, plane, side = tracer_block(
            count, values_ref, cells_ref, 1, first_row, block_rows, cells_side
        )
        table[...] += hot_product(
            loads, *fold_inner(plane - moved_planes, side, inner_planes, cells_side)
        )

    count = jnp.max(count_ref[...]).astype(jnp.int32)
    for_used_blocks(count, group_rows, block_rows, lane_total, [], step)

    fetches.wait(0, None)
    for plane in range(planes):
        x = plane - margin
        own = 0 <= x < cells_lateral
        for q in range(3):
            put(VELOCITY + q, plane, velocity[q, x] if own else nothing)
        for q in range(2):
            put(SOURCE + q, plane, forcing[q, x] if own else nothing)
    late = VISCOSITY, SOURCE + 2
    lay_out(field for field in range(LINE_FIELDS) if field not in late)

    for q in range(3):

        def put_sums(plane, column, block):
            height, width = block.shape
            sums[q, pl.ds(plane, height), column : column + width] = block

        unfold_inner(table, q, inner_planes, cells_side, put_sums)
    for plane in range(planes):
        x = plane - 2 * margin
        viscosity, source = nothing, nothing
        if 0 <= x < inner:
            rows = pl.ds(x * cells_radial, cells_radial)
            cell_sums = [sums[q, rows, :] for q in range(3)]
            basalt_share, melt_share, viscosity = composition_of(cell_sums, base[x + margin])
            source = forcing[2, x + margin] - BUOYANCY * basalt_share
            composition_ref[0, x] = basalt_share
            composition_ref[1, x] = melt_share
        put(VISCOSITY, plane, viscosity)
        put(SOURCE + 2, plane, source)
    lay_out(late)
    for offset in range(margin):
        for place, x in ((offset, offset), (margin + offset, cells_lateral - margin + offset)):
            outer_ref[0, place] = base[x]
            outer_ref[1, place] = forcing[2, x]


BLOCK_ROWS = 64


def dense_tracers(tracer_values, tracer_cell):
    lane_total = 128
    return tracer_values.reshape(3, 3, -1, lane_total), tracer_cell.reshape(3, -1, lane_total)


def outgoing_sums(tracer_count, values, cells, base_viscosity, velocity, forcing):
    cells_lateral, cells_radial, cells_side = base_viscosity.shape
    moved_planes = MIGRATION_PLANES * cells_radial
    group_rows, lane_total = cells.shape[1:]
    block_rows = min(BLOCK_ROWS, group_rows // 2)
    _, payload_rows = payload_sections(cells_radial)
    hbm = pl.BlockSpec(memory_space=pltpu.HBM)
    vmem = pl.BlockSpec(memory_space=pltpu.VMEM)
    payload = jax.ShapeDtypeStruct((payload_rows, cells_side), jnp.float32)
    outer_planes = (MIGRATION_PLANES, cells_radial, cells_side)
    return pl.pallas_call(
        functools.partial(outgoing_kernel, block_rows),
        out_shape=(
            jax.ShapeDtypeStruct((6 * moved_planes, cells_side), jnp.float32),
            payload,
            payload,
            jax.ShapeDtypeStruct((8, lane_total), jnp.float32),
            jax.ShapeDtypeStruct(values.shape, jnp.float32),
            jax.ShapeDtypeStruct(cells.shape, jnp.int32),
        ),
        in_specs=[hbm] * 6,
        out_specs=(vmem,) * 6,
        scratch_shapes=[
            pltpu.SMEM(tracer_count.shape, jnp.int32),
            pltpu.VMEM((2,) + outer_planes, jnp.float32),
            pltpu.VMEM((2, 3) + outer_planes, jnp.float32),
            pltpu.VMEM((2, 3, 1, cells_radial, cells_side), jnp.float32),
            pltpu.VMEM(hot_shape(2 * moved_planes, cells_side), jnp.float32),
            pltpu.VMEM((2,) + hot_shape(moved_planes, cells_side), jnp.float32),
            pltpu.SemaphoreType.DMA((13,)),
        ],
        compiler_params=pltpu.CompilerParams(vmem_limit_bytes=32 * 2**20),
        cost_estimate=pl.CostEstimate(
            flops=30 * group_rows * lane_total * moved_planes * cells_side,
            bytes_accessed=4 * (values.size + cells.size),
            transcendentals=0,
        ),
        name="outgoing_sums",
    )(
        *(
            pltpu.with_memory_space_constraint(array, pltpu.HBM)
            for array in (tracer_count, values, cells, base_viscosity, velocity, forcing)
        )
    )


def inner_lines(count, values, cells, base_viscosity, velocity, forcing):
    cells_lateral, cells_radial, cells_side = base_viscosity.shape
    planes = cells_lateral + 2 * MIGRATION_PLANES
    inner = cells_lateral - 2 * MIGRATION_PLANES
    inner_planes = inner * cells_radial
    group_rows, lane_total = cells.shape[1:]
    block_rows = min(BLOCK_ROWS, group_rows // 2)
    vmem = pl.BlockSpec(memory_space=pltpu.VMEM)
    return pl.pallas_call(
        functools.partial(inner_kernel, block_rows),
        out_shape=(
            jax.ShapeDtypeStruct((2, inner, cells_radial, cells_side), jnp.float32),
            jax.ShapeDtypeStruct((LINE_FIELDS, cells_radial, planes, cells_side), jnp.float32),
            jax.ShapeDtypeStruct(
                (2, 2 * MIGRATION_PLANES, cells_radial, cells_side), jnp.float32
            ),
        ),
        in_specs=[vmem] * 3 + [pl.BlockSpec(memory_space=pltpu.HBM)] * 3,
        out_specs=(vmem,) * 3,
        scratch_shapes=[
            pltpu.VMEM((3 * (inner_planes * 5 // 6), cells_side * 5 // 4), jnp.float32),
            pltpu.VMEM((3, inner_planes, cells_side), jnp.float32),
            pltpu.VMEM((LINE_FIELDS, planes * round_up(cells_radial, 8), cells_side), jnp.float32),
            pltpu.VMEM(base_viscosity.shape, jnp.float32),
            pltpu.VMEM(velocity.shape, jnp.float32),
            pltpu.VMEM(forcing.shape, jnp.float32),
            pltpu.SemaphoreType.DMA((3,)),
        ],
        compiler_params=pltpu.CompilerParams(vmem_limit_bytes=32 * 2**20),
        cost_estimate=pl.CostEstimate(
            flops=6 * group_rows * lane_total * inner * cells_radial * cells_side,
            bytes_accessed=4 * (values.size + cells.size),
            transcendentals=0,
        ),
        name="inner_lines",
    )(
        count,
        values,
        cells,
        *(
            pltpu.with_memory_space_constraint(array, pltpu.HBM)
            for array in (base_viscosity, velocity, forcing)
        ),
    )


def pair_swaps(first, second):
    count = lax.axis_size("lat")
    received = []
    for payload, start in ((second, 1), (first, 0)):
        target = list(range(count))
        for low in range(start, count - 1, 2):
            target[low], target[low + 1] = low + 1, low
        received.append(lax.ppermute(payload, "lat", list(enumerate(target))))
    return received[::-1]


def shift_planes(block, step):
    return pltpu.roll(block, step % block.shape[0], 0)


def shift_side(block, step):
    return pltpu.roll(block, step % block.shape[1], 1)


def neighbours(block):
    return (
        shift_planes(block, 1),
        shift_planes(block, -1),
        shift_side(block, 1),
        shift_side(block, -1),
    )


def inside_side(values):
    lane = lax.broadcasted_iota(jnp.int32, values[2].shape, 1)
    lower = jnp.where(lane > 0, values[2], 0.0)
    upper = jnp.where(lane < lane.shape[1] - 1, values[3], 0.0)
    return values[0], values[1], lower, upper


def total_of(terms):
    result = terms[0]
    for term in terms[1:]:
        result = result + term
    return result


def inside_grid(shape, margin, cells_lateral):
    plane = lax.broadcasted_iota(jnp.int32, shape, 0)
    lateral = lax.axis_index("lat")
    first = jnp.where(lateral == 0, margin, 1)
    last = jnp.where(lateral == lax.axis_size("lat") - 1, margin + cells_lateral, shape[0] - 1)
    return (plane >= first) & (plane < last)


LONG_FIELDS, SHORT_FIELDS = 5, 7


def message_rows(cells_lateral):
    planes = cells_lateral + 2 * MIGRATION_PLANES
    return round_up(LONG_FIELDS * planes + SHORT_FIELDS * cells_lateral + MIGRATION_PLANES, 8)


def message_part(cells_lateral, field):
    planes = cells_lateral + 2 * MIGRATION_PLANES
    if field < LONG_FIELDS:
        return pl.ds(field * planes, planes), 0, planes
    first = LONG_FIELDS * planes + (field - LONG_FIELDS) * cells_lateral
    return pl.ds(first, cells_lateral), MIGRATION_PLANES, cells_lateral


def solve_lines(radial, cells_radial, valid, keep, keep_part):
    last = cells_radial - 1
    viscosity = [radial(VISCOSITY, t) for t in range(cells_radial)]
    lateral_faces, lateral_sums = [], []
    for here in viscosity:
        faces = [LATERAL * 0.5 * (here + there) for there in inside_side(neighbours(here))]
        lateral_sums.append(total_of(faces))
        lateral_faces.append(inside_side(faces))
    radial_faces = [RADIAL * 0.5 * viscosity[0]] + [
        RADIAL * 0.5 * (viscosity[t - 1] + viscosity[t]) for t in range(1, cells_radial)
    ]

    excess = lateral_sums[0] + radial_faces[0]
    inverse, coupling = [], []
    for t in range(last):
        inverse.append(1.0 / (excess + radial_faces[t + 1]))
        coupling.append(radial_faces[t + 1] * inverse[t])
        excess = lateral_sums[t + 1] + coupling[t] * excess

    def lateral_terms(t, around):
        return [face * there for face, there in zip(lateral_faces[t], around)]

    def forward(right_side):
        eliminated = [right_side[0]]
        for t in range(1, cells_radial):
            eliminated.append(right_side[t] + coupling[t - 1] * eliminated[t - 1])
        return eliminated

    def backward(eliminated):
        solved = [jnp.zeros_like(excess)]
        for t in range(last - 1, -1, -1):
            solved.append(eliminated[t] * inverse[t] + coupling[t] * solved[-1])
        return solved[::-1]

    response = [jnp.ones_like(excess)]
    for t in range(last - 1, -1, -1):
        response.append(coupling[t] * response[-1])
    response = response[::-1]

    def finish(part, eliminated):
        keep(LONG_FIELDS + part, eliminated[last])
        for t, value in enumerate(eliminated[:last]):
            keep_part(part, t, value)

    keep(0, viscosity[last])
    keep(1, excess)
    for q in range(3):
        source = [radial(SOURCE + q, t) for t in range(cells_radial)]
        eliminated = forward(
            [
                total_of([source[t]] + lateral_terms(t, neighbours(radial(VELOCITY + q, t))))
                for t in range(cells_radial)
            ]
        )
        keep(2 + q, eliminated[last])
        particular = [jnp.where(valid, value, 0.0) for value in backward(eliminated)]
        finish(
            q,
            forward(
                [
                    total_of([source[t]] + lateral_terms(t, neighbours(particular[t])))
                    for t in range(cells_radial)
                ]
            ),
        )
    around = [neighbours(jnp.where(valid, value, 0.0)) for value in response]
    for side in range(4):
        finish(
            3 + side,
            forward([lateral_faces[t][side] * around[t][side] for t in range(cells_radial)]),
        )
    for t in range(last):
        keep_part(SHORT_FIELDS, t, inverse[t])
        keep_part(SHORT_FIELDS + 1, t, coupling[t])


def eliminate_kernel(
    inner_ref,
    lines_ref,
    edge_ref,
    second_ref,
    first_ref,
    from_second_ref,
    from_first_ref,
    outer_ref,
    composition_ref,
    mine_ref,
    message_ref,
    parts_ref,
    fields,
):
    _, cells_lateral, cells_radial, cells_side = composition_ref.shape
    margin = MIGRATION_PLANES
    planes = cells_lateral + 2 * margin
    pitch = round_up(cells_radial, 8)
    moved_planes = margin * cells_radial
    starts, _ = payload_sections(cells_radial)
    odd = lax.rem(lax.axis_index("lat"), 2) == 1

    def sent(upward, start):
        part = pl.ds(start, cells_radial)
        mine_first = odd if not upward else jnp.logical_not(odd)
        return jnp.where(mine_first, first_ref[part, :], second_ref[part, :])

    def arrived(from_above, start):
        part = pl.ds(start, cells_radial)
        is_first = odd if not from_above else jnp.logical_not(odd)
        return jnp.where(is_first, from_first_ref[part, :], from_second_ref[part, :])

    outer = 2 * margin

    def put(field, slot, value):
        fields[field, pl.ds(slot * pitch, cells_radial), :] = value

    for above in (False, True):
        for offset in range(margin):
            shift = offset * cells_radial
            halo = offset + (outer + margin if above else 0)
            own = offset + (outer if above else margin)
            x = offset + (cells_lateral - margin if above else 0)
            place = offset + (margin if above else 0)
            halo_sums, own_sums = [], []
            for q in range(3):
                row = q * moved_planes + shift
                rows = pl.ds((2 * q + int(above)) * moved_planes + shift, cells_radial)
                own_sums.append(edge_ref[rows, :] + arrived(above, starts[0] + row))
                halo_sums.append(sent(above, starts[0] + row) + arrived(above, starts[1] + row))
                put(VELOCITY + q, halo, arrived(above, starts[2] + row))
            basalt_share, melt_share, viscosity = composition_of(own_sums, outer_ref[0, place])
            composition_ref[0, x] = basalt_share
            composition_ref[1, x] = melt_share
            put(VISCOSITY, own, viscosity)
            put(SOURCE + 2, own, outer_ref[1, place] - BUOYANCY * basalt_share)
            basalt_share, _, viscosity = composition_of(
                halo_sums, arrived(above, starts[3] + shift)
            )
            put(VISCOSITY, halo, viscosity)
            beside = offset == (0 if above else margin - 1)
            for q in range(3):
                source = jnp.zeros_like(viscosity)
                if beside:
                    source = arrived(above, starts[4] + q * cells_radial)
                    if q == 2:
                        source = source - BUOYANCY * basalt_share
                put(SOURCE + q, halo, source)
    for x in range(margin, cells_lateral - margin):
        for q in range(2):
            composition_ref[q, x] = inner_ref[q, x - margin]

    def radial(field, t):
        replaced = outer if field in (VISCOSITY, SOURCE + 2) else margin
        plane = lax.broadcasted_iota(jnp.int32, (planes, cells_side), 0)
        own = (plane >= replaced) & (plane < planes - replaced)
        row = outward_row(t, cells_radial)
        edges = fields[field, pl.ds(row, 2 * outer, stride=pitch), :]
        if 2 * outer * 2 == planes:
            edges = jnp.concatenate([edges, edges], 0)
        else:
            gap = jnp.zeros((planes - 2 * outer, cells_side), jnp.float32)
            edges = jnp.concatenate([edges[:outer], gap, edges[outer:]], 0)
        return jnp.where(own, lines_ref[field, t], edges)

    unused = LONG_FIELDS * planes + SHORT_FIELDS * cells_lateral
    if unused < message_ref.shape[0]:
        message_ref[unused:, :] = jnp.zeros((message_ref.shape[0] - unused, cells_side), jnp.float32)

    def keep(field, value):
        rows, first, count = message_part(cells_lateral, field)
        mine_ref[field] = value
        message_ref[rows, :] = value[first : first + count]

    def keep_part(part, t, value):
        parts_ref[part, t] = value

    valid = inside_grid((planes, cells_side), margin, cells_lateral)
    solve_lines(radial, cells_radial, valid, keep, keep_part)


def eliminate(inner, lines, outer, edge, sent, received, cells_lateral):
    cells_radial, cells_side = inner.shape[2:]
    planes = cells_lateral + 2 * MIGRATION_PLANES
    vmem = pl.BlockSpec(memory_space=pltpu.VMEM)
    line = (planes, cells_side)
    return pl.pallas_call(
        eliminate_kernel,
        out_shape=(
            jax.ShapeDtypeStruct((2, cells_lateral, cells_radial, cells_side), jnp.float32),
            jax.ShapeDtypeStruct((LONG_FIELDS + SHORT_FIELDS,) + line, jnp.float32),
            jax.ShapeDtypeStruct((message_rows(cells_lateral), cells_side), jnp.float32),
            jax.ShapeDtypeStruct((SHORT_FIELDS + 2, cells_radial - 1) + line, jnp.float32),
        ),
        in_specs=[vmem] * 8,
        out_specs=(vmem,) * 4,
        scratch_shapes=[
            pltpu.VMEM(
                (LINE_FIELDS, 4 * MIGRATION_PLANES * round_up(cells_radial, 8), cells_side),
                jnp.float32,
            )
        ],
        compiler_params=pltpu.CompilerParams(vmem_limit_bytes=32 * 2**20),
        name="eliminate",
    )(inner, lines, edge, *sent[::-1], *received[::-1], outer)


def join_kernel(mine_ref, message_ref, parts_ref, smoothed_ref, lines):
    _, cells_lateral, cells_radial, cells_side = smoothed_ref.shape
    margin = MIGRATION_PLANES
    planes = cells_lateral + 2 * margin
    pitch = round_up(cells_radial, 8)
    valid = inside_grid((planes, cells_side), margin, cells_lateral)

    def mine(field):
        return mine_ref[field]

    def other(field):
        rows, first, _ = message_part(cells_lateral, field)
        return message_ref[pl.ds(rows.start - first, planes), :]

    face = RADIAL * 0.5 * (mine(0) + other(0))
    excess, other_excess = mine(1), other(1)
    scale = 1.0 / (excess * other_excess + face * (excess + other_excess))
    own_weight = (other_excess + face) * scale
    other_weight = (excess + face) * scale
    cross = face * scale

    def second_right(field_of, q, around):
        terms = [field_of(LONG_FIELDS + 3 + side) * there for side, there in enumerate(around)]
        return total_of([field_of(LONG_FIELDS + q)] + terms)

    around, values = [], []
    for q in range(3):
        right, other_right = mine(2 + q), other(2 + q)
        own = jnp.where(valid, own_weight * right + cross * other_right, 0.0)
        beyond = jnp.where(valid, other_weight * other_right + cross * right, 0.0)
        around.append(neighbours(own))
        right = second_right(mine, q, around[q])
        other_right = second_right(other, q, neighbours(beyond))
        values.append(own_weight * right + cross * other_right)
    for t in range(cells_radial - 1, -1, -1):
        row = outward_row(t, cells_radial)
        if t < cells_radial - 1:
            factors = [parts_ref[3 + side, t] for side in range(4)]
            inverse, coupling = parts_ref[SHORT_FIELDS, t], parts_ref[SHORT_FIELDS + 1, t]
        for q in range(3):
            if t < cells_radial - 1:
                terms = [factor * there for factor, there in zip(factors, around[q])]
                right = total_of([parts_ref[q, t]] + terms)
                values[q] = right * inverse + coupling * values[q]
            lines[q, pl.ds(row, cells_lateral, stride=pitch), :] = values[q][
                margin : margin + cells_lateral
            ]
    for q in range(3):
        for x in range(cells_lateral):
            smoothed_ref[q, x] = lines[q, pl.ds(x * pitch, cells_radial), :]


def join(mine, message, parts, like):
    cells_lateral, cells_radial, cells_side = like.shape[1:]
    vmem = pl.BlockSpec(memory_space=pltpu.VMEM)
    return pl.pallas_call(
        join_kernel,
        out_shape=jax.ShapeDtypeStruct(like.shape, jnp.float32),
        in_specs=[vmem] * 3,
        out_specs=vmem,
        scratch_shapes=[
            pltpu.VMEM((3, cells_lateral * round_up(cells_radial, 8), cells_side), jnp.float32),
        ],
        compiler_params=pltpu.CompilerParams(vmem_limit_bytes=32 * 2**20),
        name="join",
    )(mine, message, parts)


def extended(block, sides, width):
    for axis, dim in sides:
        count = lax.axis_size(axis)
        forward = [(i, i + 1) for i in range(count - 1)]
        backward = [(target, source) for source, target in forward]
        low = lax.ppermute(
            lax.slice_in_dim(block, block.shape[dim] - width, None, axis=dim), axis, forward
        )
        high = lax.ppermute(lax.slice_in_dim(block, 0, width, axis=dim), axis, backward)
        block = jnp.concatenate([low, block, high], axis=dim)
    return block


def block_factor(diagonal, lower_band, upper_band):
    pivots = []
    upper_scaled = []
    for row_index in range(diagonal.shape[1]):
        if row_index == 0:
            pivot_row = diagonal[:, 0]
        else:
            pivot_row = diagonal[:, row_index] - lower_band[:, row_index] * upper_scaled[-1]
        pivots.append(pivot_row)
        upper_scaled.append(upper_band[:, row_index] / pivot_row)
    return (pivots, upper_scaled)


def block_solve(pivots, upper_scaled, lower_band, right_side):
    row_total = len(pivots)
    modified = []
    for row_index in range(row_total):
        if row_index == 0:
            value_row = right_side[:, :, 0] / pivots[0]
        else:
            value_row = (
                right_side[:, :, row_index] - lower_band[:, row_index] * modified[-1]
            ) / pivots[row_index]
        modified.append(value_row)
    solved = [modified[-1]]
    for row_index in range(row_total - 2, -1, -1):
        solved.append(modified[row_index] - upper_scaled[row_index] * solved[-1])
    ordered = solved[::-1]
    return jnp.stack(ordered, 2)


def interface_solve(coefficients):
    column_total = coefficients.shape[2]

    def forward(carried, inputs):
        offset, carried_slope = carried
        left_first, right_first, left_last, right_last, free_first, free_last = inputs
        divisor = 1.0 - left_first * carried_slope
        first_fixed = (free_first + left_first * offset) / divisor
        first_slope = right_first / divisor
        next_offset = free_last + left_last * (offset + carried_slope * first_fixed)
        next_slope = left_last * carried_slope * first_slope + right_last
        return ((next_offset, next_slope), (first_fixed, first_slope, next_offset, next_slope))

    start_state = (
        jnp.zeros((3, column_total), jnp.float32),
        jnp.zeros((column_total,), jnp.float32),
    )
    scan_inputs = (
        coefficients[:, 0],
        coefficients[:, 1],
        coefficients[:, 2],
        coefficients[:, 3],
        coefficients[:, 4:7],
        coefficients[:, 7:10],
    )
    final_state, eliminated = lax.scan(forward, start_state, scan_inputs)

    def backward(first_next, inputs):
        fixed_first, slope_first, fixed_last, slope_last = inputs
        first_value = fixed_first + slope_first * first_next
        last_value = fixed_last + slope_last * first_next
        return (first_value, (first_value, last_value))

    final_first, values_pair = lax.scan(
        backward, jnp.zeros((3, column_total), jnp.float32), eliminated, reverse=True
    )
    first_values, last_values = values_pair
    nothing_row = jnp.zeros((1, 3, column_total), jnp.float32)
    from_below = jnp.concatenate([nothing_row, last_values[:-1]], 0)
    from_above = jnp.concatenate([first_values[1:], nothing_row], 0)
    return jnp.concatenate([from_below, from_above], 1)


def reduced_boundary(interface):
    gathered = lax.all_gather(interface, "rad", axis=0, tiled=True)
    solved = interface_solve(gathered)
    return lax.dynamic_index_in_dim(solved, lax.axis_index("rad"), 0, keepdims=False)


def many_blocks(values, cells, count, edge, received, base_viscosity, velocity, forcing):
    cells_lateral, cells_radial, cells_side = base_viscosity.shape
    moved_rows = MIGRATION_PLANES * cells_radial
    odd = lax.rem(lax.axis_index("lat"), 2) == 1
    from_below = jnp.where(odd, received[0], received[1])[: 3 * moved_rows]
    from_above = jnp.where(odd, received[1], received[0])[: 3 * moved_rows]
    edge = edge.reshape(3, 2, moved_rows, cells_side)
    below = edge[:, 0] + from_below.reshape(3, moved_rows, cells_side)
    above = edge[:, 1] + from_above.reshape(3, moved_rows, cells_side)
    shares = [
        (sums[1:] / (sums[0] + PRIOR_WEIGHT)).reshape(2, -1, cells_radial, cells_side)
        for sums in (below, above)
    ]
    inner, _, _ = inner_lines(count, values, cells, base_viscosity, velocity, forcing)
    basalt_share, melt_share = jnp.concatenate([shares[0], inner, shares[1]], 1)
    viscosity = base_viscosity * jnp.exp(
        CONTRAST_BASALT * basalt_share - CONTRAST_MELT * melt_share
    )
    viscosity_pad = extended(viscosity, (("lat", 0), ("rad", 1)), 1)
    side_pad = jnp.pad(viscosity, ((0, 0), (0, 0), (1, 1)))
    face_west = LATERAL * 0.5 * (viscosity + viscosity_pad[:-2, 1:-1])
    face_east = LATERAL * 0.5 * (viscosity + viscosity_pad[2:, 1:-1])
    face_south = LATERAL * 0.5 * (viscosity + side_pad[:, :, :-2])
    face_north = LATERAL * 0.5 * (viscosity + side_pad[:, :, 2:])
    face_below = RADIAL * 0.5 * (viscosity + viscosity_pad[1:-1, :-2])
    face_above = RADIAL * 0.5 * (viscosity + viscosity_pad[1:-1, 2:])
    diagonal = face_west + face_east + face_south + face_north + face_below + face_above
    source = jnp.concatenate([forcing[:2], (forcing[2] - BUOYANCY * basalt_share)[None]], 0)
    lower_band = -face_below
    upper_band = -face_above
    pivots, upper_scaled = block_factor(diagonal, lower_band, upper_band)
    radial_iota = lax.broadcasted_iota(jnp.int32, viscosity.shape, 1)
    response_side = jnp.stack(
        [
            jnp.where(radial_iota == 0, face_below, jnp.float32(0.0)),
            jnp.where(radial_iota == cells_radial - 1, face_above, jnp.float32(0.0)),
        ]
    )
    response = block_solve(pivots, upper_scaled, lower_band, response_side)
    current = velocity
    for sweep_index in range(SWEEPS):
        velocity_pad = extended(current, (("lat", 1),), 1)
        side_velocity = jnp.pad(current, ((0, 0), (0, 0), (0, 0), (1, 1)))
        right_side = (
            source
            + face_west * velocity_pad[:, :-2]
            + face_east * velocity_pad[:, 2:]
            + face_south * side_velocity[..., :-2]
            + face_north * side_velocity[..., 2:]
        )
        particular = block_solve(pivots, upper_scaled, lower_band, right_side)
        interface = jnp.concatenate(
            [response[:, :, 0], response[:, :, -1], particular[:, :, 0], particular[:, :, -1]], 0
        )
        interface = interface.reshape(1, 10, cells_lateral * cells_side)
        boundary = reduced_boundary(interface).reshape(6, cells_lateral, 1, cells_side)
        current = particular + response[0][None] * boundary[:3] + response[1][None] * boundary[3:]
    composition = jnp.stack([basalt_share, melt_share])
    return (current, composition)

def local(tracer_values, tracer_cell, tracer_count, base_viscosity, velocity, forcing):
    values, cells = dense_tracers(tracer_values, tracer_cell)
    edge, first, second, count, values, cells = outgoing_sums(
        tracer_count, values, cells, base_viscosity, velocity, forcing
    )
    sent = first, second
    received = pair_swaps(first, second)
    if lax.axis_size("rad") != 2:
        return many_blocks(
            values, cells, count, edge, received, base_viscosity, velocity, forcing
        )
    inner, lines, outer = inner_lines(count, values, cells, base_viscosity, velocity, forcing)
    composition, mine, message, parts = eliminate(
        inner, lines, outer, edge, sent, received, base_viscosity.shape[0]
    )
    other = lax.ppermute(message, "rad", [(0, 1), (1, 0)])
    return join(mine, other, parts, velocity), composition


def solution(mesh):
    return jax.shard_map(
        local,
        mesh=mesh,
        in_specs=(
            P("lat", "rad", None, None),
            P("lat", "rad", None),
            P("lat", "rad", None),
            P("lat", "rad", None),
            P(None, "lat", "rad", None),
            P(None, "lat", "rad", None),
        ),
        out_specs=(P(None, "lat", "rad", None), P(None, "lat", "rad", None)),
        check_vma=False,
    )
```

```python
import functools

import jax
import jax.numpy as jnp
from jax import lax
from jax.experimental import pallas as pl
from jax.experimental.pallas import tpu as pltpu
from jax.sharding import PartitionSpec as P

SWEEPS = 2
MIGRATION_PLANES = 2

LATERAL = 0.015625
RADIAL = 32.0
BUOYANCY = 0.1
PRIOR_WEIGHT = 0.5
CONTRAST_BASALT = 2.3
CONTRAST_MELT = 1.5

TILE_ROWS = 16


def round_up(value, multiple):
    return -(-value // multiple) * multiple


def split_index(index, count):
    if count & (count - 1) == 0:
        return lax.shift_right_logical(index, count.bit_length() - 1), index & (count - 1)
    quotient = lax.div(index, count)
    return quotient, index - quotient * count


def payload_sections(cells_radial):
    pair = MIGRATION_PLANES * cells_radial
    starts = [0, 3 * pair, 6 * pair, 9 * pair, 10 * pair]
    return starts, round_up(10 * pair + 3 * cells_radial, 8)


def spread_row(row):
    return jnp.broadcast_to(row, (TILE_ROWS, row.shape[1])).astype(jnp.bfloat16)


def hot_tiles(index, row_total):
    iota = lax.broadcasted_iota(jnp.int32, index.shape, 0)
    return [
        index == (iota + first).astype(jnp.float32).astype(jnp.bfloat16)
        for first in range(0, row_total, TILE_ROWS)
    ]


def hot_product(sums, loads, high, low, high_rows, low_rows, chunk_rows):
    high, low = high.astype(jnp.float32), low.astype(jnp.float32)
    zero = jnp.zeros((TILE_ROWS, high.shape[1]), jnp.bfloat16)
    one = jnp.ones((TILE_ROWS, high.shape[1]), jnp.bfloat16)
    for first_row in range(0, high.shape[0], chunk_rows):
        left, right = [], []
        for row in range(first_row, first_row + chunk_rows):
            pick = slice(row, row + 1)
            high_masks = hot_tiles(spread_row(high[pick]), high_rows)
            low_masks = hot_tiles(spread_row(low[pick]), low_rows)
            spread = [spread_row(load[pick]) for load in loads]
            tiles = [jnp.where(mask, load, zero) for load in spread for mask in high_masks]
            left.append(jnp.concatenate(tiles, 0))
            right.append(jnp.concatenate([jnp.where(mask, one, zero) for mask in low_masks], 0))
        sums = sums + lax.dot_general(
            jnp.concatenate(left, 1),
            jnp.concatenate(right, 1),
            (((1,), (1,)), ((), ())),
            preferred_element_type=jnp.float32,
        )
    return sums


def edge_row(plane, plane_total, moved_total):
    inner = (plane >= moved_total) & (plane < plane_total - moved_total)
    last = plane - (plane_total - 2 * moved_total)
    return jnp.where(inner, -plane_total, jnp.where(plane < moved_total, plane, last))


def fold_moved(plane, side, plane_total, side_total):
    width, third = side_total // 4, plane_total // 3
    part = jnp.where(plane >= third, 1, 0) + jnp.where(plane >= 2 * third, 1, 0)
    other = side >= 3 * width
    high = jnp.where(other, plane_total + plane - part * third, plane)
    low = jnp.where(other, side - 3 * width + part * width, side)
    return high, low, plane_total + third, 3 * width


def unfold_moved(table, q, plane_total, side_total, put):
    width, third = side_total // 4, plane_total // 3
    rows = plane_total + third
    put(0, 0, table[pl.ds(q * rows, plane_total), 0 : 3 * width])
    for part in range(3):
        block = table[
            pl.ds(q * rows + plane_total, third), part * width : (part + 1) * width
        ]
        put(part * third, 3 * width, block)


def fold_inner(plane, side, plane_total, side_total):
    rows, width = plane_total * 5 // 6, side_total // 4
    part, rest = split_index(side, width)
    other = plane >= rows
    high = jnp.where(other, plane - rows + part * (plane_total - rows), plane)
    high = jnp.where(plane < plane_total, high, -1)
    low = jnp.where(other, side_total + rest, side)
    return high, low, rows, side_total + width


def unfold_inner(table, q, plane_total, side_total, put):
    rows, width = plane_total * 5 // 6, side_total // 4
    left = plane_total - rows
    put(0, 0, table[pl.ds(q * rows, rows), 0:side_total])
    for part in range(4):
        block = table[pl.ds(q * rows + part * left, left), side_total : side_total + width]
        put(rows, part * width, block)


def tracer_block(count, values, cells, group, first_row, block_rows, cells_side):
    rows = pl.ds(first_row, block_rows)
    lane_total = cells.shape[2]
    shape = (block_rows, lane_total)
    slot = (first_row + lax.broadcasted_iota(jnp.int32, shape, 0)) * lane_total
    slot = slot + lax.broadcasted_iota(jnp.int32, shape, 1)
    weight = jnp.where(slot < count, 0.5 + values[0, group, rows, :], jnp.float32(0.0))
    loads = [weight, weight * values[1, group, rows, :], weight * values[2, group, rows, :]]
    plane, side = split_index(cells[group, rows, :], cells_side)
    return loads, plane, side


def for_used_blocks(used, group_rows, block_rows, lane_total, late_copies, step):
    block_slots = block_rows * lane_total
    blocks = lax.div(used + (block_slots - 1), block_slots)
    blocks = jnp.clip(blocks, 1, group_rows // block_rows)

    def wait_late():
        for copy in late_copies:
            copy.wait()

    def repeat(index, carried):
        pl.when(index == 1)(wait_late)
        step(pl.multiple_of(index * block_rows, block_rows))
        return carried

    lax.fori_loop(0, blocks, repeat, 0)
    pl.when(blocks == 1)(wait_late)


VISCOSITY, VELOCITY, SOURCE, LINE_FIELDS = 0, 1, 4, 7


def composition_of(cell_sums, base):
    scale = 1.0 / (cell_sums[0] + PRIOR_WEIGHT)
    basalt_share, melt_share = cell_sums[1] * scale, cell_sums[2] * scale
    weakening = jnp.exp(CONTRAST_BASALT * basalt_share - CONTRAST_MELT * melt_share)
    return basalt_share, melt_share, base * weakening


def outward_row(t, cells_radial):
    return jnp.where(lax.axis_index("rad") == 0, t, cells_radial - 1 - t)


class Fetches:
    def __init__(self, semaphores):
        self.semaphores = semaphores
        self.copies = []

    def start(self, source, target):
        copy = pltpu.make_async_copy(source, target, self.semaphores.at[len(self.copies)])
        copy.start()
        self.copies.append(copy)

    def wait(self, first, last):
        for copy in self.copies[first:last]:
            copy.wait()


def has_partners():
    lateral, count = lax.axis_index("lat"), lax.axis_size("lat")
    odd = lax.rem(lateral, 2) == 1
    above, below = lateral + 1 < count, lateral > 0
    return jnp.logical_or(odd, above), jnp.where(odd, above, below)


def outgoing_kernel(
    block_rows,
    counts_hbm,
    values_hbm,
    cells_hbm,
    base_hbm,
    velocity_hbm,
    forcing_hbm,
    edge_ref,
    first_ref,
    second_ref,
    count_ref,
    values,
    cells,
    counts,
    base,
    velocity,
    forcing,
    moved_sums,
    semaphores,
):
    cells_lateral, cells_radial, cells_side = base_hbm.shape
    plane_total = cells_lateral * cells_radial
    moved_planes = MIGRATION_PLANES * cells_radial
    group_rows, lane_total = cells.shape[1:]

    fetches = Fetches(semaphores)
    fetches.start(counts_hbm, counts)
    part = pl.ds(0, block_rows)
    fetches.start(cells_hbm.at[:, part], cells.at[:, part])
    for q in range(3):
        fetches.start(values_hbm.at[q, :, part], values.at[q, :, part])
    part = pl.ds(block_rows, group_rows - block_rows)
    fetches.start(cells_hbm.at[:, part], cells.at[:, part])
    fetches.start(values_hbm.at[:, :, part], values.at[:, :, part])
    for upward in (0, 1):
        outer = pl.ds((cells_lateral - MIGRATION_PLANES) * upward, MIGRATION_PLANES)
        fetches.start(base_hbm.at[outer], base.at[upward])
        fetches.start(velocity_hbm.at[:, outer], velocity.at[upward])
        outermost = pl.ds((cells_lateral - 1) * upward, 1)
        fetches.start(forcing_hbm.at[:, outermost], forcing.at[upward])

    edge_ref[...] = jnp.zeros_like(edge_ref)
    moved_sums[...] = jnp.zeros_like(moved_sums)

    def step(first_row):
        def block_of(group):
            count = counts[0, 0, group]
            return tracer_block(count, values, cells, group, first_row, block_rows, cells_side)

        loads, plane, side = block_of(1)
        row = edge_row(plane, plane_total, moved_planes)
        edge_ref[...] = hot_product(
            edge_ref[...], loads, row, side, 2 * moved_planes, cells_side, CHUNK_ROWS
        )
        for slot, group in enumerate((0, 2)):
            loads, plane, side = block_of(group)
            if group == 0:
                plane = plane - (plane_total - moved_planes)
            table = fold_moved(plane, side, moved_planes, cells_side)
            moved_sums[slot] = hot_product(moved_sums[slot], loads, *table, CHUNK_ROWS)

    fetches.wait(0, 5)
    count_ref[...] = jnp.full(count_ref.shape, counts[0, 0, 1], jnp.int32).astype(jnp.float32)
    used = jnp.maximum(jnp.maximum(counts[0, 0, 0], counts[0, 0, 1]), counts[0, 0, 2])
    for_used_blocks(used, group_rows, block_rows, lane_total, fetches.copies[5:7], step)
    fetches.wait(7, None)

    starts, rows_total = payload_sections(cells_radial)
    unused = starts[4] + 3 * cells_radial

    def fill(payload, upward):
        for q in range(3):

            def put_moved(plane, column, block):
                height, width = block.shape
                rows = pl.ds(starts[0] + q * moved_planes + plane, height)
                payload[rows, column : column + width] = block

            unfold_moved(moved_sums.at[upward], q, moved_planes, cells_side, put_moved)
            payload[pl.ds(starts[1] + q * moved_planes, moved_planes), :] = edge_ref[
                pl.ds((2 * q + upward) * moved_planes, moved_planes), :
            ]
            for offset in range(MIGRATION_PLANES):
                row = starts[2] + q * moved_planes + offset * cells_radial
                payload[pl.ds(row, cells_radial), :] = velocity[upward, q, offset]
            row = starts[4] + q * cells_radial
            payload[pl.ds(row, cells_radial), :] = forcing[upward, q, 0]
        for offset in range(MIGRATION_PLANES):
            row = starts[3] + offset * cells_radial
            payload[pl.ds(row, cells_radial), :] = base[upward, offset]
        if unused < rows_total:
            payload[unused:, :] = jnp.zeros((rows_total - unused, cells_side), jnp.float32)

    odd = lax.rem(lax.axis_index("lat"), 2) == 1

    @pl.when(odd)
    def _():
        fill(first_ref, 0)
        fill(second_ref, 1)

    @pl.when(jnp.logical_not(odd))
    def _():
        fill(first_ref, 1)
        fill(second_ref, 0)

    for payload, exists in zip((first_ref, second_ref), has_partners()):

        @pl.when(jnp.logical_not(exists))
        def _():
            payload[...] = jnp.zeros_like(payload)


def inner_kernel(
    block_rows,
    count_ref,
    values_ref,
    cells_ref,
    base_hbm,
    velocity_hbm,
    forcing_hbm,
    composition_ref,
    lines_ref,
    outer_ref,
    table,
    sums,
    fields,
    base,
    velocity,
    forcing,
    semaphores,
):
    cells_lateral, cells_radial, cells_side = base.shape
    margin = MIGRATION_PLANES
    planes = cells_lateral + 2 * margin
    pitch = round_up(cells_radial, 8)
    moved_planes = margin * cells_radial
    inner = cells_lateral - 2 * margin
    inner_planes = inner * cells_radial
    group_rows, lane_total = cells_ref.shape[1:]
    fetches = Fetches(semaphores)
    fetches.start(velocity_hbm, velocity)
    fetches.start(forcing_hbm, forcing)
    fetches.start(base_hbm, base)
    table[...] = jnp.zeros_like(table)

    nothing = jnp.zeros((cells_radial, cells_side), jnp.float32)

    def put(field, plane, value):
        fields[field, pl.ds(plane * pitch, cells_radial), :] = value

    def lay_out(those):
        for field in those:
            for t in range(cells_radial):
                row = outward_row(t, cells_radial)
                lines_ref[field, t] = fields[field, pl.ds(row, planes, stride=pitch), :]

    def step(first_row):
        loads, plane, side = tracer_block(
            count, values_ref, cells_ref, 1, first_row, block_rows, cells_side
        )
        where = fold_inner(plane - moved_planes, side, inner_planes, cells_side)
        table[...] = hot_product(table[...], loads, *where, block_rows)

    count = jnp.max(count_ref[...]).astype(jnp.int32)
    for_used_blocks(count, group_rows, block_rows, lane_total, [], step)

    fetches.wait(0, None)
    for plane in range(planes):
        x = plane - margin
        own = 0 <= x < cells_lateral
        for q in range(3):
            put(VELOCITY + q, plane, velocity[q, x] if own else nothing)
        for q in range(2):
            put(SOURCE + q, plane, forcing[q, x] if own else nothing)
    late = VISCOSITY, SOURCE + 2
    lay_out(field for field in range(LINE_FIELDS) if field not in late)

    for q in range(3):

        def put_sums(plane, column, block):
            height, width = block.shape
            sums[q, pl.ds(plane, height), column : column + width] = block

        unfold_inner(table, q, inner_planes, cells_side, put_sums)
    for plane in range(planes):
        x = plane - 2 * margin
        viscosity, source = nothing, nothing
        if 0 <= x < inner:
            rows = pl.ds(x * cells_radial, cells_radial)
            cell_sums = [sums[q, rows, :] for q in range(3)]
            basalt_share, melt_share, viscosity = composition_of(cell_sums, base[x + margin])
            source = forcing[2, x + margin] - BUOYANCY * basalt_share
            composition_ref[0, x] = basalt_share
            composition_ref[1, x] = melt_share
        put(VISCOSITY, plane, viscosity)
        put(SOURCE + 2, plane, source)
    lay_out(late)
    for offset in range(margin):
        for place, x in ((offset, offset), (margin + offset, cells_lateral - margin + offset)):
            outer_ref[0, place] = base[x]
            outer_ref[1, place] = forcing[2, x]


BLOCK_ROWS = 64
CHUNK_ROWS = 2


def dense_tracers(tracer_values, tracer_cell):
    lane_total = 128
    return tracer_values.reshape(3, 3, -1, lane_total), tracer_cell.reshape(3, -1, lane_total)


def outgoing_sums(tracer_count, values, cells, base_viscosity, velocity, forcing):
    cells_lateral, cells_radial, cells_side = base_viscosity.shape
    moved_planes = MIGRATION_PLANES * cells_radial
    group_rows, lane_total = cells.shape[1:]
    block_rows = min(BLOCK_ROWS, group_rows // 2)
    _, payload_rows = payload_sections(cells_radial)
    hbm = pl.BlockSpec(memory_space=pltpu.HBM)
    vmem = pl.BlockSpec(memory_space=pltpu.VMEM)
    payload = jax.ShapeDtypeStruct((payload_rows, cells_side), jnp.float32)
    outer_planes = (MIGRATION_PLANES, cells_radial, cells_side)
    return pl.pallas_call(
        functools.partial(outgoing_kernel, block_rows),
        out_shape=(
            jax.ShapeDtypeStruct((6 * moved_planes, cells_side), jnp.float32),
            payload,
            payload,
            jax.ShapeDtypeStruct((8, lane_total), jnp.float32),
            jax.ShapeDtypeStruct(values.shape, jnp.float32),
            jax.ShapeDtypeStruct(cells.shape, jnp.int32),
        ),
        in_specs=[hbm] * 6,
        out_specs=(vmem,) * 6,
        scratch_shapes=[
            pltpu.SMEM(tracer_count.shape, jnp.int32),
            pltpu.VMEM((2,) + outer_planes, jnp.float32),
            pltpu.VMEM((2, 3) + outer_planes, jnp.float32),
            pltpu.VMEM((2, 3, 1, cells_radial, cells_side), jnp.float32),
            pltpu.VMEM((2, 4 * moved_planes, cells_side * 3 // 4), jnp.float32),
            pltpu.SemaphoreType.DMA((13,)),
        ],
        compiler_params=pltpu.CompilerParams(vmem_limit_bytes=32 * 2**20),
        cost_estimate=pl.CostEstimate(
            flops=30 * group_rows * lane_total * moved_planes * cells_side,
            bytes_accessed=4 * (values.size + cells.size),
            transcendentals=0,
        ),
        name="outgoing_sums",
    )(
        *(
            pltpu.with_memory_space_constraint(array, pltpu.HBM)
            for array in (tracer_count, values, cells, base_viscosity, velocity, forcing)
        )
    )


def inner_lines(count, values, cells, base_viscosity, velocity, forcing):
    cells_lateral, cells_radial, cells_side = base_viscosity.shape
    planes = cells_lateral + 2 * MIGRATION_PLANES
    inner = cells_lateral - 2 * MIGRATION_PLANES
    inner_planes = inner * cells_radial
    group_rows, lane_total = cells.shape[1:]
    block_rows = min(BLOCK_ROWS, group_rows // 2)
    vmem = pl.BlockSpec(memory_space=pltpu.VMEM)
    return pl.pallas_call(
        functools.partial(inner_kernel, block_rows),
        out_shape=(
            jax.ShapeDtypeStruct((2, inner, cells_radial, cells_side), jnp.float32),
            jax.ShapeDtypeStruct((LINE_FIELDS, cells_radial, planes, cells_side), jnp.float32),
            jax.ShapeDtypeStruct(
                (2, 2 * MIGRATION_PLANES, cells_radial, cells_side), jnp.float32
            ),
        ),
        in_specs=[vmem] * 3 + [pl.BlockSpec(memory_space=pltpu.HBM)] * 3,
        out_specs=(vmem,) * 3,
        scratch_shapes=[
            pltpu.VMEM((3 * (inner_planes * 5 // 6), cells_side * 5 // 4), jnp.float32),
            pltpu.VMEM((3, inner_planes, cells_side), jnp.float32),
            pltpu.VMEM((LINE_FIELDS, planes * round_up(cells_radial, 8), cells_side), jnp.float32),
            pltpu.VMEM(base_viscosity.shape, jnp.float32),
            pltpu.VMEM(velocity.shape, jnp.float32),
            pltpu.VMEM(forcing.shape, jnp.float32),
            pltpu.SemaphoreType.DMA((3,)),
        ],
        compiler_params=pltpu.CompilerParams(vmem_limit_bytes=32 * 2**20),
        cost_estimate=pl.CostEstimate(
            flops=6 * group_rows * lane_total * inner * cells_radial * cells_side,
            bytes_accessed=4 * (values.size + cells.size),
            transcendentals=0,
        ),
        name="inner_lines",
    )(
        count,
        values,
        cells,
        *(
            pltpu.with_memory_space_constraint(array, pltpu.HBM)
            for array in (base_viscosity, velocity, forcing)
        ),
    )


def pair_swaps(first, second):
    count = lax.axis_size("lat")
    received = []
    for payload, start in ((second, 1), (first, 0)):
        target = list(range(count))
        for low in range(start, count - 1, 2):
            target[low], target[low + 1] = low + 1, low
        received.append(lax.ppermute(payload, "lat", list(enumerate(target))))
    return received[::-1]


def shift_planes(block, step):
    return pltpu.roll(block, step % block.shape[0], 0)


def shift_side(block, step):
    return pltpu.roll(block, step % block.shape[1], 1)


def neighbours(block):
    return (
        shift_planes(block, 1),
        shift_planes(block, -1),
        shift_side(block, 1),
        shift_side(block, -1),
    )


def inside_side(values):
    lane = lax.broadcasted_iota(jnp.int32, values[2].shape, 1)
    lower = jnp.where(lane > 0, values[2], 0.0)
    upper = jnp.where(lane < lane.shape[1] - 1, values[3], 0.0)
    return values[0], values[1], lower, upper


def total_of(terms):
    result = terms[0]
    for term in terms[1:]:
        result = result + term
    return result


def inside_grid(shape, margin, cells_lateral):
    plane = lax.broadcasted_iota(jnp.int32, shape, 0)
    lateral = lax.axis_index("lat")
    first = jnp.where(lateral == 0, margin, 1)
    last = jnp.where(lateral == lax.axis_size("lat") - 1, margin + cells_lateral, shape[0] - 1)
    return (plane >= first) & (plane < last)


LONG_FIELDS, SHORT_FIELDS = 5, 7


def message_rows(cells_lateral):
    planes = cells_lateral + 2 * MIGRATION_PLANES
    return round_up(LONG_FIELDS * planes + SHORT_FIELDS * cells_lateral + MIGRATION_PLANES, 8)


def message_part(cells_lateral, field):
    planes = cells_lateral + 2 * MIGRATION_PLANES
    if field < LONG_FIELDS:
        return pl.ds(field * planes, planes), 0, planes
    first = LONG_FIELDS * planes + (field - LONG_FIELDS) * cells_lateral
    return pl.ds(first, cells_lateral), MIGRATION_PLANES, cells_lateral


def solve_lines(radial, cells_radial, valid, keep, keep_part):
    last = cells_radial - 1
    viscosity = [radial(VISCOSITY, t) for t in range(cells_radial)]
    lateral_faces, lateral_sums = [], []
    for here in viscosity:
        faces = [LATERAL * 0.5 * (here + there) for there in inside_side(neighbours(here))]
        lateral_sums.append(total_of(faces))
        lateral_faces.append(inside_side(faces))
    radial_faces = [RADIAL * 0.5 * viscosity[0]] + [
        RADIAL * 0.5 * (viscosity[t - 1] + viscosity[t]) for t in range(1, cells_radial)
    ]

    excess = lateral_sums[0] + radial_faces[0]
    inverse, coupling = [], []
    for t in range(last):
        inverse.append(1.0 / (excess + radial_faces[t + 1]))
        coupling.append(radial_faces[t + 1] * inverse[t])
        excess = lateral_sums[t + 1] + coupling[t] * excess

    def lateral_terms(t, around):
        return [face * there for face, there in zip(lateral_faces[t], around)]

    def forward(right_side):
        eliminated = [right_side[0]]
        for t in range(1, cells_radial):
            eliminated.append(right_side[t] + coupling[t - 1] * eliminated[t - 1])
        return eliminated

    def backward(eliminated):
        solved = [jnp.zeros_like(excess)]
        for t in range(last - 1, -1, -1):
            solved.append(eliminated[t] * inverse[t] + coupling[t] * solved[-1])
        return solved[::-1]

    response = [jnp.ones_like(excess)]
    for t in range(last - 1, -1, -1):
        response.append(coupling[t] * response[-1])
    response = response[::-1]

    def finish(part, eliminated):
        keep(LONG_FIELDS + part, eliminated[last])
        for t, value in enumerate(eliminated[:last]):
            keep_part(part, t, value)

    keep(0, viscosity[last])
    keep(1, excess)
    for q in range(3):
        source = [radial(SOURCE + q, t) for t in range(cells_radial)]
        eliminated = forward(
            [
                total_of([source[t]] + lateral_terms(t, neighbours(radial(VELOCITY + q, t))))
                for t in range(cells_radial)
            ]
        )
        keep(2 + q, eliminated[last])
        particular = [jnp.where(valid, value, 0.0) for value in backward(eliminated)]
        finish(
            q,
            forward(
                [
                    total_of([source[t]] + lateral_terms(t, neighbours(particular[t])))
                    for t in range(cells_radial)
                ]
            ),
        )
    around = [neighbours(jnp.where(valid, value, 0.0)) for value in response]
    for side in range(4):
        finish(
            3 + side,
            forward([lateral_faces[t][side] * around[t][side] for t in range(cells_radial)]),
        )
    for t in range(last):
        keep_part(SHORT_FIELDS, t, inverse[t])
        keep_part(SHORT_FIELDS + 1, t, coupling[t])


def eliminate_kernel(
    inner_ref,
    lines_ref,
    edge_ref,
    second_ref,
    first_ref,
    from_second_ref,
    from_first_ref,
    outer_ref,
    composition_ref,
    mine_ref,
    message_ref,
    parts_ref,
    fields,
):
    _, cells_lateral, cells_radial, cells_side = composition_ref.shape
    margin = MIGRATION_PLANES
    planes = cells_lateral + 2 * margin
    pitch = round_up(cells_radial, 8)
    moved_planes = margin * cells_radial
    starts, _ = payload_sections(cells_radial)
    odd = lax.rem(lax.axis_index("lat"), 2) == 1

    def sent(upward, start):
        part = pl.ds(start, cells_radial)
        mine_first = odd if not upward else jnp.logical_not(odd)
        return jnp.where(mine_first, first_ref[part, :], second_ref[part, :])

    def arrived(from_above, start):
        part = pl.ds(start, cells_radial)
        is_first = odd if not from_above else jnp.logical_not(odd)
        return jnp.where(is_first, from_first_ref[part, :], from_second_ref[part, :])

    outer = 2 * margin

    def put(field, slot, value):
        fields[field, pl.ds(slot * pitch, cells_radial), :] = value

    for above in (False, True):
        for offset in range(margin):
            shift = offset * cells_radial
            halo = offset + (outer + margin if above else 0)
            own = offset + (outer if above else margin)
            x = offset + (cells_lateral - margin if above else 0)
            place = offset + (margin if above else 0)
            halo_sums, own_sums = [], []
            for q in range(3):
                row = q * moved_planes + shift
                rows = pl.ds((2 * q + int(above)) * moved_planes + shift, cells_radial)
                own_sums.append(edge_ref[rows, :] + arrived(above, starts[0] + row))
                halo_sums.append(sent(above, starts[0] + row) + arrived(above, starts[1] + row))
                put(VELOCITY + q, halo, arrived(above, starts[2] + row))
            basalt_share, melt_share, viscosity = composition_of(own_sums, outer_ref[0, place])
            composition_ref[0, x] = basalt_share
            composition_ref[1, x] = melt_share
            put(VISCOSITY, own, viscosity)
            put(SOURCE + 2, own, outer_ref[1, place] - BUOYANCY * basalt_share)
            basalt_share, _, viscosity = composition_of(
                halo_sums, arrived(above, starts[3] + shift)
            )
            put(VISCOSITY, halo, viscosity)
            beside = offset == (0 if above else margin - 1)
            for q in range(3):
                source = jnp.zeros_like(viscosity)
                if beside:
                    source = arrived(above, starts[4] + q * cells_radial)
                    if q == 2:
                        source = source - BUOYANCY * basalt_share
                put(SOURCE + q, halo, source)
    for x in range(margin, cells_lateral - margin):
        for q in range(2):
            composition_ref[q, x] = inner_ref[q, x - margin]

    def radial(field, t):
        replaced = outer if field in (VISCOSITY, SOURCE + 2) else margin
        plane = lax.broadcasted_iota(jnp.int32, (planes, cells_side), 0)
        own = (plane >= replaced) & (plane < planes - replaced)
        row = outward_row(t, cells_radial)
        edges = fields[field, pl.ds(row, 2 * outer, stride=pitch), :]
        if 2 * outer * 2 == planes:
            edges = jnp.concatenate([edges, edges], 0)
        else:
            gap = jnp.zeros((planes - 2 * outer, cells_side), jnp.float32)
            edges = jnp.concatenate([edges[:outer], gap, edges[outer:]], 0)
        return jnp.where(own, lines_ref[field, t], edges)

    unused = LONG_FIELDS * planes + SHORT_FIELDS * cells_lateral
    if unused < message_ref.shape[0]:
        message_ref[unused:, :] = jnp.zeros((message_ref.shape[0] - unused, cells_side), jnp.float32)

    def keep(field, value):
        rows, first, count = message_part(cells_lateral, field)
        mine_ref[field] = value
        message_ref[rows, :] = value[first : first + count]

    def keep_part(part, t, value):
        parts_ref[part, t] = value

    valid = inside_grid((planes, cells_side), margin, cells_lateral)
    solve_lines(radial, cells_radial, valid, keep, keep_part)


def eliminate(inner, lines, outer, edge, sent, received, cells_lateral):
    cells_radial, cells_side = inner.shape[2:]
    planes = cells_lateral + 2 * MIGRATION_PLANES
    vmem = pl.BlockSpec(memory_space=pltpu.VMEM)
    line = (planes, cells_side)
    return pl.pallas_call(
        eliminate_kernel,
        out_shape=(
            jax.ShapeDtypeStruct((2, cells_lateral, cells_radial, cells_side), jnp.float32),
            jax.ShapeDtypeStruct((LONG_FIELDS + SHORT_FIELDS,) + line, jnp.float32),
            jax.ShapeDtypeStruct((message_rows(cells_lateral), cells_side), jnp.float32),
            jax.ShapeDtypeStruct((SHORT_FIELDS + 2, cells_radial - 1) + line, jnp.float32),
        ),
        in_specs=[vmem] * 8,
        out_specs=(vmem,) * 4,
        scratch_shapes=[
            pltpu.VMEM(
                (LINE_FIELDS, 4 * MIGRATION_PLANES * round_up(cells_radial, 8), cells_side),
                jnp.float32,
            )
        ],
        compiler_params=pltpu.CompilerParams(vmem_limit_bytes=32 * 2**20),
        name="eliminate",
    )(inner, lines, edge, *sent[::-1], *received[::-1], outer)


def join_kernel(mine_ref, message_ref, parts_ref, smoothed_ref, lines):
    _, cells_lateral, cells_radial, cells_side = smoothed_ref.shape
    margin = MIGRATION_PLANES
    planes = cells_lateral + 2 * margin
    pitch = round_up(cells_radial, 8)
    valid = inside_grid((planes, cells_side), margin, cells_lateral)

    def mine(field):
        return mine_ref[field]

    def other(field):
        rows, first, _ = message_part(cells_lateral, field)
        return message_ref[pl.ds(rows.start - first, planes), :]

    face = RADIAL * 0.5 * (mine(0) + other(0))
    excess, other_excess = mine(1), other(1)
    scale = 1.0 / (excess * other_excess + face * (excess + other_excess))
    own_weight = (other_excess + face) * scale
    other_weight = (excess + face) * scale
    cross = face * scale

    def second_right(field_of, q, around):
        terms = [field_of(LONG_FIELDS + 3 + side) * there for side, there in enumerate(around)]
        return total_of([field_of(LONG_FIELDS + q)] + terms)

    around, values = [], []
    for q in range(3):
        right, other_right = mine(2 + q), other(2 + q)
        own = jnp.where(valid, own_weight * right + cross * other_right, 0.0)
        beyond = jnp.where(valid, other_weight * other_right + cross * right, 0.0)
        around.append(neighbours(own))
        right = second_right(mine, q, around[q])
        other_right = second_right(other, q, neighbours(beyond))
        values.append(own_weight * right + cross * other_right)
    for t in range(cells_radial - 1, -1, -1):
        row = outward_row(t, cells_radial)
        if t < cells_radial - 1:
            factors = [parts_ref[3 + side, t] for side in range(4)]
            inverse, coupling = parts_ref[SHORT_FIELDS, t], parts_ref[SHORT_FIELDS + 1, t]
        for q in range(3):
            if t < cells_radial - 1:
                terms = [factor * there for factor, there in zip(factors, around[q])]
                right = total_of([parts_ref[q, t]] + terms)
                values[q] = right * inverse + coupling * values[q]
            lines[q, pl.ds(row, cells_lateral, stride=pitch), :] = values[q][
                margin : margin + cells_lateral
            ]
    for q in range(3):
        for x in range(cells_lateral):
            smoothed_ref[q, x] = lines[q, pl.ds(x * pitch, cells_radial), :]


def join(mine, message, parts, like):
    cells_lateral, cells_radial, cells_side = like.shape[1:]
    vmem = pl.BlockSpec(memory_space=pltpu.VMEM)
    return pl.pallas_call(
        join_kernel,
        out_shape=jax.ShapeDtypeStruct(like.shape, jnp.float32),
        in_specs=[vmem] * 3,
        out_specs=vmem,
        scratch_shapes=[
            pltpu.VMEM((3, cells_lateral * round_up(cells_radial, 8), cells_side), jnp.float32),
        ],
        compiler_params=pltpu.CompilerParams(vmem_limit_bytes=32 * 2**20),
        name="join",
    )(mine, message, parts)


def extended(block, sides, width):
    for axis, dim in sides:
        count = lax.axis_size(axis)
        forward = [(i, i + 1) for i in range(count - 1)]
        backward = [(target, source) for source, target in forward]
        low = lax.ppermute(
            lax.slice_in_dim(block, block.shape[dim] - width, None, axis=dim), axis, forward
        )
        high = lax.ppermute(lax.slice_in_dim(block, 0, width, axis=dim), axis, backward)
        block = jnp.concatenate([low, block, high], axis=dim)
    return block


def block_factor(diagonal, lower_band, upper_band):
    pivots = []
    upper_scaled = []
    for row_index in range(diagonal.shape[1]):
        if row_index == 0:
            pivot_row = diagonal[:, 0]
        else:
            pivot_row = diagonal[:, row_index] - lower_band[:, row_index] * upper_scaled[-1]
        pivots.append(pivot_row)
        upper_scaled.append(upper_band[:, row_index] / pivot_row)
    return (pivots, upper_scaled)


def block_solve(pivots, upper_scaled, lower_band, right_side):
    row_total = len(pivots)
    modified = []
    for row_index in range(row_total):
        if row_index == 0:
            value_row = right_side[:, :, 0] / pivots[0]
        else:
            value_row = (
                right_side[:, :, row_index] - lower_band[:, row_index] * modified[-1]
            ) / pivots[row_index]
        modified.append(value_row)
    solved = [modified[-1]]
    for row_index in range(row_total - 2, -1, -1):
        solved.append(modified[row_index] - upper_scaled[row_index] * solved[-1])
    ordered = solved[::-1]
    return jnp.stack(ordered, 2)


def interface_solve(coefficients):
    column_total = coefficients.shape[2]

    def forward(carried, inputs):
        offset, carried_slope = carried
        left_first, right_first, left_last, right_last, free_first, free_last = inputs
        divisor = 1.0 - left_first * carried_slope
        first_fixed = (free_first + left_first * offset) / divisor
        first_slope = right_first / divisor
        next_offset = free_last + left_last * (offset + carried_slope * first_fixed)
        next_slope = left_last * carried_slope * first_slope + right_last
        return ((next_offset, next_slope), (first_fixed, first_slope, next_offset, next_slope))

    start_state = (
        jnp.zeros((3, column_total), jnp.float32),
        jnp.zeros((column_total,), jnp.float32),
    )
    scan_inputs = (
        coefficients[:, 0],
        coefficients[:, 1],
        coefficients[:, 2],
        coefficients[:, 3],
        coefficients[:, 4:7],
        coefficients[:, 7:10],
    )
    final_state, eliminated = lax.scan(forward, start_state, scan_inputs)

    def backward(first_next, inputs):
        fixed_first, slope_first, fixed_last, slope_last = inputs
        first_value = fixed_first + slope_first * first_next
        last_value = fixed_last + slope_last * first_next
        return (first_value, (first_value, last_value))

    final_first, values_pair = lax.scan(
        backward, jnp.zeros((3, column_total), jnp.float32), eliminated, reverse=True
    )
    first_values, last_values = values_pair
    nothing_row = jnp.zeros((1, 3, column_total), jnp.float32)
    from_below = jnp.concatenate([nothing_row, last_values[:-1]], 0)
    from_above = jnp.concatenate([first_values[1:], nothing_row], 0)
    return jnp.concatenate([from_below, from_above], 1)


def reduced_boundary(interface):
    gathered = lax.all_gather(interface, "rad", axis=0, tiled=True)
    solved = interface_solve(gathered)
    return lax.dynamic_index_in_dim(solved, lax.axis_index("rad"), 0, keepdims=False)


def many_blocks(values, cells, count, edge, received, base_viscosity, velocity, forcing):
    cells_lateral, cells_radial, cells_side = base_viscosity.shape
    moved_rows = MIGRATION_PLANES * cells_radial
    odd = lax.rem(lax.axis_index("lat"), 2) == 1
    from_below = jnp.where(odd, received[0], received[1])[: 3 * moved_rows]
    from_above = jnp.where(odd, received[1], received[0])[: 3 * moved_rows]
    edge = edge.reshape(3, 2, moved_rows, cells_side)
    below = edge[:, 0] + from_below.reshape(3, moved_rows, cells_side)
    above = edge[:, 1] + from_above.reshape(3, moved_rows, cells_side)
    shares = [
        (sums[1:] / (sums[0] + PRIOR_WEIGHT)).reshape(2, -1, cells_radial, cells_side)
        for sums in (below, above)
    ]
    inner, _, _ = inner_lines(count, values, cells, base_viscosity, velocity, forcing)
    basalt_share, melt_share = jnp.concatenate([shares[0], inner, shares[1]], 1)
    viscosity = base_viscosity * jnp.exp(
        CONTRAST_BASALT * basalt_share - CONTRAST_MELT * melt_share
    )
    viscosity_pad = extended(viscosity, (("lat", 0), ("rad", 1)), 1)
    side_pad = jnp.pad(viscosity, ((0, 0), (0, 0), (1, 1)))
    face_west = LATERAL * 0.5 * (viscosity + viscosity_pad[:-2, 1:-1])
    face_east = LATERAL * 0.5 * (viscosity + viscosity_pad[2:, 1:-1])
    face_south = LATERAL * 0.5 * (viscosity + side_pad[:, :, :-2])
    face_north = LATERAL * 0.5 * (viscosity + side_pad[:, :, 2:])
    face_below = RADIAL * 0.5 * (viscosity + viscosity_pad[1:-1, :-2])
    face_above = RADIAL * 0.5 * (viscosity + viscosity_pad[1:-1, 2:])
    diagonal = face_west + face_east + face_south + face_north + face_below + face_above
    source = jnp.concatenate([forcing[:2], (forcing[2] - BUOYANCY * basalt_share)[None]], 0)
    lower_band = -face_below
    upper_band = -face_above
    pivots, upper_scaled = block_factor(diagonal, lower_band, upper_band)
    radial_iota = lax.broadcasted_iota(jnp.int32, viscosity.shape, 1)
    response_side = jnp.stack(
        [
            jnp.where(radial_iota == 0, face_below, jnp.float32(0.0)),
            jnp.where(radial_iota == cells_radial - 1, face_above, jnp.float32(0.0)),
        ]
    )
    response = block_solve(pivots, upper_scaled, lower_band, response_side)
    current = velocity
    for sweep_index in range(SWEEPS):
        velocity_pad = extended(current, (("lat", 1),), 1)
        side_velocity = jnp.pad(current, ((0, 0), (0, 0), (0, 0), (1, 1)))
        right_side = (
            source
            + face_west * velocity_pad[:, :-2]
            + face_east * velocity_pad[:, 2:]
            + face_south * side_velocity[..., :-2]
            + face_north * side_velocity[..., 2:]
        )
        particular = block_solve(pivots, upper_scaled, lower_band, right_side)
        interface = jnp.concatenate(
            [response[:, :, 0], response[:, :, -1], particular[:, :, 0], particular[:, :, -1]], 0
        )
        interface = interface.reshape(1, 10, cells_lateral * cells_side)
        boundary = reduced_boundary(interface).reshape(6, cells_lateral, 1, cells_side)
        current = particular + response[0][None] * boundary[:3] + response[1][None] * boundary[3:]
    composition = jnp.stack([basalt_share, melt_share])
    return (current, composition)

def local(tracer_values, tracer_cell, tracer_count, base_viscosity, velocity, forcing):
    values, cells = dense_tracers(tracer_values, tracer_cell)
    edge, first, second, count, values, cells = outgoing_sums(
        tracer_count, values, cells, base_viscosity, velocity, forcing
    )
    sent = first, second
    received = pair_swaps(first, second)
    if lax.axis_size("rad") != 2:
        return many_blocks(
            values, cells, count, edge, received, base_viscosity, velocity, forcing
        )
    inner, lines, outer = inner_lines(count, values, cells, base_viscosity, velocity, forcing)
    composition, mine, message, parts = eliminate(
        inner, lines, outer, edge, sent, received, base_viscosity.shape[0]
    )
    other = lax.ppermute(message, "rad", [(0, 1), (1, 0)])
    return join(mine, other, parts, velocity), composition


def solution(mesh):
    return jax.shard_map(
        local,
        mesh=mesh,
        in_specs=(
            P("lat", "rad", None, None),
            P("lat", "rad", None),
            P("lat", "rad", None),
            P("lat", "rad", None),
            P(None, "lat", "rad", None),
            P(None, "lat", "rad", None),
        ),
        out_specs=(P(None, "lat", "rad", None), P(None, "lat", "rad", None)),
        check_vma=False,
    )
```

```python
import functools

import jax
import jax.numpy as jnp
from jax import lax
from jax.experimental import pallas as pl
from jax.experimental.pallas import tpu as pltpu
from jax.sharding import PartitionSpec as P

SWEEPS = 2
MIGRATION_PLANES = 2

LATERAL = 0.015625
RADIAL = 32.0
BUOYANCY = 0.1
PRIOR_WEIGHT = 0.5
CONTRAST_BASALT = 2.3
CONTRAST_MELT = 1.5

TILE_ROWS = 16


def round_up(value, multiple):
    return -(-value // multiple) * multiple


def split_index(index, count):
    if count & (count - 1) == 0:
        return lax.shift_right_logical(index, count.bit_length() - 1), index & (count - 1)
    quotient = lax.div(index, count)
    return quotient, index - quotient * count


def payload_sections(cells_radial):
    pair = MIGRATION_PLANES * cells_radial
    starts = [0, 3 * pair, 6 * pair, 9 * pair, 10 * pair]
    return starts, round_up(10 * pair + 3 * cells_radial, 8)


def spread_row(row):
    return jnp.broadcast_to(row, (TILE_ROWS, row.shape[1])).astype(jnp.bfloat16)


def hot_tiles(index, row_total):
    iota = lax.broadcasted_iota(jnp.int32, index.shape, 0)
    return [
        index == (iota + first).astype(jnp.float32).astype(jnp.bfloat16)
        for first in range(0, row_total, TILE_ROWS)
    ]


def hot_product(sums, loads, high, low, high_rows, low_rows, chunk_rows):
    high, low = high.astype(jnp.float32), low.astype(jnp.float32)
    zero = jnp.zeros((TILE_ROWS, high.shape[1]), jnp.bfloat16)
    one = jnp.ones((TILE_ROWS, high.shape[1]), jnp.bfloat16)
    for first_row in range(0, high.shape[0], chunk_rows):
        left, right = [], []
        for row in range(first_row, first_row + chunk_rows):
            pick = slice(row, row + 1)
            high_masks = hot_tiles(spread_row(high[pick]), high_rows)
            low_masks = hot_tiles(spread_row(low[pick]), low_rows)
            spread = [spread_row(load[pick]) for load in loads]
            tiles = [jnp.where(mask, load, zero) for load in spread for mask in high_masks]
            left.append(jnp.concatenate(tiles, 0))
            right.append(jnp.concatenate([jnp.where(mask, one, zero) for mask in low_masks], 0))
        sums = sums + lax.dot_general(
            jnp.concatenate(left, 1),
            jnp.concatenate(right, 1),
            (((1,), (1,)), ((), ())),
            preferred_element_type=jnp.float32,
        )
    return sums


def edge_row(plane, plane_total, moved_total):
    inner = (plane >= moved_total) & (plane < plane_total - moved_total)
    last = plane - (plane_total - 2 * moved_total)
    return jnp.where(inner, -plane_total, jnp.where(plane < moved_total, plane, last))


def fold_moved(plane, side, plane_total, side_total):
    width, third = side_total // 4, plane_total // 3
    part = jnp.where(plane >= third, 1, 0) + jnp.where(plane >= 2 * third, 1, 0)
    other = side >= 3 * width
    high = jnp.where(other, plane_total + plane - part * third, plane)
    low = jnp.where(other, side - 3 * width + part * width, side)
    return high, low, plane_total + third, 3 * width


def unfold_moved(table, q, plane_total, side_total, put):
    width, third = side_total // 4, plane_total // 3
    rows = plane_total + third
    put(0, 0, table[pl.ds(q * rows, plane_total), 0 : 3 * width])
    for part in range(3):
        block = table[
            pl.ds(q * rows + plane_total, third), part * width : (part + 1) * width
        ]
        put(part * third, 3 * width, block)


def fold_inner(plane, side, plane_total, side_total):
    rows, width = plane_total * 5 // 6, side_total // 4
    part, rest = split_index(side, width)
    other = plane >= rows
    high = jnp.where(other, plane - rows + part * (plane_total - rows), plane)
    high = jnp.where(plane < plane_total, high, -1)
    low = jnp.where(other, side_total + rest, side)
    return high, low, rows, side_total + width


def unfold_inner(table, q, plane_total, side_total, put):
    rows, width = plane_total * 5 // 6, side_total // 4
    left = plane_total - rows
    put(0, 0, table[pl.ds(q * rows, rows), 0:side_total])
    for part in range(4):
        block = table[pl.ds(q * rows + part * left, left), side_total : side_total + width]
        put(rows, part * width, block)


def tracer_block(count, values, cells, group, first_row, block_rows, cells_side):
    rows = pl.ds(first_row, block_rows)
    lane_total = cells.shape[2]
    shape = (block_rows, lane_total)
    slot = (first_row + lax.broadcasted_iota(jnp.int32, shape, 0)) * lane_total
    slot = slot + lax.broadcasted_iota(jnp.int32, shape, 1)
    weight = jnp.where(slot < count, 0.5 + values[0, group, rows, :], jnp.float32(0.0))
    loads = [weight, weight * values[1, group, rows, :], weight * values[2, group, rows, :]]
    plane, side = split_index(cells[group, rows, :], cells_side)
    return loads, plane, side


def for_used_blocks(used, group_rows, block_rows, lane_total, late_copies, step):
    block_slots = block_rows * lane_total
    blocks = lax.div(used + (block_slots - 1), block_slots)
    blocks = jnp.clip(blocks, 1, group_rows // block_rows)

    def wait_late():
        for copy in late_copies:
            copy.wait()

    def repeat(index, carried):
        pl.when(index == 1)(wait_late)
        step(pl.multiple_of(index * block_rows, block_rows))
        return carried

    lax.fori_loop(0, blocks, repeat, 0)
    pl.when(blocks == 1)(wait_late)


VISCOSITY, VELOCITY, SOURCE, LINE_FIELDS = 0, 1, 4, 7


def composition_of(cell_sums, base):
    scale = 1.0 / (cell_sums[0] + PRIOR_WEIGHT)
    basalt_share, melt_share = cell_sums[1] * scale, cell_sums[2] * scale
    weakening = jnp.exp(CONTRAST_BASALT * basalt_share - CONTRAST_MELT * melt_share)
    return basalt_share, melt_share, base * weakening


def outward_row(t, cells_radial):
    return jnp.where(lax.axis_index("rad") == 0, t, cells_radial - 1 - t)


class Fetches:
    def __init__(self, semaphores):
        self.semaphores = semaphores
        self.copies = []

    def start(self, source, target):
        copy = pltpu.make_async_copy(source, target, self.semaphores.at[len(self.copies)])
        copy.start()
        self.copies.append(copy)

    def wait(self, first, last):
        for copy in self.copies[first:last]:
            copy.wait()


def has_partners():
    lateral, count = lax.axis_index("lat"), lax.axis_size("lat")
    odd = lax.rem(lateral, 2) == 1
    above, below = lateral + 1 < count, lateral > 0
    return jnp.logical_or(odd, above), jnp.where(odd, above, below)


def outgoing_kernel(
    block_rows,
    counts_hbm,
    values_hbm,
    cells_hbm,
    base_hbm,
    velocity_hbm,
    forcing_hbm,
    edge_ref,
    first_ref,
    second_ref,
    count_ref,
    values,
    cells,
    counts,
    base,
    velocity,
    forcing,
    moved_sums,
    semaphores,
):
    cells_lateral, cells_radial, cells_side = base_hbm.shape
    plane_total = cells_lateral * cells_radial
    moved_planes = MIGRATION_PLANES * cells_radial
    group_rows, lane_total = cells.shape[1:]

    fetches = Fetches(semaphores)
    fetches.start(counts_hbm, counts)
    part = pl.ds(0, block_rows)
    fetches.start(cells_hbm.at[:, part], cells.at[:, part])
    for q in range(3):
        fetches.start(values_hbm.at[q, :, part], values.at[q, :, part])
    part = pl.ds(block_rows, group_rows - block_rows)
    fetches.start(cells_hbm.at[:, part], cells.at[:, part])
    fetches.start(values_hbm.at[:, :, part], values.at[:, :, part])
    for upward in (0, 1):
        outer = pl.ds((cells_lateral - MIGRATION_PLANES) * upward, MIGRATION_PLANES)
        fetches.start(base_hbm.at[outer], base.at[upward])
        fetches.start(velocity_hbm.at[:, outer], velocity.at[upward])
        outermost = pl.ds((cells_lateral - 1) * upward, 1)
        fetches.start(forcing_hbm.at[:, outermost], forcing.at[upward])

    edge_ref[...] = jnp.zeros_like(edge_ref)
    moved_sums[...] = jnp.zeros_like(moved_sums)

    def step(first_row):
        def block_of(group):
            count = counts[0, 0, group]
            return tracer_block(count, values, cells, group, first_row, block_rows, cells_side)

        loads, plane, side = block_of(1)
        row = edge_row(plane, plane_total, moved_planes)
        edge_ref[...] = hot_product(
            edge_ref[...], loads, row, side, 2 * moved_planes, cells_side, CHUNK_ROWS
        )
        for slot, group in enumerate((0, 2)):
            loads, plane, side = block_of(group)
            if group == 0:
                plane = plane - (plane_total - moved_planes)
            table = fold_moved(plane, side, moved_planes, cells_side)
            moved_sums[slot] = hot_product(moved_sums[slot], loads, *table, CHUNK_ROWS)

    fetches.wait(0, 5)
    count_ref[...] = jnp.full(count_ref.shape, counts[0, 0, 1], jnp.int32).astype(jnp.float32)
    used = jnp.maximum(jnp.maximum(counts[0, 0, 0], counts[0, 0, 1]), counts[0, 0, 2])
    for_used_blocks(used, group_rows, block_rows, lane_total, fetches.copies[5:7], step)
    fetches.wait(7, None)

    starts, rows_total = payload_sections(cells_radial)
    unused = starts[4] + 3 * cells_radial

    def fill(payload, upward):
        for q in range(3):

            def put_moved(plane, column, block):
                height, width = block.shape
                rows = pl.ds(starts[0] + q * moved_planes + plane, height)
                payload[rows, column : column + width] = block

            unfold_moved(moved_sums.at[upward], q, moved_planes, cells_side, put_moved)
            payload[pl.ds(starts[1] + q * moved_planes, moved_planes), :] = edge_ref[
                pl.ds((2 * q + upward) * moved_planes, moved_planes), :
            ]
            for offset in range(MIGRATION_PLANES):
                row = starts[2] + q * moved_planes + offset * cells_radial
                payload[pl.ds(row, cells_radial), :] = velocity[upward, q, offset]
            row = starts[4] + q * cells_radial
            payload[pl.ds(row, cells_radial), :] = forcing[upward, q, 0]
        for offset in range(MIGRATION_PLANES):
            row = starts[3] + offset * cells_radial
            payload[pl.ds(row, cells_radial), :] = base[upward, offset]
        if unused < rows_total:
            payload[unused:, :] = jnp.zeros((rows_total - unused, cells_side), jnp.float32)

    odd = lax.rem(lax.axis_index("lat"), 2) == 1

    @pl.when(odd)
    def _():
        fill(first_ref, 0)
        fill(second_ref, 1)

    @pl.when(jnp.logical_not(odd))
    def _():
        fill(first_ref, 1)
        fill(second_ref, 0)

    for payload, exists in zip((first_ref, second_ref), has_partners()):

        @pl.when(jnp.logical_not(exists))
        def _():
            payload[...] = jnp.zeros_like(payload)


def inner_kernel(
    block_rows,
    count_ref,
    values_ref,
    cells_ref,
    base_hbm,
    velocity_hbm,
    forcing_hbm,
    composition_ref,
    lines_ref,
    outer_ref,
    table,
    sums,
    fields,
    base,
    velocity,
    forcing,
    semaphores,
):
    cells_lateral, cells_radial, cells_side = base.shape
    margin = MIGRATION_PLANES
    planes = cells_lateral + 2 * margin
    pitch = round_up(cells_radial, 8)
    moved_planes = margin * cells_radial
    inner = cells_lateral - 2 * margin
    inner_planes = inner * cells_radial
    group_rows, lane_total = cells_ref.shape[1:]
    fetches = Fetches(semaphores)
    fetches.start(velocity_hbm, velocity)
    fetches.start(forcing_hbm, forcing)
    fetches.start(base_hbm, base)
    table[...] = jnp.zeros_like(table)

    nothing = jnp.zeros((cells_radial, cells_side), jnp.float32)

    def put(field, plane, value):
        fields[field, pl.ds(plane * pitch, cells_radial), :] = value

    def lay_out(those):
        for field in those:
            for t in range(cells_radial):
                row = outward_row(t, cells_radial)
                lines_ref[field, t] = fields[field, pl.ds(row, planes, stride=pitch), :]

    def step(first_row):
        loads, plane, side = tracer_block(
            count, values_ref, cells_ref, 1, first_row, block_rows, cells_side
        )
        where = fold_inner(plane - moved_planes, side, inner_planes, cells_side)
        table[...] = hot_product(table[...], loads, *where, block_rows)

    count = jnp.max(count_ref[...]).astype(jnp.int32)
    for_used_blocks(count, group_rows, block_rows, lane_total, [], step)

    fetches.wait(0, None)
    for plane in range(planes):
        x = plane - margin
        own = 0 <= x < cells_lateral
        for q in range(3):
            put(VELOCITY + q, plane, velocity[q, x] if own else nothing)
        for q in range(2):
            put(SOURCE + q, plane, forcing[q, x] if own else nothing)
    late = VISCOSITY, SOURCE + 2
    lay_out(field for field in range(LINE_FIELDS) if field not in late)

    for q in range(3):

        def put_sums(plane, column, block):
            height, width = block.shape
            sums[q, pl.ds(plane, height), column : column + width] = block

        unfold_inner(table, q, inner_planes, cells_side, put_sums)
    for plane in range(planes):
        x = plane - 2 * margin
        viscosity, source = nothing, nothing
        if 0 <= x < inner:
            rows = pl.ds(x * cells_radial, cells_radial)
            cell_sums = [sums[q, rows, :] for q in range(3)]
            basalt_share, melt_share, viscosity = composition_of(cell_sums, base[x + margin])
            source = forcing[2, x + margin] - BUOYANCY * basalt_share
            composition_ref[0, x] = basalt_share
            composition_ref[1, x] = melt_share
        put(VISCOSITY, plane, viscosity)
        put(SOURCE + 2, plane, source)
    lay_out(late)
    for offset in range(margin):
        for place, x in ((offset, offset), (margin + offset, cells_lateral - margin + offset)):
            outer_ref[0, place] = base[x]
            outer_ref[1, place] = forcing[2, x]


BLOCK_ROWS = 64
CHUNK_ROWS = 2


def dense_tracers(tracer_values, tracer_cell):
    lane_total = 128
    return tracer_values.reshape(3, 3, -1, lane_total), tracer_cell.reshape(3, -1, lane_total)


def outgoing_sums(tracer_count, values, cells, base_viscosity, velocity, forcing):
    cells_lateral, cells_radial, cells_side = base_viscosity.shape
    moved_planes = MIGRATION_PLANES * cells_radial
    group_rows, lane_total = cells.shape[1:]
    block_rows = min(BLOCK_ROWS, group_rows // 2)
    _, payload_rows = payload_sections(cells_radial)
    hbm = pl.BlockSpec(memory_space=pltpu.HBM)
    vmem = pl.BlockSpec(memory_space=pltpu.VMEM)
    payload = jax.ShapeDtypeStruct((payload_rows, cells_side), jnp.float32)
    outer_planes = (MIGRATION_PLANES, cells_radial, cells_side)
    return pl.pallas_call(
        functools.partial(outgoing_kernel, block_rows),
        out_shape=(
            jax.ShapeDtypeStruct((6 * moved_planes, cells_side), jnp.float32),
            payload,
            payload,
            jax.ShapeDtypeStruct((8, lane_total), jnp.float32),
            jax.ShapeDtypeStruct(values.shape, jnp.float32),
            jax.ShapeDtypeStruct(cells.shape, jnp.int32),
        ),
        in_specs=[hbm] * 6,
        out_specs=(vmem,) * 6,
        scratch_shapes=[
            pltpu.SMEM(tracer_count.shape, jnp.int32),
            pltpu.VMEM((2,) + outer_planes, jnp.float32),
            pltpu.VMEM((2, 3) + outer_planes, jnp.float32),
            pltpu.VMEM((2, 3, 1, cells_radial, cells_side), jnp.float32),
            pltpu.VMEM((2, 4 * moved_planes, cells_side * 3 // 4), jnp.float32),
            pltpu.SemaphoreType.DMA((13,)),
        ],
        compiler_params=pltpu.CompilerParams(vmem_limit_bytes=32 * 2**20),
        cost_estimate=pl.CostEstimate(
            flops=30 * group_rows * lane_total * moved_planes * cells_side,
            bytes_accessed=4 * (values.size + cells.size),
            transcendentals=0,
        ),
        name="outgoing_sums",
    )(
        *(
            pltpu.with_memory_space_constraint(array, pltpu.HBM)
            for array in (tracer_count, values, cells, base_viscosity, velocity, forcing)
        )
    )


def inner_lines(count, values, cells, base_viscosity, velocity, forcing):
    cells_lateral, cells_radial, cells_side = base_viscosity.shape
    planes = cells_lateral + 2 * MIGRATION_PLANES
    inner = cells_lateral - 2 * MIGRATION_PLANES
    inner_planes = inner * cells_radial
    group_rows, lane_total = cells.shape[1:]
    block_rows = min(BLOCK_ROWS, group_rows // 2)
    vmem = pl.BlockSpec(memory_space=pltpu.VMEM)
    return pl.pallas_call(
        functools.partial(inner_kernel, block_rows),
        out_shape=(
            jax.ShapeDtypeStruct((2, inner, cells_radial, cells_side), jnp.float32),
            jax.ShapeDtypeStruct((LINE_FIELDS, cells_radial, planes, cells_side), jnp.float32),
            jax.ShapeDtypeStruct(
                (2, 2 * MIGRATION_PLANES, cells_radial, cells_side), jnp.float32
            ),
        ),
        in_specs=[vmem] * 3 + [pl.BlockSpec(memory_space=pltpu.HBM)] * 3,
        out_specs=(vmem,) * 3,
        scratch_shapes=[
            pltpu.VMEM((3 * (inner_planes * 5 // 6), cells_side * 5 // 4), jnp.float32),
            pltpu.VMEM((3, inner_planes, cells_side), jnp.float32),
            pltpu.VMEM((LINE_FIELDS, planes * round_up(cells_radial, 8), cells_side), jnp.float32),
            pltpu.VMEM(base_viscosity.shape, jnp.float32),
            pltpu.VMEM(velocity.shape, jnp.float32),
            pltpu.VMEM(forcing.shape, jnp.float32),
            pltpu.SemaphoreType.DMA((3,)),
        ],
        compiler_params=pltpu.CompilerParams(vmem_limit_bytes=32 * 2**20),
        cost_estimate=pl.CostEstimate(
            flops=6 * group_rows * lane_total * inner * cells_radial * cells_side,
            bytes_accessed=4 * (values.size + cells.size),
            transcendentals=0,
        ),
        name="inner_lines",
    )(
        count,
        values,
        cells,
        *(
            pltpu.with_memory_space_constraint(array, pltpu.HBM)
            for array in (base_viscosity, velocity, forcing)
        ),
    )


def pair_swaps(first, second):
    count = lax.axis_size("lat")
    received = []
    for payload, start in ((second, 1), (first, 0)):
        target = list(range(count))
        for low in range(start, count - 1, 2):
            target[low], target[low + 1] = low + 1, low
        received.append(lax.ppermute(payload, "lat", list(enumerate(target))))
    return received[::-1]


def shift_planes(block, step):
    return pltpu.roll(block, step % block.shape[0], 0)


def shift_side(block, step):
    return pltpu.roll(block, step % block.shape[1], 1)


def neighbours(block):
    return (
        shift_planes(block, 1),
        shift_planes(block, -1),
        shift_side(block, 1),
        shift_side(block, -1),
    )


def inside_side(values):
    lane = lax.broadcasted_iota(jnp.int32, values[2].shape, 1)
    lower = jnp.where(lane > 0, values[2], 0.0)
    upper = jnp.where(lane < lane.shape[1] - 1, values[3], 0.0)
    return values[0], values[1], lower, upper


def total_of(terms):
    result = terms[0]
    for term in terms[1:]:
        result = result + term
    return result


def inside_grid(shape, margin, cells_lateral):
    plane = lax.broadcasted_iota(jnp.int32, shape, 0)
    lateral = lax.axis_index("lat")
    first = jnp.where(lateral == 0, margin, 1)
    last = jnp.where(lateral == lax.axis_size("lat") - 1, margin + cells_lateral, shape[0] - 1)
    return (plane >= first) & (plane < last)


LONG_FIELDS, SHORT_FIELDS = 5, 7


def message_rows(cells_lateral):
    planes = cells_lateral + 2 * MIGRATION_PLANES
    return round_up(LONG_FIELDS * planes + SHORT_FIELDS * cells_lateral + MIGRATION_PLANES, 8)


def message_part(cells_lateral, field):
    planes = cells_lateral + 2 * MIGRATION_PLANES
    if field < LONG_FIELDS:
        return pl.ds(field * planes, planes), 0, planes
    first = LONG_FIELDS * planes + (field - LONG_FIELDS) * cells_lateral
    return pl.ds(first, cells_lateral), MIGRATION_PLANES, cells_lateral


def running_sums(terms):
    sums = [terms[0]]
    for term in terms[1:]:
        sums.append(sums[-1] + term)
    return sums


def solve_lines(radial, cells_radial, valid, keep, keep_part):
    last = cells_radial - 1
    viscosity = [radial(VISCOSITY, t) for t in range(cells_radial)]
    lateral_faces, lateral_sums = [], []
    for here in viscosity:
        faces = [LATERAL * 0.5 * (here + there) for there in inside_side(neighbours(here))]
        lateral_sums.append(total_of(faces))
        lateral_faces.append(inside_side(faces))
    resistance = [
        1.0 / (RADIAL * 0.5 * (viscosity[t] + viscosity[t + 1])) for t in range(last)
    ]

    flux = lateral_sums[0] + RADIAL * 0.5 * viscosity[0]
    growth = [jnp.ones_like(flux)]
    for t in range(last):
        growth.append(growth[t] + resistance[t] * flux)
        flux = flux + lateral_sums[t + 1] * growth[t + 1]
    shrink = [1.0 / value for value in growth]
    weights = [resistance[t] * shrink[t] * shrink[t + 1] for t in range(last)]
    weighted_faces = [
        [growth[t] * face for face in lateral_faces[t]] for t in range(cells_radial)
    ]

    def forward(weighted_source, values):
        terms = []
        for t in range(cells_radial):
            around = zip(weighted_faces[t], neighbours(values[t]))
            terms.append(total_of([weighted_source[t]] + [face * there for face, there in around]))
        return running_sums(terms)

    def finish(part, sums):
        keep(LONG_FIELDS + part, sums[last] * shrink[last])
        for t in range(last):
            keep_part(part, t, sums[t])

    keep(0, viscosity[last])
    keep(1, flux * shrink[last])
    for q in range(3):
        source = [growth[t] * radial(SOURCE + q, t) for t in range(cells_radial)]
        sums = forward(source, [radial(VELOCITY + q, t) for t in range(cells_radial)])
        keep(2 + q, sums[last] * shrink[last])
        particular, value = [jnp.zeros_like(flux)], None
        for t in range(last - 1, -1, -1):
            value = weights[t] * sums[t] if value is None else value + weights[t] * sums[t]
            particular.append(jnp.where(valid, growth[t] * value, 0.0))
        finish(q, forward(source, particular[::-1]))
    around = [neighbours(jnp.where(valid, value * shrink[last], 0.0)) for value in growth]
    for side in range(4):
        terms = [weighted_faces[t][side] * around[t][side] for t in range(cells_radial)]
        finish(3 + side, running_sums(terms))
    for t in range(last):
        keep_part(SHORT_FIELDS, t, weights[t])
    keep_part(SHORT_FIELDS, last, shrink[last])
    for t in range(cells_radial):
        keep_part(SHORT_FIELDS + 1, t, growth[t])


def eliminate_kernel(
    inner_ref,
    lines_ref,
    edge_ref,
    second_ref,
    first_ref,
    from_second_ref,
    from_first_ref,
    outer_ref,
    composition_ref,
    mine_ref,
    message_ref,
    parts_ref,
    fields,
):
    _, cells_lateral, cells_radial, cells_side = composition_ref.shape
    margin = MIGRATION_PLANES
    planes = cells_lateral + 2 * margin
    pitch = round_up(cells_radial, 8)
    moved_planes = margin * cells_radial
    starts, _ = payload_sections(cells_radial)
    odd = lax.rem(lax.axis_index("lat"), 2) == 1

    def sent(upward, start):
        part = pl.ds(start, cells_radial)
        mine_first = odd if not upward else jnp.logical_not(odd)
        return jnp.where(mine_first, first_ref[part, :], second_ref[part, :])

    def arrived(from_above, start):
        part = pl.ds(start, cells_radial)
        is_first = odd if not from_above else jnp.logical_not(odd)
        return jnp.where(is_first, from_first_ref[part, :], from_second_ref[part, :])

    outer = 2 * margin

    def put(field, slot, value):
        fields[field, pl.ds(slot * pitch, cells_radial), :] = value

    for above in (False, True):
        for offset in range(margin):
            shift = offset * cells_radial
            halo = offset + (outer + margin if above else 0)
            own = offset + (outer if above else margin)
            x = offset + (cells_lateral - margin if above else 0)
            place = offset + (margin if above else 0)
            halo_sums, own_sums = [], []
            for q in range(3):
                row = q * moved_planes + shift
                rows = pl.ds((2 * q + int(above)) * moved_planes + shift, cells_radial)
                own_sums.append(edge_ref[rows, :] + arrived(above, starts[0] + row))
                halo_sums.append(sent(above, starts[0] + row) + arrived(above, starts[1] + row))
                put(VELOCITY + q, halo, arrived(above, starts[2] + row))
            basalt_share, melt_share, viscosity = composition_of(own_sums, outer_ref[0, place])
            composition_ref[0, x] = basalt_share
            composition_ref[1, x] = melt_share
            put(VISCOSITY, own, viscosity)
            put(SOURCE + 2, own, outer_ref[1, place] - BUOYANCY * basalt_share)
            basalt_share, _, viscosity = composition_of(
                halo_sums, arrived(above, starts[3] + shift)
            )
            put(VISCOSITY, halo, viscosity)
            beside = offset == (0 if above else margin - 1)
            for q in range(3):
                source = jnp.zeros_like(viscosity)
                if beside:
                    source = arrived(above, starts[4] + q * cells_radial)
                    if q == 2:
                        source = source - BUOYANCY * basalt_share
                put(SOURCE + q, halo, source)
    for x in range(margin, cells_lateral - margin):
        for q in range(2):
            composition_ref[q, x] = inner_ref[q, x - margin]

    def radial(field, t):
        replaced = outer if field in (VISCOSITY, SOURCE + 2) else margin
        plane = lax.broadcasted_iota(jnp.int32, (planes, cells_side), 0)
        own = (plane >= replaced) & (plane < planes - replaced)
        row = outward_row(t, cells_radial)
        edges = fields[field, pl.ds(row, 2 * outer, stride=pitch), :]
        if 2 * outer * 2 == planes:
            edges = jnp.concatenate([edges, edges], 0)
        else:
            gap = jnp.zeros((planes - 2 * outer, cells_side), jnp.float32)
            edges = jnp.concatenate([edges[:outer], gap, edges[outer:]], 0)
        return jnp.where(own, lines_ref[field, t], edges)

    unused = LONG_FIELDS * planes + SHORT_FIELDS * cells_lateral
    if unused < message_ref.shape[0]:
        message_ref[unused:, :] = jnp.zeros((message_ref.shape[0] - unused, cells_side), jnp.float32)

    def keep(field, value):
        rows, first, count = message_part(cells_lateral, field)
        mine_ref[field] = value
        message_ref[rows, :] = value[first : first + count]

    def keep_part(part, t, value):
        parts_ref[part, t] = value

    valid = inside_grid((planes, cells_side), margin, cells_lateral)
    solve_lines(radial, cells_radial, valid, keep, keep_part)


def eliminate(inner, lines, outer, edge, sent, received, cells_lateral):
    cells_radial, cells_side = inner.shape[2:]
    planes = cells_lateral + 2 * MIGRATION_PLANES
    vmem = pl.BlockSpec(memory_space=pltpu.VMEM)
    line = (planes, cells_side)
    return pl.pallas_call(
        eliminate_kernel,
        out_shape=(
            jax.ShapeDtypeStruct((2, cells_lateral, cells_radial, cells_side), jnp.float32),
            jax.ShapeDtypeStruct((LONG_FIELDS + SHORT_FIELDS,) + line, jnp.float32),
            jax.ShapeDtypeStruct((message_rows(cells_lateral), cells_side), jnp.float32),
            jax.ShapeDtypeStruct((SHORT_FIELDS + 2, cells_radial) + line, jnp.float32),
        ),
        in_specs=[vmem] * 8,
        out_specs=(vmem,) * 4,
        scratch_shapes=[
            pltpu.VMEM(
                (LINE_FIELDS, 4 * MIGRATION_PLANES * round_up(cells_radial, 8), cells_side),
                jnp.float32,
            )
        ],
        compiler_params=pltpu.CompilerParams(vmem_limit_bytes=32 * 2**20),
        name="eliminate",
    )(inner, lines, edge, *sent[::-1], *received[::-1], outer)


def join_kernel(mine_ref, message_ref, parts_ref, smoothed_ref, lines):
    _, cells_lateral, cells_radial, cells_side = smoothed_ref.shape
    margin = MIGRATION_PLANES
    planes = cells_lateral + 2 * margin
    pitch = round_up(cells_radial, 8)
    valid = inside_grid((planes, cells_side), margin, cells_lateral)

    def mine(field):
        return mine_ref[field]

    def other(field):
        rows, first, _ = message_part(cells_lateral, field)
        return message_ref[pl.ds(rows.start - first, planes), :]

    face = RADIAL * 0.5 * (mine(0) + other(0))
    excess, other_excess = mine(1), other(1)
    scale = 1.0 / (excess * other_excess + face * (excess + other_excess))
    own_weight = (other_excess + face) * scale
    other_weight = (excess + face) * scale
    cross = face * scale

    def second_right(field_of, q, around):
        terms = [field_of(LONG_FIELDS + 3 + side) * there for side, there in enumerate(around)]
        return total_of([field_of(LONG_FIELDS + q)] + terms)

    around, values = [], []
    for q in range(3):
        right, other_right = mine(2 + q), other(2 + q)
        own = jnp.where(valid, own_weight * right + cross * other_right, 0.0)
        beyond = jnp.where(valid, other_weight * other_right + cross * right, 0.0)
        around.append(neighbours(own))
        right = second_right(mine, q, around[q])
        other_right = second_right(other, q, neighbours(beyond))
        values.append(own_weight * right + cross * other_right)
    last = cells_radial - 1
    carried = [value * parts_ref[SHORT_FIELDS, last] for value in values]
    for t in range(last, -1, -1):
        row = outward_row(t, cells_radial)
        if t < last:
            factors = [parts_ref[3 + side, t] for side in range(4)]
            weight, growth = parts_ref[SHORT_FIELDS, t], parts_ref[SHORT_FIELDS + 1, t]
        for q in range(3):
            if t < last:
                terms = [factor * there for factor, there in zip(factors, around[q])]
                carried[q] = carried[q] + weight * total_of([parts_ref[q, t]] + terms)
                values[q] = growth * carried[q]
            lines[q, pl.ds(row, cells_lateral, stride=pitch), :] = values[q][
                margin : margin + cells_lateral
            ]
    for q in range(3):
        for x in range(cells_lateral):
            smoothed_ref[q, x] = lines[q, pl.ds(x * pitch, cells_radial), :]


def join(mine, message, parts, like):
    cells_lateral, cells_radial, cells_side = like.shape[1:]
    vmem = pl.BlockSpec(memory_space=pltpu.VMEM)
    return pl.pallas_call(
        join_kernel,
        out_shape=jax.ShapeDtypeStruct(like.shape, jnp.float32),
        in_specs=[vmem] * 3,
        out_specs=vmem,
        scratch_shapes=[
            pltpu.VMEM((3, cells_lateral * round_up(cells_radial, 8), cells_side), jnp.float32),
        ],
        compiler_params=pltpu.CompilerParams(vmem_limit_bytes=32 * 2**20),
        name="join",
    )(mine, message, parts)


def extended(block, sides, width):
    for axis, dim in sides:
        count = lax.axis_size(axis)
        forward = [(i, i + 1) for i in range(count - 1)]
        backward = [(target, source) for source, target in forward]
        low = lax.ppermute(
            lax.slice_in_dim(block, block.shape[dim] - width, None, axis=dim), axis, forward
        )
        high = lax.ppermute(lax.slice_in_dim(block, 0, width, axis=dim), axis, backward)
        block = jnp.concatenate([low, block, high], axis=dim)
    return block


def block_factor(diagonal, lower_band, upper_band):
    pivots = []
    upper_scaled = []
    for row_index in range(diagonal.shape[1]):
        if row_index == 0:
            pivot_row = diagonal[:, 0]
        else:
            pivot_row = diagonal[:, row_index] - lower_band[:, row_index] * upper_scaled[-1]
        pivots.append(pivot_row)
        upper_scaled.append(upper_band[:, row_index] / pivot_row)
    return (pivots, upper_scaled)


def block_solve(pivots, upper_scaled, lower_band, right_side):
    row_total = len(pivots)
    modified = []
    for row_index in range(row_total):
        if row_index == 0:
            value_row = right_side[:, :, 0] / pivots[0]
        else:
            value_row = (
                right_side[:, :, row_index] - lower_band[:, row_index] * modified[-1]
            ) / pivots[row_index]
        modified.append(value_row)
    solved = [modified[-1]]
    for row_index in range(row_total - 2, -1, -1):
        solved.append(modified[row_index] - upper_scaled[row_index] * solved[-1])
    ordered = solved[::-1]
    return jnp.stack(ordered, 2)


def interface_solve(coefficients):
    column_total = coefficients.shape[2]

    def forward(carried, inputs):
        offset, carried_slope = carried
        left_first, right_first, left_last, right_last, free_first, free_last = inputs
        divisor = 1.0 - left_first * carried_slope
        first_fixed = (free_first + left_first * offset) / divisor
        first_slope = right_first / divisor
        next_offset = free_last + left_last * (offset + carried_slope * first_fixed)
        next_slope = left_last * carried_slope * first_slope + right_last
        return ((next_offset, next_slope), (first_fixed, first_slope, next_offset, next_slope))

    start_state = (
        jnp.zeros((3, column_total), jnp.float32),
        jnp.zeros((column_total,), jnp.float32),
    )
    scan_inputs = (
        coefficients[:, 0],
        coefficients[:, 1],
        coefficients[:, 2],
        coefficients[:, 3],
        coefficients[:, 4:7],
        coefficients[:, 7:10],
    )
    final_state, eliminated = lax.scan(forward, start_state, scan_inputs)

    def backward(first_next, inputs):
        fixed_first, slope_first, fixed_last, slope_last = inputs
        first_value = fixed_first + slope_first * first_next
        last_value = fixed_last + slope_last * first_next
        return (first_value, (first_value, last_value))

    final_first, values_pair = lax.scan(
        backward, jnp.zeros((3, column_total), jnp.float32), eliminated, reverse=True
    )
    first_values, last_values = values_pair
    nothing_row = jnp.zeros((1, 3, column_total), jnp.float32)
    from_below = jnp.concatenate([nothing_row, last_values[:-1]], 0)
    from_above = jnp.concatenate([first_values[1:], nothing_row], 0)
    return jnp.concatenate([from_below, from_above], 1)


def reduced_boundary(interface):
    gathered = lax.all_gather(interface, "rad", axis=0, tiled=True)
    solved = interface_solve(gathered)
    return lax.dynamic_index_in_dim(solved, lax.axis_index("rad"), 0, keepdims=False)


def many_blocks(values, cells, count, edge, received, base_viscosity, velocity, forcing):
    cells_lateral, cells_radial, cells_side = base_viscosity.shape
    moved_rows = MIGRATION_PLANES * cells_radial
    odd = lax.rem(lax.axis_index("lat"), 2) == 1
    from_below = jnp.where(odd, received[0], received[1])[: 3 * moved_rows]
    from_above = jnp.where(odd, received[1], received[0])[: 3 * moved_rows]
    edge = edge.reshape(3, 2, moved_rows, cells_side)
    below = edge[:, 0] + from_below.reshape(3, moved_rows, cells_side)
    above = edge[:, 1] + from_above.reshape(3, moved_rows, cells_side)
    shares = [
        (sums[1:] / (sums[0] + PRIOR_WEIGHT)).reshape(2, -1, cells_radial, cells_side)
        for sums in (below, above)
    ]
    inner, _, _ = inner_lines(count, values, cells, base_viscosity, velocity, forcing)
    basalt_share, melt_share = jnp.concatenate([shares[0], inner, shares[1]], 1)
    viscosity = base_viscosity * jnp.exp(
        CONTRAST_BASALT * basalt_share - CONTRAST_MELT * melt_share
    )
    viscosity_pad = extended(viscosity, (("lat", 0), ("rad", 1)), 1)
    side_pad = jnp.pad(viscosity, ((0, 0), (0, 0), (1, 1)))
    face_west = LATERAL * 0.5 * (viscosity + viscosity_pad[:-2, 1:-1])
    face_east = LATERAL * 0.5 * (viscosity + viscosity_pad[2:, 1:-1])
    face_south = LATERAL * 0.5 * (viscosity + side_pad[:, :, :-2])
    face_north = LATERAL * 0.5 * (viscosity + side_pad[:, :, 2:])
    face_below = RADIAL * 0.5 * (viscosity + viscosity_pad[1:-1, :-2])
    face_above = RADIAL * 0.5 * (viscosity + viscosity_pad[1:-1, 2:])
    diagonal = face_west + face_east + face_south + face_north + face_below + face_above
    source = jnp.concatenate([forcing[:2], (forcing[2] - BUOYANCY * basalt_share)[None]], 0)
    lower_band = -face_below
    upper_band = -face_above
    pivots, upper_scaled = block_factor(diagonal, lower_band, upper_band)
    radial_iota = lax.broadcasted_iota(jnp.int32, viscosity.shape, 1)
    response_side = jnp.stack(
        [
            jnp.where(radial_iota == 0, face_below, jnp.float32(0.0)),
            jnp.where(radial_iota == cells_radial - 1, face_above, jnp.float32(0.0)),
        ]
    )
    response = block_solve(pivots, upper_scaled, lower_band, response_side)
    current = velocity
    for sweep_index in range(SWEEPS):
        velocity_pad = extended(current, (("lat", 1),), 1)
        side_velocity = jnp.pad(current, ((0, 0), (0, 0), (0, 0), (1, 1)))
        right_side = (
            source
            + face_west * velocity_pad[:, :-2]
            + face_east * velocity_pad[:, 2:]
            + face_south * side_velocity[..., :-2]
            + face_north * side_velocity[..., 2:]
        )
        particular = block_solve(pivots, upper_scaled, lower_band, right_side)
        interface = jnp.concatenate(
            [response[:, :, 0], response[:, :, -1], particular[:, :, 0], particular[:, :, -1]], 0
        )
        interface = interface.reshape(1, 10, cells_lateral * cells_side)
        boundary = reduced_boundary(interface).reshape(6, cells_lateral, 1, cells_side)
        current = particular + response[0][None] * boundary[:3] + response[1][None] * boundary[3:]
    composition = jnp.stack([basalt_share, melt_share])
    return (current, composition)

def local(tracer_values, tracer_cell, tracer_count, base_viscosity, velocity, forcing):
    values, cells = dense_tracers(tracer_values, tracer_cell)
    edge, first, second, count, values, cells = outgoing_sums(
        tracer_count, values, cells, base_viscosity, velocity, forcing
    )
    sent = first, second
    received = pair_swaps(first, second)
    if lax.axis_size("rad") != 2:
        return many_blocks(
            values, cells, count, edge, received, base_viscosity, velocity, forcing
        )
    inner, lines, outer = inner_lines(count, values, cells, base_viscosity, velocity, forcing)
    composition, mine, message, parts = eliminate(
        inner, lines, outer, edge, sent, received, base_viscosity.shape[0]
    )
    other = lax.ppermute(message, "rad", [(0, 1), (1, 0)])
    return join(mine, other, parts, velocity), composition


def solution(mesh):
    return jax.shard_map(
        local,
        mesh=mesh,
        in_specs=(
            P("lat", "rad", None, None),
            P("lat", "rad", None),
            P("lat", "rad", None),
            P("lat", "rad", None),
            P(None, "lat", "rad", None),
            P(None, "lat", "rad", None),
        ),
        out_specs=(P(None, "lat", "rad", None), P(None, "lat", "rad", None)),
        check_vma=False,
    )
```

```python
import functools

import jax
import jax.numpy as jnp
from jax import lax
from jax.experimental import pallas as pl
from jax.experimental.pallas import tpu as pltpu
from jax.sharding import PartitionSpec as P

SWEEPS = 2
MIGRATION_PLANES = 2

LATERAL = 0.015625
RADIAL = 32.0
BUOYANCY = 0.1
PRIOR_WEIGHT = 0.5
CONTRAST_BASALT = 2.3
CONTRAST_MELT = 1.5

TILE_ROWS = 16


def round_up(value, multiple):
    return -(-value // multiple) * multiple


def split_index(index, count):
    if count & (count - 1) == 0:
        return lax.shift_right_logical(index, count.bit_length() - 1), index & (count - 1)
    quotient = lax.div(index, count)
    return quotient, index - quotient * count


def payload_sections(cells_radial):
    pair = MIGRATION_PLANES * cells_radial
    starts = [0, 3 * pair, 6 * pair, 9 * pair, 10 * pair]
    return starts, round_up(10 * pair + 3 * cells_radial, 8)


def spread_row(row):
    return jnp.broadcast_to(row, (TILE_ROWS, row.shape[1])).astype(jnp.bfloat16)


def hot_tiles(index, row_total):
    iota = lax.broadcasted_iota(jnp.int32, index.shape, 0)
    return [
        index == (iota + first).astype(jnp.float32).astype(jnp.bfloat16)
        for first in range(0, row_total, TILE_ROWS)
    ]


def hot_product(sums, loads, high, low, high_rows, low_rows, chunk_rows):
    high, low = high.astype(jnp.float32), low.astype(jnp.float32)
    zero = jnp.zeros((TILE_ROWS, high.shape[1]), jnp.bfloat16)
    one = jnp.ones((TILE_ROWS, high.shape[1]), jnp.bfloat16)
    for first_row in range(0, high.shape[0], chunk_rows):
        left, right = [], []
        for row in range(first_row, first_row + chunk_rows):
            pick = slice(row, row + 1)
            high_masks = hot_tiles(spread_row(high[pick]), high_rows)
            low_masks = hot_tiles(spread_row(low[pick]), low_rows)
            spread = [spread_row(load[pick]) for load in loads]
            tiles = [jnp.where(mask, load, zero) for load in spread for mask in high_masks]
            left.append(jnp.concatenate(tiles, 0))
            right.append(jnp.concatenate([jnp.where(mask, one, zero) for mask in low_masks], 0))
        sums = sums + lax.dot_general(
            jnp.concatenate(left, 1),
            jnp.concatenate(right, 1),
            (((1,), (1,)), ((), ())),
            preferred_element_type=jnp.float32,
        )
    return sums


def edge_row(plane, plane_total, moved_total):
    inner = (plane >= moved_total) & (plane < plane_total - moved_total)
    last = plane - (plane_total - 2 * moved_total)
    return jnp.where(inner, -plane_total, jnp.where(plane < moved_total, plane, last))


def fold_moved(plane, side, plane_total, side_total):
    width, third = side_total // 4, plane_total // 3
    part = jnp.where(plane >= third, 1, 0) + jnp.where(plane >= 2 * third, 1, 0)
    other = side >= 3 * width
    high = jnp.where(other, plane_total + plane - part * third, plane)
    low = jnp.where(other, side - 3 * width + part * width, side)
    return high, low, plane_total + third, 3 * width


def unfold_moved(table, q, plane_total, side_total, put):
    width, third = side_total // 4, plane_total // 3
    rows = plane_total + third
    put(0, 0, table[pl.ds(q * rows, plane_total), 0 : 3 * width])
    for part in range(3):
        block = table[
            pl.ds(q * rows + plane_total, third), part * width : (part + 1) * width
        ]
        put(part * third, 3 * width, block)


def fold_inner(plane, side, plane_total, side_total):
    rows, width = plane_total * 5 // 6, side_total // 4
    part, rest = split_index(side, width)
    other = plane >= rows
    high = jnp.where(other, plane - rows + part * (plane_total - rows), plane)
    high = jnp.where(plane < plane_total, high, -1)
    low = jnp.where(other, side_total + rest, side)
    return high, low, rows, side_total + width


def unfold_inner(table, q, plane_total, side_total, put):
    rows, width = plane_total * 5 // 6, side_total // 4
    left = plane_total - rows
    put(0, 0, table[pl.ds(q * rows, rows), 0:side_total])
    for part in range(4):
        block = table[pl.ds(q * rows + part * left, left), side_total : side_total + width]
        put(rows, part * width, block)


def tracer_block(count, values, cells, group, first_row, block_rows, cells_side):
    rows = pl.ds(first_row, block_rows)
    lane_total = cells.shape[2]
    shape = (block_rows, lane_total)
    slot = (first_row + lax.broadcasted_iota(jnp.int32, shape, 0)) * lane_total
    slot = slot + lax.broadcasted_iota(jnp.int32, shape, 1)
    weight = jnp.where(slot < count, 0.5 + values[0, group, rows, :], jnp.float32(0.0))
    loads = [weight, weight * values[1, group, rows, :], weight * values[2, group, rows, :]]
    plane, side = split_index(cells[group, rows, :], cells_side)
    return loads, plane, side


def for_used_blocks(used, group_rows, block_rows, lane_total, late_copies, step):
    block_slots = block_rows * lane_total
    blocks = lax.div(used + (block_slots - 1), block_slots)
    blocks = jnp.clip(blocks, 1, group_rows // block_rows)

    def wait_late():
        for copy in late_copies:
            copy.wait()

    def repeat(index, carried):
        pl.when(index == 1)(wait_late)
        step(pl.multiple_of(index * block_rows, block_rows))
        return carried

    lax.fori_loop(0, blocks, repeat, 0)
    pl.when(blocks == 1)(wait_late)


VISCOSITY, VELOCITY, SOURCE, LINE_FIELDS = 0, 1, 4, 7


def composition_of(cell_sums, base):
    scale = 1.0 / (cell_sums[0] + PRIOR_WEIGHT)
    basalt_share, melt_share = cell_sums[1] * scale, cell_sums[2] * scale
    weakening = jnp.exp(CONTRAST_BASALT * basalt_share - CONTRAST_MELT * melt_share)
    return basalt_share, melt_share, base * weakening


def outward_row(t, cells_radial):
    return jnp.where(lax.axis_index("rad") == 0, t, cells_radial - 1 - t)


class Fetches:
    def __init__(self, semaphores):
        self.semaphores = semaphores
        self.copies = []

    def start(self, source, target):
        copy = pltpu.make_async_copy(source, target, self.semaphores.at[len(self.copies)])
        copy.start()
        self.copies.append(copy)

    def wait(self, first, last):
        for copy in self.copies[first:last]:
            copy.wait()


def has_partners():
    lateral, count = lax.axis_index("lat"), lax.axis_size("lat")
    odd = lax.rem(lateral, 2) == 1
    above, below = lateral + 1 < count, lateral > 0
    return jnp.logical_or(odd, above), jnp.where(odd, above, below)


def outgoing_kernel(
    block_rows,
    counts_hbm,
    values_hbm,
    cells_hbm,
    base_hbm,
    velocity_hbm,
    forcing_hbm,
    edge_ref,
    first_ref,
    second_ref,
    count_ref,
    values,
    cells,
    counts,
    base,
    velocity,
    forcing,
    moved_sums,
    semaphores,
):
    cells_lateral, cells_radial, cells_side = base_hbm.shape
    plane_total = cells_lateral * cells_radial
    moved_planes = MIGRATION_PLANES * cells_radial
    group_rows, lane_total = cells.shape[1:]

    fetches = Fetches(semaphores)
    fetches.start(counts_hbm, counts)
    part = pl.ds(0, block_rows)
    fetches.start(cells_hbm.at[:, part], cells.at[:, part])
    for q in range(3):
        fetches.start(values_hbm.at[q, :, part], values.at[q, :, part])
    part = pl.ds(block_rows, group_rows - block_rows)
    fetches.start(cells_hbm.at[:, part], cells.at[:, part])
    fetches.start(values_hbm.at[:, :, part], values.at[:, :, part])
    for upward in (0, 1):
        outer = pl.ds((cells_lateral - MIGRATION_PLANES) * upward, MIGRATION_PLANES)
        fetches.start(base_hbm.at[outer], base.at[upward])
        fetches.start(velocity_hbm.at[:, outer], velocity.at[upward])
        outermost = pl.ds((cells_lateral - 1) * upward, 1)
        fetches.start(forcing_hbm.at[:, outermost], forcing.at[upward])

    edge_ref[...] = jnp.zeros_like(edge_ref)
    moved_sums[...] = jnp.zeros_like(moved_sums)

    def step(first_row):
        def block_of(group):
            count = counts[0, 0, group]
            return tracer_block(count, values, cells, group, first_row, block_rows, cells_side)

        loads, plane, side = block_of(1)
        row = edge_row(plane, plane_total, moved_planes)
        edge_ref[...] = hot_product(
            edge_ref[...], loads, row, side, 2 * moved_planes, cells_side, CHUNK_ROWS
        )
        for slot, group in enumerate((0, 2)):
            loads, plane, side = block_of(group)
            if group == 0:
                plane = plane - (plane_total - moved_planes)
            table = fold_moved(plane, side, moved_planes, cells_side)
            moved_sums[slot] = hot_product(moved_sums[slot], loads, *table, CHUNK_ROWS)

    fetches.wait(0, 5)
    count_ref[...] = jnp.full(count_ref.shape, counts[0, 0, 1], jnp.int32).astype(jnp.float32)
    used = jnp.maximum(jnp.maximum(counts[0, 0, 0], counts[0, 0, 1]), counts[0, 0, 2])
    for_used_blocks(used, group_rows, block_rows, lane_total, fetches.copies[5:7], step)
    fetches.wait(7, None)

    starts, rows_total = payload_sections(cells_radial)
    unused = starts[4] + 3 * cells_radial

    def fill(payload, upward):
        for q in range(3):

            def put_moved(plane, column, block):
                height, width = block.shape
                rows = pl.ds(starts[0] + q * moved_planes + plane, height)
                payload[rows, column : column + width] = block

            unfold_moved(moved_sums.at[upward], q, moved_planes, cells_side, put_moved)
            payload[pl.ds(starts[1] + q * moved_planes, moved_planes), :] = edge_ref[
                pl.ds((2 * q + upward) * moved_planes, moved_planes), :
            ]
            for offset in range(MIGRATION_PLANES):
                row = starts[2] + q * moved_planes + offset * cells_radial
                payload[pl.ds(row, cells_radial), :] = velocity[upward, q, offset]
            row = starts[4] + q * cells_radial
            payload[pl.ds(row, cells_radial), :] = forcing[upward, q, 0]
        for offset in range(MIGRATION_PLANES):
            row = starts[3] + offset * cells_radial
            payload[pl.ds(row, cells_radial), :] = base[upward, offset]
        if unused < rows_total:
            payload[unused:, :] = jnp.zeros((rows_total - unused, cells_side), jnp.float32)

    odd = lax.rem(lax.axis_index("lat"), 2) == 1

    @pl.when(odd)
    def _():
        fill(first_ref, 0)
        fill(second_ref, 1)

    @pl.when(jnp.logical_not(odd))
    def _():
        fill(first_ref, 1)
        fill(second_ref, 0)

    for payload, exists in zip((first_ref, second_ref), has_partners()):

        @pl.when(jnp.logical_not(exists))
        def _():
            payload[...] = jnp.zeros_like(payload)


def inner_kernel(
    block_rows,
    count_ref,
    values_ref,
    cells_ref,
    base_hbm,
    velocity_hbm,
    forcing_hbm,
    composition_ref,
    lines_ref,
    outer_ref,
    table,
    sums,
    fields,
    base,
    velocity,
    forcing,
    semaphores,
):
    cells_lateral, cells_radial, cells_side = base.shape
    margin = MIGRATION_PLANES
    planes = cells_lateral + 2 * margin
    pitch = round_up(cells_radial, 8)
    moved_planes = margin * cells_radial
    inner = cells_lateral - 2 * margin
    inner_planes = inner * cells_radial
    group_rows, lane_total = cells_ref.shape[1:]
    fetches = Fetches(semaphores)
    fetches.start(velocity_hbm, velocity)
    fetches.start(forcing_hbm, forcing)
    fetches.start(base_hbm, base)
    table[...] = jnp.zeros_like(table)

    nothing = jnp.zeros((cells_radial, cells_side), jnp.float32)

    def put(field, plane, value):
        fields[field, pl.ds(plane * pitch, cells_radial), :] = value

    def lay_out(those):
        for field in those:
            for t in range(cells_radial):
                row = outward_row(t, cells_radial)
                lines_ref[field, t] = fields[field, pl.ds(row, planes, stride=pitch), :]

    def step(first_row):
        loads, plane, side = tracer_block(
            count, values_ref, cells_ref, 1, first_row, block_rows, cells_side
        )
        where = fold_inner(plane - moved_planes, side, inner_planes, cells_side)
        table[...] = hot_product(table[...], loads, *where, block_rows)

    count = jnp.max(count_ref[...]).astype(jnp.int32)
    for_used_blocks(count, group_rows, block_rows, lane_total, [], step)

    fetches.wait(0, None)
    for plane in range(planes):
        x = plane - margin
        own = 0 <= x < cells_lateral
        for q in range(3):
            put(VELOCITY + q, plane, velocity[q, x] if own else nothing)
        for q in range(2):
            put(SOURCE + q, plane, forcing[q, x] if own else nothing)
    late = VISCOSITY, SOURCE + 2
    lay_out(field for field in range(LINE_FIELDS) if field not in late)

    for q in range(3):

        def put_sums(plane, column, block):
            height, width = block.shape
            sums[q, pl.ds(plane, height), column : column + width] = block

        unfold_inner(table, q, inner_planes, cells_side, put_sums)
    for plane in range(planes):
        x = plane - 2 * margin
        viscosity, source = nothing, nothing
        if 0 <= x < inner:
            rows = pl.ds(x * cells_radial, cells_radial)
            cell_sums = [sums[q, rows, :] for q in range(3)]
            basalt_share, melt_share, viscosity = composition_of(cell_sums, base[x + margin])
            source = forcing[2, x + margin] - BUOYANCY * basalt_share
            composition_ref[0, x] = basalt_share
            composition_ref[1, x] = melt_share
        put(VISCOSITY, plane, viscosity)
        put(SOURCE + 2, plane, source)
    lay_out(late)
    for offset in range(margin):
        for place, x in ((offset, offset), (margin + offset, cells_lateral - margin + offset)):
            outer_ref[0, place] = base[x]
            outer_ref[1, place] = forcing[2, x]


BLOCK_ROWS = 64
CHUNK_ROWS = 2


def dense_tracers(tracer_values, tracer_cell):
    lane_total = 128
    return tracer_values.reshape(3, 3, -1, lane_total), tracer_cell.reshape(3, -1, lane_total)


def outgoing_sums(tracer_count, values, cells, base_viscosity, velocity, forcing):
    cells_lateral, cells_radial, cells_side = base_viscosity.shape
    moved_planes = MIGRATION_PLANES * cells_radial
    group_rows, lane_total = cells.shape[1:]
    block_rows = min(BLOCK_ROWS, group_rows // 2)
    _, payload_rows = payload_sections(cells_radial)
    hbm = pl.BlockSpec(memory_space=pltpu.HBM)
    vmem = pl.BlockSpec(memory_space=pltpu.VMEM)
    payload = jax.ShapeDtypeStruct((payload_rows, cells_side), jnp.float32)
    outer_planes = (MIGRATION_PLANES, cells_radial, cells_side)
    return pl.pallas_call(
        functools.partial(outgoing_kernel, block_rows),
        out_shape=(
            jax.ShapeDtypeStruct((6 * moved_planes, cells_side), jnp.float32),
            payload,
            payload,
            jax.ShapeDtypeStruct((8, lane_total), jnp.float32),
            jax.ShapeDtypeStruct(values.shape, jnp.float32),
            jax.ShapeDtypeStruct(cells.shape, jnp.int32),
        ),
        in_specs=[hbm] * 6,
        out_specs=(vmem,) * 6,
        scratch_shapes=[
            pltpu.SMEM(tracer_count.shape, jnp.int32),
            pltpu.VMEM((2,) + outer_planes, jnp.float32),
            pltpu.VMEM((2, 3) + outer_planes, jnp.float32),
            pltpu.VMEM((2, 3, 1, cells_radial, cells_side), jnp.float32),
            pltpu.VMEM((2, 4 * moved_planes, cells_side * 3 // 4), jnp.float32),
            pltpu.SemaphoreType.DMA((13,)),
        ],
        compiler_params=pltpu.CompilerParams(vmem_limit_bytes=32 * 2**20),
        cost_estimate=pl.CostEstimate(
            flops=30 * group_rows * lane_total * moved_planes * cells_side,
            bytes_accessed=4 * (values.size + cells.size),
            transcendentals=0,
        ),
        name="outgoing_sums",
    )(
        *(
            pltpu.with_memory_space_constraint(array, pltpu.HBM)
            for array in (tracer_count, values, cells, base_viscosity, velocity, forcing)
        )
    )


def inner_lines(count, values, cells, base_viscosity, velocity, forcing):
    cells_lateral, cells_radial, cells_side = base_viscosity.shape
    planes = cells_lateral + 2 * MIGRATION_PLANES
    inner = cells_lateral - 2 * MIGRATION_PLANES
    inner_planes = inner * cells_radial
    group_rows, lane_total = cells.shape[1:]
    block_rows = min(BLOCK_ROWS, group_rows // 2)
    vmem = pl.BlockSpec(memory_space=pltpu.VMEM)
    return pl.pallas_call(
        functools.partial(inner_kernel, block_rows),
        out_shape=(
            jax.ShapeDtypeStruct((2, inner, cells_radial, cells_side), jnp.float32),
            jax.ShapeDtypeStruct((LINE_FIELDS, cells_radial, planes, cells_side), jnp.float32),
            jax.ShapeDtypeStruct(
                (2, 2 * MIGRATION_PLANES, cells_radial, cells_side), jnp.float32
            ),
        ),
        in_specs=[vmem] * 3 + [pl.BlockSpec(memory_space=pltpu.HBM)] * 3,
        out_specs=(vmem,) * 3,
        scratch_shapes=[
            pltpu.VMEM((3 * (inner_planes * 5 // 6), cells_side * 5 // 4), jnp.float32),
            pltpu.VMEM((3, inner_planes, cells_side), jnp.float32),
            pltpu.VMEM((LINE_FIELDS, planes * round_up(cells_radial, 8), cells_side), jnp.float32),
            pltpu.VMEM(base_viscosity.shape, jnp.float32),
            pltpu.VMEM(velocity.shape, jnp.float32),
            pltpu.VMEM(forcing.shape, jnp.float32),
            pltpu.SemaphoreType.DMA((3,)),
        ],
        compiler_params=pltpu.CompilerParams(vmem_limit_bytes=32 * 2**20),
        cost_estimate=pl.CostEstimate(
            flops=6 * group_rows * lane_total * inner * cells_radial * cells_side,
            bytes_accessed=4 * (values.size + cells.size),
            transcendentals=0,
        ),
        name="inner_lines",
    )(
        count,
        values,
        cells,
        *(
            pltpu.with_memory_space_constraint(array, pltpu.HBM)
            for array in (base_viscosity, velocity, forcing)
        ),
    )


def pair_swaps(first, second):
    count = lax.axis_size("lat")
    received = []
    for payload, start in ((second, 1), (first, 0)):
        target = list(range(count))
        for low in range(start, count - 1, 2):
            target[low], target[low + 1] = low + 1, low
        received.append(lax.ppermute(payload, "lat", list(enumerate(target))))
    return received[::-1]


def shift_planes(block, step):
    return pltpu.roll(block, step % block.shape[0], 0)


def shift_side(block, step):
    return pltpu.roll(block, step % block.shape[1], 1)


def neighbours(block):
    return (
        shift_planes(block, 1),
        shift_planes(block, -1),
        shift_side(block, 1),
        shift_side(block, -1),
    )


def inside_side(values):
    lane = lax.broadcasted_iota(jnp.int32, values[2].shape, 1)
    lower = jnp.where(lane > 0, values[2], 0.0)
    upper = jnp.where(lane < lane.shape[1] - 1, values[3], 0.0)
    return values[0], values[1], lower, upper


def total_of(terms):
    result = terms[0]
    for term in terms[1:]:
        result = result + term
    return result


def inside_grid(shape, margin, cells_lateral):
    plane = lax.broadcasted_iota(jnp.int32, shape, 0)
    lateral = lax.axis_index("lat")
    first = jnp.where(lateral == 0, margin, 1)
    last = jnp.where(lateral == lax.axis_size("lat") - 1, margin + cells_lateral, shape[0] - 1)
    return (plane >= first) & (plane < last)


LONG_FIELDS, SHORT_FIELDS = 5, 7


def message_rows(cells_lateral):
    planes = cells_lateral + 2 * MIGRATION_PLANES
    return round_up(LONG_FIELDS * planes + SHORT_FIELDS * cells_lateral + MIGRATION_PLANES, 8)


def message_part(cells_lateral, field):
    planes = cells_lateral + 2 * MIGRATION_PLANES
    if field < LONG_FIELDS:
        return pl.ds(field * planes, planes), 0, planes
    first = LONG_FIELDS * planes + (field - LONG_FIELDS) * cells_lateral
    return pl.ds(first, cells_lateral), MIGRATION_PLANES, cells_lateral


def solve_lines(radial, beside, cells_radial, valid, keep, keep_part):
    last = cells_radial - 1
    viscosity = [radial(VISCOSITY, t) for t in range(cells_radial)]
    lateral_faces, lateral_sums = [], []
    for here in viscosity:
        faces = [LATERAL * 0.5 * (here + there) for there in inside_side(beside(here))]
        lateral_sums.append(total_of(faces))
        lateral_faces.append(inside_side(faces))
    radial_faces = [RADIAL * 0.5 * viscosity[0]] + [
        RADIAL * 0.5 * (viscosity[t - 1] + viscosity[t]) for t in range(1, cells_radial)
    ]

    excess = lateral_sums[0] + radial_faces[0]
    inverse, coupling = [], []
    for t in range(last):
        inverse.append(1.0 / (excess + radial_faces[t + 1]))
        coupling.append(radial_faces[t + 1] * inverse[t])
        excess = lateral_sums[t + 1] + coupling[t] * excess

    def lateral_terms(t, around):
        return [face * there for face, there in zip(lateral_faces[t], around)]

    def forward(right_side):
        eliminated = [right_side[0]]
        for t in range(1, cells_radial):
            eliminated.append(right_side[t] + coupling[t - 1] * eliminated[t - 1])
        return eliminated

    def backward(eliminated):
        solved = [jnp.zeros_like(excess)]
        for t in range(last - 1, -1, -1):
            solved.append(eliminated[t] * inverse[t] + coupling[t] * solved[-1])
        return solved[::-1]

    response = [jnp.ones_like(excess)]
    for t in range(last - 1, -1, -1):
        response.append(coupling[t] * response[-1])
    response = response[::-1]

    def finish(part, eliminated):
        keep(LONG_FIELDS + part, eliminated[last])
        for t, value in enumerate(eliminated[:last]):
            keep_part(part, t, value)

    keep(0, viscosity[last])
    keep(1, excess)
    for q in range(3):
        source = [radial(SOURCE + q, t) for t in range(cells_radial)]
        eliminated = forward(
            [
                total_of([source[t]] + lateral_terms(t, beside(radial(VELOCITY + q, t))))
                for t in range(cells_radial)
            ]
        )
        keep(2 + q, eliminated[last])
        particular = [jnp.where(valid, value, 0.0) for value in backward(eliminated)]
        finish(
            q,
            forward(
                [
                    total_of([source[t]] + lateral_terms(t, beside(particular[t])))
                    for t in range(cells_radial)
                ]
            ),
        )
    around = [beside(jnp.where(valid, value, 0.0)) for value in response]
    for side in range(4):
        finish(
            3 + side,
            forward([lateral_faces[t][side] * around[t][side] for t in range(cells_radial)]),
        )
    for t in range(last):
        keep_part(SHORT_FIELDS, t, inverse[t])
        keep_part(SHORT_FIELDS + 1, t, coupling[t])


def eliminate_kernel(
    inner_ref,
    lines_ref,
    edge_ref,
    second_ref,
    first_ref,
    from_second_ref,
    from_first_ref,
    outer_ref,
    composition_ref,
    mine_ref,
    message_ref,
    parts_ref,
    fields,
    shifted,
):
    _, cells_lateral, cells_radial, cells_side = composition_ref.shape
    margin = MIGRATION_PLANES
    planes = cells_lateral + 2 * margin
    pitch = round_up(cells_radial, 8)
    moved_planes = margin * cells_radial
    starts, _ = payload_sections(cells_radial)
    odd = lax.rem(lax.axis_index("lat"), 2) == 1

    def sent(upward, start):
        part = pl.ds(start, cells_radial)
        mine_first = odd if not upward else jnp.logical_not(odd)
        return jnp.where(mine_first, first_ref[part, :], second_ref[part, :])

    def arrived(from_above, start):
        part = pl.ds(start, cells_radial)
        is_first = odd if not from_above else jnp.logical_not(odd)
        return jnp.where(is_first, from_first_ref[part, :], from_second_ref[part, :])

    outer = 2 * margin

    def put(field, slot, value):
        fields[field, pl.ds(slot * pitch, cells_radial), :] = value

    for above in (False, True):
        for offset in range(margin):
            shift = offset * cells_radial
            halo = offset + (outer + margin if above else 0)
            own = offset + (outer if above else margin)
            x = offset + (cells_lateral - margin if above else 0)
            place = offset + (margin if above else 0)
            halo_sums, own_sums = [], []
            for q in range(3):
                row = q * moved_planes + shift
                rows = pl.ds((2 * q + int(above)) * moved_planes + shift, cells_radial)
                own_sums.append(edge_ref[rows, :] + arrived(above, starts[0] + row))
                halo_sums.append(sent(above, starts[0] + row) + arrived(above, starts[1] + row))
                put(VELOCITY + q, halo, arrived(above, starts[2] + row))
            basalt_share, melt_share, viscosity = composition_of(own_sums, outer_ref[0, place])
            composition_ref[0, x] = basalt_share
            composition_ref[1, x] = melt_share
            put(VISCOSITY, own, viscosity)
            put(SOURCE + 2, own, outer_ref[1, place] - BUOYANCY * basalt_share)
            basalt_share, _, viscosity = composition_of(
                halo_sums, arrived(above, starts[3] + shift)
            )
            put(VISCOSITY, halo, viscosity)
            beside = offset == (0 if above else margin - 1)
            for q in range(3):
                source = jnp.zeros_like(viscosity)
                if beside:
                    source = arrived(above, starts[4] + q * cells_radial)
                    if q == 2:
                        source = source - BUOYANCY * basalt_share
                put(SOURCE + q, halo, source)
    for x in range(margin, cells_lateral - margin):
        for q in range(2):
            composition_ref[q, x] = inner_ref[q, x - margin]

    def radial(field, t):
        replaced = outer if field in (VISCOSITY, SOURCE + 2) else margin
        plane = lax.broadcasted_iota(jnp.int32, (planes, cells_side), 0)
        own = (plane >= replaced) & (plane < planes - replaced)
        row = outward_row(t, cells_radial)
        edges = fields[field, pl.ds(row, 2 * outer, stride=pitch), :]
        if 2 * outer * 2 == planes:
            edges = jnp.concatenate([edges, edges], 0)
        else:
            gap = jnp.zeros((planes - 2 * outer, cells_side), jnp.float32)
            edges = jnp.concatenate([edges[:outer], gap, edges[outer:]], 0)
        return jnp.where(own, lines_ref[field, t], edges)

    unused = LONG_FIELDS * planes + SHORT_FIELDS * cells_lateral
    if unused < message_ref.shape[0]:
        message_ref[unused:, :] = jnp.zeros((message_ref.shape[0] - unused, cells_side), jnp.float32)

    def keep(field, value):
        rows, first, count = message_part(cells_lateral, field)
        mine_ref[field] = value
        message_ref[rows, :] = value[first : first + count]

    def keep_part(part, t, value):
        parts_ref[part, t] = value

    used = []

    def beside(values):
        place = shifted.at[len(used)]
        used.append(values)
        place[pl.ds(8, planes), :] = values
        lower, upper = place[pl.ds(7, planes), :], place[pl.ds(9, planes), :]
        return lower, upper, shift_side(values, 1), shift_side(values, -1)

    valid = inside_grid((planes, cells_side), margin, cells_lateral)
    solve_lines(radial, beside, cells_radial, valid, keep, keep_part)


def eliminate(inner, lines, outer, edge, sent, received, cells_lateral):
    cells_radial, cells_side = inner.shape[2:]
    planes = cells_lateral + 2 * MIGRATION_PLANES
    vmem = pl.BlockSpec(memory_space=pltpu.VMEM)
    line = (planes, cells_side)
    return pl.pallas_call(
        eliminate_kernel,
        out_shape=(
            jax.ShapeDtypeStruct((2, cells_lateral, cells_radial, cells_side), jnp.float32),
            jax.ShapeDtypeStruct((LONG_FIELDS + SHORT_FIELDS,) + line, jnp.float32),
            jax.ShapeDtypeStruct((message_rows(cells_lateral), cells_side), jnp.float32),
            jax.ShapeDtypeStruct((SHORT_FIELDS + 2, cells_radial - 1) + line, jnp.float32),
        ),
        in_specs=[vmem] * 8,
        out_specs=(vmem,) * 4,
        scratch_shapes=[
            pltpu.VMEM(
                (LINE_FIELDS, 4 * MIGRATION_PLANES * round_up(cells_radial, 8), cells_side),
                jnp.float32,
            ),
            pltpu.VMEM((8 * cells_radial, round_up(planes, 8) + 16, cells_side), jnp.float32),
        ],
        compiler_params=pltpu.CompilerParams(vmem_limit_bytes=32 * 2**20),
        name="eliminate",
    )(inner, lines, edge, *sent[::-1], *received[::-1], outer)


def join_kernel(mine_ref, message_ref, parts_ref, smoothed_hbm, smoothed, lines, semaphores):
    _, cells_lateral, cells_radial, cells_side = smoothed.shape
    margin = MIGRATION_PLANES
    planes = cells_lateral + 2 * margin
    pitch = round_up(cells_radial, 8)
    valid = inside_grid((planes, cells_side), margin, cells_lateral)

    def mine(field):
        return mine_ref[field]

    def other(field):
        rows, first, _ = message_part(cells_lateral, field)
        return message_ref[pl.ds(rows.start - first, planes), :]

    face = RADIAL * 0.5 * (mine(0) + other(0))
    excess, other_excess = mine(1), other(1)
    scale = 1.0 / (excess * other_excess + face * (excess + other_excess))
    own_weight = (other_excess + face) * scale
    other_weight = (excess + face) * scale
    cross = face * scale

    def second_right(field_of, q, around):
        terms = [field_of(LONG_FIELDS + 3 + side) * there for side, there in enumerate(around)]
        return total_of([field_of(LONG_FIELDS + q)] + terms)

    fetches = Fetches(semaphores)
    for q in range(3):
        right, other_right = mine(2 + q), other(2 + q)
        own = jnp.where(valid, own_weight * right + cross * other_right, 0.0)
        beyond = jnp.where(valid, other_weight * other_right + cross * right, 0.0)
        around = neighbours(own)
        right = second_right(mine, q, around)
        other_right = second_right(other, q, neighbours(beyond))
        value = own_weight * right + cross * other_right
        for t in range(cells_radial - 1, -1, -1):
            if t < cells_radial - 1:
                terms = [parts_ref[3 + side, t] * there for side, there in enumerate(around)]
                right = total_of([parts_ref[q, t]] + terms)
                value = right * parts_ref[SHORT_FIELDS, t] + parts_ref[SHORT_FIELDS + 1, t] * value
            row = outward_row(t, cells_radial)
            lines[q, pl.ds(row, cells_lateral, stride=pitch), :] = value[
                margin : margin + cells_lateral
            ]
        for x in range(cells_lateral):
            smoothed[q, x] = lines[q, pl.ds(x * pitch, cells_radial), :]
        fetches.start(smoothed.at[q], smoothed_hbm.at[q])
    fetches.wait(0, None)


def join(mine, message, parts, like):
    cells_lateral, cells_radial, cells_side = like.shape[1:]
    vmem = pl.BlockSpec(memory_space=pltpu.VMEM)
    return pl.pallas_call(
        join_kernel,
        out_shape=jax.ShapeDtypeStruct(like.shape, jnp.float32),
        in_specs=[vmem] * 3,
        out_specs=pl.BlockSpec(memory_space=pltpu.HBM),
        scratch_shapes=[
            pltpu.VMEM(like.shape, jnp.float32),
            pltpu.VMEM((3, cells_lateral * round_up(cells_radial, 8), cells_side), jnp.float32),
            pltpu.SemaphoreType.DMA((3,)),
        ],
        compiler_params=pltpu.CompilerParams(vmem_limit_bytes=32 * 2**20),
        name="join",
    )(mine, message, parts)


def extended(block, sides, width):
    for axis, dim in sides:
        count = lax.axis_size(axis)
        forward = [(i, i + 1) for i in range(count - 1)]
        backward = [(target, source) for source, target in forward]
        low = lax.ppermute(
            lax.slice_in_dim(block, block.shape[dim] - width, None, axis=dim), axis, forward
        )
        high = lax.ppermute(lax.slice_in_dim(block, 0, width, axis=dim), axis, backward)
        block = jnp.concatenate([low, block, high], axis=dim)
    return block


def block_factor(diagonal, lower_band, upper_band):
    pivots = []
    upper_scaled = []
    for row_index in range(diagonal.shape[1]):
        if row_index == 0:
            pivot_row = diagonal[:, 0]
        else:
            pivot_row = diagonal[:, row_index] - lower_band[:, row_index] * upper_scaled[-1]
        pivots.append(pivot_row)
        upper_scaled.append(upper_band[:, row_index] / pivot_row)
    return (pivots, upper_scaled)


def block_solve(pivots, upper_scaled, lower_band, right_side):
    row_total = len(pivots)
    modified = []
    for row_index in range(row_total):
        if row_index == 0:
            value_row = right_side[:, :, 0] / pivots[0]
        else:
            value_row = (
                right_side[:, :, row_index] - lower_band[:, row_index] * modified[-1]
            ) / pivots[row_index]
        modified.append(value_row)
    solved = [modified[-1]]
    for row_index in range(row_total - 2, -1, -1):
        solved.append(modified[row_index] - upper_scaled[row_index] * solved[-1])
    ordered = solved[::-1]
    return jnp.stack(ordered, 2)


def interface_solve(coefficients):
    column_total = coefficients.shape[2]

    def forward(carried, inputs):
        offset, carried_slope = carried
        left_first, right_first, left_last, right_last, free_first, free_last = inputs
        divisor = 1.0 - left_first * carried_slope
        first_fixed = (free_first + left_first * offset) / divisor
        first_slope = right_first / divisor
        next_offset = free_last + left_last * (offset + carried_slope * first_fixed)
        next_slope = left_last * carried_slope * first_slope + right_last
        return ((next_offset, next_slope), (first_fixed, first_slope, next_offset, next_slope))

    start_state = (
        jnp.zeros((3, column_total), jnp.float32),
        jnp.zeros((column_total,), jnp.float32),
    )
    scan_inputs = (
        coefficients[:, 0],
        coefficients[:, 1],
        coefficients[:, 2],
        coefficients[:, 3],
        coefficients[:, 4:7],
        coefficients[:, 7:10],
    )
    final_state, eliminated = lax.scan(forward, start_state, scan_inputs)

    def backward(first_next, inputs):
        fixed_first, slope_first, fixed_last, slope_last = inputs
        first_value = fixed_first + slope_first * first_next
        last_value = fixed_last + slope_last * first_next
        return (first_value, (first_value, last_value))

    final_first, values_pair = lax.scan(
        backward, jnp.zeros((3, column_total), jnp.float32), eliminated, reverse=True
    )
    first_values, last_values = values_pair
    nothing_row = jnp.zeros((1, 3, column_total), jnp.float32)
    from_below = jnp.concatenate([nothing_row, last_values[:-1]], 0)
    from_above = jnp.concatenate([first_values[1:], nothing_row], 0)
    return jnp.concatenate([from_below, from_above], 1)


def reduced_boundary(interface):
    gathered = lax.all_gather(interface, "rad", axis=0, tiled=True)
    solved = interface_solve(gathered)
    return lax.dynamic_index_in_dim(solved, lax.axis_index("rad"), 0, keepdims=False)


def many_blocks(values, cells, count, edge, received, base_viscosity, velocity, forcing):
    cells_lateral, cells_radial, cells_side = base_viscosity.shape
    moved_rows = MIGRATION_PLANES * cells_radial
    odd = lax.rem(lax.axis_index("lat"), 2) == 1
    from_below = jnp.where(odd, received[0], received[1])[: 3 * moved_rows]
    from_above = jnp.where(odd, received[1], received[0])[: 3 * moved_rows]
    edge = edge.reshape(3, 2, moved_rows, cells_side)
    below = edge[:, 0] + from_below.reshape(3, moved_rows, cells_side)
    above = edge[:, 1] + from_above.reshape(3, moved_rows, cells_side)
    shares = [
        (sums[1:] / (sums[0] + PRIOR_WEIGHT)).reshape(2, -1, cells_radial, cells_side)
        for sums in (below, above)
    ]
    inner, _, _ = inner_lines(count, values, cells, base_viscosity, velocity, forcing)
    basalt_share, melt_share = jnp.concatenate([shares[0], inner, shares[1]], 1)
    viscosity = base_viscosity * jnp.exp(
        CONTRAST_BASALT * basalt_share - CONTRAST_MELT * melt_share
    )
    viscosity_pad = extended(viscosity, (("lat", 0), ("rad", 1)), 1)
    side_pad = jnp.pad(viscosity, ((0, 0), (0, 0), (1, 1)))
    face_west = LATERAL * 0.5 * (viscosity + viscosity_pad[:-2, 1:-1])
    face_east = LATERAL * 0.5 * (viscosity + viscosity_pad[2:, 1:-1])
    face_south = LATERAL * 0.5 * (viscosity + side_pad[:, :, :-2])
    face_north = LATERAL * 0.5 * (viscosity + side_pad[:, :, 2:])
    face_below = RADIAL * 0.5 * (viscosity + viscosity_pad[1:-1, :-2])
    face_above = RADIAL * 0.5 * (viscosity + viscosity_pad[1:-1, 2:])
    diagonal = face_west + face_east + face_south + face_north + face_below + face_above
    source = jnp.concatenate([forcing[:2], (forcing[2] - BUOYANCY * basalt_share)[None]], 0)
    lower_band = -face_below
    upper_band = -face_above
    pivots, upper_scaled = block_factor(diagonal, lower_band, upper_band)
    radial_iota = lax.broadcasted_iota(jnp.int32, viscosity.shape, 1)
    response_side = jnp.stack(
        [
            jnp.where(radial_iota == 0, face_below, jnp.float32(0.0)),
            jnp.where(radial_iota == cells_radial - 1, face_above, jnp.float32(0.0)),
        ]
    )
    response = block_solve(pivots, upper_scaled, lower_band, response_side)
    current = velocity
    for sweep_index in range(SWEEPS):
        velocity_pad = extended(current, (("lat", 1),), 1)
        side_velocity = jnp.pad(current, ((0, 0), (0, 0), (0, 0), (1, 1)))
        right_side = (
            source
            + face_west * velocity_pad[:, :-2]
            + face_east * velocity_pad[:, 2:]
            + face_south * side_velocity[..., :-2]
            + face_north * side_velocity[..., 2:]
        )
        particular = block_solve(pivots, upper_scaled, lower_band, right_side)
        interface = jnp.concatenate(
            [response[:, :, 0], response[:, :, -1], particular[:, :, 0], particular[:, :, -1]], 0
        )
        interface = interface.reshape(1, 10, cells_lateral * cells_side)
        boundary = reduced_boundary(interface).reshape(6, cells_lateral, 1, cells_side)
        current = particular + response[0][None] * boundary[:3] + response[1][None] * boundary[3:]
    composition = jnp.stack([basalt_share, melt_share])
    return (current, composition)

def local(tracer_values, tracer_cell, tracer_count, base_viscosity, velocity, forcing):
    values, cells = dense_tracers(tracer_values, tracer_cell)
    edge, first, second, count, values, cells = outgoing_sums(
        tracer_count, values, cells, base_viscosity, velocity, forcing
    )
    sent = first, second
    received = pair_swaps(first, second)
    if lax.axis_size("rad") != 2:
        return many_blocks(
            values, cells, count, edge, received, base_viscosity, velocity, forcing
        )
    inner, lines, outer = inner_lines(count, values, cells, base_viscosity, velocity, forcing)
    composition, mine, message, parts = eliminate(
        inner, lines, outer, edge, sent, received, base_viscosity.shape[0]
    )
    other = lax.ppermute(message, "rad", [(0, 1), (1, 0)])
    return join(mine, other, parts, velocity), composition


def solution(mesh):
    return jax.shard_map(
        local,
        mesh=mesh,
        in_specs=(
            P("lat", "rad", None, None),
            P("lat", "rad", None),
            P("lat", "rad", None),
            P("lat", "rad", None),
            P(None, "lat", "rad", None),
            P(None, "lat", "rad", None),
        ),
        out_specs=(P(None, "lat", "rad", None), P(None, "lat", "rad", None)),
        check_vma=False,
    )
```

```python
import functools

import jax
import jax.numpy as jnp
from jax import lax
from jax.experimental import pallas as pl
from jax.experimental.pallas import tpu as pltpu
from jax.sharding import PartitionSpec as P

SWEEPS = 2
MIGRATION_PLANES = 2

LATERAL = 0.015625
RADIAL = 32.0
BUOYANCY = 0.1
PRIOR_WEIGHT = 0.5
CONTRAST_BASALT = 2.3
CONTRAST_MELT = 1.5

TILE_ROWS = 16


def round_up(value, multiple):
    return -(-value // multiple) * multiple


def split_index(index, count):
    if count & (count - 1) == 0:
        return lax.shift_right_logical(index, count.bit_length() - 1), index & (count - 1)
    quotient = lax.div(index, count)
    return quotient, index - quotient * count


def payload_sections(cells_radial):
    pair = MIGRATION_PLANES * cells_radial
    starts = [0, 3 * pair, 6 * pair, 9 * pair, 10 * pair]
    return starts, round_up(10 * pair + 3 * cells_radial, 8)


def spread_row(row):
    return jnp.broadcast_to(row, (TILE_ROWS, row.shape[1])).astype(jnp.bfloat16)


def hot_tiles(index, row_total):
    iota = lax.broadcasted_iota(jnp.int32, index.shape, 0)
    return [
        index == (iota + first).astype(jnp.float32).astype(jnp.bfloat16)
        for first in range(0, row_total, TILE_ROWS)
    ]


def hot_product(rows, sums, loads, high, low, high_rows, low_rows, chunk_rows):
    dense = [high.astype(jnp.float32), low.astype(jnp.float32), *loads]
    for index, block in enumerate(dense):
        rows[index] = block
    zero = jnp.zeros((TILE_ROWS, high.shape[1]), jnp.bfloat16)
    one = jnp.ones((TILE_ROWS, high.shape[1]), jnp.bfloat16)
    for first_row in range(0, high.shape[0], chunk_rows):
        left, right = [], []
        for row in range(first_row, first_row + chunk_rows):
            spread = [spread_row(rows[index, row : row + 1, :]) for index in range(len(dense))]
            high_masks = hot_tiles(spread[0], high_rows)
            low_masks = hot_tiles(spread[1], low_rows)
            tiles = [jnp.where(mask, load, zero) for load in spread[2:] for mask in high_masks]
            left.append(jnp.concatenate(tiles, 0))
            right.append(jnp.concatenate([jnp.where(mask, one, zero) for mask in low_masks], 0))
        sums = sums + lax.dot_general(
            jnp.concatenate(left, 1),
            jnp.concatenate(right, 1),
            (((1,), (1,)), ((), ())),
            preferred_element_type=jnp.float32,
        )
    return sums


def edge_row(plane, plane_total, moved_total):
    inner = (plane >= moved_total) & (plane < plane_total - moved_total)
    last = plane - (plane_total - 2 * moved_total)
    return jnp.where(inner, -plane_total, jnp.where(plane < moved_total, plane, last))


def fold_moved(plane, side, plane_total, side_total):
    width, third = side_total // 4, plane_total // 3
    part = jnp.where(plane >= third, 1, 0) + jnp.where(plane >= 2 * third, 1, 0)
    other = side >= 3 * width
    high = jnp.where(other, plane_total + plane - part * third, plane)
    low = jnp.where(other, side - 3 * width + part * width, side)
    return high, low, plane_total + third, 3 * width


def unfold_moved(table, q, plane_total, side_total, put):
    width, third = side_total // 4, plane_total // 3
    rows = plane_total + third
    put(0, 0, table[pl.ds(q * rows, plane_total), 0 : 3 * width])
    for part in range(3):
        block = table[
            pl.ds(q * rows + plane_total, third), part * width : (part + 1) * width
        ]
        put(part * third, 3 * width, block)


def fold_inner(plane, side, plane_total, side_total):
    rows, width = plane_total * 5 // 6, side_total // 4
    part, rest = split_index(side, width)
    other = plane >= rows
    high = jnp.where(other, plane - rows + part * (plane_total - rows), plane)
    high = jnp.where(plane < plane_total, high, -1)
    low = jnp.where(other, side_total + rest, side)
    return high, low, rows, side_total + width


def unfold_inner(table, q, plane_total, side_total, put):
    rows, width = plane_total * 5 // 6, side_total // 4
    left = plane_total - rows
    put(0, 0, table[pl.ds(q * rows, rows), 0:side_total])
    for part in range(4):
        block = table[pl.ds(q * rows + part * left, left), side_total : side_total + width]
        put(rows, part * width, block)


def tracer_block(count, values, cells, group, first_row, block_rows, cells_side):
    rows = pl.ds(first_row, block_rows)
    lane_total = cells.shape[2]
    shape = (block_rows, lane_total)
    slot = (first_row + lax.broadcasted_iota(jnp.int32, shape, 0)) * lane_total
    slot = slot + lax.broadcasted_iota(jnp.int32, shape, 1)
    weight = jnp.where(slot < count, 0.5 + values[0, group, rows, :], jnp.float32(0.0))
    loads = [weight, weight * values[1, group, rows, :], weight * values[2, group, rows, :]]
    plane, side = split_index(cells[group, rows, :], cells_side)
    return loads, plane, side


def for_used_blocks(used, group_rows, block_rows, lane_total, late_copies, step):
    block_slots = block_rows * lane_total
    blocks = lax.div(used + (block_slots - 1), block_slots)
    blocks = jnp.clip(blocks, 1, group_rows // block_rows)

    def wait_late():
        for copy in late_copies:
            copy.wait()

    def repeat(index, carried):
        pl.when(index == 1)(wait_late)
        step(pl.multiple_of(index * block_rows, block_rows))
        return carried

    lax.fori_loop(0, blocks, repeat, 0)
    pl.when(blocks == 1)(wait_late)


VISCOSITY, VELOCITY, SOURCE, LINE_FIELDS = 0, 1, 4, 7


def composition_of(cell_sums, base):
    scale = 1.0 / (cell_sums[0] + PRIOR_WEIGHT)
    basalt_share, melt_share = cell_sums[1] * scale, cell_sums[2] * scale
    weakening = jnp.exp(CONTRAST_BASALT * basalt_share - CONTRAST_MELT * melt_share)
    return basalt_share, melt_share, base * weakening


def outward_row(t, cells_radial):
    return jnp.where(lax.axis_index("rad") == 0, t, cells_radial - 1 - t)


class Fetches:
    def __init__(self, semaphores):
        self.semaphores = semaphores
        self.copies = []

    def start(self, source, target):
        copy = pltpu.make_async_copy(source, target, self.semaphores.at[len(self.copies)])
        copy.start()
        self.copies.append(copy)

    def wait(self, first, last):
        for copy in self.copies[first:last]:
            copy.wait()


def has_partners():
    lateral, count = lax.axis_index("lat"), lax.axis_size("lat")
    odd = lax.rem(lateral, 2) == 1
    above, below = lateral + 1 < count, lateral > 0
    return jnp.logical_or(odd, above), jnp.where(odd, above, below)


def outgoing_kernel(
    block_rows,
    counts_hbm,
    values_hbm,
    cells_hbm,
    base_hbm,
    velocity_hbm,
    forcing_hbm,
    edge_ref,
    first_ref,
    second_ref,
    count_ref,
    values,
    cells,
    counts,
    base,
    velocity,
    forcing,
    moved_sums,
    rows,
    semaphores,
):
    cells_lateral, cells_radial, cells_side = base_hbm.shape
    plane_total = cells_lateral * cells_radial
    moved_planes = MIGRATION_PLANES * cells_radial
    group_rows, lane_total = cells.shape[1:]

    fetches = Fetches(semaphores)
    fetches.start(counts_hbm, counts)
    part = pl.ds(0, block_rows)
    fetches.start(cells_hbm.at[:, part], cells.at[:, part])
    for q in range(3):
        fetches.start(values_hbm.at[q, :, part], values.at[q, :, part])
    part = pl.ds(block_rows, group_rows - block_rows)
    fetches.start(cells_hbm.at[:, part], cells.at[:, part])
    fetches.start(values_hbm.at[:, :, part], values.at[:, :, part])
    for upward in (0, 1):
        outer = pl.ds((cells_lateral - MIGRATION_PLANES) * upward, MIGRATION_PLANES)
        fetches.start(base_hbm.at[outer], base.at[upward])
        fetches.start(velocity_hbm.at[:, outer], velocity.at[upward])
        outermost = pl.ds((cells_lateral - 1) * upward, 1)
        fetches.start(forcing_hbm.at[:, outermost], forcing.at[upward])

    edge_ref[...] = jnp.zeros_like(edge_ref)
    moved_sums[...] = jnp.zeros_like(moved_sums)

    def step(first_row):
        def block_of(group):
            count = counts[0, 0, group]
            return tracer_block(count, values, cells, group, first_row, block_rows, cells_side)

        loads, plane, side = block_of(1)
        row = edge_row(plane, plane_total, moved_planes)
        edge_ref[...] = hot_product(
            rows.at[1], edge_ref[...], loads, row, side, 2 * moved_planes, cells_side, CHUNK_ROWS
        )
        for slot, group in enumerate((0, 2)):
            loads, plane, side = block_of(group)
            if group == 0:
                plane = plane - (plane_total - moved_planes)
            table = fold_moved(plane, side, moved_planes, cells_side)
            moved_sums[slot] = hot_product(
                rows.at[group], moved_sums[slot], loads, *table, CHUNK_ROWS
            )

    fetches.wait(0, 5)
    count_ref[...] = jnp.full(count_ref.shape, counts[0, 0, 1], jnp.int32).astype(jnp.float32)
    used = jnp.maximum(jnp.maximum(counts[0, 0, 0], counts[0, 0, 1]), counts[0, 0, 2])
    for_used_blocks(used, group_rows, block_rows, lane_total, fetches.copies[5:7], step)
    fetches.wait(7, None)

    starts, rows_total = payload_sections(cells_radial)
    unused = starts[4] + 3 * cells_radial

    def fill(payload, upward):
        for q in range(3):

            def put_moved(plane, column, block):
                height, width = block.shape
                rows = pl.ds(starts[0] + q * moved_planes + plane, height)
                payload[rows, column : column + width] = block

            unfold_moved(moved_sums.at[upward], q, moved_planes, cells_side, put_moved)
            payload[pl.ds(starts[1] + q * moved_planes, moved_planes), :] = edge_ref[
                pl.ds((2 * q + upward) * moved_planes, moved_planes), :
            ]
            for offset in range(MIGRATION_PLANES):
                row = starts[2] + q * moved_planes + offset * cells_radial
                payload[pl.ds(row, cells_radial), :] = velocity[upward, q, offset]
            row = starts[4] + q * cells_radial
            payload[pl.ds(row, cells_radial), :] = forcing[upward, q, 0]
        for offset in range(MIGRATION_PLANES):
            row = starts[3] + offset * cells_radial
            payload[pl.ds(row, cells_radial), :] = base[upward, offset]
        if unused < rows_total:
            payload[unused:, :] = jnp.zeros((rows_total - unused, cells_side), jnp.float32)

    odd = lax.rem(lax.axis_index("lat"), 2) == 1

    @pl.when(odd)
    def _():
        fill(first_ref, 0)
        fill(second_ref, 1)

    @pl.when(jnp.logical_not(odd))
    def _():
        fill(first_ref, 1)
        fill(second_ref, 0)

    for payload, exists in zip((first_ref, second_ref), has_partners()):

        @pl.when(jnp.logical_not(exists))
        def _():
            payload[...] = jnp.zeros_like(payload)


def inner_kernel(
    block_rows,
    count_ref,
    values_ref,
    cells_ref,
    base_hbm,
    velocity_hbm,
    forcing_hbm,
    composition_ref,
    lines_ref,
    outer_ref,
    table,
    sums,
    fields,
    base,
    velocity,
    forcing,
    rows,
    semaphores,
):
    cells_lateral, cells_radial, cells_side = base.shape
    margin = MIGRATION_PLANES
    planes = cells_lateral + 2 * margin
    pitch = round_up(cells_radial, 8)
    moved_planes = margin * cells_radial
    inner = cells_lateral - 2 * margin
    inner_planes = inner * cells_radial
    group_rows, lane_total = cells_ref.shape[1:]
    fetches = Fetches(semaphores)
    fetches.start(velocity_hbm, velocity)
    fetches.start(forcing_hbm, forcing)
    fetches.start(base_hbm, base)
    table[...] = jnp.zeros_like(table)

    nothing = jnp.zeros((cells_radial, cells_side), jnp.float32)

    def put(field, plane, value):
        fields[field, pl.ds(plane * pitch, cells_radial), :] = value

    def lay_out(those):
        for field in those:
            for t in range(cells_radial):
                row = outward_row(t, cells_radial)
                lines_ref[field, t] = fields[field, pl.ds(row, planes, stride=pitch), :]

    def step(first_row):
        loads, plane, side = tracer_block(
            count, values_ref, cells_ref, 1, first_row, block_rows, cells_side
        )
        where = fold_inner(plane - moved_planes, side, inner_planes, cells_side)
        table[...] = hot_product(rows, table[...], loads, *where, block_rows)

    count = jnp.max(count_ref[...]).astype(jnp.int32)
    for_used_blocks(count, group_rows, block_rows, lane_total, [], step)

    fetches.wait(0, None)
    for plane in range(planes):
        x = plane - margin
        own = 0 <= x < cells_lateral
        for q in range(3):
            put(VELOCITY + q, plane, velocity[q, x] if own else nothing)
        for q in range(2):
            put(SOURCE + q, plane, forcing[q, x] if own else nothing)
    late = VISCOSITY, SOURCE + 2
    lay_out(field for field in range(LINE_FIELDS) if field not in late)

    for q in range(3):

        def put_sums(plane, column, block):
            height, width = block.shape
            sums[q, pl.ds(plane, height), column : column + width] = block

        unfold_inner(table, q, inner_planes, cells_side, put_sums)
    for plane in range(planes):
        x = plane - 2 * margin
        viscosity, source = nothing, nothing
        if 0 <= x < inner:
            part = pl.ds(x * cells_radial, cells_radial)
            cell_sums = [sums[q, part, :] for q in range(3)]
            basalt_share, melt_share, viscosity = composition_of(cell_sums, base[x + margin])
            source = forcing[2, x + margin] - BUOYANCY * basalt_share
            composition_ref[0, x] = basalt_share
            composition_ref[1, x] = melt_share
        put(VISCOSITY, plane, viscosity)
        put(SOURCE + 2, plane, source)
    lay_out(late)
    for offset in range(margin):
        for place, x in ((offset, offset), (margin + offset, cells_lateral - margin + offset)):
            outer_ref[0, place] = base[x]
            outer_ref[1, place] = forcing[2, x]


BLOCK_ROWS = 64
CHUNK_ROWS = 2


def dense_tracers(tracer_values, tracer_cell):
    lane_total = 128
    return tracer_values.reshape(3, 3, -1, lane_total), tracer_cell.reshape(3, -1, lane_total)


def outgoing_sums(tracer_count, values, cells, base_viscosity, velocity, forcing):
    cells_lateral, cells_radial, cells_side = base_viscosity.shape
    moved_planes = MIGRATION_PLANES * cells_radial
    group_rows, lane_total = cells.shape[1:]
    block_rows = min(BLOCK_ROWS, group_rows // 2)
    _, payload_rows = payload_sections(cells_radial)
    hbm = pl.BlockSpec(memory_space=pltpu.HBM)
    vmem = pl.BlockSpec(memory_space=pltpu.VMEM)
    payload = jax.ShapeDtypeStruct((payload_rows, cells_side), jnp.float32)
    outer_planes = (MIGRATION_PLANES, cells_radial, cells_side)
    return pl.pallas_call(
        functools.partial(outgoing_kernel, block_rows),
        out_shape=(
            jax.ShapeDtypeStruct((6 * moved_planes, cells_side), jnp.float32),
            payload,
            payload,
            jax.ShapeDtypeStruct((8, lane_total), jnp.float32),
            jax.ShapeDtypeStruct(values.shape, jnp.float32),
            jax.ShapeDtypeStruct(cells.shape, jnp.int32),
        ),
        in_specs=[hbm] * 6,
        out_specs=(vmem,) * 6,
        scratch_shapes=[
            pltpu.SMEM(tracer_count.shape, jnp.int32),
            pltpu.VMEM((2,) + outer_planes, jnp.float32),
            pltpu.VMEM((2, 3) + outer_planes, jnp.float32),
            pltpu.VMEM((2, 3, 1, cells_radial, cells_side), jnp.float32),
            pltpu.VMEM((2, 4 * moved_planes, cells_side * 3 // 4), jnp.float32),
            pltpu.VMEM((3, 5, block_rows, lane_total), jnp.float32),
            pltpu.SemaphoreType.DMA((13,)),
        ],
        compiler_params=pltpu.CompilerParams(vmem_limit_bytes=32 * 2**20),
        cost_estimate=pl.CostEstimate(
            flops=30 * group_rows * lane_total * moved_planes * cells_side,
            bytes_accessed=4 * (values.size + cells.size),
            transcendentals=0,
        ),
        name="outgoing_sums",
    )(
        *(
            pltpu.with_memory_space_constraint(array, pltpu.HBM)
            for array in (tracer_count, values, cells, base_viscosity, velocity, forcing)
        )
    )


def inner_lines(count, values, cells, base_viscosity, velocity, forcing):
    cells_lateral, cells_radial, cells_side = base_viscosity.shape
    planes = cells_lateral + 2 * MIGRATION_PLANES
    inner = cells_lateral - 2 * MIGRATION_PLANES
    inner_planes = inner * cells_radial
    group_rows, lane_total = cells.shape[1:]
    block_rows = min(BLOCK_ROWS, group_rows // 2)
    vmem = pl.BlockSpec(memory_space=pltpu.VMEM)
    return pl.pallas_call(
        functools.partial(inner_kernel, block_rows),
        out_shape=(
            jax.ShapeDtypeStruct((2, inner, cells_radial, cells_side), jnp.float32),
            jax.ShapeDtypeStruct((LINE_FIELDS, cells_radial, planes, cells_side), jnp.float32),
            jax.ShapeDtypeStruct(
                (2, 2 * MIGRATION_PLANES, cells_radial, cells_side), jnp.float32
            ),
        ),
        in_specs=[vmem] * 3 + [pl.BlockSpec(memory_space=pltpu.HBM)] * 3,
        out_specs=(vmem,) * 3,
        scratch_shapes=[
            pltpu.VMEM((3 * (inner_planes * 5 // 6), cells_side * 5 // 4), jnp.float32),
            pltpu.VMEM((3, inner_planes, cells_side), jnp.float32),
            pltpu.VMEM((LINE_FIELDS, planes * round_up(cells_radial, 8), cells_side), jnp.float32),
            pltpu.VMEM(base_viscosity.shape, jnp.float32),
            pltpu.VMEM(velocity.shape, jnp.float32),
            pltpu.VMEM(forcing.shape, jnp.float32),
            pltpu.VMEM((5, block_rows, lane_total), jnp.float32),
            pltpu.SemaphoreType.DMA((3,)),
        ],
        compiler_params=pltpu.CompilerParams(vmem_limit_bytes=32 * 2**20),
        cost_estimate=pl.CostEstimate(
            flops=6 * group_rows * lane_total * inner * cells_radial * cells_side,
            bytes_accessed=4 * (values.size + cells.size),
            transcendentals=0,
        ),
        name="inner_lines",
    )(
        count,
        values,
        cells,
        *(
            pltpu.with_memory_space_constraint(array, pltpu.HBM)
            for array in (base_viscosity, velocity, forcing)
        ),
    )


def pair_swaps(first, second):
    count = lax.axis_size("lat")
    received = []
    for payload, start in ((second, 1), (first, 0)):
        target = list(range(count))
        for low in range(start, count - 1, 2):
            target[low], target[low + 1] = low + 1, low
        received.append(lax.ppermute(payload, "lat", list(enumerate(target))))
    return received[::-1]


def shift_planes(block, step):
    return pltpu.roll(block, step % block.shape[0], 0)


def shift_side(block, step):
    return pltpu.roll(block, step % block.shape[1], 1)


def neighbours(block):
    return (
        shift_planes(block, 1),
        shift_planes(block, -1),
        shift_side(block, 1),
        shift_side(block, -1),
    )


def inside_side(values):
    lane = lax.broadcasted_iota(jnp.int32, values[2].shape, 1)
    lower = jnp.where(lane > 0, values[2], 0.0)
    upper = jnp.where(lane < lane.shape[1] - 1, values[3], 0.0)
    return values[0], values[1], lower, upper


def total_of(terms):
    result = terms[0]
    for term in terms[1:]:
        result = result + term
    return result


def inside_grid(shape, margin, cells_lateral):
    plane = lax.broadcasted_iota(jnp.int32, shape, 0)
    lateral = lax.axis_index("lat")
    first = jnp.where(lateral == 0, margin, 1)
    last = jnp.where(lateral == lax.axis_size("lat") - 1, margin + cells_lateral, shape[0] - 1)
    return (plane >= first) & (plane < last)


LONG_FIELDS, SHORT_FIELDS = 5, 7


def message_rows(cells_lateral):
    planes = cells_lateral + 2 * MIGRATION_PLANES
    return round_up(LONG_FIELDS * planes + SHORT_FIELDS * cells_lateral + MIGRATION_PLANES, 8)


def message_part(cells_lateral, field):
    planes = cells_lateral + 2 * MIGRATION_PLANES
    if field < LONG_FIELDS:
        return pl.ds(field * planes, planes), 0, planes
    first = LONG_FIELDS * planes + (field - LONG_FIELDS) * cells_lateral
    return pl.ds(first, cells_lateral), MIGRATION_PLANES, cells_lateral


def solve_lines(radial, cells_radial, valid, keep, keep_part):
    last = cells_radial - 1
    viscosity = [radial(VISCOSITY, t) for t in range(cells_radial)]
    lateral_faces, lateral_sums = [], []
    for here in viscosity:
        faces = [LATERAL * 0.5 * (here + there) for there in inside_side(neighbours(here))]
        lateral_sums.append(total_of(faces))
        lateral_faces.append(inside_side(faces))
    radial_faces = [RADIAL * 0.5 * viscosity[0]] + [
        RADIAL * 0.5 * (viscosity[t - 1] + viscosity[t]) for t in range(1, cells_radial)
    ]

    excess = lateral_sums[0] + radial_faces[0]
    inverse, coupling = [], []
    for t in range(last):
        inverse.append(1.0 / (excess + radial_faces[t + 1]))
        coupling.append(radial_faces[t + 1] * inverse[t])
        excess = lateral_sums[t + 1] + coupling[t] * excess

    def lateral_terms(t, around):
        return [face * there for face, there in zip(lateral_faces[t], around)]

    def forward(right_side):
        eliminated = [right_side[0]]
        for t in range(1, cells_radial):
            eliminated.append(right_side[t] + coupling[t - 1] * eliminated[t - 1])
        return eliminated

    def backward(eliminated):
        solved = [jnp.zeros_like(excess)]
        for t in range(last - 1, -1, -1):
            solved.append(eliminated[t] * inverse[t] + coupling[t] * solved[-1])
        return solved[::-1]

    response = [jnp.ones_like(excess)]
    for t in range(last - 1, -1, -1):
        response.append(coupling[t] * response[-1])
    response = response[::-1]

    def finish(part, eliminated):
        keep(LONG_FIELDS + part, eliminated[last])
        for t, value in enumerate(eliminated[:last]):
            keep_part(part, t, value)

    keep(0, viscosity[last])
    keep(1, excess)
    for q in range(3):
        source = [radial(SOURCE + q, t) for t in range(cells_radial)]
        eliminated = forward(
            [
                total_of([source[t]] + lateral_terms(t, neighbours(radial(VELOCITY + q, t))))
                for t in range(cells_radial)
            ]
        )
        keep(2 + q, eliminated[last])
        particular = [jnp.where(valid, value, 0.0) for value in backward(eliminated)]
        finish(
            q,
            forward(
                [
                    total_of([source[t]] + lateral_terms(t, neighbours(particular[t])))
                    for t in range(cells_radial)
                ]
            ),
        )
    around = [neighbours(jnp.where(valid, value, 0.0)) for value in response]
    for side in range(4):
        finish(
            3 + side,
            forward([lateral_faces[t][side] * around[t][side] for t in range(cells_radial)]),
        )
    for t in range(last):
        keep_part(SHORT_FIELDS, t, inverse[t])
        keep_part(SHORT_FIELDS + 1, t, coupling[t])


def eliminate_kernel(
    inner_ref,
    lines_ref,
    edge_ref,
    second_ref,
    first_ref,
    from_second_ref,
    from_first_ref,
    outer_ref,
    composition_ref,
    mine_ref,
    message_ref,
    parts_ref,
    fields,
):
    _, cells_lateral, cells_radial, cells_side = composition_ref.shape
    margin = MIGRATION_PLANES
    planes = cells_lateral + 2 * margin
    pitch = round_up(cells_radial, 8)
    moved_planes = margin * cells_radial
    starts, _ = payload_sections(cells_radial)
    odd = lax.rem(lax.axis_index("lat"), 2) == 1

    def sent(upward, start):
        part = pl.ds(start, cells_radial)
        mine_first = odd if not upward else jnp.logical_not(odd)
        return jnp.where(mine_first, first_ref[part, :], second_ref[part, :])

    def arrived(from_above, start):
        part = pl.ds(start, cells_radial)
        is_first = odd if not from_above else jnp.logical_not(odd)
        return jnp.where(is_first, from_first_ref[part, :], from_second_ref[part, :])

    outer = 2 * margin

    def put(field, slot, value):
        fields[field, pl.ds(slot * pitch, cells_radial), :] = value

    for above in (False, True):
        for offset in range(margin):
            shift = offset * cells_radial
            halo = offset + (outer + margin if above else 0)
            own = offset + (outer if above else margin)
            x = offset + (cells_lateral - margin if above else 0)
            place = offset + (margin if above else 0)
            halo_sums, own_sums = [], []
            for q in range(3):
                row = q * moved_planes + shift
                rows = pl.ds((2 * q + int(above)) * moved_planes + shift, cells_radial)
                own_sums.append(edge_ref[rows, :] + arrived(above, starts[0] + row))
                halo_sums.append(sent(above, starts[0] + row) + arrived(above, starts[1] + row))
                put(VELOCITY + q, halo, arrived(above, starts[2] + row))
            basalt_share, melt_share, viscosity = composition_of(own_sums, outer_ref[0, place])
            composition_ref[0, x] = basalt_share
            composition_ref[1, x] = melt_share
            put(VISCOSITY, own, viscosity)
            put(SOURCE + 2, own, outer_ref[1, place] - BUOYANCY * basalt_share)
            basalt_share, _, viscosity = composition_of(
                halo_sums, arrived(above, starts[3] + shift)
            )
            put(VISCOSITY, halo, viscosity)
            beside = offset == (0 if above else margin - 1)
            for q in range(3):
                source = jnp.zeros_like(viscosity)
                if beside:
                    source = arrived(above, starts[4] + q * cells_radial)
                    if q == 2:
                        source = source - BUOYANCY * basalt_share
                put(SOURCE + q, halo, source)
    for x in range(margin, cells_lateral - margin):
        for q in range(2):
            composition_ref[q, x] = inner_ref[q, x - margin]

    def radial(field, t):
        replaced = outer if field in (VISCOSITY, SOURCE + 2) else margin
        plane = lax.broadcasted_iota(jnp.int32, (planes, cells_side), 0)
        own = (plane >= replaced) & (plane < planes - replaced)
        row = outward_row(t, cells_radial)
        edges = fields[field, pl.ds(row, 2 * outer, stride=pitch), :]
        if 2 * outer * 2 == planes:
            edges = jnp.concatenate([edges, edges], 0)
        else:
            gap = jnp.zeros((planes - 2 * outer, cells_side), jnp.float32)
            edges = jnp.concatenate([edges[:outer], gap, edges[outer:]], 0)
        return jnp.where(own, lines_ref[field, t], edges)

    unused = LONG_FIELDS * planes + SHORT_FIELDS * cells_lateral
    if unused < message_ref.shape[0]:
        message_ref[unused:, :] = jnp.zeros((message_ref.shape[0] - unused, cells_side), jnp.float32)

    def keep(field, value):
        rows, first, count = message_part(cells_lateral, field)
        mine_ref[field] = value
        message_ref[rows, :] = value[first : first + count]

    def keep_part(part, t, value):
        parts_ref[part, t] = value

    valid = inside_grid((planes, cells_side), margin, cells_lateral)
    solve_lines(radial, cells_radial, valid, keep, keep_part)


def eliminate(inner, lines, outer, edge, sent, received, cells_lateral):
    cells_radial, cells_side = inner.shape[2:]
    planes = cells_lateral + 2 * MIGRATION_PLANES
    vmem = pl.BlockSpec(memory_space=pltpu.VMEM)
    line = (planes, cells_side)
    return pl.pallas_call(
        eliminate_kernel,
        out_shape=(
            jax.ShapeDtypeStruct((2, cells_lateral, cells_radial, cells_side), jnp.float32),
            jax.ShapeDtypeStruct((LONG_FIELDS + SHORT_FIELDS,) + line, jnp.float32),
            jax.ShapeDtypeStruct((message_rows(cells_lateral), cells_side), jnp.float32),
            jax.ShapeDtypeStruct((SHORT_FIELDS + 2, cells_radial - 1) + line, jnp.float32),
        ),
        in_specs=[vmem] * 8,
        out_specs=(vmem,) * 4,
        scratch_shapes=[
            pltpu.VMEM(
                (LINE_FIELDS, 4 * MIGRATION_PLANES * round_up(cells_radial, 8), cells_side),
                jnp.float32,
            )
        ],
        compiler_params=pltpu.CompilerParams(vmem_limit_bytes=32 * 2**20),
        name="eliminate",
    )(inner, lines, edge, *sent[::-1], *received[::-1], outer)


def join_kernel(mine_ref, message_ref, parts_ref, smoothed_hbm, smoothed, lines, semaphores):
    _, cells_lateral, cells_radial, cells_side = smoothed.shape
    margin = MIGRATION_PLANES
    planes = cells_lateral + 2 * margin
    pitch = round_up(cells_radial, 8)
    valid = inside_grid((planes, cells_side), margin, cells_lateral)

    def mine(field):
        return mine_ref[field]

    def other(field):
        rows, first, _ = message_part(cells_lateral, field)
        return message_ref[pl.ds(rows.start - first, planes), :]

    face = RADIAL * 0.5 * (mine(0) + other(0))
    excess, other_excess = mine(1), other(1)
    scale = 1.0 / (excess * other_excess + face * (excess + other_excess))
    own_weight = (other_excess + face) * scale
    other_weight = (excess + face) * scale
    cross = face * scale

    def second_right(field_of, q, around):
        terms = [field_of(LONG_FIELDS + 3 + side) * there for side, there in enumerate(around)]
        return total_of([field_of(LONG_FIELDS + q)] + terms)

    fetches = Fetches(semaphores)
    for q in range(3):
        right, other_right = mine(2 + q), other(2 + q)
        own = jnp.where(valid, own_weight * right + cross * other_right, 0.0)
        beyond = jnp.where(valid, other_weight * other_right + cross * right, 0.0)
        around = neighbours(own)
        right = second_right(mine, q, around)
        other_right = second_right(other, q, neighbours(beyond))
        value = own_weight * right + cross * other_right
        for t in range(cells_radial - 1, -1, -1):
            if t < cells_radial - 1:
                terms = [parts_ref[3 + side, t] * there for side, there in enumerate(around)]
                right = total_of([parts_ref[q, t]] + terms)
                value = right * parts_ref[SHORT_FIELDS, t] + parts_ref[SHORT_FIELDS + 1, t] * value
            row = outward_row(t, cells_radial)
            lines[q, pl.ds(row, cells_lateral, stride=pitch), :] = value[
                margin : margin + cells_lateral
            ]
        for x in range(cells_lateral):
            smoothed[q, x] = lines[q, pl.ds(x * pitch, cells_radial), :]
        fetches.start(smoothed.at[q], smoothed_hbm.at[q])
    fetches.wait(0, None)


def join(mine, message, parts, like):
    cells_lateral, cells_radial, cells_side = like.shape[1:]
    vmem = pl.BlockSpec(memory_space=pltpu.VMEM)
    return pl.pallas_call(
        join_kernel,
        out_shape=jax.ShapeDtypeStruct(like.shape, jnp.float32),
        in_specs=[vmem] * 3,
        out_specs=pl.BlockSpec(memory_space=pltpu.HBM),
        scratch_shapes=[
            pltpu.VMEM(like.shape, jnp.float32),
            pltpu.VMEM((3, cells_lateral * round_up(cells_radial, 8), cells_side), jnp.float32),
            pltpu.SemaphoreType.DMA((3,)),
        ],
        compiler_params=pltpu.CompilerParams(vmem_limit_bytes=32 * 2**20),
        name="join",
    )(mine, message, parts)


def extended(block, sides, width):
    for axis, dim in sides:
        count = lax.axis_size(axis)
        forward = [(i, i + 1) for i in range(count - 1)]
        backward = [(target, source) for source, target in forward]
        low = lax.ppermute(
            lax.slice_in_dim(block, block.shape[dim] - width, None, axis=dim), axis, forward
        )
        high = lax.ppermute(lax.slice_in_dim(block, 0, width, axis=dim), axis, backward)
        block = jnp.concatenate([low, block, high], axis=dim)
    return block


def block_factor(diagonal, lower_band, upper_band):
    pivots = []
    upper_scaled = []
    for row_index in range(diagonal.shape[1]):
        if row_index == 0:
            pivot_row = diagonal[:, 0]
        else:
            pivot_row = diagonal[:, row_index] - lower_band[:, row_index] * upper_scaled[-1]
        pivots.append(pivot_row)
        upper_scaled.append(upper_band[:, row_index] / pivot_row)
    return (pivots, upper_scaled)


def block_solve(pivots, upper_scaled, lower_band, right_side):
    row_total = len(pivots)
    modified = []
    for row_index in range(row_total):
        if row_index == 0:
            value_row = right_side[:, :, 0] / pivots[0]
        else:
            value_row = (
                right_side[:, :, row_index] - lower_band[:, row_index] * modified[-1]
            ) / pivots[row_index]
        modified.append(value_row)
    solved = [modified[-1]]
    for row_index in range(row_total - 2, -1, -1):
        solved.append(modified[row_index] - upper_scaled[row_index] * solved[-1])
    ordered = solved[::-1]
    return jnp.stack(ordered, 2)


def interface_solve(coefficients):
    column_total = coefficients.shape[2]

    def forward(carried, inputs):
        offset, carried_slope = carried
        left_first, right_first, left_last, right_last, free_first, free_last = inputs
        divisor = 1.0 - left_first * carried_slope
        first_fixed = (free_first + left_first * offset) / divisor
        first_slope = right_first / divisor
        next_offset = free_last + left_last * (offset + carried_slope * first_fixed)
        next_slope = left_last * carried_slope * first_slope + right_last
        return ((next_offset, next_slope), (first_fixed, first_slope, next_offset, next_slope))

    start_state = (
        jnp.zeros((3, column_total), jnp.float32),
        jnp.zeros((column_total,), jnp.float32),
    )
    scan_inputs = (
        coefficients[:, 0],
        coefficients[:, 1],
        coefficients[:, 2],
        coefficients[:, 3],
        coefficients[:, 4:7],
        coefficients[:, 7:10],
    )
    final_state, eliminated = lax.scan(forward, start_state, scan_inputs)

    def backward(first_next, inputs):
        fixed_first, slope_first, fixed_last, slope_last = inputs
        first_value = fixed_first + slope_first * first_next
        last_value = fixed_last + slope_last * first_next
        return (first_value, (first_value, last_value))

    final_first, values_pair = lax.scan(
        backward, jnp.zeros((3, column_total), jnp.float32), eliminated, reverse=True
    )
    first_values, last_values = values_pair
    nothing_row = jnp.zeros((1, 3, column_total), jnp.float32)
    from_below = jnp.concatenate([nothing_row, last_values[:-1]], 0)
    from_above = jnp.concatenate([first_values[1:], nothing_row], 0)
    return jnp.concatenate([from_below, from_above], 1)


def reduced_boundary(interface):
    gathered = lax.all_gather(interface, "rad", axis=0, tiled=True)
    solved = interface_solve(gathered)
    return lax.dynamic_index_in_dim(solved, lax.axis_index("rad"), 0, keepdims=False)


def many_blocks(values, cells, count, edge, received, base_viscosity, velocity, forcing):
    cells_lateral, cells_radial, cells_side = base_viscosity.shape
    moved_rows = MIGRATION_PLANES * cells_radial
    odd = lax.rem(lax.axis_index("lat"), 2) == 1
    from_below = jnp.where(odd, received[0], received[1])[: 3 * moved_rows]
    from_above = jnp.where(odd, received[1], received[0])[: 3 * moved_rows]
    edge = edge.reshape(3, 2, moved_rows, cells_side)
    below = edge[:, 0] + from_below.reshape(3, moved_rows, cells_side)
    above = edge[:, 1] + from_above.reshape(3, moved_rows, cells_side)
    shares = [
        (sums[1:] / (sums[0] + PRIOR_WEIGHT)).reshape(2, -1, cells_radial, cells_side)
        for sums in (below, above)
    ]
    inner, _, _ = inner_lines(count, values, cells, base_viscosity, velocity, forcing)
    basalt_share, melt_share = jnp.concatenate([shares[0], inner, shares[1]], 1)
    viscosity = base_viscosity * jnp.exp(
        CONTRAST_BASALT * basalt_share - CONTRAST_MELT * melt_share
    )
    viscosity_pad = extended(viscosity, (("lat", 0), ("rad", 1)), 1)
    side_pad = jnp.pad(viscosity, ((0, 0), (0, 0), (1, 1)))
    face_west = LATERAL * 0.5 * (viscosity + viscosity_pad[:-2, 1:-1])
    face_east = LATERAL * 0.5 * (viscosity + viscosity_pad[2:, 1:-1])
    face_south = LATERAL * 0.5 * (viscosity + side_pad[:, :, :-2])
    face_north = LATERAL * 0.5 * (viscosity + side_pad[:, :, 2:])
    face_below = RADIAL * 0.5 * (viscosity + viscosity_pad[1:-1, :-2])
    face_above = RADIAL * 0.5 * (viscosity + viscosity_pad[1:-1, 2:])
    diagonal = face_west + face_east + face_south + face_north + face_below + face_above
    source = jnp.concatenate([forcing[:2], (forcing[2] - BUOYANCY * basalt_share)[None]], 0)
    lower_band = -face_below
    upper_band = -face_above
    pivots, upper_scaled = block_factor(diagonal, lower_band, upper_band)
    radial_iota = lax.broadcasted_iota(jnp.int32, viscosity.shape, 1)
    response_side = jnp.stack(
        [
            jnp.where(radial_iota == 0, face_below, jnp.float32(0.0)),
            jnp.where(radial_iota == cells_radial - 1, face_above, jnp.float32(0.0)),
        ]
    )
    response = block_solve(pivots, upper_scaled, lower_band, response_side)
    current = velocity
    for sweep_index in range(SWEEPS):
        velocity_pad = extended(current, (("lat", 1),), 1)
        side_velocity = jnp.pad(current, ((0, 0), (0, 0), (0, 0), (1, 1)))
        right_side = (
            source
            + face_west * velocity_pad[:, :-2]
            + face_east * velocity_pad[:, 2:]
            + face_south * side_velocity[..., :-2]
            + face_north * side_velocity[..., 2:]
        )
        particular = block_solve(pivots, upper_scaled, lower_band, right_side)
        interface = jnp.concatenate(
            [response[:, :, 0], response[:, :, -1], particular[:, :, 0], particular[:, :, -1]], 0
        )
        interface = interface.reshape(1, 10, cells_lateral * cells_side)
        boundary = reduced_boundary(interface).reshape(6, cells_lateral, 1, cells_side)
        current = particular + response[0][None] * boundary[:3] + response[1][None] * boundary[3:]
    composition = jnp.stack([basalt_share, melt_share])
    return (current, composition)

def local(tracer_values, tracer_cell, tracer_count, base_viscosity, velocity, forcing):
    values, cells = dense_tracers(tracer_values, tracer_cell)
    edge, first, second, count, values, cells = outgoing_sums(
        tracer_count, values, cells, base_viscosity, velocity, forcing
    )
    sent = first, second
    received = pair_swaps(first, second)
    if lax.axis_size("rad") != 2:
        return many_blocks(
            values, cells, count, edge, received, base_viscosity, velocity, forcing
        )
    inner, lines, outer = inner_lines(count, values, cells, base_viscosity, velocity, forcing)
    composition, mine, message, parts = eliminate(
        inner, lines, outer, edge, sent, received, base_viscosity.shape[0]
    )
    other = lax.ppermute(message, "rad", [(0, 1), (1, 0)])
    return join(mine, other, parts, velocity), composition


def solution(mesh):
    return jax.shard_map(
        local,
        mesh=mesh,
        in_specs=(
            P("lat", "rad", None, None),
            P("lat", "rad", None),
            P("lat", "rad", None),
            P("lat", "rad", None),
            P(None, "lat", "rad", None),
            P(None, "lat", "rad", None),
        ),
        out_specs=(P(None, "lat", "rad", None), P(None, "lat", "rad", None)),
        check_vma=False,
    )
```

```python
import functools

import jax
import jax.numpy as jnp
from jax import lax
from jax.experimental import pallas as pl
from jax.experimental.pallas import tpu as pltpu
from jax.sharding import PartitionSpec as P

SWEEPS = 2
MIGRATION_PLANES = 2

LATERAL = 0.015625
RADIAL = 32.0
BUOYANCY = 0.1
PRIOR_WEIGHT = 0.5
CONTRAST_BASALT = 2.3
CONTRAST_MELT = 1.5

TILE_ROWS = 16


def round_up(value, multiple):
    return -(-value // multiple) * multiple


def split_index(index, count):
    if count & (count - 1) == 0:
        return lax.shift_right_logical(index, count.bit_length() - 1), index & (count - 1)
    quotient = lax.div(index, count)
    return quotient, index - quotient * count


def payload_sections(cells_radial):
    pair = MIGRATION_PLANES * cells_radial
    starts = [0, 3 * pair, 6 * pair, 9 * pair, 10 * pair]
    return starts, round_up(10 * pair + 3 * cells_radial, 8)


def spread_row(row):
    return jnp.broadcast_to(row, (TILE_ROWS, row.shape[1])).astype(jnp.bfloat16)


def hot_tiles(index, row_total):
    iota = lax.broadcasted_iota(jnp.int32, index.shape, 0)
    return [
        index == (iota + first).astype(jnp.float32).astype(jnp.bfloat16)
        for first in range(0, row_total, TILE_ROWS)
    ]


def hot_product(sums, loads, high, low, high_rows, low_rows, chunk_rows, upright=False):
    high, low = high.astype(jnp.float32), low.astype(jnp.float32)
    lane_total = high.shape[1]
    zero = jnp.zeros((TILE_ROWS, lane_total), jnp.bfloat16)
    one = jnp.ones((TILE_ROWS, lane_total), jnp.bfloat16)
    if upright:
        turned = jnp.transpose(low)
        square = (lane_total, low_rows)
        number = lax.broadcasted_iota(jnp.int32, square, 1).astype(jnp.float32).astype(jnp.bfloat16)
        full, empty = jnp.ones(square, jnp.bfloat16), jnp.zeros(square, jnp.bfloat16)
    for first_row in range(0, high.shape[0], chunk_rows):
        left, right = [], []
        for row in range(first_row, first_row + chunk_rows):
            pick = slice(row, row + 1)
            high_masks = hot_tiles(spread_row(high[pick]), high_rows)
            spread = [spread_row(load[pick]) for load in loads]
            tiles = [jnp.where(mask, load, zero) for load in spread for mask in high_masks]
            left.append(jnp.concatenate(tiles, 0))
            if upright:
                index = jnp.broadcast_to(turned[:, pick], square).astype(jnp.bfloat16)
                right.append(jnp.where(index == number, full, empty))
            else:
                low_masks = hot_tiles(spread_row(low[pick]), low_rows)
                tiles = [jnp.where(mask, one, zero) for mask in low_masks]
                right.append(jnp.concatenate(tiles, 0))
        sums = sums + lax.dot_general(
            jnp.concatenate(left, 1),
            jnp.concatenate(right, 0 if upright else 1),
            (((1,), (0 if upright else 1,)), ((), ())),
            preferred_element_type=jnp.float32,
        )
    return sums


def edge_row(plane, plane_total, moved_total):
    inner = (plane >= moved_total) & (plane < plane_total - moved_total)
    last = plane - (plane_total - 2 * moved_total)
    return jnp.where(inner, -plane_total, jnp.where(plane < moved_total, plane, last))


def fold_moved(plane, side, plane_total, side_total):
    width, third = side_total // 4, plane_total // 3
    part = jnp.where(plane >= third, 1, 0) + jnp.where(plane >= 2 * third, 1, 0)
    other = side >= 3 * width
    high = jnp.where(other, plane_total + plane - part * third, plane)
    low = jnp.where(other, side - 3 * width + part * width, side)
    return high, low, plane_total + third, 3 * width


def unfold_moved(table, q, plane_total, side_total, put):
    width, third = side_total // 4, plane_total // 3
    rows = plane_total + third
    put(0, 0, table[pl.ds(q * rows, plane_total), 0 : 3 * width])
    for part in range(3):
        block = table[
            pl.ds(q * rows + plane_total, third), part * width : (part + 1) * width
        ]
        put(part * third, 3 * width, block)


def fold_inner(plane, side, plane_total, side_total):
    rows, width = plane_total * 5 // 6, side_total // 4
    part, rest = split_index(side, width)
    other = plane >= rows
    high = jnp.where(other, plane - rows + part * (plane_total - rows), plane)
    high = jnp.where(plane < plane_total, high, -1)
    low = jnp.where(other, side_total + rest, side)
    return high, low, rows, side_total + width


def unfold_inner(table, q, plane_total, side_total, put):
    rows, width = plane_total * 5 // 6, side_total // 4
    left = plane_total - rows
    put(0, 0, table[pl.ds(q * rows, rows), 0:side_total])
    for part in range(4):
        block = table[pl.ds(q * rows + part * left, left), side_total : side_total + width]
        put(rows, part * width, block)


def tracer_block(count, values, cells, group, first_row, block_rows, cells_side):
    rows = pl.ds(first_row, block_rows)
    lane_total = cells.shape[2]
    shape = (block_rows, lane_total)
    slot = (first_row + lax.broadcasted_iota(jnp.int32, shape, 0)) * lane_total
    slot = slot + lax.broadcasted_iota(jnp.int32, shape, 1)
    weight = jnp.where(slot < count, 0.5 + values[0, group, rows, :], jnp.float32(0.0))
    loads = [weight, weight * values[1, group, rows, :], weight * values[2, group, rows, :]]
    plane, side = split_index(cells[group, rows, :], cells_side)
    return loads, plane, side


def for_used_blocks(used, group_rows, block_rows, lane_total, late_copies, step):
    block_slots = block_rows * lane_total
    blocks = lax.div(used + (block_slots - 1), block_slots)
    blocks = jnp.clip(blocks, 1, group_rows // block_rows)

    def wait_late():
        for copy in late_copies:
            copy.wait()

    def repeat(index, carried):
        pl.when(index == 1)(wait_late)
        step(pl.multiple_of(index * block_rows, block_rows))
        return carried

    lax.fori_loop(0, blocks, repeat, 0)
    pl.when(blocks == 1)(wait_late)


VISCOSITY, VELOCITY, SOURCE, LINE_FIELDS = 0, 1, 4, 7


def composition_of(cell_sums, base):
    scale = 1.0 / (cell_sums[0] + PRIOR_WEIGHT)
    basalt_share, melt_share = cell_sums[1] * scale, cell_sums[2] * scale
    weakening = jnp.exp(CONTRAST_BASALT * basalt_share - CONTRAST_MELT * melt_share)
    return basalt_share, melt_share, base * weakening


def outward_row(t, cells_radial):
    return jnp.where(lax.axis_index("rad") == 0, t, cells_radial - 1 - t)


class Fetches:
    def __init__(self, semaphores):
        self.semaphores = semaphores
        self.copies = []

    def start(self, source, target):
        copy = pltpu.make_async_copy(source, target, self.semaphores.at[len(self.copies)])
        copy.start()
        self.copies.append(copy)

    def wait(self, first, last):
        for copy in self.copies[first:last]:
            copy.wait()


def has_partners():
    lateral, count = lax.axis_index("lat"), lax.axis_size("lat")
    odd = lax.rem(lateral, 2) == 1
    above, below = lateral + 1 < count, lateral > 0
    return jnp.logical_or(odd, above), jnp.where(odd, above, below)


def outgoing_kernel(
    block_rows,
    counts_hbm,
    values_hbm,
    cells_hbm,
    base_hbm,
    velocity_hbm,
    forcing_hbm,
    edge_ref,
    first_ref,
    second_ref,
    count_ref,
    values,
    cells,
    counts,
    base,
    velocity,
    forcing,
    moved_sums,
    semaphores,
):
    cells_lateral, cells_radial, cells_side = base_hbm.shape
    plane_total = cells_lateral * cells_radial
    moved_planes = MIGRATION_PLANES * cells_radial
    group_rows, lane_total = cells.shape[1:]

    fetches = Fetches(semaphores)
    fetches.start(counts_hbm, counts)
    part = pl.ds(0, block_rows)
    fetches.start(cells_hbm.at[:, part], cells.at[:, part])
    for q in range(3):
        fetches.start(values_hbm.at[q, :, part], values.at[q, :, part])
    part = pl.ds(block_rows, group_rows - block_rows)
    fetches.start(cells_hbm.at[:, part], cells.at[:, part])
    fetches.start(values_hbm.at[:, :, part], values.at[:, :, part])
    for upward in (0, 1):
        outer = pl.ds((cells_lateral - MIGRATION_PLANES) * upward, MIGRATION_PLANES)
        fetches.start(base_hbm.at[outer], base.at[upward])
        fetches.start(velocity_hbm.at[:, outer], velocity.at[upward])
        outermost = pl.ds((cells_lateral - 1) * upward, 1)
        fetches.start(forcing_hbm.at[:, outermost], forcing.at[upward])

    edge_ref[...] = jnp.zeros_like(edge_ref)
    moved_sums[...] = jnp.zeros_like(moved_sums)

    def step(first_row):
        def block_of(group):
            count = counts[0, 0, group]
            return tracer_block(count, values, cells, group, first_row, block_rows, cells_side)

        loads, plane, side = block_of(1)
        row = edge_row(plane, plane_total, moved_planes)
        edge_ref[...] = hot_product(
            edge_ref[...], loads, row, side, 2 * moved_planes, cells_side, CHUNK_ROWS, upright=True
        )
        for slot, group in enumerate((0, 2)):
            loads, plane, side = block_of(group)
            if group == 0:
                plane = plane - (plane_total - moved_planes)
            table = fold_moved(plane, side, moved_planes, cells_side)
            moved_sums[slot] = hot_product(moved_sums[slot], loads, *table, CHUNK_ROWS)

    fetches.wait(0, 5)
    count_ref[...] = jnp.full(count_ref.shape, counts[0, 0, 1], jnp.int32).astype(jnp.float32)
    used = jnp.maximum(jnp.maximum(counts[0, 0, 0], counts[0, 0, 1]), counts[0, 0, 2])
    for_used_blocks(used, group_rows, block_rows, lane_total, fetches.copies[5:7], step)
    fetches.wait(7, None)

    starts, rows_total = payload_sections(cells_radial)
    unused = starts[4] + 3 * cells_radial

    def fill(payload, upward):
        for q in range(3):

            def put_moved(plane, column, block):
                height, width = block.shape
                rows = pl.ds(starts[0] + q * moved_planes + plane, height)
                payload[rows, column : column + width] = block

            unfold_moved(moved_sums.at[upward], q, moved_planes, cells_side, put_moved)
            payload[pl.ds(starts[1] + q * moved_planes, moved_planes), :] = edge_ref[
                pl.ds((2 * q + upward) * moved_planes, moved_planes), :
            ]
            for offset in range(MIGRATION_PLANES):
                row = starts[2] + q * moved_planes + offset * cells_radial
                payload[pl.ds(row, cells_radial), :] = velocity[upward, q, offset]
            row = starts[4] + q * cells_radial
            payload[pl.ds(row, cells_radial), :] = forcing[upward, q, 0]
        for offset in range(MIGRATION_PLANES):
            row = starts[3] + offset * cells_radial
            payload[pl.ds(row, cells_radial), :] = base[upward, offset]
        if unused < rows_total:
            payload[unused:, :] = jnp.zeros((rows_total - unused, cells_side), jnp.float32)

    odd = lax.rem(lax.axis_index("lat"), 2) == 1

    @pl.when(odd)
    def _():
        fill(first_ref, 0)
        fill(second_ref, 1)

    @pl.when(jnp.logical_not(odd))
    def _():
        fill(first_ref, 1)
        fill(second_ref, 0)

    for payload, exists in zip((first_ref, second_ref), has_partners()):

        @pl.when(jnp.logical_not(exists))
        def _():
            payload[...] = jnp.zeros_like(payload)


def inner_kernel(
    block_rows,
    count_ref,
    values_ref,
    cells_ref,
    base_hbm,
    velocity_hbm,
    forcing_hbm,
    composition_ref,
    lines_ref,
    outer_ref,
    table,
    sums,
    fields,
    base,
    velocity,
    forcing,
    semaphores,
):
    cells_lateral, cells_radial, cells_side = base.shape
    margin = MIGRATION_PLANES
    planes = cells_lateral + 2 * margin
    pitch = round_up(cells_radial, 8)
    moved_planes = margin * cells_radial
    inner = cells_lateral - 2 * margin
    inner_planes = inner * cells_radial
    group_rows, lane_total = cells_ref.shape[1:]
    fetches = Fetches(semaphores)
    fetches.start(velocity_hbm, velocity)
    fetches.start(forcing_hbm, forcing)
    fetches.start(base_hbm, base)
    table[...] = jnp.zeros_like(table)

    nothing = jnp.zeros((cells_radial, cells_side), jnp.float32)

    def put(field, plane, value):
        fields[field, pl.ds(plane * pitch, cells_radial), :] = value

    def lay_out(those):
        for field in those:
            for t in range(cells_radial):
                row = outward_row(t, cells_radial)
                lines_ref[field, t] = fields[field, pl.ds(row, planes, stride=pitch), :]

    def step(first_row):
        loads, plane, side = tracer_block(
            count, values_ref, cells_ref, 1, first_row, block_rows, cells_side
        )
        where = fold_inner(plane - moved_planes, side, inner_planes, cells_side)
        table[...] = hot_product(table[...], loads, *where, block_rows)

    count = jnp.max(count_ref[...]).astype(jnp.int32)
    for_used_blocks(count, group_rows, block_rows, lane_total, [], step)

    fetches.wait(0, None)
    for plane in range(planes):
        x = plane - margin
        own = 0 <= x < cells_lateral
        for q in range(3):
            put(VELOCITY + q, plane, velocity[q, x] if own else nothing)
        for q in range(2):
            put(SOURCE + q, plane, forcing[q, x] if own else nothing)
    late = VISCOSITY, SOURCE + 2
    lay_out(field for field in range(LINE_FIELDS) if field not in late)

    for q in range(3):

        def put_sums(plane, column, block):
            height, width = block.shape
            sums[q, pl.ds(plane, height), column : column + width] = block

        unfold_inner(table, q, inner_planes, cells_side, put_sums)
    for plane in range(planes):
        x = plane - 2 * margin
        viscosity, source = nothing, nothing
        if 0 <= x < inner:
            part = pl.ds(x * cells_radial, cells_radial)
            cell_sums = [sums[q, part, :] for q in range(3)]
            basalt_share, melt_share, viscosity = composition_of(cell_sums, base[x + margin])
            source = forcing[2, x + margin] - BUOYANCY * basalt_share
            composition_ref[0, x] = basalt_share
            composition_ref[1, x] = melt_share
        put(VISCOSITY, plane, viscosity)
        put(SOURCE + 2, plane, source)
    lay_out(late)
    for offset in range(margin):
        for place, x in ((offset, offset), (margin + offset, cells_lateral - margin + offset)):
            outer_ref[0, place] = base[x]
            outer_ref[1, place] = forcing[2, x]


BLOCK_ROWS = 64
CHUNK_ROWS = 2


def dense_tracers(tracer_values, tracer_cell):
    lane_total = 128
    return tracer_values.reshape(3, 3, -1, lane_total), tracer_cell.reshape(3, -1, lane_total)


def outgoing_sums(tracer_count, values, cells, base_viscosity, velocity, forcing):
    cells_lateral, cells_radial, cells_side = base_viscosity.shape
    moved_planes = MIGRATION_PLANES * cells_radial
    group_rows, lane_total = cells.shape[1:]
    block_rows = min(BLOCK_ROWS, group_rows // 2)
    _, payload_rows = payload_sections(cells_radial)
    hbm = pl.BlockSpec(memory_space=pltpu.HBM)
    vmem = pl.BlockSpec(memory_space=pltpu.VMEM)
    payload = jax.ShapeDtypeStruct((payload_rows, cells_side), jnp.float32)
    outer_planes = (MIGRATION_PLANES, cells_radial, cells_side)
    return pl.pallas_call(
        functools.partial(outgoing_kernel, block_rows),
        out_shape=(
            jax.ShapeDtypeStruct((6 * moved_planes, cells_side), jnp.float32),
            payload,
            payload,
            jax.ShapeDtypeStruct((8, lane_total), jnp.float32),
            jax.ShapeDtypeStruct(values.shape, jnp.float32),
            jax.ShapeDtypeStruct(cells.shape, jnp.int32),
        ),
        in_specs=[hbm] * 6,
        out_specs=(vmem,) * 6,
        scratch_shapes=[
            pltpu.SMEM(tracer_count.shape, jnp.int32),
            pltpu.VMEM((2,) + outer_planes, jnp.float32),
            pltpu.VMEM((2, 3) + outer_planes, jnp.float32),
            pltpu.VMEM((2, 3, 1, cells_radial, cells_side), jnp.float32),
            pltpu.VMEM((2, 4 * moved_planes, cells_side * 3 // 4), jnp.float32),
            pltpu.SemaphoreType.DMA((13,)),
        ],
        compiler_params=pltpu.CompilerParams(vmem_limit_bytes=32 * 2**20),
        cost_estimate=pl.CostEstimate(
            flops=30 * group_rows * lane_total * moved_planes * cells_side,
            bytes_accessed=4 * (values.size + cells.size),
            transcendentals=0,
        ),
        name="outgoing_sums",
    )(
        *(
            pltpu.with_memory_space_constraint(array, pltpu.HBM)
            for array in (tracer_count, values, cells, base_viscosity, velocity, forcing)
        )
    )


def inner_lines(count, values, cells, base_viscosity, velocity, forcing):
    cells_lateral, cells_radial, cells_side = base_viscosity.shape
    planes = cells_lateral + 2 * MIGRATION_PLANES
    inner = cells_lateral - 2 * MIGRATION_PLANES
    inner_planes = inner * cells_radial
    group_rows, lane_total = cells.shape[1:]
    block_rows = min(BLOCK_ROWS, group_rows // 2)
    vmem = pl.BlockSpec(memory_space=pltpu.VMEM)
    return pl.pallas_call(
        functools.partial(inner_kernel, block_rows),
        out_shape=(
            jax.ShapeDtypeStruct((2, inner, cells_radial, cells_side), jnp.float32),
            jax.ShapeDtypeStruct((LINE_FIELDS, cells_radial, planes, cells_side), jnp.float32),
            jax.ShapeDtypeStruct(
                (2, 2 * MIGRATION_PLANES, cells_radial, cells_side), jnp.float32
            ),
        ),
        in_specs=[vmem] * 3 + [pl.BlockSpec(memory_space=pltpu.HBM)] * 3,
        out_specs=(vmem,) * 3,
        scratch_shapes=[
            pltpu.VMEM((3 * (inner_planes * 5 // 6), cells_side * 5 // 4), jnp.float32),
            pltpu.VMEM((3, inner_planes, cells_side), jnp.float32),
            pltpu.VMEM((LINE_FIELDS, planes * round_up(cells_radial, 8), cells_side), jnp.float32),
            pltpu.VMEM(base_viscosity.shape, jnp.float32),
            pltpu.VMEM(velocity.shape, jnp.float32),
            pltpu.VMEM(forcing.shape, jnp.float32),
            pltpu.SemaphoreType.DMA((3,)),
        ],
        compiler_params=pltpu.CompilerParams(vmem_limit_bytes=32 * 2**20),
        cost_estimate=pl.CostEstimate(
            flops=6 * group_rows * lane_total * inner * cells_radial * cells_side,
            bytes_accessed=4 * (values.size + cells.size),
            transcendentals=0,
        ),
        name="inner_lines",
    )(
        count,
        values,
        cells,
        *(
            pltpu.with_memory_space_constraint(array, pltpu.HBM)
            for array in (base_viscosity, velocity, forcing)
        ),
    )


def pair_swaps(first, second):
    count = lax.axis_size("lat")
    received = []
    for payload, start in ((second, 1), (first, 0)):
        target = list(range(count))
        for low in range(start, count - 1, 2):
            target[low], target[low + 1] = low + 1, low
        received.append(lax.ppermute(payload, "lat", list(enumerate(target))))
    return received[::-1]


def shift_planes(block, step):
    return pltpu.roll(block, step % block.shape[0], 0)


def shift_side(block, step):
    return pltpu.roll(block, step % block.shape[1], 1)


def neighbours(block):
    return (
        shift_planes(block, 1),
        shift_planes(block, -1),
        shift_side(block, 1),
        shift_side(block, -1),
    )


def inside_side(values):
    lane = lax.broadcasted_iota(jnp.int32, values[2].shape, 1)
    lower = jnp.where(lane > 0, values[2], 0.0)
    upper = jnp.where(lane < lane.shape[1] - 1, values[3], 0.0)
    return values[0], values[1], lower, upper


def total_of(terms):
    result = terms[0]
    for term in terms[1:]:
        result = result + term
    return result


def inside_grid(shape, margin, cells_lateral):
    plane = lax.broadcasted_iota(jnp.int32, shape, 0)
    lateral = lax.axis_index("lat")
    first = jnp.where(lateral == 0, margin, 1)
    last = jnp.where(lateral == lax.axis_size("lat") - 1, margin + cells_lateral, shape[0] - 1)
    return (plane >= first) & (plane < last)


LONG_FIELDS, SHORT_FIELDS = 5, 7


def message_rows(cells_lateral):
    planes = cells_lateral + 2 * MIGRATION_PLANES
    return round_up(LONG_FIELDS * planes + SHORT_FIELDS * cells_lateral + MIGRATION_PLANES, 8)


def message_part(cells_lateral, field):
    planes = cells_lateral + 2 * MIGRATION_PLANES
    if field < LONG_FIELDS:
        return pl.ds(field * planes, planes), 0, planes
    first = LONG_FIELDS * planes + (field - LONG_FIELDS) * cells_lateral
    return pl.ds(first, cells_lateral), MIGRATION_PLANES, cells_lateral


def solve_lines(radial, cells_radial, valid, keep, keep_part):
    last = cells_radial - 1
    viscosity = [radial(VISCOSITY, t) for t in range(cells_radial)]
    lateral_faces, lateral_sums = [], []
    for here in viscosity:
        faces = [LATERAL * 0.5 * (here + there) for there in inside_side(neighbours(here))]
        lateral_sums.append(total_of(faces))
        lateral_faces.append(inside_side(faces))
    radial_faces = [RADIAL * 0.5 * viscosity[0]] + [
        RADIAL * 0.5 * (viscosity[t - 1] + viscosity[t]) for t in range(1, cells_radial)
    ]

    excess = lateral_sums[0] + radial_faces[0]
    inverse, coupling = [], []
    for t in range(last):
        inverse.append(1.0 / (excess + radial_faces[t + 1]))
        coupling.append(radial_faces[t + 1] * inverse[t])
        excess = lateral_sums[t + 1] + coupling[t] * excess

    def lateral_terms(t, around):
        return [face * there for face, there in zip(lateral_faces[t], around)]

    def forward(right_side):
        eliminated = [right_side[0]]
        for t in range(1, cells_radial):
            eliminated.append(right_side[t] + coupling[t - 1] * eliminated[t - 1])
        return eliminated

    def backward(eliminated):
        solved = [jnp.zeros_like(excess)]
        for t in range(last - 1, -1, -1):
            solved.append(eliminated[t] * inverse[t] + coupling[t] * solved[-1])
        return solved[::-1]

    response = [jnp.ones_like(excess)]
    for t in range(last - 1, -1, -1):
        response.append(coupling[t] * response[-1])
    response = response[::-1]

    def finish(part, eliminated):
        keep(LONG_FIELDS + part, eliminated[last])
        for t, value in enumerate(eliminated[:last]):
            keep_part(part, t, value)

    keep(0, viscosity[last])
    keep(1, excess)
    for q in range(3):
        source = [radial(SOURCE + q, t) for t in range(cells_radial)]
        eliminated = forward(
            [
                total_of([source[t]] + lateral_terms(t, neighbours(radial(VELOCITY + q, t))))
                for t in range(cells_radial)
            ]
        )
        keep(2 + q, eliminated[last])
        particular = [jnp.where(valid, value, 0.0) for value in backward(eliminated)]
        finish(
            q,
            forward(
                [
                    total_of([source[t]] + lateral_terms(t, neighbours(particular[t])))
                    for t in range(cells_radial)
                ]
            ),
        )
    around = [neighbours(jnp.where(valid, value, 0.0)) for value in response]
    for side in range(4):
        finish(
            3 + side,
            forward([lateral_faces[t][side] * around[t][side] for t in range(cells_radial)]),
        )
    for t in range(last):
        keep_part(SHORT_FIELDS, t, inverse[t])
        keep_part(SHORT_FIELDS + 1, t, coupling[t])


def eliminate_kernel(
    inner_ref,
    lines_ref,
    edge_ref,
    second_ref,
    first_ref,
    from_second_ref,
    from_first_ref,
    outer_ref,
    composition_ref,
    mine_ref,
    message_ref,
    parts_ref,
    fields,
):
    _, cells_lateral, cells_radial, cells_side = composition_ref.shape
    margin = MIGRATION_PLANES
    planes = cells_lateral + 2 * margin
    pitch = round_up(cells_radial, 8)
    moved_planes = margin * cells_radial
    starts, _ = payload_sections(cells_radial)
    odd = lax.rem(lax.axis_index("lat"), 2) == 1

    def sent(upward, start):
        part = pl.ds(start, cells_radial)
        mine_first = odd if not upward else jnp.logical_not(odd)
        return jnp.where(mine_first, first_ref[part, :], second_ref[part, :])

    def arrived(from_above, start):
        part = pl.ds(start, cells_radial)
        is_first = odd if not from_above else jnp.logical_not(odd)
        return jnp.where(is_first, from_first_ref[part, :], from_second_ref[part, :])

    outer = 2 * margin

    def put(field, slot, value):
        fields[field, pl.ds(slot * pitch, cells_radial), :] = value

    for above in (False, True):
        for offset in range(margin):
            shift = offset * cells_radial
            halo = offset + (outer + margin if above else 0)
            own = offset + (outer if above else margin)
            x = offset + (cells_lateral - margin if above else 0)
            place = offset + (margin if above else 0)
            halo_sums, own_sums = [], []
            for q in range(3):
                row = q * moved_planes + shift
                rows = pl.ds((2 * q + int(above)) * moved_planes + shift, cells_radial)
                own_sums.append(edge_ref[rows, :] + arrived(above, starts[0] + row))
                halo_sums.append(sent(above, starts[0] + row) + arrived(above, starts[1] + row))
                put(VELOCITY + q, halo, arrived(above, starts[2] + row))
            basalt_share, melt_share, viscosity = composition_of(own_sums, outer_ref[0, place])
            composition_ref[0, x] = basalt_share
            composition_ref[1, x] = melt_share
            put(VISCOSITY, own, viscosity)
            put(SOURCE + 2, own, outer_ref[1, place] - BUOYANCY * basalt_share)
            basalt_share, _, viscosity = composition_of(
                halo_sums, arrived(above, starts[3] + shift)
            )
            put(VISCOSITY, halo, viscosity)
            beside = offset == (0 if above else margin - 1)
            for q in range(3):
                source = jnp.zeros_like(viscosity)
                if beside:
                    source = arrived(above, starts[4] + q * cells_radial)
                    if q == 2:
                        source = source - BUOYANCY * basalt_share
                put(SOURCE + q, halo, source)
    for x in range(margin, cells_lateral - margin):
        for q in range(2):
            composition_ref[q, x] = inner_ref[q, x - margin]

    def radial(field, t):
        replaced = outer if field in (VISCOSITY, SOURCE + 2) else margin
        plane = lax.broadcasted_iota(jnp.int32, (planes, cells_side), 0)
        own = (plane >= replaced) & (plane < planes - replaced)
        row = outward_row(t, cells_radial)
        edges = fields[field, pl.ds(row, 2 * outer, stride=pitch), :]
        if 2 * outer * 2 == planes:
            edges = jnp.concatenate([edges, edges], 0)
        else:
            gap = jnp.zeros((planes - 2 * outer, cells_side), jnp.float32)
            edges = jnp.concatenate([edges[:outer], gap, edges[outer:]], 0)
        return jnp.where(own, lines_ref[field, t], edges)

    unused = LONG_FIELDS * planes + SHORT_FIELDS * cells_lateral
    if unused < message_ref.shape[0]:
        message_ref[unused:, :] = jnp.zeros((message_ref.shape[0] - unused, cells_side), jnp.float32)

    def keep(field, value):
        rows, first, count = message_part(cells_lateral, field)
        mine_ref[field] = value
        message_ref[rows, :] = value[first : first + count]

    def keep_part(part, t, value):
        parts_ref[part, t] = value

    valid = inside_grid((planes, cells_side), margin, cells_lateral)
    solve_lines(radial, cells_radial, valid, keep, keep_part)


def eliminate(inner, lines, outer, edge, sent, received, cells_lateral):
    cells_radial, cells_side = inner.shape[2:]
    planes = cells_lateral + 2 * MIGRATION_PLANES
    vmem = pl.BlockSpec(memory_space=pltpu.VMEM)
    line = (planes, cells_side)
    return pl.pallas_call(
        eliminate_kernel,
        out_shape=(
            jax.ShapeDtypeStruct((2, cells_lateral, cells_radial, cells_side), jnp.float32),
            jax.ShapeDtypeStruct((LONG_FIELDS + SHORT_FIELDS,) + line, jnp.float32),
            jax.ShapeDtypeStruct((message_rows(cells_lateral), cells_side), jnp.float32),
            jax.ShapeDtypeStruct((SHORT_FIELDS + 2, cells_radial - 1) + line, jnp.float32),
        ),
        in_specs=[vmem] * 8,
        out_specs=(vmem,) * 4,
        scratch_shapes=[
            pltpu.VMEM(
                (LINE_FIELDS, 4 * MIGRATION_PLANES * round_up(cells_radial, 8), cells_side),
                jnp.float32,
            )
        ],
        compiler_params=pltpu.CompilerParams(vmem_limit_bytes=32 * 2**20),
        name="eliminate",
    )(inner, lines, edge, *sent[::-1], *received[::-1], outer)


def join_kernel(mine_ref, message_ref, parts_ref, smoothed_hbm, smoothed, lines, semaphores):
    _, cells_lateral, cells_radial, cells_side = smoothed.shape
    margin = MIGRATION_PLANES
    planes = cells_lateral + 2 * margin
    pitch = round_up(cells_radial, 8)
    valid = inside_grid((planes, cells_side), margin, cells_lateral)

    def mine(field):
        return mine_ref[field]

    def other(field):
        rows, first, _ = message_part(cells_lateral, field)
        return message_ref[pl.ds(rows.start - first, planes), :]

    face = RADIAL * 0.5 * (mine(0) + other(0))
    excess, other_excess = mine(1), other(1)
    scale = 1.0 / (excess * other_excess + face * (excess + other_excess))
    own_weight = (other_excess + face) * scale
    other_weight = (excess + face) * scale
    cross = face * scale

    def second_right(field_of, q, around):
        terms = [field_of(LONG_FIELDS + 3 + side) * there for side, there in enumerate(around)]
        return total_of([field_of(LONG_FIELDS + q)] + terms)

    fetches = Fetches(semaphores)
    for q in range(3):
        right, other_right = mine(2 + q), other(2 + q)
        own = jnp.where(valid, own_weight * right + cross * other_right, 0.0)
        beyond = jnp.where(valid, other_weight * other_right + cross * right, 0.0)
        around = neighbours(own)
        right = second_right(mine, q, around)
        other_right = second_right(other, q, neighbours(beyond))
        value = own_weight * right + cross * other_right
        for t in range(cells_radial - 1, -1, -1):
            if t < cells_radial - 1:
                terms = [parts_ref[3 + side, t] * there for side, there in enumerate(around)]
                right = total_of([parts_ref[q, t]] + terms)
                value = right * parts_ref[SHORT_FIELDS, t] + parts_ref[SHORT_FIELDS + 1, t] * value
            row = outward_row(t, cells_radial)
            lines[q, pl.ds(row, cells_lateral, stride=pitch), :] = value[
                margin : margin + cells_lateral
            ]
        for x in range(cells_lateral):
            smoothed[q, x] = lines[q, pl.ds(x * pitch, cells_radial), :]
        fetches.start(smoothed.at[q], smoothed_hbm.at[q])
    fetches.wait(0, None)


def join(mine, message, parts, like):
    cells_lateral, cells_radial, cells_side = like.shape[1:]
    vmem = pl.BlockSpec(memory_space=pltpu.VMEM)
    return pl.pallas_call(
        join_kernel,
        out_shape=jax.ShapeDtypeStruct(like.shape, jnp.float32),
        in_specs=[vmem] * 3,
        out_specs=pl.BlockSpec(memory_space=pltpu.HBM),
        scratch_shapes=[
            pltpu.VMEM(like.shape, jnp.float32),
            pltpu.VMEM((3, cells_lateral * round_up(cells_radial, 8), cells_side), jnp.float32),
            pltpu.SemaphoreType.DMA((3,)),
        ],
        compiler_params=pltpu.CompilerParams(vmem_limit_bytes=32 * 2**20),
        name="join",
    )(mine, message, parts)


def extended(block, sides, width):
    for axis, dim in sides:
        count = lax.axis_size(axis)
        forward = [(i, i + 1) for i in range(count - 1)]
        backward = [(target, source) for source, target in forward]
        low = lax.ppermute(
            lax.slice_in_dim(block, block.shape[dim] - width, None, axis=dim), axis, forward
        )
        high = lax.ppermute(lax.slice_in_dim(block, 0, width, axis=dim), axis, backward)
        block = jnp.concatenate([low, block, high], axis=dim)
    return block


def block_factor(diagonal, lower_band, upper_band):
    pivots = []
    upper_scaled = []
    for row_index in range(diagonal.shape[1]):
        if row_index == 0:
            pivot_row = diagonal[:, 0]
        else:
            pivot_row = diagonal[:, row_index] - lower_band[:, row_index] * upper_scaled[-1]
        pivots.append(pivot_row)
        upper_scaled.append(upper_band[:, row_index] / pivot_row)
    return (pivots, upper_scaled)


def block_solve(pivots, upper_scaled, lower_band, right_side):
    row_total = len(pivots)
    modified = []
    for row_index in range(row_total):
        if row_index == 0:
            value_row = right_side[:, :, 0] / pivots[0]
        else:
            value_row = (
                right_side[:, :, row_index] - lower_band[:, row_index] * modified[-1]
            ) / pivots[row_index]
        modified.append(value_row)
    solved = [modified[-1]]
    for row_index in range(row_total - 2, -1, -1):
        solved.append(modified[row_index] - upper_scaled[row_index] * solved[-1])
    ordered = solved[::-1]
    return jnp.stack(ordered, 2)


def interface_solve(coefficients):
    column_total = coefficients.shape[2]

    def forward(carried, inputs):
        offset, carried_slope = carried
        left_first, right_first, left_last, right_last, free_first, free_last = inputs
        divisor = 1.0 - left_first * carried_slope
        first_fixed = (free_first + left_first * offset) / divisor
        first_slope = right_first / divisor
        next_offset = free_last + left_last * (offset + carried_slope * first_fixed)
        next_slope = left_last * carried_slope * first_slope + right_last
        return ((next_offset, next_slope), (first_fixed, first_slope, next_offset, next_slope))

    start_state = (
        jnp.zeros((3, column_total), jnp.float32),
        jnp.zeros((column_total,), jnp.float32),
    )
    scan_inputs = (
        coefficients[:, 0],
        coefficients[:, 1],
        coefficients[:, 2],
        coefficients[:, 3],
        coefficients[:, 4:7],
        coefficients[:, 7:10],
    )
    final_state, eliminated = lax.scan(forward, start_state, scan_inputs)

    def backward(first_next, inputs):
        fixed_first, slope_first, fixed_last, slope_last = inputs
        first_value = fixed_first + slope_first * first_next
        last_value = fixed_last + slope_last * first_next
        return (first_value, (first_value, last_value))

    final_first, values_pair = lax.scan(
        backward, jnp.zeros((3, column_total), jnp.float32), eliminated, reverse=True
    )
    first_values, last_values = values_pair
    nothing_row = jnp.zeros((1, 3, column_total), jnp.float32)
    from_below = jnp.concatenate([nothing_row, last_values[:-1]], 0)
    from_above = jnp.concatenate([first_values[1:], nothing_row], 0)
    return jnp.concatenate([from_below, from_above], 1)


def reduced_boundary(interface):
    gathered = lax.all_gather(interface, "rad", axis=0, tiled=True)
    solved = interface_solve(gathered)
    return lax.dynamic_index_in_dim(solved, lax.axis_index("rad"), 0, keepdims=False)


def many_blocks(values, cells, count, edge, received, base_viscosity, velocity, forcing):
    cells_lateral, cells_radial, cells_side = base_viscosity.shape
    moved_rows = MIGRATION_PLANES * cells_radial
    odd = lax.rem(lax.axis_index("lat"), 2) == 1
    from_below = jnp.where(odd, received[0], received[1])[: 3 * moved_rows]
    from_above = jnp.where(odd, received[1], received[0])[: 3 * moved_rows]
    edge = edge.reshape(3, 2, moved_rows, cells_side)
    below = edge[:, 0] + from_below.reshape(3, moved_rows, cells_side)
    above = edge[:, 1] + from_above.reshape(3, moved_rows, cells_side)
    shares = [
        (sums[1:] / (sums[0] + PRIOR_WEIGHT)).reshape(2, -1, cells_radial, cells_side)
        for sums in (below, above)
    ]
    inner, _, _ = inner_lines(count, values, cells, base_viscosity, velocity, forcing)
    basalt_share, melt_share = jnp.concatenate([shares[0], inner, shares[1]], 1)
    viscosity = base_viscosity * jnp.exp(
        CONTRAST_BASALT * basalt_share - CONTRAST_MELT * melt_share
    )
    viscosity_pad = extended(viscosity, (("lat", 0), ("rad", 1)), 1)
    side_pad = jnp.pad(viscosity, ((0, 0), (0, 0), (1, 1)))
    face_west = LATERAL * 0.5 * (viscosity + viscosity_pad[:-2, 1:-1])
    face_east = LATERAL * 0.5 * (viscosity + viscosity_pad[2:, 1:-1])
    face_south = LATERAL * 0.5 * (viscosity + side_pad[:, :, :-2])
    face_north = LATERAL * 0.5 * (viscosity + side_pad[:, :, 2:])
    face_below = RADIAL * 0.5 * (viscosity + viscosity_pad[1:-1, :-2])
    face_above = RADIAL * 0.5 * (viscosity + viscosity_pad[1:-1, 2:])
    diagonal = face_west + face_east + face_south + face_north + face_below + face_above
    source = jnp.concatenate([forcing[:2], (forcing[2] - BUOYANCY * basalt_share)[None]], 0)
    lower_band = -face_below
    upper_band = -face_above
    pivots, upper_scaled = block_factor(diagonal, lower_band, upper_band)
    radial_iota = lax.broadcasted_iota(jnp.int32, viscosity.shape, 1)
    response_side = jnp.stack(
        [
            jnp.where(radial_iota == 0, face_below, jnp.float32(0.0)),
            jnp.where(radial_iota == cells_radial - 1, face_above, jnp.float32(0.0)),
        ]
    )
    response = block_solve(pivots, upper_scaled, lower_band, response_side)
    current = velocity
    for sweep_index in range(SWEEPS):
        velocity_pad = extended(current, (("lat", 1),), 1)
        side_velocity = jnp.pad(current, ((0, 0), (0, 0), (0, 0), (1, 1)))
        right_side = (
            source
            + face_west * velocity_pad[:, :-2]
            + face_east * velocity_pad[:, 2:]
            + face_south * side_velocity[..., :-2]
            + face_north * side_velocity[..., 2:]
        )
        particular = block_solve(pivots, upper_scaled, lower_band, right_side)
        interface = jnp.concatenate(
            [response[:, :, 0], response[:, :, -1], particular[:, :, 0], particular[:, :, -1]], 0
        )
        interface = interface.reshape(1, 10, cells_lateral * cells_side)
        boundary = reduced_boundary(interface).reshape(6, cells_lateral, 1, cells_side)
        current = particular + response[0][None] * boundary[:3] + response[1][None] * boundary[3:]
    composition = jnp.stack([basalt_share, melt_share])
    return (current, composition)

def local(tracer_values, tracer_cell, tracer_count, base_viscosity, velocity, forcing):
    values, cells = dense_tracers(tracer_values, tracer_cell)
    edge, first, second, count, values, cells = outgoing_sums(
        tracer_count, values, cells, base_viscosity, velocity, forcing
    )
    sent = first, second
    received = pair_swaps(first, second)
    if lax.axis_size("rad") != 2:
        return many_blocks(
            values, cells, count, edge, received, base_viscosity, velocity, forcing
        )
    inner, lines, outer = inner_lines(count, values, cells, base_viscosity, velocity, forcing)
    composition, mine, message, parts = eliminate(
        inner, lines, outer, edge, sent, received, base_viscosity.shape[0]
    )
    other = lax.ppermute(message, "rad", [(0, 1), (1, 0)])
    return join(mine, other, parts, velocity), composition


def solution(mesh):
    return jax.shard_map(
        local,
        mesh=mesh,
        in_specs=(
            P("lat", "rad", None, None),
            P("lat", "rad", None),
            P("lat", "rad", None),
            P("lat", "rad", None),
            P(None, "lat", "rad", None),
            P(None, "lat", "rad", None),
        ),
        out_specs=(P(None, "lat", "rad", None), P(None, "lat", "rad", None)),
        check_vma=False,
    )
```

```python
import functools

import jax
import jax.numpy as jnp
from jax import lax
from jax.experimental import pallas as pl
from jax.experimental.pallas import tpu as pltpu
from jax.sharding import PartitionSpec as P

SWEEPS = 2
MIGRATION_PLANES = 2

LATERAL = 0.015625
RADIAL = 32.0
BUOYANCY = 0.1
PRIOR_WEIGHT = 0.5
CONTRAST_BASALT = 2.3
CONTRAST_MELT = 1.5

TILE_ROWS = 16


def round_up(value, multiple):
    return -(-value // multiple) * multiple


def split_index(index, count):
    if count & (count - 1) == 0:
        return lax.shift_right_logical(index, count.bit_length() - 1), index & (count - 1)
    quotient = lax.div(index, count)
    return quotient, index - quotient * count


def payload_sections(cells_radial):
    pair = MIGRATION_PLANES * cells_radial
    starts = [0, 3 * pair, 6 * pair, 9 * pair, 10 * pair]
    return starts, round_up(10 * pair + 3 * cells_radial, 8)


def spread_row(row):
    return jnp.broadcast_to(row, (TILE_ROWS, row.shape[1])).astype(jnp.bfloat16)


def hot_tiles(index, row_total):
    iota = lax.broadcasted_iota(jnp.int32, index.shape, 0)
    return [
        index == (iota + first).astype(jnp.float32).astype(jnp.bfloat16)
        for first in range(0, row_total, TILE_ROWS)
    ]


def hot_product(sums, loads, high, low, high_rows, low_rows, chunk_rows):
    high, low = high.astype(jnp.float32), low.astype(jnp.float32)
    zero = jnp.zeros((TILE_ROWS, high.shape[1]), jnp.bfloat16)
    one = jnp.ones((TILE_ROWS, high.shape[1]), jnp.bfloat16)
    for first_row in range(0, high.shape[0], chunk_rows):
        left, right = [], []
        for row in range(first_row, first_row + chunk_rows):
            pick = slice(row, row + 1)
            high_masks = hot_tiles(spread_row(high[pick]), high_rows)
            low_masks = hot_tiles(spread_row(low[pick]), low_rows)
            spread = [spread_row(load[pick]) for load in loads]
            tiles = [jnp.where(mask, load, zero) for load in spread for mask in high_masks]
            left.append(jnp.concatenate(tiles, 0))
            right.append(jnp.concatenate([jnp.where(mask, one, zero) for mask in low_masks], 0))
        sums = sums + lax.dot_general(
            jnp.concatenate(left, 1),
            jnp.concatenate(right, 1),
            (((1,), (1,)), ((), ())),
            preferred_element_type=jnp.float32,
        )
    return sums


def edge_row(plane, plane_total, moved_total):
    inner = (plane >= moved_total) & (plane < plane_total - moved_total)
    last = plane - (plane_total - 2 * moved_total)
    return jnp.where(inner, -plane_total, jnp.where(plane < moved_total, plane, last))


def fold_moved(plane, side, plane_total, side_total):
    width, third = side_total // 4, plane_total // 3
    part = jnp.where(plane >= third, 1, 0) + jnp.where(plane >= 2 * third, 1, 0)
    other = side >= 3 * width
    high = jnp.where(other, plane_total + plane - part * third, plane)
    low = jnp.where(other, side - 3 * width + part * width, side)
    return high, low, plane_total + third, 3 * width


def unfold_moved(table, q, plane_total, side_total, put):
    width, third = side_total // 4, plane_total // 3
    rows = plane_total + third
    put(0, 0, table[pl.ds(q * rows, plane_total), 0 : 3 * width])
    for part in range(3):
        block = table[
            pl.ds(q * rows + plane_total, third), part * width : (part + 1) * width
        ]
        put(part * third, 3 * width, block)


def fold_inner(plane, side, plane_total, side_total):
    rows, width = plane_total * 5 // 6, side_total // 4
    part, rest = split_index(side, width)
    other = plane >= rows
    high = jnp.where(other, plane - rows + part * (plane_total - rows), plane)
    high = jnp.where(plane < plane_total, high, -1)
    low = jnp.where(other, side_total + rest, side)
    return high, low, rows, side_total + width


def unfold_inner(table, q, plane_total, side_total, put):
    rows, width = plane_total * 5 // 6, side_total // 4
    left = plane_total - rows
    put(0, 0, table[pl.ds(q * rows, rows), 0:side_total])
    for part in range(4):
        block = table[pl.ds(q * rows + part * left, left), side_total : side_total + width]
        put(rows, part * width, block)


def tracer_block(count, values, cells, group, first_row, block_rows, cells_side):
    rows = pl.ds(first_row, block_rows)
    lane_total = cells.shape[2]
    shape = (block_rows, lane_total)
    slot = (first_row + lax.broadcasted_iota(jnp.int32, shape, 0)) * lane_total
    slot = slot + lax.broadcasted_iota(jnp.int32, shape, 1)
    weight = jnp.where(slot < count, 0.5 + values[0, group, rows, :], jnp.float32(0.0))
    loads = [weight, weight * values[1, group, rows, :], weight * values[2, group, rows, :]]
    plane, side = split_index(cells[group, rows, :], cells_side)
    return loads, plane, side


def for_used_blocks(used, group_rows, block_rows, lane_total, late_copies, step):
    block_slots = block_rows * lane_total
    blocks = lax.div(used + (block_slots - 1), block_slots)
    blocks = jnp.clip(blocks, 1, group_rows // block_rows)

    def wait_late():
        for copy in late_copies:
            copy.wait()

    def repeat(index, carried):
        pl.when(index == 1)(wait_late)
        step(pl.multiple_of(index * block_rows, block_rows))
        return carried

    lax.fori_loop(0, blocks, repeat, 0)
    pl.when(blocks == 1)(wait_late)


VISCOSITY, VELOCITY, SOURCE, LINE_FIELDS = 0, 1, 4, 7


def composition_of(cell_sums, base):
    scale = 1.0 / (cell_sums[0] + PRIOR_WEIGHT)
    basalt_share, melt_share = cell_sums[1] * scale, cell_sums[2] * scale
    weakening = jnp.exp(CONTRAST_BASALT * basalt_share - CONTRAST_MELT * melt_share)
    return basalt_share, melt_share, base * weakening


def outward_row(t, cells_radial):
    return jnp.where(lax.axis_index("rad") == 0, t, cells_radial - 1 - t)


class Fetches:
    def __init__(self, semaphores):
        self.semaphores = semaphores
        self.copies = []

    def start(self, source, target):
        copy = pltpu.make_async_copy(source, target, self.semaphores.at[len(self.copies)])
        copy.start()
        self.copies.append(copy)

    def wait(self, first, last):
        for copy in self.copies[first:last]:
            copy.wait()


def has_partners():
    lateral, count = lax.axis_index("lat"), lax.axis_size("lat")
    odd = lax.rem(lateral, 2) == 1
    above, below = lateral + 1 < count, lateral > 0
    return jnp.logical_or(odd, above), jnp.where(odd, above, below)


def outgoing_kernel(
    block_rows,
    counts_hbm,
    values_hbm,
    cells_hbm,
    base_hbm,
    velocity_hbm,
    forcing_hbm,
    edge_ref,
    first_ref,
    second_ref,
    count_ref,
    values,
    cells,
    counts,
    base,
    velocity,
    forcing,
    moved_sums,
    semaphores,
):
    cells_lateral, cells_radial, cells_side = base_hbm.shape
    plane_total = cells_lateral * cells_radial
    moved_planes = MIGRATION_PLANES * cells_radial
    group_rows, lane_total = cells.shape[1:]

    fetches = Fetches(semaphores)
    fetches.start(counts_hbm, counts)
    part = pl.ds(0, block_rows)
    fetches.start(cells_hbm.at[:, part], cells.at[:, part])
    for q in range(3):
        fetches.start(values_hbm.at[q, :, part], values.at[q, :, part])
    part = pl.ds(block_rows, group_rows - block_rows)
    fetches.start(cells_hbm.at[:, part], cells.at[:, part])
    fetches.start(values_hbm.at[:, :, part], values.at[:, :, part])
    for upward in (0, 1):
        outer = pl.ds((cells_lateral - MIGRATION_PLANES) * upward, MIGRATION_PLANES)
        fetches.start(base_hbm.at[outer], base.at[upward])
        fetches.start(velocity_hbm.at[:, outer], velocity.at[upward])
        outermost = pl.ds((cells_lateral - 1) * upward, 1)
        fetches.start(forcing_hbm.at[:, outermost], forcing.at[upward])

    edge_ref[...] = jnp.zeros_like(edge_ref)
    moved_sums[...] = jnp.zeros_like(moved_sums)

    def step(first_row):
        def block_of(group):
            count = counts[0, 0, group]
            return tracer_block(count, values, cells, group, first_row, block_rows, cells_side)

        loads, plane, side = block_of(1)
        row = edge_row(plane, plane_total, moved_planes)
        edge_ref[...] = hot_product(
            edge_ref[...], loads, row, side, 2 * moved_planes, cells_side, CHUNK_ROWS
        )
        for slot, group in enumerate((0, 2)):
            loads, plane, side = block_of(group)
            if group == 0:
                plane = plane - (plane_total - moved_planes)
            table = fold_moved(plane, side, moved_planes, cells_side)
            moved_sums[slot] = hot_product(moved_sums[slot], loads, *table, CHUNK_ROWS)

    fetches.wait(0, 5)
    count_ref[...] = jnp.full(count_ref.shape, counts[0, 0, 1], jnp.int32).astype(jnp.float32)
    used = jnp.maximum(jnp.maximum(counts[0, 0, 0], counts[0, 0, 1]), counts[0, 0, 2])
    for_used_blocks(used, group_rows, block_rows, lane_total, fetches.copies[5:7], step)
    fetches.wait(7, None)

    starts, rows_total = payload_sections(cells_radial)
    unused = starts[4] + 3 * cells_radial

    def fill(payload, upward):
        for q in range(3):

            def put_moved(plane, column, block):
                height, width = block.shape
                rows = pl.ds(starts[0] + q * moved_planes + plane, height)
                payload[rows, column : column + width] = block

            unfold_moved(moved_sums.at[upward], q, moved_planes, cells_side, put_moved)
            payload[pl.ds(starts[1] + q * moved_planes, moved_planes), :] = edge_ref[
                pl.ds((2 * q + upward) * moved_planes, moved_planes), :
            ]
            for offset in range(MIGRATION_PLANES):
                row = starts[2] + q * moved_planes + offset * cells_radial
                payload[pl.ds(row, cells_radial), :] = velocity[upward, q, offset]
            row = starts[4] + q * cells_radial
            payload[pl.ds(row, cells_radial), :] = forcing[upward, q, 0]
        for offset in range(MIGRATION_PLANES):
            row = starts[3] + offset * cells_radial
            payload[pl.ds(row, cells_radial), :] = base[upward, offset]
        if unused < rows_total:
            payload[unused:, :] = jnp.zeros((rows_total - unused, cells_side), jnp.float32)

    odd = lax.rem(lax.axis_index("lat"), 2) == 1

    @pl.when(odd)
    def _():
        fill(first_ref, 0)
        fill(second_ref, 1)

    @pl.when(jnp.logical_not(odd))
    def _():
        fill(first_ref, 1)
        fill(second_ref, 0)

    for payload, exists in zip((first_ref, second_ref), has_partners()):

        @pl.when(jnp.logical_not(exists))
        def _():
            payload[...] = jnp.zeros_like(payload)


def inner_kernel(
    block_rows,
    count_ref,
    values_ref,
    cells_ref,
    base_hbm,
    velocity_hbm,
    forcing_hbm,
    composition_ref,
    lines_ref,
    outer_ref,
    table,
    sums,
    fields,
    base,
    velocity,
    forcing,
    semaphores,
):
    cells_lateral, cells_radial, cells_side = base.shape
    margin = MIGRATION_PLANES
    planes = cells_lateral + 2 * margin
    pitch = round_up(cells_radial, 8)
    moved_planes = margin * cells_radial
    inner = cells_lateral - 2 * margin
    inner_planes = inner * cells_radial
    group_rows, lane_total = cells_ref.shape[1:]
    fetches = Fetches(semaphores)
    fetches.start(velocity_hbm, velocity)
    fetches.start(forcing_hbm, forcing)
    fetches.start(base_hbm, base)
    table[...] = jnp.zeros_like(table)

    nothing = jnp.zeros((cells_radial, cells_side), jnp.float32)

    def put(field, plane, value):
        fields[field, pl.ds(plane * pitch, cells_radial), :] = value

    def lay_out(those):
        for field in those:
            for t in range(cells_radial):
                row = outward_row(t, cells_radial)
                lines_ref[field, t] = fields[field, pl.ds(row, planes, stride=pitch), :]

    def step(first_row):
        loads, plane, side = tracer_block(
            count, values_ref, cells_ref, 1, first_row, block_rows, cells_side
        )
        where = fold_inner(plane - moved_planes, side, inner_planes, cells_side)
        table[...] = hot_product(table[...], loads, *where, block_rows)

    count = jnp.max(count_ref[...]).astype(jnp.int32)
    for_used_blocks(count, group_rows, block_rows, lane_total, [], step)

    fetches.wait(0, None)
    for plane in range(planes):
        x = plane - margin
        own = 0 <= x < cells_lateral
        for q in range(3):
            put(VELOCITY + q, plane, velocity[q, x] if own else nothing)
        for q in range(2):
            put(SOURCE + q, plane, forcing[q, x] if own else nothing)
    late = VISCOSITY, SOURCE + 2
    lay_out(field for field in range(LINE_FIELDS) if field not in late)

    for q in range(3):

        def put_sums(plane, column, block):
            height, width = block.shape
            sums[q, pl.ds(plane, height), column : column + width] = block

        unfold_inner(table, q, inner_planes, cells_side, put_sums)
    for plane in range(planes):
        x = plane - 2 * margin
        viscosity, source = nothing, nothing
        if 0 <= x < inner:
            part = pl.ds(x * cells_radial, cells_radial)
            cell_sums = [sums[q, part, :] for q in range(3)]
            basalt_share, melt_share, viscosity = composition_of(cell_sums, base[x + margin])
            source = forcing[2, x + margin] - BUOYANCY * basalt_share
            composition_ref[0, x] = basalt_share
            composition_ref[1, x] = melt_share
        put(VISCOSITY, plane, viscosity)
        put(SOURCE + 2, plane, source)
    lay_out(late)
    for offset in range(margin):
        for place, x in ((offset, offset), (margin + offset, cells_lateral - margin + offset)):
            outer_ref[0, place] = base[x]
            outer_ref[1, place] = forcing[2, x]


BLOCK_ROWS = 64
CHUNK_ROWS = 2


def dense_tracers(tracer_values, tracer_cell):
    lane_total = 128
    return tracer_values.reshape(3, 3, -1, lane_total), tracer_cell.reshape(3, -1, lane_total)


def outgoing_sums(tracer_count, values, cells, base_viscosity, velocity, forcing):
    cells_lateral, cells_radial, cells_side = base_viscosity.shape
    moved_planes = MIGRATION_PLANES * cells_radial
    group_rows, lane_total = cells.shape[1:]
    block_rows = min(BLOCK_ROWS, group_rows // 2)
    _, payload_rows = payload_sections(cells_radial)
    hbm = pl.BlockSpec(memory_space=pltpu.HBM)
    vmem = pl.BlockSpec(memory_space=pltpu.VMEM)
    payload = jax.ShapeDtypeStruct((payload_rows, cells_side), jnp.float32)
    outer_planes = (MIGRATION_PLANES, cells_radial, cells_side)
    return pl.pallas_call(
        functools.partial(outgoing_kernel, block_rows),
        out_shape=(
            jax.ShapeDtypeStruct((6 * moved_planes, cells_side), jnp.float32),
            payload,
            payload,
            jax.ShapeDtypeStruct((8, lane_total), jnp.float32),
            jax.ShapeDtypeStruct(values.shape, jnp.float32),
            jax.ShapeDtypeStruct(cells.shape, jnp.int32),
        ),
        in_specs=[hbm] * 6,
        out_specs=(vmem,) * 6,
        scratch_shapes=[
            pltpu.SMEM(tracer_count.shape, jnp.int32),
            pltpu.VMEM((2,) + outer_planes, jnp.float32),
            pltpu.VMEM((2, 3) + outer_planes, jnp.float32),
            pltpu.VMEM((2, 3, 1, cells_radial, cells_side), jnp.float32),
            pltpu.VMEM((2, 4 * moved_planes, cells_side * 3 // 4), jnp.float32),
            pltpu.SemaphoreType.DMA((13,)),
        ],
        compiler_params=pltpu.CompilerParams(vmem_limit_bytes=32 * 2**20),
        cost_estimate=pl.CostEstimate(
            flops=30 * group_rows * lane_total * moved_planes * cells_side,
            bytes_accessed=4 * (values.size + cells.size),
            transcendentals=0,
        ),
        name="outgoing_sums",
    )(
        *(
            pltpu.with_memory_space_constraint(array, pltpu.HBM)
            for array in (tracer_count, values, cells, base_viscosity, velocity, forcing)
        )
    )


def inner_lines(count, values, cells, base_viscosity, velocity, forcing):
    cells_lateral, cells_radial, cells_side = base_viscosity.shape
    planes = cells_lateral + 2 * MIGRATION_PLANES
    inner = cells_lateral - 2 * MIGRATION_PLANES
    inner_planes = inner * cells_radial
    group_rows, lane_total = cells.shape[1:]
    block_rows = min(BLOCK_ROWS, group_rows // 2)
    vmem = pl.BlockSpec(memory_space=pltpu.VMEM)
    return pl.pallas_call(
        functools.partial(inner_kernel, block_rows),
        out_shape=(
            jax.ShapeDtypeStruct((2, inner, cells_radial, cells_side), jnp.float32),
            jax.ShapeDtypeStruct((LINE_FIELDS, cells_radial, planes, cells_side), jnp.float32),
            jax.ShapeDtypeStruct(
                (2, 2 * MIGRATION_PLANES, cells_radial, cells_side), jnp.float32
            ),
        ),
        in_specs=[vmem] * 3 + [pl.BlockSpec(memory_space=pltpu.HBM)] * 3,
        out_specs=(vmem,) * 3,
        scratch_shapes=[
            pltpu.VMEM((3 * (inner_planes * 5 // 6), cells_side * 5 // 4), jnp.float32),
            pltpu.VMEM((3, inner_planes, cells_side), jnp.float32),
            pltpu.VMEM((LINE_FIELDS, planes * round_up(cells_radial, 8), cells_side), jnp.float32),
            pltpu.VMEM(base_viscosity.shape, jnp.float32),
            pltpu.VMEM(velocity.shape, jnp.float32),
            pltpu.VMEM(forcing.shape, jnp.float32),
            pltpu.SemaphoreType.DMA((3,)),
        ],
        compiler_params=pltpu.CompilerParams(vmem_limit_bytes=32 * 2**20),
        cost_estimate=pl.CostEstimate(
            flops=6 * group_rows * lane_total * inner * cells_radial * cells_side,
            bytes_accessed=4 * (values.size + cells.size),
            transcendentals=0,
        ),
        name="inner_lines",
    )(
        count,
        values,
        cells,
        *(
            pltpu.with_memory_space_constraint(array, pltpu.HBM)
            for array in (base_viscosity, velocity, forcing)
        ),
    )


def pair_swaps(first, second):
    count = lax.axis_size("lat")
    received = []
    for payload, start in ((second, 1), (first, 0)):
        target = list(range(count))
        for low in range(start, count - 1, 2):
            target[low], target[low + 1] = low + 1, low
        received.append(lax.ppermute(payload, "lat", list(enumerate(target))))
    return received[::-1]


def shift_planes(block, step):
    return pltpu.roll(block, step % block.shape[0], 0)


def shift_side(block, step):
    return pltpu.roll(block, step % block.shape[1], 1)


def neighbours(block):
    return (
        shift_planes(block, 1),
        shift_planes(block, -1),
        shift_side(block, 1),
        shift_side(block, -1),
    )


def inside_side(values):
    lane = lax.broadcasted_iota(jnp.int32, values[2].shape, 1)
    lower = jnp.where(lane > 0, values[2], 0.0)
    upper = jnp.where(lane < lane.shape[1] - 1, values[3], 0.0)
    return values[0], values[1], lower, upper


def total_of(terms):
    result = terms[0]
    for term in terms[1:]:
        result = result + term
    return result


def inside_grid(shape, margin, cells_lateral):
    plane = lax.broadcasted_iota(jnp.int32, shape, 0)
    lateral = lax.axis_index("lat")
    first = jnp.where(lateral == 0, margin, 1)
    last = jnp.where(lateral == lax.axis_size("lat") - 1, margin + cells_lateral, shape[0] - 1)
    return (plane >= first) & (plane < last)


LONG_FIELDS, SHORT_FIELDS = 5, 7


def message_rows(cells_lateral):
    planes = cells_lateral + 2 * MIGRATION_PLANES
    return round_up(LONG_FIELDS * planes + SHORT_FIELDS * cells_lateral + MIGRATION_PLANES, 8)


def message_part(cells_lateral, field):
    planes = cells_lateral + 2 * MIGRATION_PLANES
    if field < LONG_FIELDS:
        return pl.ds(field * planes, planes), 0, planes
    first = LONG_FIELDS * planes + (field - LONG_FIELDS) * cells_lateral
    return pl.ds(first, cells_lateral), MIGRATION_PLANES, cells_lateral


def solve_lines(radial, cells_radial, valid, keep, keep_part):
    last = cells_radial - 1
    viscosity = [radial(VISCOSITY, t) for t in range(cells_radial)]
    lateral_faces, lateral_sums = [], []
    for here in viscosity:
        faces = [LATERAL * 0.5 * (here + there) for there in inside_side(neighbours(here))]
        lateral_sums.append(total_of(faces))
        lateral_faces.append(inside_side(faces))
    radial_faces = [RADIAL * 0.5 * viscosity[0]] + [
        RADIAL * 0.5 * (viscosity[t - 1] + viscosity[t]) for t in range(1, cells_radial)
    ]

    excess = lateral_sums[0] + radial_faces[0]
    inverse, coupling = [], []
    for t in range(last):
        inverse.append(1.0 / (excess + radial_faces[t + 1]))
        coupling.append(radial_faces[t + 1] * inverse[t])
        excess = lateral_sums[t + 1] + coupling[t] * excess

    def lateral_terms(t, around):
        return [face * there for face, there in zip(lateral_faces[t], around)]

    def forward(right_side):
        eliminated = [right_side[0]]
        for t in range(1, cells_radial):
            eliminated.append(right_side[t] + coupling[t - 1] * eliminated[t - 1])
        return eliminated

    def backward(eliminated):
        solved = [jnp.zeros_like(excess)]
        for t in range(last - 1, -1, -1):
            solved.append(eliminated[t] * inverse[t] + coupling[t] * solved[-1])
        return solved[::-1]

    response = [jnp.ones_like(excess)]
    for t in range(last - 1, -1, -1):
        response.append(coupling[t] * response[-1])
    response = response[::-1]

    def finish(part, eliminated):
        keep(LONG_FIELDS + part, eliminated[last])
        for t, value in enumerate(eliminated[:last]):
            keep_part(part, t, value)

    keep(0, viscosity[last])
    keep(1, excess)
    for q in range(3):
        source = [radial(SOURCE + q, t) for t in range(cells_radial)]
        eliminated = forward(
            [
                total_of([source[t]] + lateral_terms(t, neighbours(radial(VELOCITY + q, t))))
                for t in range(cells_radial)
            ]
        )
        keep(2 + q, eliminated[last])
        particular = [jnp.where(valid, value, 0.0) for value in backward(eliminated)]
        finish(
            q,
            forward(
                [
                    total_of([source[t]] + lateral_terms(t, neighbours(particular[t])))
                    for t in range(cells_radial)
                ]
            ),
        )
    around = [neighbours(jnp.where(valid, value, 0.0)) for value in response]
    for side in range(4):
        finish(
            3 + side,
            forward([lateral_faces[t][side] * around[t][side] for t in range(cells_radial)]),
        )
    for t in range(last):
        keep_part(SHORT_FIELDS, t, inverse[t])
        keep_part(SHORT_FIELDS + 1, t, coupling[t])


def eliminate_kernel(
    inner_ref,
    lines_ref,
    edge_ref,
    second_ref,
    first_ref,
    from_second_ref,
    from_first_ref,
    outer_ref,
    composition_ref,
    mine_ref,
    message_ref,
    parts_ref,
    fields,
):
    _, cells_lateral, cells_radial, cells_side = composition_ref.shape
    margin = MIGRATION_PLANES
    planes = cells_lateral + 2 * margin
    pitch = round_up(cells_radial, 8)
    moved_planes = margin * cells_radial
    starts, _ = payload_sections(cells_radial)
    odd = lax.rem(lax.axis_index("lat"), 2) == 1

    def sent(upward, start):
        part = pl.ds(start, cells_radial)
        mine_first = odd if not upward else jnp.logical_not(odd)
        return jnp.where(mine_first, first_ref[part, :], second_ref[part, :])

    def arrived(from_above, start):
        part = pl.ds(start, cells_radial)
        is_first = odd if not from_above else jnp.logical_not(odd)
        return jnp.where(is_first, from_first_ref[part, :], from_second_ref[part, :])

    outer = 2 * margin

    def put(field, slot, value):
        fields[field, pl.ds(slot * pitch, cells_radial), :] = value

    for above in (False, True):
        for offset in range(margin):
            shift = offset * cells_radial
            halo = offset + (outer + margin if above else 0)
            own = offset + (outer if above else margin)
            x = offset + (cells_lateral - margin if above else 0)
            place = offset + (margin if above else 0)
            halo_sums, own_sums = [], []
            for q in range(3):
                row = q * moved_planes + shift
                rows = pl.ds((2 * q + int(above)) * moved_planes + shift, cells_radial)
                own_sums.append(edge_ref[rows, :] + arrived(above, starts[0] + row))
                halo_sums.append(sent(above, starts[0] + row) + arrived(above, starts[1] + row))
                put(VELOCITY + q, halo, arrived(above, starts[2] + row))
            basalt_share, melt_share, viscosity = composition_of(own_sums, outer_ref[0, place])
            composition_ref[0, x] = basalt_share
            composition_ref[1, x] = melt_share
            put(VISCOSITY, own, viscosity)
            put(SOURCE + 2, own, outer_ref[1, place] - BUOYANCY * basalt_share)
            basalt_share, _, viscosity = composition_of(
                halo_sums, arrived(above, starts[3] + shift)
            )
            put(VISCOSITY, halo, viscosity)
            beside = offset == (0 if above else margin - 1)
            for q in range(3):
                source = jnp.zeros_like(viscosity)
                if beside:
                    source = arrived(above, starts[4] + q * cells_radial)
                    if q == 2:
                        source = source - BUOYANCY * basalt_share
                put(SOURCE + q, halo, source)
    for x in range(margin, cells_lateral - margin):
        for q in range(2):
            composition_ref[q, x] = inner_ref[q, x - margin]

    def radial(field, t):
        replaced = outer if field in (VISCOSITY, SOURCE + 2) else margin
        plane = lax.broadcasted_iota(jnp.int32, (planes, cells_side), 0)
        own = (plane >= replaced) & (plane < planes - replaced)
        row = outward_row(t, cells_radial)
        edges = fields[field, pl.ds(row, 2 * outer, stride=pitch), :]
        if 2 * outer * 2 == planes:
            edges = jnp.concatenate([edges, edges], 0)
        else:
            gap = jnp.zeros((planes - 2 * outer, cells_side), jnp.float32)
            edges = jnp.concatenate([edges[:outer], gap, edges[outer:]], 0)
        return jnp.where(own, lines_ref[field, t], edges)

    unused = LONG_FIELDS * planes + SHORT_FIELDS * cells_lateral
    if unused < message_ref.shape[0]:
        message_ref[unused:, :] = jnp.zeros((message_ref.shape[0] - unused, cells_side), jnp.float32)

    def keep(field, value):
        rows, first, count = message_part(cells_lateral, field)
        mine_ref[field] = value
        message_ref[rows, :] = value[first : first + count]

    def keep_part(part, t, value):
        parts_ref[part, t] = value

    valid = inside_grid((planes, cells_side), margin, cells_lateral)
    solve_lines(radial, cells_radial, valid, keep, keep_part)


def eliminate(inner, lines, outer, edge, sent, received, cells_lateral):
    cells_radial, cells_side = inner.shape[2:]
    planes = cells_lateral + 2 * MIGRATION_PLANES
    vmem = pl.BlockSpec(memory_space=pltpu.VMEM)
    line = (planes, cells_side)
    return pl.pallas_call(
        eliminate_kernel,
        out_shape=(
            jax.ShapeDtypeStruct((2, cells_lateral, cells_radial, cells_side), jnp.float32),
            jax.ShapeDtypeStruct((LONG_FIELDS + SHORT_FIELDS,) + line, jnp.float32),
            jax.ShapeDtypeStruct((message_rows(cells_lateral), cells_side), jnp.float32),
            jax.ShapeDtypeStruct((SHORT_FIELDS + 2, cells_radial - 1) + line, jnp.float32),
        ),
        in_specs=[vmem] * 8,
        out_specs=(vmem,) * 4,
        scratch_shapes=[
            pltpu.VMEM(
                (LINE_FIELDS, 4 * MIGRATION_PLANES * round_up(cells_radial, 8), cells_side),
                jnp.float32,
            )
        ],
        compiler_params=pltpu.CompilerParams(vmem_limit_bytes=32 * 2**20),
        name="eliminate",
    )(inner, lines, edge, *sent[::-1], *received[::-1], outer)


def join_kernel(mine_ref, message_ref, parts_ref, smoothed_hbm, smoothed, lines, semaphores):
    _, cells_lateral, cells_radial, cells_side = smoothed.shape
    margin = MIGRATION_PLANES
    planes = cells_lateral + 2 * margin
    pitch = round_up(cells_radial, 8)
    valid = inside_grid((planes, cells_side), margin, cells_lateral)

    def mine(field):
        return mine_ref[field]

    def other(field):
        rows, first, _ = message_part(cells_lateral, field)
        return message_ref[pl.ds(rows.start - first, planes), :]

    face = RADIAL * 0.5 * (mine(0) + other(0))
    excess, other_excess = mine(1), other(1)
    scale = 1.0 / (excess * other_excess + face * (excess + other_excess))
    own_weight = (other_excess + face) * scale
    other_weight = (excess + face) * scale
    cross = face * scale

    def second_right(field_of, q, around):
        terms = [field_of(LONG_FIELDS + 3 + side) * there for side, there in enumerate(around)]
        return total_of([field_of(LONG_FIELDS + q)] + terms)

    fetches = Fetches(semaphores)
    for q in range(3):
        right, other_right = mine(2 + q), other(2 + q)
        own = jnp.where(valid, own_weight * right + cross * other_right, 0.0)
        beyond = jnp.where(valid, other_weight * other_right + cross * right, 0.0)
        around = neighbours(own)
        right = second_right(mine, q, around)
        other_right = second_right(other, q, neighbours(beyond))
        value = own_weight * right + cross * other_right
        for t in range(cells_radial - 1, -1, -1):
            if t < cells_radial - 1:
                terms = [parts_ref[3 + side, t] * there for side, there in enumerate(around)]
                right = total_of([parts_ref[q, t]] + terms)
                value = right * parts_ref[SHORT_FIELDS, t] + parts_ref[SHORT_FIELDS + 1, t] * value
            row = outward_row(t, cells_radial)
            lines[q, pl.ds(row, cells_lateral, stride=pitch), :] = value[
                margin : margin + cells_lateral
            ]
        for x in range(cells_lateral):
            smoothed[q, x] = lines[q, pl.ds(x * pitch, cells_radial), :]
        fetches.start(smoothed.at[q], smoothed_hbm.at[q])
    fetches.wait(0, None)


def join(mine, message, parts, like):
    cells_lateral, cells_radial, cells_side = like.shape[1:]
    vmem = pl.BlockSpec(memory_space=pltpu.VMEM)
    return pl.pallas_call(
        join_kernel,
        out_shape=jax.ShapeDtypeStruct(like.shape, jnp.float32),
        in_specs=[vmem] * 3,
        out_specs=pl.BlockSpec(memory_space=pltpu.HBM),
        scratch_shapes=[
            pltpu.VMEM(like.shape, jnp.float32),
            pltpu.VMEM((3, cells_lateral * round_up(cells_radial, 8), cells_side), jnp.float32),
            pltpu.SemaphoreType.DMA((3,)),
        ],
        compiler_params=pltpu.CompilerParams(vmem_limit_bytes=32 * 2**20),
        name="join",
    )(mine, message, parts)


def extended(block, sides, width):
    for axis, dim in sides:
        count = lax.axis_size(axis)
        forward = [(i, i + 1) for i in range(count - 1)]
        backward = [(target, source) for source, target in forward]
        low = lax.ppermute(
            lax.slice_in_dim(block, block.shape[dim] - width, None, axis=dim), axis, forward
        )
        high = lax.ppermute(lax.slice_in_dim(block, 0, width, axis=dim), axis, backward)
        block = jnp.concatenate([low, block, high], axis=dim)
    return block


def block_factor(diagonal, lower_band, upper_band):
    pivots = []
    upper_scaled = []
    for row_index in range(diagonal.shape[1]):
        if row_index == 0:
            pivot_row = diagonal[:, 0]
        else:
            pivot_row = diagonal[:, row_index] - lower_band[:, row_index] * upper_scaled[-1]
        pivots.append(pivot_row)
        upper_scaled.append(upper_band[:, row_index] / pivot_row)
    return (pivots, upper_scaled)


def block_solve(pivots, upper_scaled, lower_band, right_side):
    row_total = len(pivots)
    modified = []
    for row_index in range(row_total):
        if row_index == 0:
            value_row = right_side[:, :, 0] / pivots[0]
        else:
            value_row = (
                right_side[:, :, row_index] - lower_band[:, row_index] * modified[-1]
            ) / pivots[row_index]
        modified.append(value_row)
    solved = [modified[-1]]
    for row_index in range(row_total - 2, -1, -1):
        solved.append(modified[row_index] - upper_scaled[row_index] * solved[-1])
    ordered = solved[::-1]
    return jnp.stack(ordered, 2)


def interface_solve(coefficients):
    column_total = coefficients.shape[2]

    def forward(carried, inputs):
        offset, carried_slope = carried
        left_first, right_first, left_last, right_last, free_first, free_last = inputs
        divisor = 1.0 - left_first * carried_slope
        first_fixed = (free_first + left_first * offset) / divisor
        first_slope = right_first / divisor
        next_offset = free_last + left_last * (offset + carried_slope * first_fixed)
        next_slope = left_last * carried_slope * first_slope + right_last
        return ((next_offset, next_slope), (first_fixed, first_slope, next_offset, next_slope))

    start_state = (
        jnp.zeros((3, column_total), jnp.float32),
        jnp.zeros((column_total,), jnp.float32),
    )
    scan_inputs = (
        coefficients[:, 0],
        coefficients[:, 1],
        coefficients[:, 2],
        coefficients[:, 3],
        coefficients[:, 4:7],
        coefficients[:, 7:10],
    )
    final_state, eliminated = lax.scan(forward, start_state, scan_inputs)

    def backward(first_next, inputs):
        fixed_first, slope_first, fixed_last, slope_last = inputs
        first_value = fixed_first + slope_first * first_next
        last_value = fixed_last + slope_last * first_next
        return (first_value, (first_value, last_value))

    final_first, values_pair = lax.scan(
        backward, jnp.zeros((3, column_total), jnp.float32), eliminated, reverse=True
    )
    first_values, last_values = values_pair
    nothing_row = jnp.zeros((1, 3, column_total), jnp.float32)
    from_below = jnp.concatenate([nothing_row, last_values[:-1]], 0)
    from_above = jnp.concatenate([first_values[1:], nothing_row], 0)
    return jnp.concatenate([from_below, from_above], 1)


def reduced_boundary(interface):
    gathered = lax.all_gather(interface, "rad", axis=0, tiled=True)
    solved = interface_solve(gathered)
    return lax.dynamic_index_in_dim(solved, lax.axis_index("rad"), 0, keepdims=False)


def many_blocks(values, cells, count, edge, received, base_viscosity, velocity, forcing):
    cells_lateral, cells_radial, cells_side = base_viscosity.shape
    moved_rows = MIGRATION_PLANES * cells_radial
    odd = lax.rem(lax.axis_index("lat"), 2) == 1
    from_below = jnp.where(odd, received[0], received[1])[: 3 * moved_rows]
    from_above = jnp.where(odd, received[1], received[0])[: 3 * moved_rows]
    edge = edge.reshape(3, 2, moved_rows, cells_side)
    below = edge[:, 0] + from_below.reshape(3, moved_rows, cells_side)
    above = edge[:, 1] + from_above.reshape(3, moved_rows, cells_side)
    shares = [
        (sums[1:] / (sums[0] + PRIOR_WEIGHT)).reshape(2, -1, cells_radial, cells_side)
        for sums in (below, above)
    ]
    inner, _, _ = inner_lines(count, values, cells, base_viscosity, velocity, forcing)
    basalt_share, melt_share = jnp.concatenate([shares[0], inner, shares[1]], 1)
    viscosity = base_viscosity * jnp.exp(
        CONTRAST_BASALT * basalt_share - CONTRAST_MELT * melt_share
    )
    viscosity_pad = extended(viscosity, (("lat", 0), ("rad", 1)), 1)
    side_pad = jnp.pad(viscosity, ((0, 0), (0, 0), (1, 1)))
    face_west = LATERAL * 0.5 * (viscosity + viscosity_pad[:-2, 1:-1])
    face_east = LATERAL * 0.5 * (viscosity + viscosity_pad[2:, 1:-1])
    face_south = LATERAL * 0.5 * (viscosity + side_pad[:, :, :-2])
    face_north = LATERAL * 0.5 * (viscosity + side_pad[:, :, 2:])
    face_below = RADIAL * 0.5 * (viscosity + viscosity_pad[1:-1, :-2])
    face_above = RADIAL * 0.5 * (viscosity + viscosity_pad[1:-1, 2:])
    diagonal = face_west + face_east + face_south + face_north + face_below + face_above
    source = jnp.concatenate([forcing[:2], (forcing[2] - BUOYANCY * basalt_share)[None]], 0)
    lower_band = -face_below
    upper_band = -face_above
    pivots, upper_scaled = block_factor(diagonal, lower_band, upper_band)
    radial_iota = lax.broadcasted_iota(jnp.int32, viscosity.shape, 1)
    response_side = jnp.stack(
        [
            jnp.where(radial_iota == 0, face_below, jnp.float32(0.0)),
            jnp.where(radial_iota == cells_radial - 1, face_above, jnp.float32(0.0)),
        ]
    )
    response = block_solve(pivots, upper_scaled, lower_band, response_side)
    current = velocity
    for sweep_index in range(SWEEPS):
        velocity_pad = extended(current, (("lat", 1),), 1)
        side_velocity = jnp.pad(current, ((0, 0), (0, 0), (0, 0), (1, 1)))
        right_side = (
            source
            + face_west * velocity_pad[:, :-2]
            + face_east * velocity_pad[:, 2:]
            + face_south * side_velocity[..., :-2]
            + face_north * side_velocity[..., 2:]
        )
        particular = block_solve(pivots, upper_scaled, lower_band, right_side)
        interface = jnp.concatenate(
            [response[:, :, 0], response[:, :, -1], particular[:, :, 0], particular[:, :, -1]], 0
        )
        interface = interface.reshape(1, 10, cells_lateral * cells_side)
        boundary = reduced_boundary(interface).reshape(6, cells_lateral, 1, cells_side)
        current = particular + response[0][None] * boundary[:3] + response[1][None] * boundary[3:]
    composition = jnp.stack([basalt_share, melt_share])
    return (current, composition)

def local(tracer_values, tracer_cell, tracer_count, base_viscosity, velocity, forcing):
    values, cells = dense_tracers(tracer_values, tracer_cell)
    edge, first, second, count, values, cells = outgoing_sums(
        tracer_count, values, cells, base_viscosity, velocity, forcing
    )
    sent = first, second
    received = pair_swaps(first, second)
    if lax.axis_size("rad") != 2:
        return many_blocks(
            values, cells, count, edge, received, base_viscosity, velocity, forcing
        )
    inner, lines, outer = inner_lines(count, values, cells, base_viscosity, velocity, forcing)
    composition, mine, message, parts = eliminate(
        inner, lines, outer, edge, sent, received, base_viscosity.shape[0]
    )
    other = lax.ppermute(message, "rad", [(0, 1), (1, 0)])
    return join(mine, other, parts, velocity), composition


def solution(mesh):
    return jax.shard_map(
        local,
        mesh=mesh,
        in_specs=(
            P("lat", "rad", None, None),
            P("lat", "rad", None),
            P("lat", "rad", None),
            P("lat", "rad", None),
            P(None, "lat", "rad", None),
            P(None, "lat", "rad", None),
        ),
        out_specs=(P(None, "lat", "rad", None), P(None, "lat", "rad", None)),
        check_vma=False,
    )
```

```python
import functools

import jax
import jax.numpy as jnp
from jax import lax
from jax.experimental import pallas as pl
from jax.experimental.pallas import tpu as pltpu
from jax.sharding import PartitionSpec as P

SWEEPS = 2
MIGRATION_PLANES = 2

LATERAL = 0.015625
RADIAL = 32.0
BUOYANCY = 0.1
PRIOR_WEIGHT = 0.5
CONTRAST_BASALT = 2.3
CONTRAST_MELT = 1.5

TILE_ROWS = 16


def round_up(value, multiple):
    return -(-value // multiple) * multiple


def split_index(index, count):
    if count & (count - 1) == 0:
        return lax.shift_right_logical(index, count.bit_length() - 1), index & (count - 1)
    quotient = lax.div(index, count)
    return quotient, index - quotient * count


def payload_sections(cells_radial):
    pair = MIGRATION_PLANES * cells_radial
    starts = [0, 3 * pair, 6 * pair, 9 * pair, 10 * pair]
    return starts, round_up(10 * pair + 3 * cells_radial, 8)


def spread_row(row):
    return jnp.broadcast_to(row, (TILE_ROWS, row.shape[1])).astype(jnp.bfloat16)


def hot_tiles(index, row_total):
    iota = lax.broadcasted_iota(jnp.int32, index.shape, 0)
    return [
        index == (iota + first).astype(jnp.float32).astype(jnp.bfloat16)
        for first in range(0, row_total, TILE_ROWS)
    ]


def hot_product(sums, loads, high, low, high_rows, low_rows, chunk_rows):
    high, low = high.astype(jnp.float32), low.astype(jnp.float32)
    zero = jnp.zeros((TILE_ROWS, high.shape[1]), jnp.bfloat16)
    one = jnp.ones((TILE_ROWS, high.shape[1]), jnp.bfloat16)
    for first_row in range(0, high.shape[0], chunk_rows):
        left, right = [], []
        for row in range(first_row, first_row + chunk_rows):
            pick = slice(row, row + 1)
            high_masks = hot_tiles(spread_row(high[pick]), high_rows)
            low_masks = hot_tiles(spread_row(low[pick]), low_rows)
            spread = [spread_row(load[pick]) for load in loads]
            tiles = [jnp.where(mask, load, zero) for load in spread for mask in high_masks]
            left.append(jnp.concatenate(tiles, 0))
            right.append(jnp.concatenate([jnp.where(mask, one, zero) for mask in low_masks], 0))
        sums = sums + lax.dot_general(
            jnp.concatenate(left, 1),
            jnp.concatenate(right, 1),
            (((1,), (1,)), ((), ())),
            preferred_element_type=jnp.float32,
        )
    return sums


def edge_row(plane, plane_total, moved_total):
    inner = (plane >= moved_total) & (plane < plane_total - moved_total)
    last = plane - (plane_total - 2 * moved_total)
    return jnp.where(inner, -plane_total, jnp.where(plane < moved_total, plane, last))


def fold_moved(plane, side, plane_total, side_total):
    width, third = side_total // 4, plane_total // 3
    part = jnp.where(plane >= third, 1, 0) + jnp.where(plane >= 2 * third, 1, 0)
    other = side >= 3 * width
    high = jnp.where(other, plane_total + plane - part * third, plane)
    low = jnp.where(other, side - 3 * width + part * width, side)
    return high, low, plane_total + third, 3 * width


def unfold_moved(table, q, plane_total, side_total, put):
    width, third = side_total // 4, plane_total // 3
    rows = plane_total + third
    put(0, 0, table[pl.ds(q * rows, plane_total), 0 : 3 * width])
    for part in range(3):
        block = table[
            pl.ds(q * rows + plane_total, third), part * width : (part + 1) * width
        ]
        put(part * third, 3 * width, block)


def fold_inner(plane, side, plane_total, side_total):
    rows, width = plane_total * 5 // 6, side_total // 4
    part, rest = split_index(side, width)
    other = plane >= rows
    high = jnp.where(other, plane - rows + part * (plane_total - rows), plane)
    high = jnp.where(plane < plane_total, high, -1)
    low = jnp.where(other, side_total + rest, side)
    return high, low, rows, side_total + width


def unfold_inner(table, q, plane_total, side_total, put):
    rows, width = plane_total * 5 // 6, side_total // 4
    left = plane_total - rows
    put(0, 0, table[pl.ds(q * rows, rows), 0:side_total])
    for part in range(4):
        block = table[pl.ds(q * rows + part * left, left), side_total : side_total + width]
        put(rows, part * width, block)


def tracer_block(count, values, cells, group, first_row, block_rows, cells_side):
    rows = pl.ds(first_row, block_rows)
    lane_total = cells.shape[2]
    shape = (block_rows, lane_total)
    slot = (first_row + lax.broadcasted_iota(jnp.int32, shape, 0)) * lane_total
    slot = slot + lax.broadcasted_iota(jnp.int32, shape, 1)
    weight = jnp.where(slot < count, 0.5 + values[0, group, rows, :], jnp.float32(0.0))
    loads = [weight, weight * values[1, group, rows, :], weight * values[2, group, rows, :]]
    plane, side = split_index(cells[group, rows, :], cells_side)
    return loads, plane, side


def for_used_blocks(used, group_rows, block_rows, lane_total, late_copies, step):
    block_slots = block_rows * lane_total
    blocks = lax.div(used + (block_slots - 1), block_slots)
    blocks = jnp.clip(blocks, 1, group_rows // block_rows)

    def wait_late():
        for copy in late_copies:
            copy.wait()

    def repeat(index, carried):
        pl.when(index == 1)(wait_late)
        step(pl.multiple_of(index * block_rows, block_rows))
        return carried

    lax.fori_loop(0, blocks, repeat, 0)
    pl.when(blocks == 1)(wait_late)


VISCOSITY, VELOCITY, SOURCE, LINE_FIELDS = 0, 1, 4, 7


def composition_of(cell_sums, base):
    scale = 1.0 / (cell_sums[0] + PRIOR_WEIGHT)
    basalt_share, melt_share = cell_sums[1] * scale, cell_sums[2] * scale
    weakening = jnp.exp(CONTRAST_BASALT * basalt_share - CONTRAST_MELT * melt_share)
    return basalt_share, melt_share, base * weakening


def outward_row(t, cells_radial):
    return jnp.where(lax.axis_index("rad") == 0, t, cells_radial - 1 - t)


class Fetches:
    def __init__(self, semaphores):
        self.semaphores = semaphores
        self.copies = []

    def start(self, source, target):
        copy = pltpu.make_async_copy(source, target, self.semaphores.at[len(self.copies)])
        copy.start()
        self.copies.append(copy)

    def wait(self, first, last):
        for copy in self.copies[first:last]:
            copy.wait()


def has_partners():
    lateral, count = lax.axis_index("lat"), lax.axis_size("lat")
    odd = lax.rem(lateral, 2) == 1
    above, below = lateral + 1 < count, lateral > 0
    return jnp.logical_or(odd, above), jnp.where(odd, above, below)


def outgoing_kernel(
    block_rows,
    counts_hbm,
    values_hbm,
    cells_hbm,
    base_hbm,
    velocity_hbm,
    forcing_hbm,
    edge_ref,
    first_ref,
    second_ref,
    count_ref,
    values,
    cells,
    counts,
    base,
    velocity,
    forcing,
    moved_sums,
    semaphores,
):
    cells_lateral, cells_radial, cells_side = base_hbm.shape
    plane_total = cells_lateral * cells_radial
    moved_planes = MIGRATION_PLANES * cells_radial
    group_rows, lane_total = cells.shape[1:]

    fetches = Fetches(semaphores)
    fetches.start(counts_hbm, counts)
    part = pl.ds(0, block_rows)
    fetches.start(cells_hbm.at[:, part], cells.at[:, part])
    for q in range(3):
        fetches.start(values_hbm.at[q, :, part], values.at[q, :, part])
    part = pl.ds(block_rows, group_rows - block_rows)
    fetches.start(cells_hbm.at[:, part], cells.at[:, part])
    fetches.start(values_hbm.at[:, :, part], values.at[:, :, part])
    for upward in (0, 1):
        outer = pl.ds((cells_lateral - MIGRATION_PLANES) * upward, MIGRATION_PLANES)
        fetches.start(base_hbm.at[outer], base.at[upward])
        fetches.start(velocity_hbm.at[:, outer], velocity.at[upward])
        outermost = pl.ds((cells_lateral - 1) * upward, 1)
        fetches.start(forcing_hbm.at[:, outermost], forcing.at[upward])

    edge_ref[...] = jnp.zeros_like(edge_ref)
    moved_sums[...] = jnp.zeros_like(moved_sums)

    def step(first_row):
        def block_of(group):
            count = counts[0, 0, group]
            return tracer_block(count, values, cells, group, first_row, block_rows, cells_side)

        loads, plane, side = block_of(1)
        row = edge_row(plane, plane_total, moved_planes)
        edge_ref[...] = hot_product(
            edge_ref[...], loads, row, side, 2 * moved_planes, cells_side, CHUNK_ROWS
        )
        for slot, group in enumerate((0, 2)):
            loads, plane, side = block_of(group)
            if group == 0:
                plane = plane - (plane_total - moved_planes)
            table = fold_moved(plane, side, moved_planes, cells_side)
            moved_sums[slot] = hot_product(moved_sums[slot], loads, *table, CHUNK_ROWS)

    fetches.wait(0, 5)
    count_ref[...] = jnp.full(count_ref.shape, counts[0, 0, 1], jnp.int32).astype(jnp.float32)
    used = jnp.maximum(jnp.maximum(counts[0, 0, 0], counts[0, 0, 1]), counts[0, 0, 2])
    for_used_blocks(used, group_rows, block_rows, lane_total, fetches.copies[5:7], step)
    fetches.wait(7, None)

    starts, rows_total = payload_sections(cells_radial)
    unused = starts[4] + 3 * cells_radial

    def fill(payload, upward):
        for q in range(3):

            def put_moved(plane, column, block):
                height, width = block.shape
                rows = pl.ds(starts[0] + q * moved_planes + plane, height)
                payload[rows, column : column + width] = block

            unfold_moved(moved_sums.at[upward], q, moved_planes, cells_side, put_moved)
            payload[pl.ds(starts[1] + q * moved_planes, moved_planes), :] = edge_ref[
                pl.ds((2 * q + upward) * moved_planes, moved_planes), :
            ]
            for offset in range(MIGRATION_PLANES):
                row = starts[2] + q * moved_planes + offset * cells_radial
                payload[pl.ds(row, cells_radial), :] = velocity[upward, q, offset]
            row = starts[4] + q * cells_radial
            payload[pl.ds(row, cells_radial), :] = forcing[upward, q, 0]
        for offset in range(MIGRATION_PLANES):
            row = starts[3] + offset * cells_radial
            payload[pl.ds(row, cells_radial), :] = base[upward, offset]
        if unused < rows_total:
            payload[unused:, :] = jnp.zeros((rows_total - unused, cells_side), jnp.float32)

    odd = lax.rem(lax.axis_index("lat"), 2) == 1

    @pl.when(odd)
    def _():
        fill(first_ref, 0)
        fill(second_ref, 1)

    @pl.when(jnp.logical_not(odd))
    def _():
        fill(first_ref, 1)
        fill(second_ref, 0)

    for payload, exists in zip((first_ref, second_ref), has_partners()):

        @pl.when(jnp.logical_not(exists))
        def _():
            payload[...] = jnp.zeros_like(payload)


def inner_kernel(
    block_rows,
    count_ref,
    values_ref,
    cells_ref,
    base_hbm,
    velocity_hbm,
    forcing_hbm,
    composition_ref,
    lines_ref,
    outer_ref,
    table,
    sums,
    fields,
    base,
    velocity,
    forcing,
    semaphores,
):
    cells_lateral, cells_radial, cells_side = base.shape
    margin = MIGRATION_PLANES
    planes = cells_lateral + 2 * margin
    pitch = round_up(cells_radial, 8)
    moved_planes = margin * cells_radial
    inner = cells_lateral - 2 * margin
    inner_planes = inner * cells_radial
    group_rows, lane_total = cells_ref.shape[1:]
    fetches = Fetches(semaphores)
    fetches.start(velocity_hbm, velocity)
    fetches.start(forcing_hbm, forcing)
    fetches.start(base_hbm, base)
    table[...] = jnp.zeros_like(table)

    nothing = jnp.zeros((cells_radial, cells_side), jnp.float32)

    def put(field, plane, value):
        fields[field, pl.ds(plane * pitch, cells_radial), :] = value

    def lay_out(those):
        for field in those:
            for t in range(cells_radial):
                row = outward_row(t, cells_radial)
                lines_ref[field, t] = fields[field, pl.ds(row, planes, stride=pitch), :]

    def step(first_row):
        loads, plane, side = tracer_block(
            count, values_ref, cells_ref, 1, first_row, block_rows, cells_side
        )
        where = fold_inner(plane - moved_planes, side, inner_planes, cells_side)
        table[...] = hot_product(table[...], loads, *where, block_rows)

    count = jnp.max(count_ref[...]).astype(jnp.int32)
    for_used_blocks(count, group_rows, block_rows, lane_total, [], step)

    fetches.wait(0, None)
    for plane in range(planes):
        x = plane - margin
        own = 0 <= x < cells_lateral
        for q in range(3):
            put(VELOCITY + q, plane, velocity[q, x] if own else nothing)
        for q in range(2):
            put(SOURCE + q, plane, forcing[q, x] if own else nothing)
    late = VISCOSITY, SOURCE + 2
    lay_out(field for field in range(LINE_FIELDS) if field not in late)

    for q in range(3):

        def put_sums(plane, column, block):
            height, width = block.shape
            sums[q, pl.ds(plane, height), column : column + width] = block

        unfold_inner(table, q, inner_planes, cells_side, put_sums)
    for plane in range(planes):
        x = plane - 2 * margin
        viscosity, source = nothing, nothing
        if 0 <= x < inner:
            part = pl.ds(x * cells_radial, cells_radial)
            cell_sums = [sums[q, part, :] for q in range(3)]
            basalt_share, melt_share, viscosity = composition_of(cell_sums, base[x + margin])
            source = forcing[2, x + margin] - BUOYANCY * basalt_share
            composition_ref[0, x] = basalt_share
            composition_ref[1, x] = melt_share
        put(VISCOSITY, plane, viscosity)
        put(SOURCE + 2, plane, source)
    lay_out(late)
    for offset in range(margin):
        for place, x in ((offset, offset), (margin + offset, cells_lateral - margin + offset)):
            outer_ref[0, place] = base[x]
            outer_ref[1, place] = forcing[2, x]


BLOCK_ROWS = 32
CHUNK_ROWS = 2


def dense_tracers(tracer_values, tracer_cell):
    lane_total = 128
    return tracer_values.reshape(3, 3, -1, lane_total), tracer_cell.reshape(3, -1, lane_total)


def outgoing_sums(tracer_count, values, cells, base_viscosity, velocity, forcing):
    cells_lateral, cells_radial, cells_side = base_viscosity.shape
    moved_planes = MIGRATION_PLANES * cells_radial
    group_rows, lane_total = cells.shape[1:]
    block_rows = min(BLOCK_ROWS, group_rows // 2)
    _, payload_rows = payload_sections(cells_radial)
    hbm = pl.BlockSpec(memory_space=pltpu.HBM)
    vmem = pl.BlockSpec(memory_space=pltpu.VMEM)
    payload = jax.ShapeDtypeStruct((payload_rows, cells_side), jnp.float32)
    outer_planes = (MIGRATION_PLANES, cells_radial, cells_side)
    return pl.pallas_call(
        functools.partial(outgoing_kernel, block_rows),
        out_shape=(
            jax.ShapeDtypeStruct((6 * moved_planes, cells_side), jnp.float32),
            payload,
            payload,
            jax.ShapeDtypeStruct((8, lane_total), jnp.float32),
            jax.ShapeDtypeStruct(values.shape, jnp.float32),
            jax.ShapeDtypeStruct(cells.shape, jnp.int32),
        ),
        in_specs=[hbm] * 6,
        out_specs=(vmem,) * 6,
        scratch_shapes=[
            pltpu.SMEM(tracer_count.shape, jnp.int32),
            pltpu.VMEM((2,) + outer_planes, jnp.float32),
            pltpu.VMEM((2, 3) + outer_planes, jnp.float32),
            pltpu.VMEM((2, 3, 1, cells_radial, cells_side), jnp.float32),
            pltpu.VMEM((2, 4 * moved_planes, cells_side * 3 // 4), jnp.float32),
            pltpu.SemaphoreType.DMA((13,)),
        ],
        compiler_params=pltpu.CompilerParams(vmem_limit_bytes=32 * 2**20),
        cost_estimate=pl.CostEstimate(
            flops=30 * group_rows * lane_total * moved_planes * cells_side,
            bytes_accessed=4 * (values.size + cells.size),
            transcendentals=0,
        ),
        name="outgoing_sums",
    )(
        *(
            pltpu.with_memory_space_constraint(array, pltpu.HBM)
            for array in (tracer_count, values, cells, base_viscosity, velocity, forcing)
        )
    )


def inner_lines(count, values, cells, base_viscosity, velocity, forcing):
    cells_lateral, cells_radial, cells_side = base_viscosity.shape
    planes = cells_lateral + 2 * MIGRATION_PLANES
    inner = cells_lateral - 2 * MIGRATION_PLANES
    inner_planes = inner * cells_radial
    group_rows, lane_total = cells.shape[1:]
    block_rows = min(BLOCK_ROWS, group_rows // 2)
    vmem = pl.BlockSpec(memory_space=pltpu.VMEM)
    return pl.pallas_call(
        functools.partial(inner_kernel, block_rows),
        out_shape=(
            jax.ShapeDtypeStruct((2, inner, cells_radial, cells_side), jnp.float32),
            jax.ShapeDtypeStruct((LINE_FIELDS, cells_radial, planes, cells_side), jnp.float32),
            jax.ShapeDtypeStruct(
                (2, 2 * MIGRATION_PLANES, cells_radial, cells_side), jnp.float32
            ),
        ),
        in_specs=[vmem] * 3 + [pl.BlockSpec(memory_space=pltpu.HBM)] * 3,
        out_specs=(vmem,) * 3,
        scratch_shapes=[
            pltpu.VMEM((3 * (inner_planes * 5 // 6), cells_side * 5 // 4), jnp.float32),
            pltpu.VMEM((3, inner_planes, cells_side), jnp.float32),
            pltpu.VMEM((LINE_FIELDS, planes * round_up(cells_radial, 8), cells_side), jnp.float32),
            pltpu.VMEM(base_viscosity.shape, jnp.float32),
            pltpu.VMEM(velocity.shape, jnp.float32),
            pltpu.VMEM(forcing.shape, jnp.float32),
            pltpu.SemaphoreType.DMA((3,)),
        ],
        compiler_params=pltpu.CompilerParams(vmem_limit_bytes=32 * 2**20),
        cost_estimate=pl.CostEstimate(
            flops=6 * group_rows * lane_total * inner * cells_radial * cells_side,
            bytes_accessed=4 * (values.size + cells.size),
            transcendentals=0,
        ),
        name="inner_lines",
    )(
        count,
        values,
        cells,
        *(
            pltpu.with_memory_space_constraint(array, pltpu.HBM)
            for array in (base_viscosity, velocity, forcing)
        ),
    )


def pair_swaps(first, second):
    count = lax.axis_size("lat")
    received = []
    for payload, start in ((second, 1), (first, 0)):
        target = list(range(count))
        for low in range(start, count - 1, 2):
            target[low], target[low + 1] = low + 1, low
        received.append(lax.ppermute(payload, "lat", list(enumerate(target))))
    return received[::-1]


def shift_planes(block, step):
    return pltpu.roll(block, step % block.shape[0], 0)


def shift_side(block, step):
    return pltpu.roll(block, step % block.shape[1], 1)


def neighbours(block):
    return (
        shift_planes(block, 1),
        shift_planes(block, -1),
        shift_side(block, 1),
        shift_side(block, -1),
    )


def inside_side(values):
    lane = lax.broadcasted_iota(jnp.int32, values[2].shape, 1)
    lower = jnp.where(lane > 0, values[2], 0.0)
    upper = jnp.where(lane < lane.shape[1] - 1, values[3], 0.0)
    return values[0], values[1], lower, upper


def total_of(terms):
    result = terms[0]
    for term in terms[1:]:
        result = result + term
    return result


def inside_grid(shape, margin, cells_lateral):
    plane = lax.broadcasted_iota(jnp.int32, shape, 0)
    lateral = lax.axis_index("lat")
    first = jnp.where(lateral == 0, margin, 1)
    last = jnp.where(lateral == lax.axis_size("lat") - 1, margin + cells_lateral, shape[0] - 1)
    return (plane >= first) & (plane < last)


LONG_FIELDS, SHORT_FIELDS = 5, 7


def message_rows(cells_lateral):
    planes = cells_lateral + 2 * MIGRATION_PLANES
    return round_up(LONG_FIELDS * planes + SHORT_FIELDS * cells_lateral + MIGRATION_PLANES, 8)


def message_part(cells_lateral, field):
    planes = cells_lateral + 2 * MIGRATION_PLANES
    if field < LONG_FIELDS:
        return pl.ds(field * planes, planes), 0, planes
    first = LONG_FIELDS * planes + (field - LONG_FIELDS) * cells_lateral
    return pl.ds(first, cells_lateral), MIGRATION_PLANES, cells_lateral


def solve_lines(radial, cells_radial, valid, keep, keep_part):
    last = cells_radial - 1
    viscosity = [radial(VISCOSITY, t) for t in range(cells_radial)]
    lateral_faces, lateral_sums = [], []
    for here in viscosity:
        faces = [LATERAL * 0.5 * (here + there) for there in inside_side(neighbours(here))]
        lateral_sums.append(total_of(faces))
        lateral_faces.append(inside_side(faces))
    radial_faces = [RADIAL * 0.5 * viscosity[0]] + [
        RADIAL * 0.5 * (viscosity[t - 1] + viscosity[t]) for t in range(1, cells_radial)
    ]

    excess = lateral_sums[0] + radial_faces[0]
    inverse, coupling = [], []
    for t in range(last):
        inverse.append(1.0 / (excess + radial_faces[t + 1]))
        coupling.append(radial_faces[t + 1] * inverse[t])
        excess = lateral_sums[t + 1] + coupling[t] * excess

    def lateral_terms(t, around):
        return [face * there for face, there in zip(lateral_faces[t], around)]

    def forward(right_side):
        eliminated = [right_side[0]]
        for t in range(1, cells_radial):
            eliminated.append(right_side[t] + coupling[t - 1] * eliminated[t - 1])
        return eliminated

    def backward(eliminated):
        solved = [jnp.zeros_like(excess)]
        for t in range(last - 1, -1, -1):
            solved.append(eliminated[t] * inverse[t] + coupling[t] * solved[-1])
        return solved[::-1]

    response = [jnp.ones_like(excess)]
    for t in range(last - 1, -1, -1):
        response.append(coupling[t] * response[-1])
    response = response[::-1]

    def finish(part, eliminated):
        keep(LONG_FIELDS + part, eliminated[last])
        for t, value in enumerate(eliminated[:last]):
            keep_part(part, t, value)

    keep(0, viscosity[last])
    keep(1, excess)
    for q in range(3):
        source = [radial(SOURCE + q, t) for t in range(cells_radial)]
        eliminated = forward(
            [
                total_of([source[t]] + lateral_terms(t, neighbours(radial(VELOCITY + q, t))))
                for t in range(cells_radial)
            ]
        )
        keep(2 + q, eliminated[last])
        particular = [jnp.where(valid, value, 0.0) for value in backward(eliminated)]
        finish(
            q,
            forward(
                [
                    total_of([source[t]] + lateral_terms(t, neighbours(particular[t])))
                    for t in range(cells_radial)
                ]
            ),
        )
    around = [neighbours(jnp.where(valid, value, 0.0)) for value in response]
    for side in range(4):
        finish(
            3 + side,
            forward([lateral_faces[t][side] * around[t][side] for t in range(cells_radial)]),
        )
    for t in range(last):
        keep_part(SHORT_FIELDS, t, inverse[t])
        keep_part(SHORT_FIELDS + 1, t, coupling[t])


def eliminate_kernel(
    inner_ref,
    lines_ref,
    edge_ref,
    second_ref,
    first_ref,
    from_second_ref,
    from_first_ref,
    outer_ref,
    composition_ref,
    mine_ref,
    message_ref,
    parts_ref,
    fields,
):
    _, cells_lateral, cells_radial, cells_side = composition_ref.shape
    margin = MIGRATION_PLANES
    planes = cells_lateral + 2 * margin
    pitch = round_up(cells_radial, 8)
    moved_planes = margin * cells_radial
    starts, _ = payload_sections(cells_radial)
    odd = lax.rem(lax.axis_index("lat"), 2) == 1

    def sent(upward, start):
        part = pl.ds(start, cells_radial)
        mine_first = odd if not upward else jnp.logical_not(odd)
        return jnp.where(mine_first, first_ref[part, :], second_ref[part, :])

    def arrived(from_above, start):
        part = pl.ds(start, cells_radial)
        is_first = odd if not from_above else jnp.logical_not(odd)
        return jnp.where(is_first, from_first_ref[part, :], from_second_ref[part, :])

    outer = 2 * margin

    def put(field, slot, value):
        fields[field, pl.ds(slot * pitch, cells_radial), :] = value

    for above in (False, True):
        for offset in range(margin):
            shift = offset * cells_radial
            halo = offset + (outer + margin if above else 0)
            own = offset + (outer if above else margin)
            x = offset + (cells_lateral - margin if above else 0)
            place = offset + (margin if above else 0)
            halo_sums, own_sums = [], []
            for q in range(3):
                row = q * moved_planes + shift
                rows = pl.ds((2 * q + int(above)) * moved_planes + shift, cells_radial)
                own_sums.append(edge_ref[rows, :] + arrived(above, starts[0] + row))
                halo_sums.append(sent(above, starts[0] + row) + arrived(above, starts[1] + row))
                put(VELOCITY + q, halo, arrived(above, starts[2] + row))
            basalt_share, melt_share, viscosity = composition_of(own_sums, outer_ref[0, place])
            composition_ref[0, x] = basalt_share
            composition_ref[1, x] = melt_share
            put(VISCOSITY, own, viscosity)
            put(SOURCE + 2, own, outer_ref[1, place] - BUOYANCY * basalt_share)
            basalt_share, _, viscosity = composition_of(
                halo_sums, arrived(above, starts[3] + shift)
            )
            put(VISCOSITY, halo, viscosity)
            beside = offset == (0 if above else margin - 1)
            for q in range(3):
                source = jnp.zeros_like(viscosity)
                if beside:
                    source = arrived(above, starts[4] + q * cells_radial)
                    if q == 2:
                        source = source - BUOYANCY * basalt_share
                put(SOURCE + q, halo, source)
    for x in range(margin, cells_lateral - margin):
        for q in range(2):
            composition_ref[q, x] = inner_ref[q, x - margin]

    def radial(field, t):
        replaced = outer if field in (VISCOSITY, SOURCE + 2) else margin
        plane = lax.broadcasted_iota(jnp.int32, (planes, cells_side), 0)
        own = (plane >= replaced) & (plane < planes - replaced)
        row = outward_row(t, cells_radial)
        edges = fields[field, pl.ds(row, 2 * outer, stride=pitch), :]
        if 2 * outer * 2 == planes:
            edges = jnp.concatenate([edges, edges], 0)
        else:
            gap = jnp.zeros((planes - 2 * outer, cells_side), jnp.float32)
            edges = jnp.concatenate([edges[:outer], gap, edges[outer:]], 0)
        return jnp.where(own, lines_ref[field, t], edges)

    unused = LONG_FIELDS * planes + SHORT_FIELDS * cells_lateral
    if unused < message_ref.shape[0]:
        message_ref[unused:, :] = jnp.zeros((message_ref.shape[0] - unused, cells_side), jnp.float32)

    def keep(field, value):
        rows, first, count = message_part(cells_lateral, field)
        mine_ref[field] = value
        message_ref[rows, :] = value[first : first + count]

    def keep_part(part, t, value):
        parts_ref[part, t] = value

    valid = inside_grid((planes, cells_side), margin, cells_lateral)
    solve_lines(radial, cells_radial, valid, keep, keep_part)


def eliminate(inner, lines, outer, edge, sent, received, cells_lateral):
    cells_radial, cells_side = inner.shape[2:]
    planes = cells_lateral + 2 * MIGRATION_PLANES
    vmem = pl.BlockSpec(memory_space=pltpu.VMEM)
    line = (planes, cells_side)
    return pl.pallas_call(
        eliminate_kernel,
        out_shape=(
            jax.ShapeDtypeStruct((2, cells_lateral, cells_radial, cells_side), jnp.float32),
            jax.ShapeDtypeStruct((LONG_FIELDS + SHORT_FIELDS,) + line, jnp.float32),
            jax.ShapeDtypeStruct((message_rows(cells_lateral), cells_side), jnp.float32),
            jax.ShapeDtypeStruct((SHORT_FIELDS + 2, cells_radial - 1) + line, jnp.float32),
        ),
        in_specs=[vmem] * 8,
        out_specs=(vmem,) * 4,
        scratch_shapes=[
            pltpu.VMEM(
                (LINE_FIELDS, 4 * MIGRATION_PLANES * round_up(cells_radial, 8), cells_side),
                jnp.float32,
            )
        ],
        compiler_params=pltpu.CompilerParams(vmem_limit_bytes=32 * 2**20),
        name="eliminate",
    )(inner, lines, edge, *sent[::-1], *received[::-1], outer)


def join_kernel(mine_ref, message_ref, parts_ref, smoothed_hbm, smoothed, lines, semaphores):
    _, cells_lateral, cells_radial, cells_side = smoothed.shape
    margin = MIGRATION_PLANES
    planes = cells_lateral + 2 * margin
    pitch = round_up(cells_radial, 8)
    valid = inside_grid((planes, cells_side), margin, cells_lateral)

    def mine(field):
        return mine_ref[field]

    def other(field):
        rows, first, _ = message_part(cells_lateral, field)
        return message_ref[pl.ds(rows.start - first, planes), :]

    face = RADIAL * 0.5 * (mine(0) + other(0))
    excess, other_excess = mine(1), other(1)
    scale = 1.0 / (excess * other_excess + face * (excess + other_excess))
    own_weight = (other_excess + face) * scale
    other_weight = (excess + face) * scale
    cross = face * scale

    def second_right(field_of, q, around):
        terms = [field_of(LONG_FIELDS + 3 + side) * there for side, there in enumerate(around)]
        return total_of([field_of(LONG_FIELDS + q)] + terms)

    fetches = Fetches(semaphores)
    for q in range(3):
        right, other_right = mine(2 + q), other(2 + q)
        own = jnp.where(valid, own_weight * right + cross * other_right, 0.0)
        beyond = jnp.where(valid, other_weight * other_right + cross * right, 0.0)
        around = neighbours(own)
        right = second_right(mine, q, around)
        other_right = second_right(other, q, neighbours(beyond))
        value = own_weight * right + cross * other_right
        for t in range(cells_radial - 1, -1, -1):
            if t < cells_radial - 1:
                terms = [parts_ref[3 + side, t] * there for side, there in enumerate(around)]
                right = total_of([parts_ref[q, t]] + terms)
                value = right * parts_ref[SHORT_FIELDS, t] + parts_ref[SHORT_FIELDS + 1, t] * value
            row = outward_row(t, cells_radial)
            lines[q, pl.ds(row, cells_lateral, stride=pitch), :] = value[
                margin : margin + cells_lateral
            ]
        for x in range(cells_lateral):
            smoothed[q, x] = lines[q, pl.ds(x * pitch, cells_radial), :]
        fetches.start(smoothed.at[q], smoothed_hbm.at[q])
    fetches.wait(0, None)


def join(mine, message, parts, like):
    cells_lateral, cells_radial, cells_side = like.shape[1:]
    vmem = pl.BlockSpec(memory_space=pltpu.VMEM)
    return pl.pallas_call(
        join_kernel,
        out_shape=jax.ShapeDtypeStruct(like.shape, jnp.float32),
        in_specs=[vmem] * 3,
        out_specs=pl.BlockSpec(memory_space=pltpu.HBM),
        scratch_shapes=[
            pltpu.VMEM(like.shape, jnp.float32),
            pltpu.VMEM((3, cells_lateral * round_up(cells_radial, 8), cells_side), jnp.float32),
            pltpu.SemaphoreType.DMA((3,)),
        ],
        compiler_params=pltpu.CompilerParams(vmem_limit_bytes=32 * 2**20),
        name="join",
    )(mine, message, parts)


def extended(block, sides, width):
    for axis, dim in sides:
        count = lax.axis_size(axis)
        forward = [(i, i + 1) for i in range(count - 1)]
        backward = [(target, source) for source, target in forward]
        low = lax.ppermute(
            lax.slice_in_dim(block, block.shape[dim] - width, None, axis=dim), axis, forward
        )
        high = lax.ppermute(lax.slice_in_dim(block, 0, width, axis=dim), axis, backward)
        block = jnp.concatenate([low, block, high], axis=dim)
    return block


def block_factor(diagonal, lower_band, upper_band):
    pivots = []
    upper_scaled = []
    for row_index in range(diagonal.shape[1]):
        if row_index == 0:
            pivot_row = diagonal[:, 0]
        else:
            pivot_row = diagonal[:, row_index] - lower_band[:, row_index] * upper_scaled[-1]
        pivots.append(pivot_row)
        upper_scaled.append(upper_band[:, row_index] / pivot_row)
    return (pivots, upper_scaled)


def block_solve(pivots, upper_scaled, lower_band, right_side):
    row_total = len(pivots)
    modified = []
    for row_index in range(row_total):
        if row_index == 0:
            value_row = right_side[:, :, 0] / pivots[0]
        else:
            value_row = (
                right_side[:, :, row_index] - lower_band[:, row_index] * modified[-1]
            ) / pivots[row_index]
        modified.append(value_row)
    solved = [modified[-1]]
    for row_index in range(row_total - 2, -1, -1):
        solved.append(modified[row_index] - upper_scaled[row_index] * solved[-1])
    ordered = solved[::-1]
    return jnp.stack(ordered, 2)


def interface_solve(coefficients):
    column_total = coefficients.shape[2]

    def forward(carried, inputs):
        offset, carried_slope = carried
        left_first, right_first, left_last, right_last, free_first, free_last = inputs
        divisor = 1.0 - left_first * carried_slope
        first_fixed = (free_first + left_first * offset) / divisor
        first_slope = right_first / divisor
        next_offset = free_last + left_last * (offset + carried_slope * first_fixed)
        next_slope = left_last * carried_slope * first_slope + right_last
        return ((next_offset, next_slope), (first_fixed, first_slope, next_offset, next_slope))

    start_state = (
        jnp.zeros((3, column_total), jnp.float32),
        jnp.zeros((column_total,), jnp.float32),
    )
    scan_inputs = (
        coefficients[:, 0],
        coefficients[:, 1],
        coefficients[:, 2],
        coefficients[:, 3],
        coefficients[:, 4:7],
        coefficients[:, 7:10],
    )
    final_state, eliminated = lax.scan(forward, start_state, scan_inputs)

    def backward(first_next, inputs):
        fixed_first, slope_first, fixed_last, slope_last = inputs
        first_value = fixed_first + slope_first * first_next
        last_value = fixed_last + slope_last * first_next
        return (first_value, (first_value, last_value))

    final_first, values_pair = lax.scan(
        backward, jnp.zeros((3, column_total), jnp.float32), eliminated, reverse=True
    )
    first_values, last_values = values_pair
    nothing_row = jnp.zeros((1, 3, column_total), jnp.float32)
    from_below = jnp.concatenate([nothing_row, last_values[:-1]], 0)
    from_above = jnp.concatenate([first_values[1:], nothing_row], 0)
    return jnp.concatenate([from_below, from_above], 1)


def reduced_boundary(interface):
    gathered = lax.all_gather(interface, "rad", axis=0, tiled=True)
    solved = interface_solve(gathered)
    return lax.dynamic_index_in_dim(solved, lax.axis_index("rad"), 0, keepdims=False)


def many_blocks(values, cells, count, edge, received, base_viscosity, velocity, forcing):
    cells_lateral, cells_radial, cells_side = base_viscosity.shape
    moved_rows = MIGRATION_PLANES * cells_radial
    odd = lax.rem(lax.axis_index("lat"), 2) == 1
    from_below = jnp.where(odd, received[0], received[1])[: 3 * moved_rows]
    from_above = jnp.where(odd, received[1], received[0])[: 3 * moved_rows]
    edge = edge.reshape(3, 2, moved_rows, cells_side)
    below = edge[:, 0] + from_below.reshape(3, moved_rows, cells_side)
    above = edge[:, 1] + from_above.reshape(3, moved_rows, cells_side)
    shares = [
        (sums[1:] / (sums[0] + PRIOR_WEIGHT)).reshape(2, -1, cells_radial, cells_side)
        for sums in (below, above)
    ]
    inner, _, _ = inner_lines(count, values, cells, base_viscosity, velocity, forcing)
    basalt_share, melt_share = jnp.concatenate([shares[0], inner, shares[1]], 1)
    viscosity = base_viscosity * jnp.exp(
        CONTRAST_BASALT * basalt_share - CONTRAST_MELT * melt_share
    )
    viscosity_pad = extended(viscosity, (("lat", 0), ("rad", 1)), 1)
    side_pad = jnp.pad(viscosity, ((0, 0), (0, 0), (1, 1)))
    face_west = LATERAL * 0.5 * (viscosity + viscosity_pad[:-2, 1:-1])
    face_east = LATERAL * 0.5 * (viscosity + viscosity_pad[2:, 1:-1])
    face_south = LATERAL * 0.5 * (viscosity + side_pad[:, :, :-2])
    face_north = LATERAL * 0.5 * (viscosity + side_pad[:, :, 2:])
    face_below = RADIAL * 0.5 * (viscosity + viscosity_pad[1:-1, :-2])
    face_above = RADIAL * 0.5 * (viscosity + viscosity_pad[1:-1, 2:])
    diagonal = face_west + face_east + face_south + face_north + face_below + face_above
    source = jnp.concatenate([forcing[:2], (forcing[2] - BUOYANCY * basalt_share)[None]], 0)
    lower_band = -face_below
    upper_band = -face_above
    pivots, upper_scaled = block_factor(diagonal, lower_band, upper_band)
    radial_iota = lax.broadcasted_iota(jnp.int32, viscosity.shape, 1)
    response_side = jnp.stack(
        [
            jnp.where(radial_iota == 0, face_below, jnp.float32(0.0)),
            jnp.where(radial_iota == cells_radial - 1, face_above, jnp.float32(0.0)),
        ]
    )
    response = block_solve(pivots, upper_scaled, lower_band, response_side)
    current = velocity
    for sweep_index in range(SWEEPS):
        velocity_pad = extended(current, (("lat", 1),), 1)
        side_velocity = jnp.pad(current, ((0, 0), (0, 0), (0, 0), (1, 1)))
        right_side = (
            source
            + face_west * velocity_pad[:, :-2]
            + face_east * velocity_pad[:, 2:]
            + face_south * side_velocity[..., :-2]
            + face_north * side_velocity[..., 2:]
        )
        particular = block_solve(pivots, upper_scaled, lower_band, right_side)
        interface = jnp.concatenate(
            [response[:, :, 0], response[:, :, -1], particular[:, :, 0], particular[:, :, -1]], 0
        )
        interface = interface.reshape(1, 10, cells_lateral * cells_side)
        boundary = reduced_boundary(interface).reshape(6, cells_lateral, 1, cells_side)
        current = particular + response[0][None] * boundary[:3] + response[1][None] * boundary[3:]
    composition = jnp.stack([basalt_share, melt_share])
    return (current, composition)

def local(tracer_values, tracer_cell, tracer_count, base_viscosity, velocity, forcing):
    values, cells = dense_tracers(tracer_values, tracer_cell)
    edge, first, second, count, values, cells = outgoing_sums(
        tracer_count, values, cells, base_viscosity, velocity, forcing
    )
    sent = first, second
    received = pair_swaps(first, second)
    if lax.axis_size("rad") != 2:
        return many_blocks(
            values, cells, count, edge, received, base_viscosity, velocity, forcing
        )
    inner, lines, outer = inner_lines(count, values, cells, base_viscosity, velocity, forcing)
    composition, mine, message, parts = eliminate(
        inner, lines, outer, edge, sent, received, base_viscosity.shape[0]
    )
    other = lax.ppermute(message, "rad", [(0, 1), (1, 0)])
    return join(mine, other, parts, velocity), composition


def solution(mesh):
    return jax.shard_map(
        local,
        mesh=mesh,
        in_specs=(
            P("lat", "rad", None, None),
            P("lat", "rad", None),
            P("lat", "rad", None),
            P("lat", "rad", None),
            P(None, "lat", "rad", None),
            P(None, "lat", "rad", None),
        ),
        out_specs=(P(None, "lat", "rad", None), P(None, "lat", "rad", None)),
        check_vma=False,
    )
```
